32 devices in a mesh: ctx: 2 (over y), tile: 4 (over z), mp: 4 (over x, core).
Axes of the slice: x: 2, y: 2, z: 4, core: 2. Of those that a mesh axis runs over, the one named last changes fastest.
Arguments:
- text_embed: bfloat16 [2048, 4096], P('ctx', ('tile', 'mp')), may hold values from -6 to 6
- latents: bfloat16 [4, 64, 512], P('ctx', 'tile'), may hold values from -6 to 6
- down_conv: bfloat16 [72, 256], P(None, 'mp'), may hold values from -0.75 to 0.75
- patch_in: bfloat16 [4096, 4096], P(None, ('tile', 'mp')), may hold values from -0.09375 to 0.09375
- norm_gain: bfloat16 [4096], P(('tile', 'mp')), may hold values from 0.25 to 1.75
- query_weight: bfloat16 [4096, 4096], P(None, ('tile', 'mp')), may hold values from -0.09375 to 0.09375
- key_weight: bfloat16 [4096, 4096], P(None, ('tile', 'mp')), may hold values from -0.09375 to 0.09375
- value_weight: bfloat16 [4096, 4096], P(None, ('tile', 'mp')), may hold values from -0.09375 to 0.09375
- query_gain: float32 [128], replicated, may hold values from 0.5 to 6
- key_gain: float32 [128], replicated, may hold values from 0.5 to 6
- out_weight: bfloat16 [4096, 4096], P(None, ('tile', 'mp')), may hold values from -0.5 to 0.5
- patch_out: bfloat16 [4096, 4096], P(('tile', 'mp')), may hold values from -0.09375 to 0.09375
- up_conv: bfloat16 [2304, 8], replicated, may hold values from -0.125 to 0.125
- span_start: int32 [4], replicated, may hold values from 0 to 1792, as said below
- image_of_slot: int32 [4], replicated, may hold values from 0 to 3, each once
Outputs:
- layer_out: bfloat16 [2048, 4096], P('ctx', ('tile', 'mp'))
- noise_pred: float32 [4, 64, 512], P('ctx', 'tile')
The draws below stay inside these ranges and needn't reach their ends.
Inputs may be any that keep to these rules, and one draw needn't show every extreme that they name: `span_start`: sorted ascending; each image spans 256 positions, spans do not intersect, the first image starts the document and the last one ends it; spans may cross the boundaries between indices of ctx. `image_of_slot`: each image appears in exactly one slot.
All inputs are finite; a program needn't handle non-finite values.
Results may differ from the reference program's by a relative error of at most 0.04.
Values may be sent and summed in bfloat16 or wider, within the bound.
No kernel may reach another device: no remote copies, remote signals or barrier semaphores. Data moves between devices by JAX's collectives and lax.ppermute only.
A program may use at most 128 MiB of HBM per device.

```python
import jax
import jax.numpy as jnp
from jax import lax

D = 4096
HEADS = 32
HD = 128
CH = 256
CIN = 8
HL = 64
WL = 64
PATCH = 4
IMG_TOK = 256
NIMG = 4
TOKENS = 2048


def draw_span_start(key, part):
    key = jax.random.fold_in(key, 11)
    spare = TOKENS - NIMG * IMG_TOK
    weights = jax.random.randint(key, (NIMG - 1,), 1, 100, dtype=jnp.int32)
    gaps = spare * weights // jnp.sum(weights)
    gaps = gaps.at[NIMG - 2].add(spare - jnp.sum(gaps))
    leading = jnp.concatenate([jnp.zeros((1,), jnp.int32), jnp.cumsum(gaps).astype(jnp.int32)])
    return (leading + jnp.arange(NIMG, dtype=jnp.int32) * IMG_TOK).astype(jnp.int32)


def draw_query_gain(key, part):
    key = jax.random.fold_in(key, 21)
    return jax.random.uniform(key, (HD,), jnp.float32, 0.5, 2.5)


def draw_key_gain(key, part):
    key = jax.random.fold_in(key, 22)
    return jax.random.uniform(key, (HD,), jnp.float32, 0.5, 2.5)


def steps_of(key, dims, pieces, least, top_value):
    def one(dim, blocks):
        steps = jax.random.uniform(jax.random.fold_in(jax.random.fold_in(key, 6), dim), (blocks,), jnp.float32, least / len(pieces), top_value / len(pieces))
        return jnp.repeat(jnp.exp(steps), dims[dim] // blocks).reshape((-1,) + (1,) * (len(dims) - dim - 1))

    level = one(*pieces[0])
    for cut in pieces[1:]:
        level = level * one(*cut)
    return level


def normal_values(own_key, shape, width, limit, split=(), kind=jnp.bfloat16):
    entries = jax.random.normal(own_key, shape, jnp.float32) * width
    if len(split) > 0:
        entries = steps_of(own_key, shape, split, -0.22, 0.18) * entries
    return jnp.clip(entries, min=-limit, max=limit).astype(kind)


def setup_inputs(seed: int = 0) -> dict:
    keys = jax.random.split(jax.random.key(seed), 16)
    text_embed = normal_values(keys[0], (TOKENS, D), 1.0, 6.0, ((0, 2), (1, 16)))
    latents = normal_values(keys[1], (NIMG, HL, WL * CIN), 1.0, 6.0, ((0, 2), (1, 4)))
    down_conv = normal_values(keys[2], (9 * CIN, CH), (9 * CIN) ** -0.5, 0.75, ((1, 4),))
    patch_in = normal_values(keys[3], (PATCH * PATCH * CH, D), (PATCH * PATCH * CH) ** -0.5, 0.09375, ((1, 16),))
    norm_gain = jnp.clip(1.0 + 0.15 * jax.random.normal(keys[4], (D,), jnp.float32), 0.25, 1.75).astype(jnp.bfloat16)
    query_weight = normal_values(keys[5], (D, HEADS * HD), D ** -0.5, 0.09375, ((1, 16),))
    key_weight = normal_values(keys[6], (D, HEADS * HD), D ** -0.5, 0.09375, ((1, 16),))
    value_weight = normal_values(keys[7], (D, HEADS * HD), D ** -0.5, 0.09375, ((1, 16),))
    query_gain = draw_query_gain(jax.random.fold_in(keys[15], 71), 0)
    key_gain = draw_key_gain(jax.random.fold_in(keys[15], 71), 0)
    out_weight = normal_values(keys[10], (HEADS * HD, D), HD ** -0.5, 0.5, ((1, 16),))
    patch_out = normal_values(keys[11], (D, PATCH * PATCH * CH), D ** -0.5, 0.09375, ((0, 16),))
    up_conv = normal_values(keys[12], (9 * CH, CIN), (9 * CH) ** -0.5, 0.125)
    span_start = draw_span_start(jax.random.fold_in(keys[15], 71), 0)
    image_of_slot = jax.random.permutation(keys[14], NIMG).astype(jnp.int32)
    return {"text_embed": text_embed, "latents": latents, "down_conv": down_conv, "patch_in": patch_in, "norm_gain": norm_gain, "query_weight": query_weight, "key_weight": key_weight, "value_weight": value_weight, "query_gain": query_gain, "key_gain": key_gain, "out_weight": out_weight, "patch_out": patch_out, "up_conv": up_conv, "span_start": span_start, "image_of_slot": image_of_slot}


EPSILON = 1e-05
NEGATIVE_FILL = -1e+30

def rms_scale(values):
    return lax.rsqrt(lax.optimization_barrier(jnp.mean(values * values, axis=-1, keepdims=True)) + EPSILON)

def conv_same(image, weight):
    height, breadth = (image.shape[0], image.shape[1])
    padded = jnp.pad(image, ((1, 1), (1, 1), (0, 0)))
    taps = [padded[row_shift:row_shift + height, col_shift:col_shift + breadth, :] for row_shift in range(3) for col_shift in range(3)]
    stacked = jnp.concatenate(taps, axis=-1).reshape(height * breadth, -1)
    return jnp.dot(stacked, weight, preferred_element_type=jnp.float32).reshape(height, breadth, weight.shape[1])

def image_ids(positions, span_start):
    inside = (positions[:, None] >= span_start[None, :]) & (positions[:, None] < span_start[None, :] + IMG_TOK)
    numbers = jnp.arange(span_start.shape[0], dtype=jnp.int32)
    return (lax.optimization_barrier(jnp.sum(jnp.where(inside, numbers[None, :] + 1, 0), axis=1)) - 1).astype(jnp.int32)

def slot_lookup(image_of_slot):
    numbers = jnp.arange(image_of_slot.shape[0], dtype=jnp.int32)
    matches = image_of_slot[None, :] == numbers[:, None]
    return lax.optimization_barrier(jnp.sum(jnp.where(matches, numbers[None, :], 0), axis=1)).astype(jnp.int32)

def reference(text_embed, latents, down_conv, patch_in, norm_gain, query_weight, key_weight, value_weight, query_gain, key_gain, out_weight, patch_out, up_conv, span_start, image_of_slot):

    def down_block(latent):
        image = latent.reshape(HL, WL, CIN)
        activated = jax.nn.silu(conv_same(image, down_conv)).astype(jnp.bfloat16)
        patches = activated.reshape(HL // PATCH, PATCH, WL // PATCH, PATCH, CH).transpose(0, 2, 1, 3, 4)
        patches = patches.reshape(IMG_TOK, PATCH * PATCH * CH)
        return jnp.dot(patches, patch_in, preferred_element_type=jnp.float32).astype(jnp.bfloat16)
    image_tokens = lax.map(down_block, latents)
    positions = jnp.arange(TOKENS, dtype=jnp.int32)
    owners = image_ids(positions, span_start)
    safe_owner = jnp.maximum(owners, 0)
    slot_table = slot_lookup(image_of_slot)
    source_rows = slot_table[safe_owner] * IMG_TOK + positions - span_start[safe_owner]
    source_rows = jnp.clip(source_rows, 0, NIMG * IMG_TOK - 1).astype(jnp.int32)
    flat_tokens = image_tokens.reshape(NIMG * IMG_TOK, D)
    stream = jnp.where((owners >= 0)[:, None], flat_tokens[source_rows], text_embed)
    widened = stream.astype(jnp.float32)
    normed = (widened * rms_scale(widened) * norm_gain.astype(jnp.float32)).astype(jnp.bfloat16)
    visible = (positions[None, :] <= positions[:, None]) | (owners[None, :] == owners[:, None]) & (owners[:, None] >= 0)

    def one_head(head):
        first_col = head * HD
        query_cols = lax.dynamic_slice_in_dim(query_weight, first_col, HD, 1)
        key_cols = lax.dynamic_slice_in_dim(key_weight, first_col, HD, 1)
        value_cols = lax.dynamic_slice_in_dim(value_weight, first_col, HD, 1)
        query_raw = jnp.dot(normed, query_cols, preferred_element_type=jnp.float32)
        key_raw = jnp.dot(normed, key_cols, preferred_element_type=jnp.float32)
        value_raw = jnp.dot(normed, value_cols, preferred_element_type=jnp.float32)
        queries = (query_raw * rms_scale(query_raw) * query_gain * HD ** (-0.5)).astype(jnp.bfloat16)
        key_rows = (key_raw * rms_scale(key_raw) * key_gain * 1.0).astype(jnp.bfloat16)
        value_rows = value_raw.astype(jnp.bfloat16)
        scores = jnp.dot(queries, key_rows.T, preferred_element_type=jnp.float32)
        scores = jnp.where(visible, scores, NEGATIVE_FILL)
        row_top = lax.optimization_barrier(jnp.max(scores, axis=1, keepdims=True))
        weights = jnp.where(visible, jnp.exp(scores - row_top), 0.0)
        row_sum = lax.optimization_barrier(jnp.sum(weights, axis=1, keepdims=True))
        summed = jnp.dot(weights.astype(jnp.bfloat16), value_rows, preferred_element_type=jnp.float32)
        return (summed / row_sum).astype(jnp.bfloat16)
    heads_out = lax.map(one_head, jnp.arange(HEADS, dtype=jnp.int32))
    attended = heads_out.transpose(1, 0, 2).reshape(TOKENS, HEADS * HD)
    mixed = jnp.dot(attended, out_weight, preferred_element_type=jnp.float32)
    layer_out = (widened + mixed).astype(jnp.bfloat16)

    def up_block(slot):
        image = image_of_slot[slot]
        rows = lax.dynamic_slice_in_dim(layer_out, span_start[image], IMG_TOK, 0)
        projected = jax.nn.silu(jnp.dot(rows, patch_out, preferred_element_type=jnp.float32)).astype(jnp.bfloat16)
        pixels = projected.reshape(HL // PATCH, WL // PATCH, PATCH, PATCH, CH).transpose(0, 2, 1, 3, 4)
        pixels = pixels.reshape(HL, WL, CH)
        return conv_same(pixels, up_conv).reshape(HL, WL * CIN)
    noise_pred = lax.map(up_block, jnp.arange(NIMG, dtype=jnp.int32))
    return (layer_out, noise_pred)
```

```python
import functools

import jax
import jax.numpy as jnp
from jax import lax
from jax.experimental import pallas as pl
from jax.experimental.pallas import tpu as pltpu
from jax.sharding import Mesh
from jax.sharding import PartitionSpec as P

HD = 128
CH = 256
CIN = 8
WL = 64
HL = 64
PATCH = 4
PIX = PATCH * PATCH
SIDE = WL // PATCH
IMG_TOK = 256
EPSILON = 1e-05
NEGATIVE_FILL = -1e30
WINDOW = (PATCH + 2) * CIN
TAPS = 3 * WINDOW
BF16 = jnp.bfloat16
F32 = jnp.float32
VMEM_LIMIT = 48 * 1024 * 1024


def params(*semantics):
    return pltpu.CompilerParams(
        dimension_semantics=semantics or None, vmem_limit_bytes=VMEM_LIMIT
    )


def cost(flops, nbytes, transcendentals=0):
    return pl.CostEstimate(
        flops=int(flops), bytes_accessed=int(nbytes), transcendentals=int(transcendentals)
    )


def silu(values):
    return values / (1.0 + jnp.exp(-values))


def mxu(left, right):
    return jnp.dot(left, right, preferred_element_type=F32)


def swap(values):
    return lax.ppermute(values, "core", [(0, 1), (1, 0)])


def down_kernel(images, half, meta, rows_ref, conv_ref, patch_ref, text_ref, out_ref, windows, total):
    step = pl.program_id(0)
    group = images * SIDE

    @pl.when(step == 0)
    def _():
        for col in range(SIDE):
            for row in range(PATCH + 2):
                piece = rows_ref[row, :, PATCH * CIN * col : PATCH * CIN * col + WINDOW]
                for shift in range(3):
                    if 0 <= row - shift < PATCH:
                        windows[
                            row - shift,
                            group * col : group * (col + 1),
                            WINDOW * shift : WINDOW * (shift + 1),
                        ] = piece

    hidden = mxu(windows[step // PATCH], conv_ref[lax.rem(step, PATCH)])
    term = mxu(silu(hidden).astype(BF16), patch_ref[...])

    @pl.when(step == 0)
    def _():
        total[...] = term

    @pl.when(step > 0)
    def _():
        total[...] += term

    @pl.when(step == PIX - 1)
    def _():
        tokens = total[...].astype(BF16)
        first = meta[2 * images]
        core = meta[2 * images + 1]
        block = 256
        for part in range(2 * half // block):
            which = part * block // half
            base = first + jnp.where(which == 0, core, 1 - core) * half + part * block - which * half
            place = base + lax.broadcasted_iota(jnp.int32, (block, 1), 0)
            source = jnp.full((block, 1), -1, jnp.int32)
            for image in range(images):
                inner = place - meta[image]
                inside = (inner >= 0) & (inner < IMG_TOK)
                index = (inner & (SIDE - 1)) * group + meta[images + image] * SIDE + (inner >> 4)
                source = jnp.where(inside, index, source)
            choice = source == lax.broadcasted_iota(jnp.int32, (block, images * IMG_TOK), 1)
            picked = mxu(jnp.where(choice, 1.0, 0.0).astype(BF16), tokens).astype(BF16)
            at = part * block - which * half
            out_ref[which, at : at + block, :] = jnp.where(
                source >= 0, picked.astype(F32), text_ref[part * block : (part + 1) * block, :].astype(F32)
            ).astype(BF16)


def down_stream(meta, rows, conv, patch_in, text, images):
    seq_rows, width = text.shape
    half = seq_rows // 2
    count = images * IMG_TOK
    return pl.pallas_call(
        functools.partial(down_kernel, images, half),
        grid_spec=pltpu.PrefetchScalarGridSpec(
            num_scalar_prefetch=1,
            grid=(PIX,),
            in_specs=[
                pl.BlockSpec(rows.shape, lambda i, m: (0, 0, 0)),
                pl.BlockSpec(conv.shape, lambda i, m: (0, 0, 0)),
                pl.BlockSpec((CH, width), lambda i, m: (i, 0)),
                pl.BlockSpec((seq_rows, width), lambda i, m: (0, 0)),
            ],
            out_specs=pl.BlockSpec((2, half, width), lambda i, m: (0, 0, 0)),
            scratch_shapes=[
                pltpu.VMEM((PATCH, count, TAPS), BF16),
                pltpu.VMEM((count, width), F32),
            ],
        ),
        out_shape=jax.ShapeDtypeStruct((2, half, width), BF16),
        compiler_params=params("arbitrary"),
        cost_estimate=cost(2 * count * PIX * CH * (256 + width), 4 << 20, count * PIX * CH),
        name="down_stream",
    )(meta, rows, conv, patch_in, text)


def head_norm(raw, gain):
    heads = raw.shape[1] // HD
    parts = []
    for head in range(heads):
        part = raw[:, head * HD : (head + 1) * HD]
        scale = lax.rsqrt(jnp.mean(part * part, axis=-1, keepdims=True) + EPSILON)
        parts.append((part * scale * gain).astype(BF16))
    return jnp.concatenate(parts, axis=1) if heads > 1 else parts[0]


def qkv_kernel(blocks, meta, x_ref, gain_ref, weight_ref, gains_ref, kvp_ref, qp_ref, kvo_ref, qo_ref, normed):
    step = pl.program_id(0)
    core = meta[0]
    half, width = x_ref.shape[1], x_ref.shape[2]

    @pl.when(step == 0)
    def _():
        chunk = 64

        def one(index, carry):
            rows = pl.ds(pl.multiple_of(index * chunk, chunk), chunk)
            square = jnp.zeros((chunk, width), F32)
            for block in range(blocks):
                value = x_ref[block, rows, :].astype(F32)
                square = square + value * value
            scale = lax.rsqrt(
                jnp.sum(square, axis=-1, keepdims=True) * (1.0 / (blocks * width)) + EPSILON
            )
            for block in range(blocks):
                place = jnp.bitwise_xor(block, core)
                value = x_ref[block, rows, :].astype(F32) * scale
                value = value * gain_ref[place].astype(F32)
                normed[rows, pl.ds(pl.multiple_of(place * width, width), width)] = value.astype(BF16)
            return carry

        lax.fori_loop(0, half // chunk, one, 0)

    raw = mxu(normed[...], weight_ref[0])

    @pl.when(step == 0)
    def _():
        kvp_ref[0] = head_norm(raw, gains_ref[1:2, :])

    @pl.when(step == 1)
    def _():
        kvp_ref[0] = raw.astype(BF16)

    @pl.when(step == 2)
    def _():
        qp_ref[...] = head_norm(raw, gains_ref[0:1, :] * HD ** (-0.5))

    @pl.when(step == 3)
    def _():
        kvo_ref[0] = head_norm(raw, gains_ref[1:2, :])

    @pl.when(step == 4)
    def _():
        kvo_ref[0] = raw.astype(BF16)

    @pl.when(step == 5)
    def _():
        qo_ref[...] = head_norm(raw, gains_ref[0:1, :] * HD ** (-0.5))


def qkv(meta, x, gain, weights, gains):
    blocks, half, width = x.shape
    model = blocks * width
    return pl.pallas_call(
        functools.partial(qkv_kernel, blocks),
        grid_spec=pltpu.PrefetchScalarGridSpec(
            num_scalar_prefetch=1,
            grid=(6,),
            in_specs=[
                pl.BlockSpec(x.shape, lambda i, m: (0, 0, 0)),
                pl.BlockSpec(gain.shape, lambda i, m: (0, 0, 0)),
                pl.BlockSpec((1, model, width), lambda i, m: (i, 0, 0)),
                pl.BlockSpec(gains.shape, lambda i, m: (0, 0)),
            ],
            out_specs=[
                pl.BlockSpec((1, half, width), lambda i, m: (jnp.minimum(i, 1), 0, 0)),
                pl.BlockSpec((half, width), lambda i, m: (0, 0)),
                pl.BlockSpec((1, half, width), lambda i, m: (jnp.clip(i - 3, 0, 1), 0, 0)),
                pl.BlockSpec((half, width), lambda i, m: (0, 0)),
            ],
            scratch_shapes=[pltpu.VMEM((half, model), BF16)],
        ),
        out_shape=[
            jax.ShapeDtypeStruct((2, half, width), BF16),
            jax.ShapeDtypeStruct((half, width), BF16),
            jax.ShapeDtypeStruct((2, half, width), BF16),
            jax.ShapeDtypeStruct((half, width), BF16),
        ],
        compiler_params=params("arbitrary"),
        cost_estimate=cost(12 * half * model * width, 18 << 20),
        name="norm_qkv",
    )(meta, x, gain, weights, gains)


def attention_kernel(images, pieces, meta, q_ref, *refs):
    kv_refs, out_ref = refs[:pieces], refs[pieces]
    rows = q_ref.shape[0]
    place = meta[images] + pl.program_id(1) * rows + lax.broadcasted_iota(jnp.int32, (rows, 1), 0)
    limit = place
    for image in range(images):
        inner = place - meta[image]
        limit = jnp.where((inner >= 0) & (inner < IMG_TOK), meta[image] + IMG_TOK - 1, limit)
    query = q_ref[...]
    scores = []
    top = None
    for piece in range(pieces):
        key = kv_refs[piece][0]
        score = lax.dot_general(
            query, key, (((1,), (1,)), ((), ())), preferred_element_type=F32
        )
        position = meta[images + 1 + piece] + lax.broadcasted_iota(jnp.int32, score.shape, 1)
        score = jnp.where(position <= limit, score, NEGATIVE_FILL)
        scores.append(score)
        best = jnp.max(score, axis=1, keepdims=True)
        top = best if top is None else jnp.maximum(top, best)
    total = jnp.zeros((rows, 1), F32)
    product = jnp.zeros((rows, HD), F32)
    for piece in range(pieces):
        weight = jnp.exp(scores[piece] - top)
        total = total + jnp.sum(weight, axis=1, keepdims=True)
        product = product + mxu(weight.astype(BF16), kv_refs[piece][1])
    out_ref[...] = (product / total).astype(BF16)


def attention(meta, query, pieces, images):
    half, width = query.shape
    block = 256 if half % 256 == 0 else half
    keys = half * len(pieces)
    return pl.pallas_call(
        functools.partial(attention_kernel, images, len(pieces)),
        grid_spec=pltpu.PrefetchScalarGridSpec(
            num_scalar_prefetch=1,
            grid=(width // HD, half // block),
            in_specs=[pl.BlockSpec((block, HD), lambda h, i, m: (i, h))]
            + [pl.BlockSpec((2, half, HD), lambda h, i, m: (0, 0, h)) for _ in pieces],
            out_specs=pl.BlockSpec((block, HD), lambda h, i, m: (i, h)),
        ),
        out_shape=jax.ShapeDtypeStruct((half, width), BF16),
        compiler_params=params("arbitrary", "arbitrary"),
        cost_estimate=cost(4 * half * keys * width, 4 * keys * width, half * keys * width // HD),
        name="attention",
    )(meta, query, *pieces)


def out_kernel(steps, meta, att_ref, own_w, par_w, own_s, par_s, par_out, own_out, own_t, par_t):
    step = pl.program_id(0)
    core = meta[0]
    blocks, half, width = att_ref.shape
    for weight_ref, stream_ref, total in ((par_w, par_s, par_t), (own_w, own_s, own_t)):
        @pl.when(step == 0)
        def _():
            total[...] = stream_ref[...].astype(F32)

        term = None
        for block in range(blocks):
            place = jnp.bitwise_xor(block, core)
            one = mxu(
                att_ref[block], weight_ref[pl.ds(pl.multiple_of(place * width, width), width), :]
            )
            term = one if term is None else term + one
        total[...] += term

    @pl.when(step == steps - 1)
    def _():
        par_out[...] = par_t[...].astype(BF16)
        own_out[...] = own_t[...].astype(BF16)


def out_project(meta, attended, own_w, par_w, own_s, par_s):
    blocks, half, width = attended.shape
    steps = 4
    deep = blocks // steps
    shape = jax.ShapeDtypeStruct((half, width), BF16)
    whole = pl.BlockSpec((half, width), lambda i, m: (0, 0))
    weight = pl.BlockSpec((deep * width, width), lambda i, m: (i, 0))
    return pl.pallas_call(
        functools.partial(out_kernel, steps),
        grid_spec=pltpu.PrefetchScalarGridSpec(
            num_scalar_prefetch=1,
            grid=(steps,),
            in_specs=[
                pl.BlockSpec((deep, half, width), lambda i, m: (i, 0, 0)),
                weight,
                weight,
                whole,
                whole,
            ],
            out_specs=[whole, whole],
            scratch_shapes=[pltpu.VMEM((half, width), F32), pltpu.VMEM((half, width), F32)],
        ),
        out_shape=[shape, shape],
        compiler_params=params("arbitrary"),
        cost_estimate=cost(4 * half * blocks * width * width, 9 << 20),
        name="out_project",
    )(meta, attended, own_w, par_w, own_s, par_s)


def pick_kernel(targets, meta, own_ref, par_ref, out_ref):
    half = own_ref.shape[0]
    own_base, par_base = meta[targets], meta[targets + 1]
    for target in range(targets):
        place = meta[target] + lax.broadcasted_iota(jnp.int32, (IMG_TOK, half), 0)
        column = lax.broadcasted_iota(jnp.int32, (IMG_TOK, half), 1)
        own = jnp.where(place == column + own_base, 1.0, 0.0).astype(BF16)
        par = jnp.where(place == column + par_base, 1.0, 0.0).astype(BF16)
        out_ref[target] = (mxu(own, own_ref[...]) + mxu(par, par_ref[...])).astype(BF16)


def pick_rows(meta, own, par, targets):
    half, width = own.shape
    whole = pl.BlockSpec((half, width), lambda i, m: (0, 0))
    return pl.pallas_call(
        functools.partial(pick_kernel, targets),
        grid_spec=pltpu.PrefetchScalarGridSpec(
            num_scalar_prefetch=1,
            grid=(1,),
            in_specs=[whole, whole],
            out_specs=pl.BlockSpec((targets, IMG_TOK, width), lambda i, m: (0, 0, 0)),
        ),
        out_shape=jax.ShapeDtypeStruct((targets, IMG_TOK, width), BF16),
        compiler_params=params("arbitrary"),
        cost_estimate=cost(targets * 4 * IMG_TOK * half * width, 1 << 20),
        name="pick_rows",
    )(meta, own, par)


def up_kernel(count, *refs):
    own_refs, par_refs = refs[:count], refs[count : 2 * count]
    own_w, par_w, out_ref = refs[2 * count :]

    def merged(parts):
        total = parts[0][...].astype(F32)
        for part in parts[1:]:
            total = total + part[...].astype(F32)
        return total.astype(BF16)

    out_ref[0] = (mxu(merged(own_refs), own_w[...]) + mxu(merged(par_refs), par_w[...])).astype(BF16)


def up_project(own_parts, par_parts, own_w, par_w, groups):
    width, features = own_w.shape
    deep = features // groups
    part = pl.BlockSpec((IMG_TOK, width), lambda i: (0, 0))
    weight = pl.BlockSpec((width, deep), lambda i: (0, i))
    return pl.pallas_call(
        functools.partial(up_kernel, len(own_parts)),
        grid=(groups,),
        in_specs=[part] * (len(own_parts) + len(par_parts)) + [weight, weight],
        out_specs=pl.BlockSpec((1, IMG_TOK, deep), lambda i: (i, 0, 0)),
        out_shape=jax.ShapeDtypeStruct((groups, IMG_TOK, deep), BF16),
        compiler_params=params("arbitrary"),
        cost_estimate=cost(4 * IMG_TOK * width * features, 6 << 20),
        name="up_project",
    )(*own_parts, *par_parts, own_w, par_w)


def spread_kernel(rows_ref, spread_ref, out_ref):
    active = silu(rows_ref[...].astype(F32)).astype(BF16)
    row = lax.broadcasted_iota(jnp.int32, (IMG_TOK, PIX * CIN), 0)
    patch_row, patch_col = row >> 4, row & (SIDE - 1)
    total = None
    for index in range(9):
        down, right = index // 3 - 1, index % 3 - 1
        part = mxu(active, spread_ref[:, index * PIX * CIN : (index + 1) * PIX * CIN])
        offset = down * SIDE + right
        if offset:
            part = pltpu.roll(part, offset % IMG_TOK, 0)
        source_row, source_col = patch_row - down, patch_col - right
        inside = (source_row >= 0) & (source_row < SIDE) & (source_col >= 0) & (source_col < SIDE)
        part = jnp.where(inside, part, 0.0)
        total = part if total is None else total + part
    out_ref[...] = total


def spread_rows(rows, spread):
    return pl.pallas_call(
        spread_kernel,
        out_shape=jax.ShapeDtypeStruct((IMG_TOK, PIX * CIN), F32),
        compiler_params=params(),
        cost_estimate=cost(2 * IMG_TOK * rows.shape[1] * 9 * PIX * CIN, 2 << 20),
        name="spread_rows",
    )(rows, spread)


def spread_weights(up_conv, pixels):
    taps = up_conv.reshape(9, CH, CIN).transpose(1, 0, 2).reshape(CH, 9 * CIN)
    shape = (pixels.shape[0], 9 * CIN, 9 * PIX * CIN)
    row = lax.broadcasted_iota(jnp.int32, shape, 1)
    col = lax.broadcasted_iota(jnp.int32, shape, 2)
    pixel = pixels[:, None, None]
    tap, channel = row >> 3, row & 7
    patch, target, out_channel = col >> 7, (col >> 3) & 15, col & 7
    tap_row, tap_col = tap // 3, tap % 3
    down, right = patch // 3 - 1, patch % 3 - 1
    hit = (
        (channel == out_channel)
        & ((pixel >> 2) + 1 - tap_row == (target >> 2) + PATCH * down)
        & ((pixel & 3) + 1 - tap_col == (target & 3) + PATCH * right)
    )
    placed = jnp.where(hit, 1.0, 0.0).astype(BF16)
    spread = jnp.einsum("ct,ptn->pcn", taps, placed, preferred_element_type=F32)
    return spread.astype(BF16).reshape(pixels.shape[0] * CH, 9 * PIX * CIN)


def gather_small(latents, down_conv, norm_gain):
    tiles, outer, cores = (lax.axis_size(name) for name in ("tile", "mpo", "core"))
    ctxs = lax.axis_size("ctx")
    parts = outer * cores
    mp_index = lax.axis_index("mpo") * cores + lax.axis_index("core")
    local, height, breadth = latents.shape
    piece = height // parts
    own = lax.dynamic_slice_in_dim(latents, mp_index * piece, piece, 1).reshape(-1)
    taps, channels = down_conv.shape
    tap_piece = taps // tiles
    conv = lax.dynamic_slice_in_dim(down_conv, lax.axis_index("tile") * tap_piece, tap_piece, 0)
    conv = conv.reshape(-1)
    flat = jnp.concatenate([own, conv, norm_gain])
    size = -(-flat.shape[0] // 2048) * 2048
    flat = jnp.pad(flat, (0, size - flat.shape[0])).reshape(1, size // 128, 128)
    every = lax.all_gather(flat, ("ctx", "tile", "mpo", "core"), axis=0, tiled=True)
    every = every.reshape(ctxs, tiles, parts, size)
    first, second = own.shape[0], own.shape[0] + conv.shape[0]
    images = every[..., :first].reshape(ctxs, tiles, parts, local, piece, breadth)
    images = images.transpose(0, 3, 1, 2, 4, 5).reshape(ctxs * local, HL, breadth)
    conv = every[0, :, :, first:second].reshape(tiles, parts, tap_piece, channels)
    conv = conv.transpose(0, 2, 1, 3).reshape(taps, parts * channels)
    gain = every[0, :, :, second : second + norm_gain.shape[0]].reshape(tiles * parts, 1, -1)
    return images, conv, gain


def shards(
    text_embed,
    latents,
    down_conv,
    patch_in,
    norm_gain,
    query_weight,
    key_weight,
    value_weight,
    query_gain,
    key_gain,
    out_weight,
    patch_out,
    up_conv,
    span_start,
    image_of_slot,
):
    ctxs, tiles, outer = (lax.axis_size(name) for name in ("ctx", "tile", "mpo"))
    ctx, tile, mpo, core = (lax.axis_index(name) for name in ("ctx", "tile", "mpo", "core"))
    seq_rows, width = text_embed.shape
    half = seq_rows // 2
    images = span_start.shape[0]
    groups = tiles * outer
    gather_axes = ("tile", "mpo")

    weights_par = [swap(w) for w in (key_weight, value_weight, query_weight)]
    out_par = swap(out_weight)
    up_par = swap(patch_out)
    every_latent, conv, gain = gather_small(latents, down_conv, norm_gain)

    numbers = jnp.arange(images, dtype=jnp.int32)
    matches = image_of_slot[None, :] == numbers[:, None]
    slot_of_image = jnp.sum(jnp.where(matches, numbers[None, :], 0), axis=1)
    first = ctx * seq_rows
    core_meta = jnp.stack([core]).astype(jnp.int32)
    stream_meta = jnp.concatenate([span_start, slot_of_image, jnp.stack([first, core])]).astype(jnp.int32)

    padded = jnp.pad(every_latent, ((0, 0), (1, 1), (CIN, 128 - CIN)))
    rows = jnp.stack(
        [padded[:, r : r + HL - PATCH + 1 : PATCH, :].reshape(images * SIDE, -1) for r in range(PATCH + 2)]
    )
    conv = conv.reshape(3, 3 * CIN, CH)
    conv = jnp.stack(
        [
            jnp.pad(conv, ((0, 0), (CIN * c, WINDOW - 3 * CIN - CIN * c), (0, 0))).reshape(TAPS, CH)
            for c in range(PATCH)
        ]
    )
    text = jnp.roll(text_embed.reshape(2, half, width), core, axis=0).reshape(seq_rows, width)
    stream = down_stream(stream_meta, rows, conv, patch_in, text, images)
    stream_own = stream[0]
    stream_par = swap(stream[1])

    x = lax.all_gather(jnp.stack([stream_own, stream_par]), gather_axes, axis=0, tiled=True)
    weights = jnp.stack(weights_par + [key_weight, value_weight, query_weight])
    gains = jnp.stack([query_gain, key_gain])
    kv_send, q_send, kv_own, q_own = qkv(core_meta, x, gain, weights, gains)

    def shifted(values, step, cross):
        pairs = [
            (2 * c + k, 2 * ((c + step) % ctxs) + (1 - k if cross else k))
            for c in range(ctxs)
            for k in range(2)
        ]
        return lax.ppermute(values, ("ctx", "core"), pairs)

    q_par = swap(q_send)
    pieces = [kv_own, swap(kv_send)]
    bases = [first + core * half, first + (1 - core) * half]
    for step in range(1, ctxs):
        from_ctx = lax.rem(ctx + ctxs - step, ctxs) * seq_rows
        pieces += [shifted(kv_own, step, False), shifted(kv_send, step, True)]
        bases += [from_ctx + core * half, from_ctx + (1 - core) * half]
    spans = [span_start[i] for i in range(images)]

    def attend(query, base):
        meta = jnp.stack(spans + [base] + bases).astype(jnp.int32)
        return attention(meta, query, pieces, images)

    att_par = swap(attend(q_par, bases[1]))
    att_own = attend(q_own, bases[0])
    attended = lax.all_gather(jnp.stack([att_own, att_par]), gather_axes, axis=0, tiled=True)
    out_send, out_own = out_project(
        core_meta, attended, out_weight, out_par, stream_own, stream_par
    )
    out_other = swap(out_send)
    ordered = jnp.where(
        core == 0, jnp.stack([out_own, out_other]), jnp.stack([out_other, out_own])
    )
    layer_out = ordered.reshape(seq_rows, width)

    starts = jnp.take(span_start, image_of_slot)
    wanted = []
    for step in range(ctxs):
        to_ctx = lax.rem(ctx + step, ctxs)
        wanted += [starts[2 * to_ctx + core], starts[2 * to_ctx + 1 - core]]
    pick_meta = jnp.stack(wanted + bases[:2]).astype(jnp.int32)
    picks = pick_rows(pick_meta, out_own, out_other, 2 * ctxs)
    own_parts, par_parts = [picks[0]], [swap(picks[1])]
    for step in range(1, ctxs):
        own_parts.append(shifted(picks[2 * step], step, False))
        par_parts.append(shifted(picks[2 * step + 1], step, True))
    partial = up_project(own_parts, par_parts, patch_out, up_par, groups)
    deep = partial.shape[2]
    own_rows = lax.psum_scatter(partial, gather_axes, scatter_dimension=0, tiled=True)
    pixels = (tile * outer + mpo) * (deep // CH) + jnp.arange(deep // CH, dtype=jnp.int32)
    spread = spread_rows(own_rows.reshape(IMG_TOK, deep), spread_weights(up_conv, pixels))

    bands = spread.reshape(tiles, IMG_TOK // tiles, PIX * CIN)
    band = lax.dynamic_index_in_dim(bands, tile, 0, keepdims=False)
    for step in range(1, tiles):
        piece = lax.dynamic_index_in_dim(bands, lax.rem(tile + step, tiles), 0, keepdims=False)
        band = band + lax.ppermute(piece, "tile", [(t, (t + step) % tiles) for t in range(tiles)])
    summed = band
    for step in range(1, outer):
        summed = summed + lax.ppermute(band, "mpo", [(m, (m + step) % outer) for m in range(outer)])
    other = swap(summed)
    slots = jnp.where(core == 0, jnp.stack([summed, other]), jnp.stack([other, summed]))
    noise = slots.reshape(2, SIDE // tiles, SIDE, PATCH, PATCH * CIN).transpose(0, 1, 3, 2, 4)
    return layer_out, noise.reshape(2, HL // tiles, WL * CIN)


def solution(mesh):
    ctxs, tiles, parts = mesh.devices.shape
    fine = Mesh(
        mesh.devices.reshape(ctxs, tiles, parts // 2, 2), ("ctx", "tile", "mpo", "core")
    )
    features = ("tile", "mpo", "core")
    return jax.shard_map(
        shards,
        mesh=fine,
        in_specs=(
            P("ctx", features),
            P("ctx", "tile", None),
            P(None, ("mpo", "core")),
            P(None, features),
            P(features),
            P(None, features),
            P(None, features),
            P(None, features),
            P(),
            P(),
            P(None, features),
            P(features, None),
            P(),
            P(),
            P(),
        ),
        out_specs=(P("ctx", features), P("ctx", "tile", None)),
        check_vma=False,
    )
```

```python
import functools

import jax
import jax.numpy as jnp
from jax import lax
from jax.experimental import pallas as pl
from jax.experimental.pallas import tpu as pltpu
from jax.sharding import Mesh
from jax.sharding import PartitionSpec as P

HD = 128
CH = 256
CIN = 8
WL = 64
HL = 64
PATCH = 4
PIX = PATCH * PATCH
SIDE = WL // PATCH
IMG_TOK = 256
EPSILON = 1e-05
NEGATIVE_FILL = -1e30
WINDOW = (PATCH + 2) * CIN
TAPS = 3 * WINDOW
BF16 = jnp.bfloat16
F32 = jnp.float32
VMEM_LIMIT = 48 * 1024 * 1024


def params(*semantics):
    return pltpu.CompilerParams(
        dimension_semantics=semantics or None, vmem_limit_bytes=VMEM_LIMIT
    )


def cost(flops, nbytes, transcendentals=0):
    return pl.CostEstimate(
        flops=int(flops), bytes_accessed=int(nbytes), transcendentals=int(transcendentals)
    )


def silu(values):
    return values / (1.0 + jnp.exp(-values))


def mxu(left, right):
    return jnp.dot(left, right, preferred_element_type=F32)


def swap(values):
    return lax.ppermute(values, "core", [(0, 1), (1, 0)])


def down_kernel(images, half, meta, rows_ref, conv_ref, patch_ref, text_ref, out_ref, windows, total):
    step = pl.program_id(0)
    group = images * SIDE

    @pl.when(step == 0)
    def _():
        for col in range(SIDE):
            for row in range(PATCH + 2):
                piece = rows_ref[row, :, PATCH * CIN * col : PATCH * CIN * col + WINDOW]
                for shift in range(3):
                    if 0 <= row - shift < PATCH:
                        windows[
                            row - shift,
                            group * col : group * (col + 1),
                            WINDOW * shift : WINDOW * (shift + 1),
                        ] = piece

    hidden = mxu(windows[step // PATCH], conv_ref[lax.rem(step, PATCH)])
    term = mxu(silu(hidden).astype(BF16), patch_ref[...])

    @pl.when(step == 0)
    def _():
        total[...] = term

    @pl.when(step > 0)
    def _():
        total[...] += term

    @pl.when(step == PIX - 1)
    def _():
        tokens = total[...].astype(BF16)
        first = meta[2 * images]
        core = meta[2 * images + 1]
        block = 256
        for part in range(2 * half // block):
            which = part * block // half
            base = first + jnp.where(which == 0, core, 1 - core) * half + part * block - which * half
            place = base + lax.broadcasted_iota(jnp.int32, (block, 1), 0)
            source = jnp.full((block, 1), -1, jnp.int32)
            for image in range(images):
                inner = place - meta[image]
                inside = (inner >= 0) & (inner < IMG_TOK)
                index = (inner & (SIDE - 1)) * group + meta[images + image] * SIDE + (inner >> 4)
                source = jnp.where(inside, index, source)
            choice = source == lax.broadcasted_iota(jnp.int32, (block, images * IMG_TOK), 1)
            picked = mxu(jnp.where(choice, 1.0, 0.0).astype(BF16), tokens).astype(BF16)
            at = part * block - which * half
            out_ref[which, at : at + block, :] = jnp.where(
                source >= 0, picked.astype(F32), text_ref[part * block : (part + 1) * block, :].astype(F32)
            ).astype(BF16)


def down_stream(meta, rows, conv, patch_in, text, images):
    seq_rows, width = text.shape
    half = seq_rows // 2
    count = images * IMG_TOK
    return pl.pallas_call(
        functools.partial(down_kernel, images, half),
        grid_spec=pltpu.PrefetchScalarGridSpec(
            num_scalar_prefetch=1,
            grid=(PIX,),
            in_specs=[
                pl.BlockSpec(rows.shape, lambda i, m: (0, 0, 0)),
                pl.BlockSpec(conv.shape, lambda i, m: (0, 0, 0)),
                pl.BlockSpec((CH, width), lambda i, m: (i, 0)),
                pl.BlockSpec((seq_rows, width), lambda i, m: (0, 0)),
            ],
            out_specs=pl.BlockSpec((2, half, width), lambda i, m: (0, 0, 0)),
            scratch_shapes=[
                pltpu.VMEM((PATCH, count, TAPS), BF16),
                pltpu.VMEM((count, width), F32),
            ],
        ),
        out_shape=jax.ShapeDtypeStruct((2, half, width), BF16),
        compiler_params=params("arbitrary"),
        cost_estimate=cost(2 * count * PIX * CH * (256 + width), 4 << 20, count * PIX * CH),
        name="down_stream",
    )(meta, rows, conv, patch_in, text)


def qkv_kernel(count, first, last, meta, *refs):
    refs = list(refs)
    x_refs = [refs.pop(0) for _ in range(count)]
    gain_refs = [refs.pop(0) for _ in range(count)]
    weight_refs = [[refs.pop(0) for _ in range(6)] for _ in range(count)]
    if not first:
        acc_in, square_in = refs.pop(0), refs.pop(0)
    if last:
        head_gains = refs.pop(0)
    scaled = refs.pop()
    half, span = x_refs[0].shape
    chunk = 64

    def scale_rows(index, carry):
        rows = pl.ds(pl.multiple_of(index * chunk, chunk), chunk)
        square = jnp.zeros((chunk, HD), F32) if first else square_in[rows, :]
        for block in range(count):
            value = x_refs[block][rows, :].astype(F32)
            scaled[block, rows, :] = (value * gain_refs[block][0].astype(F32)).astype(BF16)
            value = value * value
            for part in range(span // HD):
                square = square + value[:, part * HD : (part + 1) * HD]
        square_out[rows, :] = square
        return carry

    if last:
        square_out = refs.pop()
        outs = refs
    else:
        acc_out, square_out = refs
    lax.fori_loop(0, half // chunk, scale_rows, 0)
    width = weight_refs[0][0].shape[1]
    heads = width // HD
    if last:
        model = meta[count] * span
        mean = jnp.sum(square_out[...], axis=-1, keepdims=True) / model.astype(F32)
        scale = lax.rsqrt(mean + EPSILON)
    for part in range(6):
        total = None if first else acc_in[part]
        for block in range(count):
            term = mxu(scaled[block], weight_refs[block][part][...])
            total = term if total is None else total + term
        if not last:
            acc_out[part] = total
            continue
        total = total * scale
        side, kind = part // 3, part % 3
        kv_outs = outs[2 * heads * side : 2 * heads * side + heads]
        q_outs = outs[2 * heads * side + heads : 2 * heads * side + 2 * heads]
        for head in range(heads):
            raw = total[:, head * HD : (head + 1) * HD]
            if kind == 1:
                kv_outs[head][1] = raw.astype(BF16)
                continue
            raw = raw * lax.rsqrt(jnp.mean(raw * raw, axis=-1, keepdims=True) + EPSILON)
            if kind == 0:
                kv_outs[head][0] = (raw * head_gains[1:2, :]).astype(BF16)
            else:
                q_outs[head][...] = (raw * (head_gains[0:1, :] * HD ** (-0.5))).astype(BF16)


def full(shape):
    return pl.BlockSpec(shape, lambda i, m: (0,) * len(shape))


def qkv_step(blocks, chips, gain, weights, state, head_gains):
    half, span = blocks[0].shape
    width = weights[0].shape[1]
    heads = width // HD
    count, first, last = len(blocks), state is None, head_gains is not None
    groups = gain.shape[0]
    inputs, specs = list(blocks), [full(b.shape) for b in blocks]
    for index in range(count):
        inputs.append(gain)
        specs.append(pl.BlockSpec((1, 1, span), lambda i, m, index=index: (m[index], 0, 0)))
    for index in range(count):
        for weight in weights:
            inputs.append(weight)
            specs.append(pl.BlockSpec((span, width), lambda i, m, index=index: (m[index], 0)))
    if not first:
        inputs += list(state)
        specs += [full(s.shape) for s in state]
    scratch = [pltpu.VMEM((count, half, span), BF16)]
    if last:
        inputs.append(head_gains)
        specs.append(full(head_gains.shape))
        kv, q = jax.ShapeDtypeStruct((2, half, HD), BF16), jax.ShapeDtypeStruct((half, HD), BF16)
        outs = ([kv] * heads + [q] * heads) * 2
        scratch = [pltpu.VMEM((half, HD), F32)] + scratch
    else:
        outs = [
            jax.ShapeDtypeStruct((6, half, width), F32),
            jax.ShapeDtypeStruct((half, HD), F32),
        ]
    meta = jnp.stack(list(chips) + [jnp.int32(groups)]).astype(jnp.int32)
    return pl.pallas_call(
        functools.partial(qkv_kernel, count, first, last),
        grid_spec=pltpu.PrefetchScalarGridSpec(
            num_scalar_prefetch=1,
            grid=(1,),
            in_specs=specs,
            out_specs=[full(o.shape) for o in outs],
            scratch_shapes=scratch,
        ),
        out_shape=outs,
        compiler_params=params("arbitrary"),
        cost_estimate=cost(12 * count * half * span * width, (6 + 2 * count) << 20),
        name="qkv_last" if last else "qkv_step",
    )(meta, *inputs)


def attention_kernel(images, pieces, meta, *refs):
    q_refs, kv_refs, out_refs = refs[:2], refs[2 : 2 + pieces], refs[2 + pieces :]
    rows = q_refs[0].shape[0]
    step = pl.program_id(0)
    for side in range(2):
        place = meta[images + side] + step * rows + lax.broadcasted_iota(jnp.int32, (rows, 1), 0)
        limit = place
        for image in range(images):
            inner = place - meta[image]
            limit = jnp.where((inner >= 0) & (inner < IMG_TOK), meta[image] + IMG_TOK - 1, limit)
        query = q_refs[side][...]
        scores = []
        top = None
        for piece in range(pieces):
            score = lax.dot_general(
                query, kv_refs[piece][0], (((1,), (1,)), ((), ())), preferred_element_type=F32
            )
            position = lax.broadcasted_iota(jnp.int32, score.shape, 1)
            score = jnp.where(position <= limit - meta[images + 2 + piece], score, NEGATIVE_FILL)
            scores.append(score)
            best = jnp.max(score, axis=1, keepdims=True)
            top = best if top is None else jnp.maximum(top, best)
        total = jnp.zeros((rows, 1), F32)
        product = jnp.zeros((rows, HD), F32)
        for piece in range(pieces):
            weight = jnp.exp(scores[piece] - top)
            total = total + jnp.sum(weight, axis=1, keepdims=True)
            product = product + mxu(weight.astype(BF16), kv_refs[piece][1])
        out_refs[side][...] = (product / total).astype(BF16)


def attention(meta, queries, pieces, images):
    half = queries[0].shape[0]
    block = 256
    keys = half * len(pieces)
    rows = pl.BlockSpec((block, HD), lambda i, m: (i, 0))
    return pl.pallas_call(
        functools.partial(attention_kernel, images, len(pieces)),
        grid_spec=pltpu.PrefetchScalarGridSpec(
            num_scalar_prefetch=1,
            grid=(half // block,),
            in_specs=[rows, rows] + [full(p.shape) for p in pieces],
            out_specs=[rows, rows],
        ),
        out_shape=[jax.ShapeDtypeStruct((half, HD), BF16)] * 2,
        compiler_params=params("arbitrary"),
        cost_estimate=cost(8 * half * keys * HD, 4 * keys * HD, 2 * half * keys),
        name="attention",
    )(meta, *queries, *pieces)


def out_kernel(count, first, last, meta, *refs):
    x_refs, weight_refs = refs[:count], refs[count : 3 * count]
    if first:
        start, outs = refs[3 * count : 3 * count + 2], refs[3 * count + 2 :]
    else:
        start, outs = [refs[3 * count].at[0], refs[3 * count].at[1]], refs[3 * count + 1 :]
    for side in range(2):
        total = start[side][...].astype(F32)
        for block in range(count):
            weight = weight_refs[2 * block + side][0, :, 0]
            total = total + mxu(x_refs[block][...], weight.reshape(2 * HD, weight.shape[2]))
        if last:
            outs[side][...] = total.astype(BF16)
        else:
            outs[0][side] = total


def out_step(blocks, chips, head, weights, state, last):
    half = blocks[0].shape[0]
    width = weights[0].shape[1]
    first = isinstance(state, tuple)
    count = len(blocks)
    views = [w.reshape(-1, 2, width // HD, HD, width) for w in weights]
    inputs, specs = list(blocks), [full(b.shape) for b in blocks]
    for index in range(count):
        for view in views:
            inputs.append(view)
            specs.append(
                pl.BlockSpec((1, 2, 1, HD, width), lambda i, m, index=index: (m[index], 0, head, 0, 0))
            )
    states = list(state) if first else [state]
    inputs += states
    specs += [full(s.shape) for s in states]
    if last:
        outs = [jax.ShapeDtypeStruct((half, width), BF16)] * 2
    else:
        outs = [jax.ShapeDtypeStruct((2, half, width), F32)]
    result = pl.pallas_call(
        functools.partial(out_kernel, count, first, last),
        grid_spec=pltpu.PrefetchScalarGridSpec(
            num_scalar_prefetch=1,
            grid=(1,),
            in_specs=specs,
            out_specs=[full(o.shape) for o in outs],
        ),
        out_shape=outs,
        compiler_params=params("arbitrary"),
        cost_estimate=cost(8 * count * half * HD * width, (2 + count) << 20),
        name="out_last" if last else "out_step",
    )(jnp.stack(list(chips)).astype(jnp.int32), *inputs)
    return result if last else result[0]


def pick_kernel(targets, meta, own_ref, par_ref, out_ref):
    half = own_ref.shape[0]
    own_base, par_base = meta[targets], meta[targets + 1]
    for target in range(targets):
        place = meta[target] + lax.broadcasted_iota(jnp.int32, (IMG_TOK, half), 0)
        column = lax.broadcasted_iota(jnp.int32, (IMG_TOK, half), 1)
        own = jnp.where(place == column + own_base, 1.0, 0.0).astype(BF16)
        par = jnp.where(place == column + par_base, 1.0, 0.0).astype(BF16)
        out_ref[target] = (mxu(own, own_ref[...]) + mxu(par, par_ref[...])).astype(BF16)


def pick_rows(meta, own, par, targets):
    half, width = own.shape
    whole = pl.BlockSpec((half, width), lambda i, m: (0, 0))
    return pl.pallas_call(
        functools.partial(pick_kernel, targets),
        grid_spec=pltpu.PrefetchScalarGridSpec(
            num_scalar_prefetch=1,
            grid=(1,),
            in_specs=[whole, whole],
            out_specs=pl.BlockSpec((targets, IMG_TOK, width), lambda i, m: (0, 0, 0)),
        ),
        out_shape=jax.ShapeDtypeStruct((targets, IMG_TOK, width), BF16),
        compiler_params=params("arbitrary"),
        cost_estimate=cost(targets * 4 * IMG_TOK * half * width, 1 << 20),
        name="pick_rows",
    )(meta, own, par)


def merge_kernel(*refs):
    out_ref = refs[-1]
    sides = refs[: len(refs) // 2], refs[len(refs) // 2 : -1]
    width = sides[0][0].shape[1]
    for side in range(2):
        total = sides[side][0][...].astype(F32)
        for part in sides[side][1:]:
            total = total + part[...].astype(F32)
        out_ref[:, side * width : (side + 1) * width] = total.astype(BF16)


def merge_picks(own_parts, par_parts):
    width = own_parts[0].shape[1]
    return pl.pallas_call(
        merge_kernel,
        out_shape=jax.ShapeDtypeStruct((IMG_TOK, 2 * width), BF16),
        compiler_params=params(),
        cost_estimate=cost(1 << 20, 1 << 20),
        name="merge_picks",
    )(*own_parts, *par_parts)


def spread(active, spread_ref):
    row = lax.broadcasted_iota(jnp.int32, (IMG_TOK, PIX * CIN), 0)
    patch_row, patch_col = row >> 4, row & (SIDE - 1)
    total = None
    for index in range(9):
        down, right = index // 3 - 1, index % 3 - 1
        part = mxu(active, spread_ref[:, index * PIX * CIN : (index + 1) * PIX * CIN])
        offset = down * SIDE + right
        if offset:
            part = pltpu.roll(part, offset % IMG_TOK, 0)
        source_row, source_col = patch_row - down, patch_col - right
        inside = (source_row >= 0) & (source_row < SIDE) & (source_col >= 0) & (source_col < SIDE)
        part = jnp.where(inside, part, 0.0)
        total = part if total is None else total + part
    return total


def up_kernel(count, halves, first, last, *refs):
    refs = list(refs)
    x_refs = [refs.pop(0) for _ in range(count)]
    weight_refs = [[[refs.pop(0) for _ in range(2)] for _ in range(halves)] for _ in range(count)]
    acc_in = None if first else refs.pop(0)
    spread_ref = refs.pop(0) if last else None
    out_ref = refs[0]
    width = x_refs[0].shape[1] // 2
    totals = []
    for part in range(halves):
        total = None if first else acc_in[part]
        for block in range(count):
            for side in range(2):
                term = mxu(
                    x_refs[block][:, side * width : (side + 1) * width],
                    weight_refs[block][part][side][0],
                )
                total = term if total is None else total + term
        totals.append(total)
        if not last:
            out_ref[part] = total
    if last:
        active = [silu(total).astype(BF16) for total in totals]
        active = jnp.concatenate(active, axis=1) if halves > 1 else active[0]
        out_ref[...] = spread(active, spread_ref)


def up_step(blocks, offsets, weights, state, spread_weight):
    span = blocks[0].shape[1]
    halves, count = len(weights), len(blocks)
    first, last = state is None, spread_weight is not None
    whole = lambda shape: pl.BlockSpec(shape, lambda i: (0,) * len(shape))
    inputs, specs = list(blocks), [whole(b.shape) for b in blocks]
    for offset in offsets:
        for sides in weights:
            for weight in sides:
                inputs.append(weight)
                specs.append(pl.BlockSpec((1, span // 2, CH), lambda i, offset=offset: (offset, 0, 0)))
    if not first:
        inputs.append(state)
        specs.append(whole(state.shape))
    if last:
        inputs.append(spread_weight)
        specs.append(whole(spread_weight.shape))
        out = jax.ShapeDtypeStruct((IMG_TOK, PIX * CIN), F32)
    else:
        out = jax.ShapeDtypeStruct((halves, IMG_TOK, CH), F32)
    return pl.pallas_call(
        functools.partial(up_kernel, count, halves, first, last),
        grid=(1,),
        in_specs=specs,
        out_specs=whole(out.shape),
        out_shape=out,
        compiler_params=params("arbitrary"),
        cost_estimate=cost(2 * count * IMG_TOK * span * CH * halves, (1 + count) << 20),
        name="up_last" if last else "up_step",
    )(*inputs)


def spread_weights(up_conv, pixels):
    taps = up_conv.reshape(9, CH, CIN).transpose(1, 0, 2).reshape(CH, 9 * CIN)
    shape = (pixels.shape[0], 9 * CIN, 9 * PIX * CIN)
    row = lax.broadcasted_iota(jnp.int32, shape, 1)
    col = lax.broadcasted_iota(jnp.int32, shape, 2)
    pixel = pixels[:, None, None]
    tap, channel = row >> 3, row & 7
    patch, target, out_channel = col >> 7, (col >> 3) & 15, col & 7
    tap_row, tap_col = tap // 3, tap % 3
    down, right = patch // 3 - 1, patch % 3 - 1
    hit = (
        (channel == out_channel)
        & ((pixel >> 2) + 1 - tap_row == (target >> 2) + PATCH * down)
        & ((pixel & 3) + 1 - tap_col == (target & 3) + PATCH * right)
    )
    placed = jnp.where(hit, 1.0, 0.0).astype(BF16)
    spread = jnp.einsum("ct,ptn->pcn", taps, placed, preferred_element_type=F32)
    return spread.astype(BF16).reshape(pixels.shape[0] * CH, 9 * PIX * CIN)


def by_core(core, own, other, axis):
    return jnp.where(
        core == 0, jnp.concatenate([own, other], axis), jnp.concatenate([other, own], axis)
    )


def shift(values, axis, step):
    count = lax.axis_size(axis)
    return lax.ppermute(values, axis, [(i, (i + step) % count) for i in range(count)])


def gather_small(latents, down_conv, norm_gain):
    ctxs, tiles = lax.axis_size("ctx"), lax.axis_size("tile")
    tile, mpo, core = (lax.axis_index(name) for name in ("tile", "mpo", "core"))
    local, height, breadth = latents.shape
    taps, channels = down_conv.shape
    width = norm_gain.shape[0]
    every = jnp.concatenate([latents] + [shift(latents, "ctx", s) for s in range(1, ctxs)])
    size = -(-(taps * channels + width) // 1024) * 1024
    flat = jnp.concatenate([down_conv.reshape(-1), norm_gain])
    flat = jnp.pad(flat, (0, size - flat.shape[0])).reshape(1, size // 128, 128)
    flat = by_core(core, flat, swap(flat), 0)[None]
    flat = by_core(mpo, flat, shift(flat, "mpo", 1), 0).reshape(4, size)
    conv = flat[:, : taps * channels].reshape(4, taps, channels)
    conv = conv.transpose(1, 0, 2).reshape(taps, 4 * channels)
    gain = flat[:, taps * channels : taps * channels + width].reshape(4 * width // 128, 128)
    rows = ctxs * local * height
    sent = every.reshape(rows * breadth // 128, 128)
    lines = sent.shape[0]
    pad = -gain.shape[0] % 16
    sent = jnp.concatenate([sent, jnp.pad(gain, ((0, pad), (0, 0)))])[None]
    turned = [shift(sent, "tile", s) for s in range(tiles - 1, 0, -1)] + [sent]
    whole = jnp.concatenate(turned + turned[:-1])
    whole = lax.dynamic_slice_in_dim(whole, tiles - 1 - tile, tiles, 0)
    images = whole[:, :lines].reshape(tiles, ctxs * local, height, breadth)
    images = images.transpose(1, 0, 2, 3).reshape(ctxs * local, tiles * height, breadth)
    gain = whole[:, lines : lines + gain.shape[0]].reshape(tiles * 2, 1, 2 * width)
    return images, conv, gain


def transpose_up(patch_out):
    ctxs, tiles, outer = (lax.axis_size(name) for name in ("ctx", "tile", "mpo"))
    ctx, tile, mpo = (lax.axis_index(name) for name in ("ctx", "tile", "mpo"))
    width, features = patch_out.shape
    deep = features // (tiles * outer)
    halves = 2 if ctxs == 2 and deep == 2 * CH else 1
    blocks = []
    for down in range(tiles):
        for right in range(outer):
            chip = lax.rem(tile + down, tiles) * outer + lax.rem(mpo + right, outer)
            start = chip * deep + (ctx * CH if halves == 2 else 0)
            block = lax.dynamic_slice_in_dim(patch_out, start, deep // halves, 1)
            if down or right:
                pairs = [
                    (t * outer + m, (t + down) % tiles * outer + (m + right) % outer)
                    for t in range(tiles)
                    for m in range(outer)
                ]
                block = lax.ppermute(block, ("tile", "mpo"), pairs)
            blocks.append(block)
    own = jnp.stack(blocks)
    weights = [own] if halves == 1 else [own, shift(own, "ctx", 1)]
    return [[weight, swap(weight)] for weight in weights]


def gather_chips(block):
    tiles = lax.axis_size("tile")
    blocks = []
    for step in range(tiles):
        if step:
            block = shift(block, "tile", 1)
        blocks += [block, shift(block, "mpo", 1)]
    return blocks


def arrivals(tiles):
    steps = [[0, 1] + ([2] if tiles > 1 else [])]
    for step in range(2, tiles):
        steps.append([2 * step, 2 * step - 1])
    return steps + [[2 * tiles - 1]]


def shards(
    text_embed,
    latents,
    down_conv,
    patch_in,
    norm_gain,
    query_weight,
    key_weight,
    value_weight,
    query_gain,
    key_gain,
    out_weight,
    patch_out,
    up_conv,
    span_start,
    image_of_slot,
):
    ctxs, tiles, outer = (lax.axis_size(name) for name in ("ctx", "tile", "mpo"))
    ctx, tile, mpo, core = (lax.axis_index(name) for name in ("ctx", "tile", "mpo", "core"))
    seq_rows, width = text_embed.shape
    half = seq_rows // 2
    heads = width // HD
    images = span_start.shape[0]
    local = latents.shape[0]

    every_latent, conv, gain = gather_small(latents, down_conv, norm_gain)
    weights = [swap(w) for w in (key_weight, value_weight, query_weight)]
    weights += [key_weight, value_weight, query_weight]
    out_par = swap(out_weight)
    up_weights = transpose_up(patch_out)

    numbers = jnp.arange(images, dtype=jnp.int32)
    matches = image_of_slot[None, :] == numbers[:, None]
    slot_of_image = jnp.sum(jnp.where(matches, numbers[None, :], 0), axis=1)
    slot_place = lax.rem(ctx + ctxs - slot_of_image // local, ctxs) * local + slot_of_image % local
    first = ctx * seq_rows
    stream_meta = jnp.concatenate([span_start, slot_place, jnp.stack([first, core])]).astype(jnp.int32)

    padded = jnp.pad(every_latent, ((0, 0), (1, 1), (CIN, 128 - CIN)))
    rows = jnp.stack(
        [padded[:, r : r + HL - PATCH + 1 : PATCH, :].reshape(images * SIDE, -1) for r in range(PATCH + 2)]
    )
    conv = conv.reshape(3, 3 * CIN, CH)
    conv = jnp.stack(
        [
            jnp.pad(conv, ((0, 0), (CIN * c, WINDOW - 3 * CIN - CIN * c), (0, 0))).reshape(TAPS, CH)
            for c in range(PATCH)
        ]
    )
    text = jnp.roll(text_embed.reshape(2, half, width), core, axis=0).reshape(seq_rows, width)
    stream = down_stream(stream_meta, rows, conv, patch_in, text, images)
    stream_own = stream[0]
    stream_par = swap(stream[1])

    def chip(index):
        return lax.rem(tile + tiles - index // 2, tiles) * outer + lax.rem(mpo + index % 2, outer)

    blocks = gather_chips(by_core(core, stream_own, stream_par, 1))
    head_gains = jnp.stack([query_gain, key_gain])
    state = None
    steps = arrivals(tiles)
    for step in steps:
        state = qkv_step(
            [blocks[b] for b in step],
            [chip(b) for b in step],
            gain,
            weights,
            state,
            head_gains if step is steps[-1] else None,
        )
    kv_send, q_send = state[:heads], state[heads : 2 * heads]
    kv_own, q_own = state[2 * heads : 3 * heads], state[3 * heads :]

    def shifted(values, step, cross):
        pairs = [
            (2 * c + k, 2 * ((c + step) % ctxs) + (1 - k if cross else k))
            for c in range(ctxs)
            for k in range(2)
        ]
        return lax.ppermute(values, ("ctx", "core"), pairs)

    bases = [first + core * half, first + (1 - core) * half]
    key_bases = list(bases)
    for step in range(1, ctxs):
        from_ctx = lax.rem(ctx + ctxs - step, ctxs) * seq_rows
        key_bases += [from_ctx + core * half, from_ctx + (1 - core) * half]
    spans = [span_start[i] for i in range(images)]
    att_meta = jnp.stack(spans + bases + key_bases).astype(jnp.int32)
    gathered = []
    for head in range(heads):
        q_par = swap(q_send[head])
        pieces = [kv_own[head], swap(kv_send[head])]
        for step in range(1, ctxs):
            pieces += [shifted(kv_own[head], step, False), shifted(kv_send[head], step, True)]
        att_own, att_send = attention(att_meta, [q_own[head], q_par], pieces, images)
        gathered.append(gather_chips(by_core(core, att_own, swap(att_send), 1)))
    state = (stream_own, stream_par)
    for head in range(heads):
        for step in steps:
            last = head == heads - 1 and step is steps[-1]
            state = out_step(
                [gathered[head][b] for b in step],
                [chip(b) for b in step],
                head,
                (out_weight, out_par),
                state,
                last,
            )
    out_own, out_send = state
    out_other = swap(out_send)
    layer_out = by_core(core, out_own, out_other, 0)

    starts = jnp.take(span_start, image_of_slot)
    wanted = []
    for step in range(ctxs):
        to_ctx = lax.rem(ctx + step, ctxs)
        wanted += [starts[2 * to_ctx + core], starts[2 * to_ctx + 1 - core]]
    pick_meta = jnp.stack(wanted + bases).astype(jnp.int32)
    picks = pick_rows(pick_meta, out_own, out_other, 2 * ctxs)
    own_parts, par_parts = [picks[0]], [swap(picks[1])]
    for step in range(1, ctxs):
        own_parts.append(shifted(picks[2 * step], step, False))
        par_parts.append(shifted(picks[2 * step + 1], step, True))

    blocks = gather_chips(merge_picks(own_parts, par_parts))
    halves = len(up_weights)
    pixel = tile * outer + mpo
    pixels = jnp.stack([pixel * halves + lax.rem(ctx + h, halves) for h in range(halves)])
    spread_weight = spread_weights(up_conv, pixels)
    state = None
    for step in steps:
        state = up_step(
            [blocks[b] for b in step], step, up_weights, state, spread_weight if step is steps[-1] else None
        )

    bands = state.reshape(tiles, IMG_TOK // tiles, PIX * CIN)
    band = lax.dynamic_index_in_dim(bands, tile, 0, keepdims=False)
    for step in range(1, tiles):
        piece = lax.dynamic_index_in_dim(bands, lax.rem(tile + step, tiles), 0, keepdims=False)
        band = band + shift(piece, "tile", step)
    summed = band
    for step in range(1, outer):
        summed = summed + shift(band, "mpo", step)
    slots = by_core(core, summed[None], swap(summed)[None], 0)
    noise = slots.reshape(2, SIDE // tiles, SIDE, PATCH, PATCH * CIN).transpose(0, 1, 3, 2, 4)
    return layer_out, noise.reshape(2, HL // tiles, WL * CIN)


def solution(mesh):
    ctxs, tiles, parts = mesh.devices.shape
    fine = Mesh(
        mesh.devices.reshape(ctxs, tiles, parts // 2, 2), ("ctx", "tile", "mpo", "core")
    )
    features = ("tile", "mpo", "core")
    return jax.shard_map(
        shards,
        mesh=fine,
        in_specs=(
            P("ctx", features),
            P("ctx", "tile", None),
            P(None, ("mpo", "core")),
            P(None, features),
            P(features),
            P(None, features),
            P(None, features),
            P(None, features),
            P(),
            P(),
            P(None, features),
            P(features, None),
            P(),
            P(),
            P(),
        ),
        out_specs=(P("ctx", features), P("ctx", "tile", None)),
        check_vma=False,
    )
```

```python
import functools

import jax
import jax.numpy as jnp
from jax import lax
from jax.experimental import pallas as pl
from jax.experimental.pallas import tpu as pltpu
from jax.sharding import Mesh
from jax.sharding import PartitionSpec as P

HD = 128
CH = 256
CIN = 8
WL = 64
HL = 64
PATCH = 4
PIX = PATCH * PATCH
SIDE = WL // PATCH
IMG_TOK = 256
EPSILON = 1e-05
NEGATIVE_FILL = -1e30
WINDOW = (PATCH + 2) * CIN
TAPS = 3 * WINDOW
BF16 = jnp.bfloat16
F32 = jnp.float32


def split_meta(meta, images):
    return meta[3 * images], meta[3 * images + 1], meta[3 * images + 2], meta[3 * images + 3]


def params(mebibytes):
    return pltpu.CompilerParams(
        dimension_semantics=("arbitrary",), vmem_limit_bytes=mebibytes * 1024 * 1024
    )


def cost(flops, nbytes, transcendentals=0):
    return pl.CostEstimate(
        flops=int(flops), bytes_accessed=int(nbytes), transcendentals=int(transcendentals)
    )


def silu(values):
    half = values * 0.5
    return half + half * jnp.tanh(half)


def mxu(left, right):
    return jnp.dot(left, right, preferred_element_type=F32)


def swap(values):
    return lax.ppermute(values, "core", [(0, 1), (1, 0)])


def down_kernel(images, half, meta, rows_ref, conv_ref, patch_ref, text_ref, out_ref, windows, total):
    step = pl.program_id(0)
    group = images * SIDE

    @pl.when(step == 0)
    def _():
        for col in range(SIDE):
            for row in range(PATCH + 2):
                piece = rows_ref[row, :, PATCH * CIN * col : PATCH * CIN * col + WINDOW]
                for shift in range(3):
                    if 0 <= row - shift < PATCH:
                        windows[
                            row - shift,
                            group * col : group * (col + 1),
                            WINDOW * shift : WINDOW * (shift + 1),
                        ] = piece

    hidden = mxu(windows[step // PATCH], conv_ref[lax.rem(step, PATCH)])
    term = mxu(silu(hidden).astype(BF16), patch_ref[...])

    @pl.when(step == 0)
    def _():
        total[...] = term

    @pl.when(step > 0)
    def _():
        total[...] += term

    @pl.when(step == PIX - 1)
    def _():
        tokens = total[...].astype(BF16)
        ctx, core, _, _ = split_meta(meta, images)
        first = ctx * (2 * half)
        block = 256
        for part in range(2 * half // block):
            which = part * block // half
            base = first + jnp.where(which == 0, core, 1 - core) * half + part * block - which * half
            place = base + lax.broadcasted_iota(jnp.int32, (block, 1), 0)
            source = jnp.full((block, 1), -1, jnp.int32)
            for image in range(images):
                inner = place - meta[image]
                inside = (inner >= 0) & (inner < IMG_TOK)
                index = (inner & (SIDE - 1)) * group + meta[images + image] * SIDE + (inner >> 4)
                source = jnp.where(inside, index, source)
            choice = source == lax.broadcasted_iota(jnp.int32, (block, images * IMG_TOK), 1)
            picked = mxu(jnp.where(choice, 1.0, 0.0).astype(BF16), tokens).astype(BF16)
            at = part * block - which * half
            out_ref[which, at : at + block, :] = jnp.where(
                source >= 0, picked.astype(F32), text_ref[part * block : (part + 1) * block, :].astype(F32)
            ).astype(BF16)


def down_stream(meta, rows, conv, patch_in, text, images):
    seq_rows, width = text.shape
    half = seq_rows // 2
    count = images * IMG_TOK
    return pl.pallas_call(
        functools.partial(down_kernel, images, half),
        grid_spec=pltpu.PrefetchScalarGridSpec(
            num_scalar_prefetch=1,
            grid=(PIX,),
            in_specs=[
                pl.BlockSpec(rows.shape, lambda i, m: (0, 0, 0)),
                pl.BlockSpec(conv.shape, lambda i, m: (0, 0, 0)),
                pl.BlockSpec((CH, width), lambda i, m: (i, 0)),
                pl.BlockSpec((seq_rows, width), lambda i, m: (0, 0)),
            ],
            out_specs=pl.BlockSpec((2, half, width), lambda i, m: (0, 0, 0)),
            scratch_shapes=[
                pltpu.VMEM((PATCH, count, TAPS), BF16),
                pltpu.VMEM((count, width), F32),
            ],
        ),
        out_shape=jax.ShapeDtypeStruct((2, half, width), BF16),
        compiler_params=params(24),
        cost_estimate=cost(2 * count * PIX * CH * (256 + width), 4 << 20, count * PIX * CH),
        name="down_stream",
    )(meta, rows, conv, patch_in, text)


def load(pieces):
    if len(pieces) == 1:
        return pieces[0][...]
    return jnp.concatenate([piece[...] for piece in pieces], axis=0)


def take_blocks(refs, shapes):
    return [[refs.pop(0) for _ in pieces] for pieces in shapes]


def chip_of(meta, images, tiles, outer, entry):
    _, _, tile, mpo = split_meta(meta, images)
    return lax.rem(tile + tiles - entry // 2, tiles) * outer + lax.rem(mpo + entry % 2, outer)


def qkv_kernel(shapes, groups, first, last, meta, *refs):
    refs = list(refs)
    count = len(shapes)
    x_refs = take_blocks(refs, shapes)
    gain_refs = [refs.pop(0) for _ in range(count)]
    weight_refs = [[refs.pop(0) for _ in range(6)] for _ in range(count)]
    if not first:
        acc_in, square_in = refs.pop(0), refs.pop(0)
    if last:
        head_gains = refs.pop(0)
    scaled = refs.pop()
    half, span = scaled.shape[1:]
    chunk = 64

    def scale_rows(block, piece, base, index, carry):
        rows = pl.ds(pl.multiple_of(base + index * chunk, chunk), chunk)
        local = pl.ds(pl.multiple_of(index * chunk, chunk), chunk)
        if block:
            square = square_out[rows, :]
        else:
            square = jnp.zeros((chunk, HD), F32) if first else square_in[rows, :]
        value = piece[local, :].astype(F32)
        scaled[block, rows, :] = (value * gain_refs[block][0].astype(F32)).astype(BF16)
        value = value * value
        for part in range(span // HD):
            square = square + value[:, part * HD : (part + 1) * HD]
        square_out[rows, :] = square
        return carry

    if last:
        square_out = refs.pop()
        outs = refs
    else:
        acc_out, square_out = refs
    for block in range(count):
        base = 0
        for piece in x_refs[block]:
            body = functools.partial(scale_rows, block, piece, base)
            lax.fori_loop(0, piece.shape[0] // chunk, body, 0)
            base += piece.shape[0]
    width = weight_refs[0][0].shape[1]
    heads = width // HD
    if last:
        mean = jnp.sum(square_out[...], axis=-1, keepdims=True) * (1.0 / (groups * span))
        scale = lax.rsqrt(mean + EPSILON)
    for part in range(6):
        total = None if first else acc_in[part]
        for block in range(count):
            term = mxu(scaled[block], weight_refs[block][part][...])
            total = term if total is None else total + term
        if not last:
            acc_out[part] = total
            continue
        total = total * scale
        side, kind = part // 3, part % 3
        kv_outs = outs[2 * heads * side : 2 * heads * side + heads]
        q_outs = outs[2 * heads * side + heads : 2 * heads * side + 2 * heads]
        for head in range(heads):
            raw = total[:, head * HD : (head + 1) * HD]
            if kind == 1:
                kv_outs[head][1] = raw.astype(BF16)
                continue
            raw = raw * lax.rsqrt(jnp.mean(raw * raw, axis=-1, keepdims=True) + EPSILON)
            if kind == 0:
                kv_outs[head][0] = (raw * head_gains[1:2, :]).astype(BF16)
            else:
                q_outs[head][...] = (raw * (head_gains[0:1, :] * HD ** (-0.5))).astype(BF16)


def full(shape):
    return pl.BlockSpec(shape, lambda i, m: (0,) * len(shape))


def qkv_step(meta, layout, blocks, entries, gain, weights, state, head_gains):
    span = blocks[0][0].shape[1]
    half = sum(piece.shape[0] for piece in blocks[0])
    width = weights[0].shape[1]
    heads = width // HD
    count, first, last = len(blocks), state is None, head_gains is not None
    groups = gain.shape[0]
    shapes = [[p.shape for p in pieces] for pieces in blocks]
    inputs = [p for pieces in blocks for p in pieces]
    specs = [full(p.shape) for p in inputs]
    for entry in entries:
        inputs.append(gain)
        specs.append(
            pl.BlockSpec((1, 1, span), lambda i, m, entry=entry: (chip_of(m, *layout, entry), 0, 0))
        )
    for entry in entries:
        for weight in weights:
            inputs.append(weight)
            specs.append(
                pl.BlockSpec((span, width), lambda i, m, entry=entry: (chip_of(m, *layout, entry), 0))
            )
    if not first:
        inputs += list(state)
        specs += [full(s.shape) for s in state]
    scratch = [pltpu.VMEM((count, half, span), BF16)]
    if last:
        inputs.append(head_gains)
        specs.append(full(head_gains.shape))
        kv, q = jax.ShapeDtypeStruct((2, half, HD), BF16), jax.ShapeDtypeStruct((half, HD), BF16)
        outs = ([kv] * heads + [q] * heads) * 2
        scratch = [pltpu.VMEM((half, HD), F32)] + scratch
    else:
        outs = [
            jax.ShapeDtypeStruct((6, half, width), F32),
            jax.ShapeDtypeStruct((half, HD), F32),
        ]
    return pl.pallas_call(
        functools.partial(qkv_kernel, shapes, groups, first, last),
        grid_spec=pltpu.PrefetchScalarGridSpec(
            num_scalar_prefetch=1,
            grid=(1,),
            in_specs=specs,
            out_specs=[full(o.shape) for o in outs],
            scratch_shapes=scratch,
        ),
        out_shape=outs,
        compiler_params=params(30),
        cost_estimate=cost(12 * count * half * span * width, (6 + 2 * count) << 20),
        name="qkv_last" if last else "qkv_step",
    )(meta, *inputs)


def attention_kernel(images, pieces, half, meta, *refs):
    ctx, core, _, _ = split_meta(meta, images)
    ctxs = pieces // 2
    bases = []
    for piece in range(pieces):
        side = jnp.bitwise_xor(core, piece % 2)
        bases.append(lax.rem(ctx + ctxs - piece // 2, ctxs) * (2 * half) + side * half)
    q_refs, kv_refs, out_refs = refs[:2], refs[2 : 2 + pieces], refs[2 + pieces :]
    rows = q_refs[0].shape[0]
    step = pl.program_id(0)
    for side in range(2):
        place = bases[side] + step * rows + lax.broadcasted_iota(jnp.int32, (rows, 1), 0)
        limit = place
        for image in range(images):
            inner = place - meta[image]
            limit = jnp.where((inner >= 0) & (inner < IMG_TOK), meta[image] + IMG_TOK - 1, limit)
        query = q_refs[side][...]
        scores = []
        top = None
        for piece in range(pieces):
            score = lax.dot_general(
                query, kv_refs[piece][0], (((1,), (1,)), ((), ())), preferred_element_type=F32
            )
            position = lax.broadcasted_iota(jnp.int32, score.shape, 1)
            score = jnp.where(position <= limit - bases[piece], score, NEGATIVE_FILL)
            scores.append(score)
            best = jnp.max(score, axis=1, keepdims=True)
            top = best if top is None else jnp.maximum(top, best)
        total = jnp.zeros((rows, 1), F32)
        product = jnp.zeros((rows, HD), F32)
        for piece in range(pieces):
            weight = jnp.exp(scores[piece] - top)
            total = total + jnp.sum(weight, axis=1, keepdims=True)
            product = product + mxu(weight.astype(BF16), kv_refs[piece][1])
        out_refs[side][...] = (product / total).astype(BF16)


def attention(meta, queries, pieces, images):
    half = queries[0].shape[0]
    block = 256
    keys = half * len(pieces)
    rows = pl.BlockSpec((block, HD), lambda i, m: (i, 0))
    return pl.pallas_call(
        functools.partial(attention_kernel, images, len(pieces), half),
        grid_spec=pltpu.PrefetchScalarGridSpec(
            num_scalar_prefetch=1,
            grid=(half // block,),
            in_specs=[rows, rows] + [full(p.shape) for p in pieces],
            out_specs=[rows, rows],
        ),
        out_shape=[jax.ShapeDtypeStruct((half, HD), BF16)] * 2,
        compiler_params=params(24),
        cost_estimate=cost(8 * half * keys * HD, 4 * keys * HD, 2 * half * keys),
        name="attention",
    )(meta, *queries, *pieces)


def out_kernel(shapes, first, last, meta, *refs):
    refs = list(refs)
    count = len(shapes)
    x_refs = take_blocks(refs, shapes)
    weight_refs = [refs.pop(0) for _ in range(2 * count)]
    start = [refs.pop(0), refs.pop(0)] if first else [refs[0].at[0], refs.pop(0).at[1]]
    outs = refs
    for side in range(2):
        total = start[side][...].astype(F32)
        for block in range(count):
            weight = weight_refs[2 * block + side][0, :, 0]
            total = total + mxu(load(x_refs[block]), weight.reshape(2 * HD, weight.shape[2]))
        if last:
            outs[side][...] = total.astype(BF16)
        else:
            outs[0][side] = total


def out_step(meta, layout, blocks, entries, head, weights, state, last):
    half = sum(piece.shape[0] for piece in blocks[0])
    width = weights[0].shape[1]
    first = isinstance(state, tuple)
    count = len(blocks)
    shapes = [[p.shape for p in pieces] for pieces in blocks]
    views = [w.reshape(-1, 2, width // HD, HD, width) for w in weights]
    inputs = [p for pieces in blocks for p in pieces]
    specs = [full(p.shape) for p in inputs]
    for entry in entries:
        for view in views:
            inputs.append(view)
            specs.append(
                pl.BlockSpec(
                    (1, 2, 1, HD, width),
                    lambda i, m, entry=entry: (chip_of(m, *layout, entry), 0, head, 0, 0),
                )
            )
    states = list(state) if first else [state]
    inputs += states
    specs += [full(s.shape) for s in states]
    if last:
        outs = [jax.ShapeDtypeStruct((half, width), BF16)] * 2
    else:
        outs = [jax.ShapeDtypeStruct((2, half, width), F32)]
    result = pl.pallas_call(
        functools.partial(out_kernel, shapes, first, last),
        grid_spec=pltpu.PrefetchScalarGridSpec(
            num_scalar_prefetch=1,
            grid=(1,),
            in_specs=specs,
            out_specs=[full(o.shape) for o in outs],
        ),
        out_shape=outs,
        compiler_params=params(16),
        cost_estimate=cost(8 * count * half * HD * width, (2 + count) << 20),
        name="out_last" if last else "out_step",
    )(meta, *inputs)
    return result if last else result[0]


def pick_kernel(images, ctxs, meta, own_ref, par_ref, *out_refs):
    half = own_ref.shape[0]
    ctx, core, _, _ = split_meta(meta, images)
    for target in range(2 * ctxs):
        to_core = jnp.bitwise_xor(core, target % 2)
        slot = 2 * lax.rem(ctx + target // 2, ctxs) + to_core
        start = meta[meta[2 * images + slot]]
        place = start + lax.broadcasted_iota(jnp.int32, (IMG_TOK, half), 0)
        column = ctx * (2 * half) + lax.broadcasted_iota(jnp.int32, (IMG_TOK, half), 1)
        own = jnp.where(place == column + core * half, 1.0, 0.0).astype(BF16)
        par = jnp.where(place == column + (1 - core) * half, 1.0, 0.0).astype(BF16)
        out_refs[target][...] = (mxu(own, own_ref[...]) + mxu(par, par_ref[...])).astype(BF16)


def pick_rows(meta, own, par, images, ctxs):
    half, width = own.shape
    targets = 2 * ctxs
    return pl.pallas_call(
        functools.partial(pick_kernel, images, ctxs),
        grid_spec=pltpu.PrefetchScalarGridSpec(
            num_scalar_prefetch=1,
            grid=(1,),
            in_specs=[full(own.shape), full(par.shape)],
            out_specs=[full((IMG_TOK, width))] * targets,
        ),
        out_shape=[jax.ShapeDtypeStruct((IMG_TOK, width), BF16)] * targets,
        compiler_params=params(16),
        cost_estimate=cost(targets * 4 * IMG_TOK * half * width, 1 << 20),
        name="pick_rows",
    )(meta, own, par)


def merge_kernel(*refs):
    out_ref = refs[-1]
    sides = refs[: len(refs) // 2], refs[len(refs) // 2 : -1]
    width = sides[0][0].shape[1]
    for side in range(2):
        total = sides[side][0][...].astype(F32)
        for part in sides[side][1:]:
            total = total + part[...].astype(F32)
        out_ref[:, side * width : (side + 1) * width] = total.astype(BF16)


def merge_picks(own_parts, par_parts):
    width = own_parts[0].shape[1]
    return pl.pallas_call(
        merge_kernel,
        out_shape=jax.ShapeDtypeStruct((IMG_TOK, 2 * width), BF16),
        compiler_params=pltpu.CompilerParams(vmem_limit_bytes=8 << 20),
        cost_estimate=cost(1 << 20, 1 << 20),
        name="merge_picks",
    )(*own_parts, *par_parts)


def spread(active, spread_ref):
    row = lax.broadcasted_iota(jnp.int32, (IMG_TOK, PIX * CIN), 0)
    patch_row, patch_col = row >> 4, row & (SIDE - 1)
    total = None
    for index in range(9):
        down, right = index // 3 - 1, index % 3 - 1
        part = mxu(active, spread_ref[:, index * PIX * CIN : (index + 1) * PIX * CIN])
        offset = down * SIDE + right
        if offset:
            part = pltpu.roll(part, offset % IMG_TOK, 0)
        source_row, source_col = patch_row - down, patch_col - right
        inside = (source_row >= 0) & (source_row < SIDE) & (source_col >= 0) & (source_col < SIDE)
        part = jnp.where(inside, part, 0.0)
        total = part if total is None else total + part
    return total


def up_kernel(shapes, halves, first, last, *refs):
    refs = list(refs)
    count = len(shapes)
    x_refs = take_blocks(refs, shapes)
    weight_refs = [[[refs.pop(0) for _ in range(2)] for _ in range(halves)] for _ in range(count)]
    acc_in = None if first else refs.pop(0)
    spread_ref = refs.pop(0) if last else None
    out_ref = refs[0]
    width = x_refs[0][0].shape[1] // 2
    values = [load(pieces) for pieces in x_refs]
    totals = []
    for part in range(halves):
        total = None if first else acc_in[part]
        for block in range(count):
            for side in range(2):
                term = mxu(
                    values[block][:, side * width : (side + 1) * width],
                    weight_refs[block][part][side][0],
                )
                total = term if total is None else total + term
        totals.append(total)
        if not last:
            out_ref[part] = total
    if last:
        active = [silu(total).astype(BF16) for total in totals]
        active = jnp.concatenate(active, axis=1) if halves > 1 else active[0]
        out_ref[...] = spread(active, spread_ref)


def up_step(blocks, offsets, weights, state, spread_weight):
    span = blocks[0][0].shape[1]
    shapes = [[p.shape for p in pieces] for pieces in blocks]
    halves, count = len(weights), len(blocks)
    first, last = state is None, spread_weight is not None
    whole = lambda shape: pl.BlockSpec(shape, lambda i: (0,) * len(shape))
    inputs = [p for pieces in blocks for p in pieces]
    specs = [whole(p.shape) for p in inputs]
    for offset in offsets:
        for sides in weights:
            for weight in sides:
                inputs.append(weight)
                specs.append(pl.BlockSpec((1, span // 2, CH), lambda i, offset=offset: (offset, 0, 0)))
    if not first:
        inputs.append(state)
        specs.append(whole(state.shape))
    if last:
        inputs.append(spread_weight)
        specs.append(whole(spread_weight.shape))
        out = jax.ShapeDtypeStruct((IMG_TOK, PIX * CIN), F32)
    else:
        out = jax.ShapeDtypeStruct((halves, IMG_TOK, CH), F32)
    return pl.pallas_call(
        functools.partial(up_kernel, shapes, halves, first, last),
        grid=(1,),
        in_specs=specs,
        out_specs=whole(out.shape),
        out_shape=out,
        compiler_params=params(16),
        cost_estimate=cost(2 * count * IMG_TOK * span * CH * halves, (1 + count) << 20),
        name="up_last" if last else "up_step",
    )(*inputs)


def spread_weights(up_conv, pixels):
    taps = up_conv.reshape(9, CH, CIN).transpose(1, 0, 2).reshape(CH, 9 * CIN)
    shape = (pixels.shape[0], 9 * CIN, 9 * PIX * CIN)
    row = lax.broadcasted_iota(jnp.int32, shape, 1)
    col = lax.broadcasted_iota(jnp.int32, shape, 2)
    pixel = pixels[:, None, None]
    tap, channel = row >> 3, row & 7
    patch, target, out_channel = col >> 7, (col >> 3) & 15, col & 7
    tap_row, tap_col = tap // 3, tap % 3
    down, right = patch // 3 - 1, patch % 3 - 1
    hit = (
        (channel == out_channel)
        & ((pixel >> 2) + 1 - tap_row == (target >> 2) + PATCH * down)
        & ((pixel & 3) + 1 - tap_col == (target & 3) + PATCH * right)
    )
    placed = jnp.where(hit, 1.0, 0.0).astype(BF16)
    spread = jnp.einsum("ct,ptn->pcn", taps, placed, preferred_element_type=F32)
    return spread.astype(BF16).reshape(pixels.shape[0] * CH, 9 * PIX * CIN)


def by_core(core, own, other, axis):
    return jnp.where(
        core == 0, jnp.concatenate([own, other], axis), jnp.concatenate([other, own], axis)
    )


def shift(values, axis, step):
    count = lax.axis_size(axis)
    return lax.ppermute(values, axis, [(i, (i + step) % count) for i in range(count)])


def gather_small(latents, down_conv, norm_gain):
    ctxs, tiles = lax.axis_size("ctx"), lax.axis_size("tile")
    tile, mpo, core = (lax.axis_index(name) for name in ("tile", "mpo", "core"))
    local, height, breadth = latents.shape
    taps, channels = down_conv.shape
    width = norm_gain.shape[0]
    every = jnp.concatenate([latents] + [shift(latents, "ctx", s) for s in range(1, ctxs)])
    size = -(-(taps * channels + width) // 1024) * 1024
    flat = jnp.concatenate([down_conv.reshape(-1), norm_gain])
    flat = jnp.pad(flat, (0, size - flat.shape[0])).reshape(1, size // 128, 128)
    flat = by_core(core, flat, swap(flat), 0)[None]
    flat = by_core(mpo, flat, shift(flat, "mpo", 1), 0).reshape(4, size)
    conv = flat[:, : taps * channels].reshape(4, taps, channels)
    conv = conv.transpose(1, 0, 2).reshape(taps, 4 * channels)
    gain = flat[:, taps * channels : taps * channels + width].reshape(4 * width // 128, 128)
    rows = ctxs * local * height
    sent = every.reshape(rows * breadth // 128, 128)
    lines = sent.shape[0]
    pad = -gain.shape[0] % 16
    sent = jnp.concatenate([sent, jnp.pad(gain, ((0, pad), (0, 0)))])[None]
    turned = [shift(sent, "tile", s) for s in range(tiles - 1, 0, -1)] + [sent]
    whole = jnp.concatenate(turned + turned[:-1])
    whole = lax.dynamic_slice_in_dim(whole, tiles - 1 - tile, tiles, 0)
    images = whole[:, :lines].reshape(tiles, ctxs * local, height, breadth)
    images = images.transpose(1, 0, 2, 3).reshape(ctxs * local, tiles * height, breadth)
    gain = whole[:, lines : lines + gain.shape[0]].reshape(tiles * 2, 1, 2 * width)
    return images, conv, gain


def transpose_up(patch_out):
    ctxs, tiles, outer = (lax.axis_size(name) for name in ("ctx", "tile", "mpo"))
    ctx, tile, mpo = (lax.axis_index(name) for name in ("ctx", "tile", "mpo"))
    width, features = patch_out.shape
    deep = features // (tiles * outer)
    halves = 2 if ctxs == 2 and deep == 2 * CH else 1
    blocks = []
    for down in range(tiles):
        for right in range(outer):
            chip = lax.rem(tile + down, tiles) * outer + lax.rem(mpo + right, outer)
            start = chip * deep + (ctx * CH if halves == 2 else 0)
            block = lax.dynamic_slice_in_dim(patch_out, start, deep // halves, 1)
            if down or right:
                pairs = [
                    (t * outer + m, (t + down) % tiles * outer + (m + right) % outer)
                    for t in range(tiles)
                    for m in range(outer)
                ]
                block = lax.ppermute(block, ("tile", "mpo"), pairs)
            blocks.append(block)
    own = jnp.stack(blocks)
    weights = [own] if halves == 1 else [own, shift(own, "ctx", 1)]
    return [[weight, swap(weight)] for weight in weights]


def gather_work(block, state, step):
    tiles = lax.axis_size("tile")
    ring, cross = block, None
    fresh, entries = [[block]], [0]
    for index in range(tiles - 1):
        ring_next, cross_next = shift(ring, "tile", 1), shift(ring, "mpo", 1)
        state = step(fresh, entries, state, False)
        ring, cross, state = lax.optimization_barrier((ring_next, cross_next, state))
        fresh, entries = [[ring], [cross]], [2 * index + 2, 2 * index + 1]
    middle = block.shape[0] // 2
    upper, lower = shift(ring[:middle], "mpo", 1), shift(cross[middle:], "tile", 1)
    state = step(fresh, entries, state, False)
    upper, lower, state = lax.optimization_barrier((upper, lower, state))
    return step([[upper, lower]], [2 * tiles - 1], state, True)


def shards(
    text_embed,
    latents,
    down_conv,
    patch_in,
    norm_gain,
    query_weight,
    key_weight,
    value_weight,
    query_gain,
    key_gain,
    out_weight,
    patch_out,
    up_conv,
    span_start,
    image_of_slot,
):
    ctxs, tiles, outer = (lax.axis_size(name) for name in ("ctx", "tile", "mpo"))
    ctx, tile, mpo, core = (lax.axis_index(name) for name in ("ctx", "tile", "mpo", "core"))
    seq_rows, width = text_embed.shape
    half = seq_rows // 2
    heads = width // HD
    images = span_start.shape[0]
    local = latents.shape[0]

    every_latent, conv, gain = gather_small(latents, down_conv, norm_gain)
    weights = [swap(w) for w in (key_weight, value_weight, query_weight)]
    weights += [key_weight, value_weight, query_weight]
    out_par = swap(out_weight)
    up_weights = transpose_up(patch_out)

    numbers = jnp.arange(images, dtype=jnp.int32)
    matches = image_of_slot[None, :] == numbers[:, None]
    slot_of_image = jnp.sum(jnp.where(matches, numbers[None, :], 0), axis=1)
    slot_place = lax.rem(ctx + ctxs - slot_of_image // local, ctxs) * local + slot_of_image % local
    meta = jnp.concatenate(
        [span_start, slot_place, image_of_slot, jnp.stack([ctx, core, tile, mpo])]
    ).astype(jnp.int32)
    layout = (images, tiles, outer)

    padded = jnp.pad(every_latent, ((0, 0), (1, 1), (CIN, 128 - CIN)))
    rows = jnp.stack(
        [padded[:, r : r + HL - PATCH + 1 : PATCH, :].reshape(images * SIDE, -1) for r in range(PATCH + 2)]
    )
    conv = conv.reshape(3, 3 * CIN, CH)
    conv = jnp.stack(
        [
            jnp.pad(conv, ((0, 0), (CIN * c, WINDOW - 3 * CIN - CIN * c), (0, 0))).reshape(TAPS, CH)
            for c in range(PATCH)
        ]
    )
    text = jnp.roll(text_embed.reshape(2, half, width), core, axis=0).reshape(seq_rows, width)
    stream = down_stream(meta, rows, conv, patch_in, text, images)
    stream_own = stream[0]
    stream_par = swap(stream[1])

    head_gains = jnp.stack([query_gain, key_gain])

    def project(blocks, entries, state, last):
        return qkv_step(
            meta, layout, blocks, entries, gain, weights, state, head_gains if last else None
        )

    state = gather_work(by_core(core, stream_own, stream_par, 1), None, project)
    kv_send, q_send = state[:heads], state[heads : 2 * heads]
    kv_own, q_own = state[2 * heads : 3 * heads], state[3 * heads :]

    def shifted(values, step, cross):
        pairs = [
            (2 * c + k, 2 * ((c + step) % ctxs) + (1 - k if cross else k))
            for c in range(ctxs)
            for k in range(2)
        ]
        return lax.ppermute(values, ("ctx", "core"), pairs)

    attended = []
    for head in range(heads):
        q_par = swap(q_send[head])
        pieces = [kv_own[head], swap(kv_send[head])]
        for step in range(1, ctxs):
            pieces += [shifted(kv_own[head], step, False), shifted(kv_send[head], step, True)]
        att_own, att_send = attention(meta, [q_own[head], q_par], pieces, images)
        attended.append(by_core(core, att_own, swap(att_send), 1))
    state = (stream_own, stream_par)
    for head in range(heads):

        def project_out(blocks, entries, state, last):
            return out_step(
                meta, layout, blocks, entries, head, (out_weight, out_par), state, last and head == heads - 1
            )

        state = gather_work(attended[head], state, project_out)
    out_own, out_send = state
    out_other = swap(out_send)
    layer_out = by_core(core, out_own, out_other, 0)

    picks = pick_rows(meta, out_own, out_other, images, ctxs)
    own_parts, par_parts = [picks[0]], [swap(picks[1])]
    for step in range(1, ctxs):
        own_parts.append(shifted(picks[2 * step], step, False))
        par_parts.append(shifted(picks[2 * step + 1], step, True))

    halves = len(up_weights)
    pixel = tile * outer + mpo
    pixels = jnp.stack([pixel * halves + lax.rem(ctx + h, halves) for h in range(halves)])
    spread_weight = spread_weights(up_conv, pixels)

    def project_up(blocks, entries, state, last):
        return up_step(blocks, entries, up_weights, state, spread_weight if last else None)

    state = gather_work(merge_picks(own_parts, par_parts), None, project_up)

    bands = state.reshape(tiles, IMG_TOK // tiles, PIX * CIN)
    band = lax.dynamic_index_in_dim(bands, tile, 0, keepdims=False)
    for step in range(1, tiles):
        piece = lax.dynamic_index_in_dim(bands, lax.rem(tile + step, tiles), 0, keepdims=False)
        band = band + shift(piece, "tile", step)
    summed = band
    for step in range(1, outer):
        summed = summed + shift(band, "mpo", step)
    slots = by_core(core, summed[None], swap(summed)[None], 0)
    noise = slots.reshape(2, SIDE // tiles, SIDE, PATCH, PATCH * CIN).transpose(0, 1, 3, 2, 4)
    return layer_out, noise.reshape(2, HL // tiles, WL * CIN)


def solution(mesh):
    ctxs, tiles, parts = mesh.devices.shape
    fine = Mesh(
        mesh.devices.reshape(ctxs, tiles, parts // 2, 2), ("ctx", "tile", "mpo", "core")
    )
    features = ("tile", "mpo", "core")
    return jax.shard_map(
        shards,
        mesh=fine,
        in_specs=(
            P("ctx", features),
            P("ctx", "tile", None),
            P(None, ("mpo", "core")),
            P(None, features),
            P(features),
            P(None, features),
            P(None, features),
            P(None, features),
            P(),
            P(),
            P(None, features),
            P(features, None),
            P(),
            P(),
            P(),
        ),
        out_specs=(P("ctx", features), P("ctx", "tile", None)),
        check_vma=False,
    )
```

```python
import functools

import jax
import jax.numpy as jnp
from jax import lax
from jax.experimental import pallas as pl
from jax.experimental.pallas import tpu as pltpu
from jax.sharding import Mesh
from jax.sharding import PartitionSpec as P

HD = 128
CH = 256
CIN = 8
WL = 64
HL = 64
PATCH = 4
PIX = PATCH * PATCH
SIDE = WL // PATCH
IMG_TOK = 256
EPSILON = 1e-05
NEGATIVE_FILL = -1e30
WINDOW = (PATCH + 2) * CIN
TAPS = 3 * WINDOW
BF16 = jnp.bfloat16
F32 = jnp.float32


def split_meta(meta, images):
    return meta[3 * images], meta[3 * images + 1], meta[3 * images + 2], meta[3 * images + 3]


def params(mebibytes):
    return pltpu.CompilerParams(
        dimension_semantics=("arbitrary",), vmem_limit_bytes=mebibytes * 1024 * 1024
    )


def cost(flops, nbytes, transcendentals=0):
    return pl.CostEstimate(
        flops=int(flops), bytes_accessed=int(nbytes), transcendentals=int(transcendentals)
    )


def silu(values):
    half = values * 0.5
    return half + half * jnp.tanh(half)


def mxu(left, right):
    return jnp.dot(left, right, preferred_element_type=F32)


def swap(values):
    return lax.ppermute(values, "core", [(0, 1), (1, 0)])


GAIN_ROWS = 16
TOP = 16


def down_kernel(images, tiles, half, meta, *refs):
    lat_refs, refs = refs[:tiles], refs[tiles:]
    conv_ref, patch_ref, own_text, par_text, gain_ref, first_ref, second_ref = refs[:7]
    grid_rows, conv_wide, conv_bf16, windows, total = refs[7:]
    step = pl.program_id(0)
    group = images * SIDE
    ctx, core, tile, _ = split_meta(meta, images)

    @pl.when(step == 0)
    def _():
        grid_rows[...] = jnp.zeros_like(grid_rows)
        blocks = grid_rows.shape[1]
        for index in range(tiles):
            band = lat_refs[index].shape[1]
            at = TOP + lax.rem(tile + tiles - index, tiles) * band
            rows = pl.ds(pl.multiple_of(at, 8), band)
            latent = lat_refs[index][...].astype(F32)
            edges = [jnp.zeros((images, band, size), F32) for size in (CIN, HD - CIN)]
            wide = jnp.concatenate([edges[0], latent, edges[1]], axis=2)
            for part in range(blocks):
                grid_rows[:, part, rows, :] = wide[:, :, part * HD : (part + 1) * HD]
        conv_wide[...] = jnp.zeros_like(conv_wide)
        conv = conv_ref[...].astype(F32)
        for col in range(PATCH):
            for tap in range(3):
                at = WINDOW * tap + CIN * col
                conv_wide[at : at + 3 * CIN, CH * col : CH * (col + 1)] = conv[
                    3 * CIN * tap : 3 * CIN * (tap + 1), :
                ]
        conv_bf16[...] = conv_wide[...].astype(BF16)

        def build(image, carry):
            for row in range(PATCH + 2):
                take = pl.ds(TOP - 1 + row, SIDE, stride=PATCH)
                line = [grid_rows[image, part, take, :] for part in range(blocks)]
                line = jnp.concatenate(line, axis=1).astype(BF16)
                for col in range(SIDE):
                    piece = line[:, PATCH * CIN * col : PATCH * CIN * col + WINDOW]
                    at = pl.ds(pl.multiple_of(group * col + image * SIDE, SIDE), SIDE)
                    for shift in range(3):
                        if 0 <= row - shift < PATCH:
                            windows[row - shift, at, WINDOW * shift : WINDOW * (shift + 1)] = piece
            return carry

        lax.fori_loop(0, images, build, 0)
        total[...] = jnp.zeros_like(total)

    chunk = 256
    for part in range(images * IMG_TOK // chunk):
        rows = slice(part * chunk, (part + 1) * chunk)
        hidden = silu(mxu(windows[step, rows, :], conv_bf16[...])).astype(BF16)
        total[rows, :] += mxu(hidden, patch_ref[...])

    @pl.when(step == PATCH - 1)
    def _():
        tokens = total[...].astype(BF16)
        block = half // 2
        for side, text_ref in enumerate((own_text, par_text)):
            base = ctx * (2 * half) + jnp.bitwise_xor(core, side) * half
            for part, out_ref in enumerate((first_ref, second_ref)):
                place = base + part * block + lax.broadcasted_iota(jnp.int32, (block, 1), 0)
                source = jnp.full((block, 1), -1, jnp.int32)
                for image in range(images):
                    inner = place - meta[image]
                    inside = (inner >= 0) & (inner < IMG_TOK)
                    index = (inner & (SIDE - 1)) * group + meta[images + image] * SIDE + (inner >> 4)
                    source = jnp.where(inside, index, source)
                choice = source == lax.broadcasted_iota(jnp.int32, (block, images * IMG_TOK), 1)
                picked = mxu(jnp.where(choice, 1.0, 0.0).astype(BF16), tokens)
                text = text_ref[0, part * block : (part + 1) * block, :].astype(F32)
                out_ref[side, :block, :] = jnp.where(source >= 0, picked, text).astype(BF16)
            gain = gain_ref[...].astype(F32)
            first_ref[side, block:, :] = jnp.broadcast_to(gain, (GAIN_ROWS, gain.shape[1])).astype(BF16)


def down_stream(meta, pieces, conv, patch_in, text, gain, images):
    seq_rows, width = text.shape
    half = seq_rows // 2
    tiles = len(pieces)
    count = images * IMG_TOK
    halves = text.reshape(2, half, width)
    core_at = 3 * images + 1
    first, second = (2, half // 2 + GAIN_ROWS, width), (2, half // 2, width)
    return pl.pallas_call(
        functools.partial(down_kernel, images, tiles, half),
        grid_spec=pltpu.PrefetchScalarGridSpec(
            num_scalar_prefetch=1,
            grid=(PATCH,),
            in_specs=[full(p.shape) for p in pieces]
            + [
                full(conv.shape),
                pl.BlockSpec((PATCH * CH, width), lambda i, m: (i, 0)),
                pl.BlockSpec((1, half, width), lambda i, m: (m[core_at], 0, 0)),
                pl.BlockSpec((1, half, width), lambda i, m: (1 - m[core_at], 0, 0)),
                full((1, width)),
            ],
            out_specs=[full(first), full(second)],
            scratch_shapes=[
                pltpu.VMEM((images, WL * CIN // HD + 1, TOP + HL + 16, HD), F32),
                pltpu.VMEM((TAPS, PATCH * CH), F32),
                pltpu.VMEM((TAPS, PATCH * CH), BF16),
                pltpu.VMEM((PATCH, count, TAPS), BF16),
                pltpu.VMEM((count, width), F32),
            ],
        ),
        out_shape=[jax.ShapeDtypeStruct(first, BF16), jax.ShapeDtypeStruct(second, BF16)],
        compiler_params=params(40),
        cost_estimate=cost(2 * count * PIX * CH * (256 + width), 4 << 20, count * PIX * CH),
        name="down_stream",
    )(meta, *pieces, conv, patch_in, halves, halves, gain.reshape(1, width))


def full(shape):
    return pl.BlockSpec(shape, lambda i, m: (0,) * len(shape))


def load(pieces):
    return jnp.concatenate([piece[...] for piece in pieces], axis=0)


def take_blocks(refs, count):
    return [[refs.pop(0), refs.pop(0)] for _ in range(count)]


def chip_of(meta, images, tiles, outer, entry):
    _, _, tile, mpo = split_meta(meta, images)
    return lax.rem(tile + tiles - entry // 2, tiles) * outer + lax.rem(mpo + entry % 2, outer)


def qkv_kernel(count, groups, first, last, meta, *refs):
    refs = list(refs)
    x_refs = take_blocks(refs, count)
    weight_refs = [[refs.pop(0) for _ in range(6)] for _ in range(count)]
    if not first:
        acc_in, square_in = refs.pop(0), refs.pop(0)
    if last:
        head_gains = refs.pop(0)
    scaled = refs.pop()
    half, span = scaled.shape[1:]
    chunk = 64

    def scale_rows(block, gain, piece, base, index, carry):
        rows = pl.ds(pl.multiple_of(base + index * chunk, chunk), chunk)
        local = pl.ds(pl.multiple_of(index * chunk, chunk), chunk)
        if block:
            square = square_out[rows, :]
        else:
            square = jnp.zeros((chunk, HD), F32) if first else square_in[rows, :]
        value = piece[local, :].astype(F32)
        scaled[block, rows, :] = (value * gain).astype(BF16)
        value = value * value
        for part in range(span // HD):
            square = square + value[:, part * HD : (part + 1) * HD]
        square_out[rows, :] = square
        return carry

    if last:
        square_out = refs.pop()
        outs = refs
    else:
        acc_out, square_out = refs
    for block in range(count):
        gain = x_refs[block][0][half // 2 :, :].astype(F32)[:1]
        for part in range(2):
            body = functools.partial(scale_rows, block, gain, x_refs[block][part], part * half // 2)
            lax.fori_loop(0, half // 2 // chunk, body, 0)
    width = weight_refs[0][0].shape[1]
    heads = width // HD
    if last:
        mean = jnp.sum(square_out[...], axis=-1, keepdims=True) * (1.0 / (groups * span))
        scale = lax.rsqrt(mean + EPSILON)
    for part in range(6):
        total = None if first else acc_in[part]
        for block in range(count):
            term = mxu(scaled[block], weight_refs[block][part][...])
            total = term if total is None else total + term
        if not last:
            acc_out[part] = total
            continue
        total = total * scale
        side, kind = part // 3, part % 3
        kv_outs = outs[2 * heads * side : 2 * heads * side + heads]
        q_outs = outs[2 * heads * side + heads : 2 * heads * side + 2 * heads]
        for head in range(heads):
            raw = total[:, head * HD : (head + 1) * HD]
            if kind == 1:
                kv_outs[head][1] = raw.astype(BF16)
                continue
            raw = raw * lax.rsqrt(jnp.mean(raw * raw, axis=-1, keepdims=True) + EPSILON)
            if kind == 0:
                kv_outs[head][0] = (raw * head_gains[1:2, :]).astype(BF16)
            else:
                q_outs[head][...] = (raw * (head_gains[0:1, :] * HD ** (-0.5))).astype(BF16)


def qkv_step(meta, layout, blocks, entries, weights, state, head_gains):
    span = blocks[0][1].shape[1]
    half = 2 * blocks[0][1].shape[0]
    width = weights[0].shape[1]
    heads = width // HD
    count, first, last = len(blocks), state is None, head_gains is not None
    groups = layout[1] * layout[2]
    inputs = [p for pieces in blocks for p in pieces]
    specs = [full(p.shape) for p in inputs]
    for entry in entries:
        for weight in weights:
            inputs.append(weight)
            specs.append(
                pl.BlockSpec((span, width), lambda i, m, entry=entry: (chip_of(m, *layout, entry), 0))
            )
    if not first:
        inputs += list(state)
        specs += [full(s.shape) for s in state]
    scratch = [pltpu.VMEM((count, half, span), BF16)]
    if last:
        inputs.append(head_gains)
        specs.append(full(head_gains.shape))
        kv, q = jax.ShapeDtypeStruct((2, half, HD), BF16), jax.ShapeDtypeStruct((half, HD), BF16)
        outs = ([kv] * heads + [q] * heads) * 2
        scratch = [pltpu.VMEM((half, HD), F32)] + scratch
    else:
        outs = [
            jax.ShapeDtypeStruct((6, half, width), F32),
            jax.ShapeDtypeStruct((half, HD), F32),
        ]
    return pl.pallas_call(
        functools.partial(qkv_kernel, count, groups, first, last),
        grid_spec=pltpu.PrefetchScalarGridSpec(
            num_scalar_prefetch=1,
            grid=(1,),
            in_specs=specs,
            out_specs=[full(o.shape) for o in outs],
            scratch_shapes=scratch,
        ),
        out_shape=outs,
        compiler_params=params(48),
        cost_estimate=cost(12 * count * half * span * width, (6 + 2 * count) << 20),
        name="qkv_last" if last else "qkv_step",
    )(meta, *inputs)


def attention_kernel(images, pieces, half, meta, *refs):
    ctx, core, _, _ = split_meta(meta, images)
    ctxs = pieces // 2
    bases = []
    for piece in range(pieces):
        side = jnp.bitwise_xor(core, piece % 2)
        bases.append(lax.rem(ctx + ctxs - piece // 2, ctxs) * (2 * half) + side * half)
    q_refs, kv_refs, out_refs = refs[:2], refs[2 : 2 + pieces], refs[2 + pieces :]
    rows = q_refs[0].shape[0]
    step = pl.program_id(0)
    for side in range(2):
        place = bases[side] + step * rows + lax.broadcasted_iota(jnp.int32, (rows, 1), 0)
        limit = place
        for image in range(images):
            inner = place - meta[image]
            limit = jnp.where((inner >= 0) & (inner < IMG_TOK), meta[image] + IMG_TOK - 1, limit)
        query = q_refs[side][...]
        scores = []
        top = None
        for piece in range(pieces):
            score = lax.dot_general(
                query, kv_refs[piece][0], (((1,), (1,)), ((), ())), preferred_element_type=F32
            )
            position = lax.broadcasted_iota(jnp.int32, score.shape, 1)
            score = jnp.where(position <= limit - bases[piece], score, NEGATIVE_FILL)
            scores.append(score)
            best = jnp.max(score, axis=1, keepdims=True)
            top = best if top is None else jnp.maximum(top, best)
        total = jnp.zeros((rows, 1), F32)
        product = jnp.zeros((rows, HD), F32)
        for piece in range(pieces):
            weight = jnp.exp(scores[piece] - top)
            total = total + jnp.sum(weight, axis=1, keepdims=True)
            product = product + mxu(weight.astype(BF16), kv_refs[piece][1])
        out_refs[side][...] = (product / total).astype(BF16)


def attention(meta, queries, pieces, images):
    half = queries[0].shape[0]
    block = 256
    keys = half * len(pieces)
    rows = pl.BlockSpec((block, HD), lambda i, m: (i, 0))
    return pl.pallas_call(
        functools.partial(attention_kernel, images, len(pieces), half),
        grid_spec=pltpu.PrefetchScalarGridSpec(
            num_scalar_prefetch=1,
            grid=(half // block,),
            in_specs=[rows, rows] + [full(p.shape) for p in pieces],
            out_specs=[rows, rows],
        ),
        out_shape=[jax.ShapeDtypeStruct((half, HD), BF16)] * 2,
        compiler_params=params(24),
        cost_estimate=cost(8 * half * keys * HD, 4 * keys * HD, 2 * half * keys),
        name="attention",
    )(meta, *queries, *pieces)


def out_kernel(count, heads, first, last, meta, *refs):
    refs = list(refs)
    x_refs = take_blocks(refs, count)
    weight_refs = [[refs.pop(0), refs.pop(0)] for _ in range(count)]
    if first:
        streams = [refs.pop(0), refs.pop(0)]
        block = streams[1].shape[1]
    else:
        acc_in = refs.pop(0)
    outs = refs
    for side in range(2):
        if first:
            rows = [streams[0][side, :block, :], streams[1][side]]
            total = jnp.concatenate(rows, axis=0).astype(F32)
        else:
            total = acc_in[side]
        for index in range(count):
            weight = weight_refs[index][side]
            if heads == 2:
                for head in range(heads):
                    part = weight[0, :, head].reshape(2 * HD, weight.shape[4])
                    total = total + mxu(x_refs[index][head][...], part)
            else:
                total = total + mxu(load(x_refs[index]), weight[0, :, 0].reshape(2 * HD, weight.shape[4]))
        if last:
            outs[side][...] = total.astype(BF16)
        else:
            outs[0][side] = total


def out_step(meta, layout, blocks, entries, weights, state, last):
    width = weights[0].shape[1]
    heads = width // HD
    half = blocks[0][0].shape[0] * (1 if heads == 2 else 2)
    first = isinstance(state, list)
    count = len(blocks)
    views = [w.reshape(-1, 2, heads, HD, width) for w in weights]
    inputs = [p for pieces in blocks for p in pieces]
    specs = [full(p.shape) for p in inputs]
    for entry in entries:
        for view in views:
            inputs.append(view)
            specs.append(
                pl.BlockSpec(
                    (1, 2, heads, HD, width),
                    lambda i, m, entry=entry: (chip_of(m, *layout, entry), 0, 0, 0, 0),
                )
            )
    states = state if first else [state]
    inputs += states
    specs += [full(s.shape) for s in states]
    if last:
        outs = [jax.ShapeDtypeStruct((half, width), BF16)] * 2
    else:
        outs = [jax.ShapeDtypeStruct((2, half, width), F32)]
    result = pl.pallas_call(
        functools.partial(out_kernel, count, heads, first, last),
        grid_spec=pltpu.PrefetchScalarGridSpec(
            num_scalar_prefetch=1,
            grid=(1,),
            in_specs=specs,
            out_specs=[full(o.shape) for o in outs],
        ),
        out_shape=outs,
        compiler_params=params(40),
        cost_estimate=cost(8 * count * half * heads * HD * width, (2 + count) << 20),
        name="out_last" if last else "out_step",
    )(meta, *inputs)
    return result if last else result[0]


def pick_kernel(images, ctxs, meta, own_ref, par_ref, *out_refs):
    half = own_ref.shape[0]
    ctx, core, _, _ = split_meta(meta, images)
    for target in range(2 * ctxs):
        to_core = jnp.bitwise_xor(core, target % 2)
        slot = 2 * lax.rem(ctx + target // 2, ctxs) + to_core
        start = meta[meta[2 * images + slot]]
        place = start + lax.broadcasted_iota(jnp.int32, (IMG_TOK, half), 0)
        column = ctx * (2 * half) + lax.broadcasted_iota(jnp.int32, (IMG_TOK, half), 1)
        own = jnp.where(place == column + core * half, 1.0, 0.0).astype(BF16)
        par = jnp.where(place == column + (1 - core) * half, 1.0, 0.0).astype(BF16)
        out_refs[target][...] = (mxu(own, own_ref[...]) + mxu(par, par_ref[...])).astype(BF16)


def pick_rows(meta, own, par, images, ctxs):
    half, width = own.shape
    targets = 2 * ctxs
    return pl.pallas_call(
        functools.partial(pick_kernel, images, ctxs),
        grid_spec=pltpu.PrefetchScalarGridSpec(
            num_scalar_prefetch=1,
            grid=(1,),
            in_specs=[full(own.shape), full(par.shape)],
            out_specs=[full((IMG_TOK, width))] * targets,
        ),
        out_shape=[jax.ShapeDtypeStruct((IMG_TOK, width), BF16)] * targets,
        compiler_params=params(16),
        cost_estimate=cost(targets * 4 * IMG_TOK * half * width, 1 << 20),
        name="pick_rows",
    )(meta, own, par)


def merge_kernel(*refs):
    out_refs = refs[-2:]
    refs = refs[:-2]
    sides = refs[: len(refs) // 2], refs[len(refs) // 2 :]
    width = sides[0][0].shape[1]
    block = IMG_TOK // 2
    for side in range(2):
        total = sides[side][0][...].astype(F32)
        for part in sides[side][1:]:
            total = total + part[...].astype(F32)
        total = total.astype(BF16)
        for index in range(2):
            out_refs[index][:, side * width : (side + 1) * width] = total[index * block : (index + 1) * block]


def merge_picks(own_parts, par_parts):
    width = own_parts[0].shape[1]
    return pl.pallas_call(
        merge_kernel,
        out_shape=[jax.ShapeDtypeStruct((IMG_TOK // 2, 2 * width), BF16)] * 2,
        compiler_params=pltpu.CompilerParams(vmem_limit_bytes=8 << 20),
        cost_estimate=cost(1 << 20, 1 << 20),
        name="merge_picks",
    )(*own_parts, *par_parts)


def finish_kernel(core_ref, own_a, own_b, par_a, par_b, out_ref, sums, lines):
    core = core_ref[0]
    for side, (left, right) in enumerate(((own_a, own_b), (par_a, par_b))):
        sums[side] = left[...] + right[...]
    rows = sums.shape[1] // SIDE
    lanes = PATCH * CIN
    per = HD // lanes
    for side in range(2):
        for part in range(SIDE // per):
            cols = [sums[side, pl.ds(part * per + k, rows, stride=SIDE), :] for k in range(per)]
            for row in range(PATCH):
                pieces = [col[:, row * lanes : (row + 1) * lanes] for col in cols]
                lines[part, pl.ds(row, rows, stride=PATCH), :] = jnp.concatenate(pieces, axis=1)
        slot = jnp.bitwise_xor(core, side)
        for part in range(SIDE // per):
            out_ref[slot, :, part * HD : (part + 1) * HD] = lines[part]


def finish(core, own_a, own_b, par_a, par_b):
    count = own_a.shape[0]
    return pl.pallas_call(
        finish_kernel,
        grid_spec=pltpu.PrefetchScalarGridSpec(
            num_scalar_prefetch=1,
            grid=(1,),
            in_specs=[full(own_a.shape)] * 4,
            out_specs=full((2, count // PATCH, WL * CIN)),
            scratch_shapes=[
                pltpu.VMEM((2, count, PIX * CIN), F32),
                pltpu.VMEM((WL * CIN // HD, count // PATCH, HD), F32),
            ],
        ),
        out_shape=jax.ShapeDtypeStruct((2, count // PATCH, WL * CIN), F32),
        compiler_params=params(8),
        cost_estimate=cost(1 << 16, 1 << 18),
        name="finish",
    )(core, own_a, own_b, par_a, par_b)


def spread(active, spread_ref):
    row = lax.broadcasted_iota(jnp.int32, (IMG_TOK, PIX * CIN), 0)
    patch_row, patch_col = row >> 4, row & (SIDE - 1)
    total = None
    for index in range(9):
        down, right = index // 3 - 1, index % 3 - 1
        part = mxu(active, spread_ref[:, index * PIX * CIN : (index + 1) * PIX * CIN])
        offset = down * SIDE + right
        if offset:
            part = pltpu.roll(part, offset % IMG_TOK, 0)
        source_row, source_col = patch_row - down, patch_col - right
        inside = (source_row >= 0) & (source_row < SIDE) & (source_col >= 0) & (source_col < SIDE)
        part = jnp.where(inside, part, 0.0)
        total = part if total is None else total + part
    return total


def up_kernel(count, halves, first, last, *refs):
    refs = list(refs)
    x_refs = take_blocks(refs, count)
    weight_refs = [[[refs.pop(0) for _ in range(2)] for _ in range(halves)] for _ in range(count)]
    acc_in = None if first else refs.pop(0)
    spread_ref = refs.pop(0) if last else None
    out_ref = refs[0]
    width = x_refs[0][0].shape[1] // 2
    values = [load(pieces) for pieces in x_refs]
    totals = []
    for part in range(halves):
        total = None if first else acc_in[part]
        for block in range(count):
            for side in range(2):
                term = mxu(
                    values[block][:, side * width : (side + 1) * width],
                    weight_refs[block][part][side][0],
                )
                total = term if total is None else total + term
        totals.append(total)
        if not last:
            out_ref[part] = total
    if last:
        active = [silu(total).astype(BF16) for total in totals]
        active = jnp.concatenate(active, axis=1) if halves > 1 else active[0]
        out_ref[...] = spread(active, spread_ref)


def up_step(blocks, entries, tiles, first_weights, second_weights, state, spread_weight):
    span = blocks[0][0].shape[1]
    halves, count = len(first_weights), len(blocks)
    first, last = state is None, spread_weight is not None
    whole = lambda shape: pl.BlockSpec(shape, lambda i: (0,) * len(shape))
    inputs = [p for pieces in blocks for p in pieces]
    specs = [whole(p.shape) for p in inputs]
    for entry in entries:
        apart = entry // 2 == tiles // 2
        offset = entry % 2 if apart else entry - 2 * (entry // 2 > tiles // 2)
        for sides in second_weights if apart else first_weights:
            for weight in sides:
                inputs.append(weight)
                specs.append(pl.BlockSpec((1, span // 2, CH), lambda i, offset=offset: (offset, 0, 0)))
    if not first:
        inputs.append(state)
        specs.append(whole(state.shape))
    if last:
        inputs.append(spread_weight)
        specs.append(whole(spread_weight.shape))
        out = jax.ShapeDtypeStruct((IMG_TOK, PIX * CIN), F32)
    else:
        out = jax.ShapeDtypeStruct((halves, IMG_TOK, CH), F32)
    return pl.pallas_call(
        functools.partial(up_kernel, count, halves, first, last),
        grid=(1,),
        in_specs=specs,
        out_specs=whole(out.shape),
        out_shape=out,
        compiler_params=params(16),
        cost_estimate=cost(2 * count * IMG_TOK * span * CH * halves, (1 + count) << 20),
        name="up_last" if last else "up_step",
    )(*inputs)


def spread_weights(up_conv, pixels):
    taps = up_conv.reshape(9, CH, CIN).transpose(1, 0, 2).reshape(CH, 9 * CIN)
    shape = (pixels.shape[0], 9 * CIN, 9 * PIX * CIN)
    row = lax.broadcasted_iota(jnp.int32, shape, 1)
    col = lax.broadcasted_iota(jnp.int32, shape, 2)
    pixel = pixels[:, None, None]
    tap, channel = row >> 3, row & 7
    patch, target, out_channel = col >> 7, (col >> 3) & 15, col & 7
    tap_row, tap_col = tap // 3, tap % 3
    down, right = patch // 3 - 1, patch % 3 - 1
    hit = (
        (channel == out_channel)
        & ((pixel >> 2) + 1 - tap_row == (target >> 2) + PATCH * down)
        & ((pixel & 3) + 1 - tap_col == (target & 3) + PATCH * right)
    )
    placed = jnp.where(hit, 1.0, 0.0).astype(BF16)
    spread = jnp.einsum("ct,ptn->pcn", taps, placed, preferred_element_type=F32)
    return spread.astype(BF16).reshape(pixels.shape[0] * CH, 9 * PIX * CIN)


def by_core(core, own, other, axis):
    return jnp.where(
        core == 0, jnp.concatenate([own, other], axis), jnp.concatenate([other, own], axis)
    )


def shift(values, axis, step):
    count = lax.axis_size(axis)
    return lax.ppermute(values, axis, [(i, (i + step) % count) for i in range(count)])


def gather_small(latents, down_conv):
    ctxs, tiles = lax.axis_size("ctx"), lax.axis_size("tile")
    every = jnp.concatenate([latents] + [shift(latents, "ctx", s) for s in range(1, ctxs)])
    conv = by_core(lax.axis_index("core"), down_conv, swap(down_conv), 1)
    conv = by_core(lax.axis_index("mpo"), conv, shift(conv, "mpo", 1), 1)
    return [every] + [shift(every, "tile", s) for s in range(1, tiles)], conv


def transpose_first(patch_out):
    ctxs, tiles, outer = (lax.axis_size(name) for name in ("ctx", "tile", "mpo"))
    ctx, mpo = lax.axis_index("ctx"), lax.axis_index("mpo")
    width, features = patch_out.shape
    deep = features // (tiles * outer)
    halves = 2 if ctxs == 2 and deep == 2 * CH else 1
    view = patch_out.reshape(width, tiles, outer, halves, deep // halves)
    at = ctx if halves == 2 else 0

    def columns(which):
        size = (width, tiles, 1, 1, deep // halves)
        return lax.dynamic_slice(view, (0, 0, which, at, 0), size)[:, :, 0, 0].transpose(1, 0, 2)

    return columns(mpo), columns(1 - mpo), halves


def transpose_second(both, step):
    tiles = lax.axis_size("tile")
    place = lax.rem(lax.axis_index("tile") + step, tiles)
    block = lax.dynamic_index_in_dim(both, place, 0, keepdims=False)
    return shift(block, "tile", step) if step else block


def transposed(blocks, halves):
    own = jnp.concatenate(blocks)
    weights = [own] if halves == 1 else [own, shift(own, "ctx", 1)]
    return [[weight, swap(weight)] for weight in weights]


def gather_pair(first, second, state, step, extras=None):
    tiles = lax.axis_size("tile")
    found, moving = [{0: first}, {}], [None, None]

    def launch(which, index):
        ring = found[which][2 * index]
        if index < tiles - 1:
            moving[which] = (shift(ring, "tile", 1), shift(ring, "mpo", 1))
        elif which:
            moving[which] = shift(found[which][2 * index - 1], "tile", 1)
        else:
            moving[which] = shift(ring, "mpo", 1)

    def work(entries, state):
        return step([[found[0][e], found[1][e]] for e in entries], entries, state, False)

    launch(0, 0)
    late = callable(second)
    if late:
        events = [(0, 1), (0, 2)]
        for index in range(1, tiles - 2):
            events += [(1, index), (0, index + 2)]
        events += [(1, tiles - 2), (1, tiles - 1)]
    else:
        found[1][0] = second
        launch(1, 0)
        events = [(which, index) for index in range(1, tiles) for which in range(2)]
    seen = first
    for which, index in events:
        ring, cross = moving[which]
        ring, cross, seen, state = lax.optimization_barrier((ring, cross, seen, state))
        found[which][2 * index], found[which][2 * index - 1] = ring, cross
        seen = ring
        launch(which, index)
        if late and (which, index) == (0, 1):
            found[1][0], extras = second(cross)
            launch(1, 0)
        if (which, index) == (1, tiles - 2):
            state = work(list(range(2 * tiles - 3)), state)
    state = work([2 * tiles - 2, 2 * tiles - 3], state)
    last = lax.optimization_barrier((moving[0], moving[1], state, extras))
    return step([[last[0], last[1]]], [2 * tiles - 1], last[2], True), last[3]


def shards(
    text_embed,
    latents,
    down_conv,
    patch_in,
    norm_gain,
    query_weight,
    key_weight,
    value_weight,
    query_gain,
    key_gain,
    out_weight,
    patch_out,
    up_conv,
    span_start,
    image_of_slot,
):
    ctxs, tiles, outer = (lax.axis_size(name) for name in ("ctx", "tile", "mpo"))
    ctx, tile, mpo, core = (lax.axis_index(name) for name in ("ctx", "tile", "mpo", "core"))
    seq_rows, width = text_embed.shape
    half = seq_rows // 2
    heads = width // HD
    images = span_start.shape[0]
    local = latents.shape[0]

    pieces, conv = gather_small(latents, down_conv)
    weights = [swap(key_weight)]
    kept, sent, halves = transpose_first(patch_out)
    pieces, conv, weights, received, later = lax.optimization_barrier(
        (pieces, conv, weights, shift(sent, "mpo", 1), [value_weight, query_weight])
    )
    later = [swap(w) for w in later]
    both = jnp.stack([kept, received], axis=1)
    up_blocks = [transpose_second(both, step) for step in range(tiles) if 2 * step != tiles]

    numbers = jnp.arange(images, dtype=jnp.int32)
    matches = image_of_slot[None, :] == numbers[:, None]
    slot_of_image = jnp.sum(jnp.where(matches, numbers[None, :], 0), axis=1)
    slot_place = lax.rem(ctx + ctxs - slot_of_image // local, ctxs) * local + slot_of_image % local
    meta = jnp.concatenate(
        [span_start, slot_place, image_of_slot, jnp.stack([ctx, core, tile, mpo])]
    ).astype(jnp.int32)
    layout = (images, tiles, outer)

    streams = down_stream(meta, pieces, conv, patch_in, text_embed, norm_gain, images)
    streams, later, up_blocks = lax.optimization_barrier((streams, later, up_blocks))
    others = [swap(s[1]) for s in streams]
    weights += later + [key_weight, value_weight, query_weight]

    head_gains = jnp.stack([query_gain, key_gain])

    def project(blocks, entries, state, last):
        return qkv_step(meta, layout, blocks, entries, weights, state, head_gains if last else None)

    extras = (swap(out_weight), transposed(up_blocks, halves))
    state, (out_par, up_first) = gather_pair(
        *[by_core(core, s[0], o, 1) for s, o in zip(streams, others)], None, project, extras
    )
    state, both = lax.optimization_barrier((state, both))
    up_block = transpose_second(both, tiles // 2)
    kv_send, q_send = state[:heads], state[heads : 2 * heads]
    kv_own, q_own = state[2 * heads : 3 * heads], state[3 * heads :]

    def shifted(values, step, cross):
        pairs = [
            (2 * c + k, 2 * ((c + step) % ctxs) + (1 - k if cross else k))
            for c in range(ctxs)
            for k in range(2)
        ]
        return lax.ppermute(values, ("ctx", "core"), pairs)

    def same_core(head):
        return [shifted(kv_own[head], step, False) for step in range(1, ctxs)]

    def pieces_of(head, same):
        pieces = [swap(q_send[head]), kv_own[head], swap(kv_send[head])]
        for step in range(1, ctxs):
            pieces += [same[step - 1], shifted(kv_send[head], step, True)]
        return pieces

    def attend(head, pieces, ahead):
        result = attention(meta, [q_own[head], pieces[0]], pieces[1:], images)
        (att_own, att_send), ahead = lax.optimization_barrier((result, ahead))
        return by_core(core, att_own, swap(att_send), 1), ahead

    pieces, up_block = lax.optimization_barrier((pieces_of(0, same_core(0)), up_block))
    attended, same = attend(0, pieces, same_core(1) if heads > 1 else None)
    if heads == 1:
        attended, second = attended[: half // 2], attended[half // 2 :]
        extras = transposed([up_block], halves)
    else:
        extras = None

        def second(token):
            pieces, token = lax.optimization_barrier((pieces_of(1, same), token))
            result, block = lax.optimization_barrier((attend(1, pieces, None)[0], up_block))
            return result, transposed([block], halves)

    def project_out(blocks, entries, state, last):
        return out_step(meta, layout, blocks, entries, (out_weight, out_par), state, last)

    state = [jnp.stack([s[0], o]) for s, o in zip(streams, others)]
    state, up_second = gather_pair(attended, second, state, project_out, extras)
    out_own, out_send = state
    out_other = swap(out_send)
    layer_out = by_core(core, out_own, out_other, 0)

    picks = pick_rows(meta, out_own, out_other, images, ctxs)
    own_parts, par_parts = [picks[0]], [swap(picks[1])]
    for step in range(1, ctxs):
        own_parts.append(shifted(picks[2 * step], step, False))
        par_parts.append(shifted(picks[2 * step + 1], step, True))

    pixel = tile * outer + mpo
    pixels = jnp.stack([pixel * halves + lax.rem(ctx + h, halves) for h in range(halves)])
    spread_weight = spread_weights(up_conv, pixels)

    def project_up(blocks, entries, state, last):
        return up_step(blocks, entries, tiles, up_first, up_second, state, spread_weight if last else None)

    state, _ = gather_pair(*merge_picks(own_parts, par_parts), None, project_up)

    bands = state.reshape(tiles, IMG_TOK // tiles, PIX * CIN)
    band = lax.dynamic_index_in_dim(bands, tile, 0, keepdims=False)
    for step in range(1, tiles):
        piece = lax.dynamic_index_in_dim(bands, lax.rem(tile + step, tiles), 0, keepdims=False)
        band = band + shift(piece, "tile", step)
    quad = {}
    for name, pairs in (
        ("mpo", [(0, 2), (1, 3), (2, 0), (3, 1)]),
        ("core", [(0, 1), (1, 0), (2, 3), (3, 2)]),
        ("both", [(0, 3), (1, 2), (2, 1), (3, 0)]),
    ):
        quad[name] = lax.ppermute(band, ("mpo", "core"), pairs)
    return layer_out, finish(meta[3 * images + 1 :], band, quad["mpo"], quad["core"], quad["both"])


def solution(mesh):
    ctxs, tiles, parts = mesh.devices.shape
    fine = Mesh(
        mesh.devices.reshape(ctxs, tiles, parts // 2, 2), ("ctx", "tile", "mpo", "core")
    )
    features = ("tile", "mpo", "core")
    return jax.shard_map(
        shards,
        mesh=fine,
        in_specs=(
            P("ctx", features),
            P("ctx", "tile", None),
            P(None, ("mpo", "core")),
            P(None, features),
            P(features),
            P(None, features),
            P(None, features),
            P(None, features),
            P(),
            P(),
            P(None, features),
            P(features, None),
            P(),
            P(),
            P(),
        ),
        out_specs=(P("ctx", features), P("ctx", "tile", None)),
        check_vma=False,
    )
```

```python
import functools

import jax
import jax.numpy as jnp
from jax import lax
from jax.experimental import pallas as pl
from jax.experimental.pallas import tpu as pltpu
from jax.sharding import Mesh
from jax.sharding import PartitionSpec as P

HD = 128
CH = 256
CIN = 8
WL = 64
HL = 64
PATCH = 4
PIX = PATCH * PATCH
SIDE = WL // PATCH
IMG_TOK = 256
EPSILON = 1e-05
NEGATIVE_FILL = -1e30
WINDOW = (PATCH + 2) * CIN
TAPS = 3 * WINDOW
BF16 = jnp.bfloat16
F32 = jnp.float32


def split_meta(meta, images):
    return meta[3 * images], meta[3 * images + 1], meta[3 * images + 2], meta[3 * images + 3]


def params(mebibytes):
    return pltpu.CompilerParams(
        dimension_semantics=("arbitrary",), vmem_limit_bytes=mebibytes * 1024 * 1024
    )


def cost(flops, nbytes, transcendentals=0):
    return pl.CostEstimate(
        flops=int(flops), bytes_accessed=int(nbytes), transcendentals=int(transcendentals)
    )


def silu(values):
    half = values * 0.5
    return half + half * jnp.tanh(half)


def mxu(left, right):
    return jnp.dot(left, right, preferred_element_type=F32)


def swap(values):
    return lax.ppermute(values, "core", [(0, 1), (1, 0)])


GAIN_ROWS = 16
TOP = 16


def down_kernel(images, tiles, half, meta, *refs):
    lat_refs, refs = refs[:tiles], refs[tiles:]
    conv_ref, patch_ref, own_text, par_text, gain_ref, first_ref, second_ref = refs[:7]
    grid_rows, conv_wide, conv_bf16, windows, total = refs[7:]
    step = pl.program_id(0)
    group = images * SIDE
    ctx, core, tile, _ = split_meta(meta, images)

    @pl.when(step == 0)
    def _():
        grid_rows[...] = jnp.zeros_like(grid_rows)
        blocks = grid_rows.shape[1]
        for index in range(tiles):
            band = lat_refs[index].shape[1]
            at = TOP + lax.rem(tile + tiles - index, tiles) * band
            rows = pl.ds(pl.multiple_of(at, 8), band)
            latent = lat_refs[index][...].astype(F32)
            edges = [jnp.zeros((images, band, size), F32) for size in (CIN, HD - CIN)]
            wide = jnp.concatenate([edges[0], latent, edges[1]], axis=2)
            for part in range(blocks):
                grid_rows[:, part, rows, :] = wide[:, :, part * HD : (part + 1) * HD]
        conv_wide[...] = jnp.zeros_like(conv_wide)
        conv = conv_ref[...].astype(F32)
        for col in range(PATCH):
            for tap in range(3):
                at = WINDOW * tap + CIN * col
                conv_wide[at : at + 3 * CIN, CH * col : CH * (col + 1)] = conv[
                    3 * CIN * tap : 3 * CIN * (tap + 1), :
                ]
        conv_bf16[...] = conv_wide[...].astype(BF16)

        def build(image, carry):
            for row in range(PATCH + 2):
                take = pl.ds(TOP - 1 + row, SIDE, stride=PATCH)
                line = [grid_rows[image, part, take, :] for part in range(blocks)]
                line = jnp.concatenate(line, axis=1).astype(BF16)
                for col in range(SIDE):
                    piece = line[:, PATCH * CIN * col : PATCH * CIN * col + WINDOW]
                    at = pl.ds(pl.multiple_of(group * col + image * SIDE, SIDE), SIDE)
                    for shift in range(3):
                        if 0 <= row - shift < PATCH:
                            windows[row - shift, at, WINDOW * shift : WINDOW * (shift + 1)] = piece
            return carry

        lax.fori_loop(0, images, build, 0)
        total[...] = jnp.zeros_like(total)

    chunk = 256
    for part in range(images * IMG_TOK // chunk):
        rows = slice(part * chunk, (part + 1) * chunk)
        hidden = silu(mxu(windows[step, rows, :], conv_bf16[...])).astype(BF16)
        total[rows, :] += mxu(hidden, patch_ref[...])

    @pl.when(step == PATCH - 1)
    def _():
        tokens = total[...].astype(BF16)
        block = half // 2
        for side, text_ref in enumerate((own_text, par_text)):
            base = ctx * (2 * half) + jnp.bitwise_xor(core, side) * half
            for part, out_ref in enumerate((first_ref, second_ref)):
                place = base + part * block + lax.broadcasted_iota(jnp.int32, (block, 1), 0)
                source = jnp.full((block, 1), -1, jnp.int32)
                for image in range(images):
                    inner = place - meta[image]
                    inside = (inner >= 0) & (inner < IMG_TOK)
                    index = (inner & (SIDE - 1)) * group + meta[images + image] * SIDE + (inner >> 4)
                    source = jnp.where(inside, index, source)
                choice = source == lax.broadcasted_iota(jnp.int32, (block, images * IMG_TOK), 1)
                picked = mxu(jnp.where(choice, 1.0, 0.0).astype(BF16), tokens)
                text = text_ref[0, part * block : (part + 1) * block, :].astype(F32)
                out_ref[side, :block, :] = jnp.where(source >= 0, picked, text).astype(BF16)
            gain = gain_ref[...].astype(F32)
            first_ref[side, block:, :] = jnp.broadcast_to(gain, (GAIN_ROWS, gain.shape[1])).astype(BF16)


def down_stream(meta, pieces, conv, patch_in, text, gain, images):
    seq_rows, width = text.shape
    half = seq_rows // 2
    tiles = len(pieces)
    count = images * IMG_TOK
    halves = text.reshape(2, half, width)
    core_at = 3 * images + 1
    first, second = (2, half // 2 + GAIN_ROWS, width), (2, half // 2, width)
    return pl.pallas_call(
        functools.partial(down_kernel, images, tiles, half),
        grid_spec=pltpu.PrefetchScalarGridSpec(
            num_scalar_prefetch=1,
            grid=(PATCH,),
            in_specs=[full(p.shape) for p in pieces]
            + [
                full(conv.shape),
                pl.BlockSpec((PATCH * CH, width), lambda i, m: (i, 0)),
                pl.BlockSpec((1, half, width), lambda i, m: (m[core_at], 0, 0)),
                pl.BlockSpec((1, half, width), lambda i, m: (1 - m[core_at], 0, 0)),
                full((1, width)),
            ],
            out_specs=[full(first), full(second)],
            scratch_shapes=[
                pltpu.VMEM((images, WL * CIN // HD + 1, TOP + HL + 16, HD), F32),
                pltpu.VMEM((TAPS, PATCH * CH), F32),
                pltpu.VMEM((TAPS, PATCH * CH), BF16),
                pltpu.VMEM((PATCH, count, TAPS), BF16),
                pltpu.VMEM((count, width), F32),
            ],
        ),
        out_shape=[jax.ShapeDtypeStruct(first, BF16), jax.ShapeDtypeStruct(second, BF16)],
        compiler_params=params(32),
        cost_estimate=cost(2 * count * PIX * CH * (256 + width), 4 << 20, count * PIX * CH),
        name="down_stream",
    )(meta, *pieces, conv, patch_in, halves, halves, gain.reshape(1, width))


def full(shape):
    return pl.BlockSpec(shape, lambda i, m: (0,) * len(shape))


def load(pieces):
    return jnp.concatenate([piece[...] for piece in pieces], axis=0)


def take_blocks(refs, count):
    return [[refs.pop(0), refs.pop(0)] for _ in range(count)]


def chip_of(meta, images, tiles, outer, entry):
    _, _, tile, mpo = split_meta(meta, images)
    return lax.rem(tile + tiles - entry // 2, tiles) * outer + lax.rem(mpo + entry % 2, outer)


def qkv_kernel(entries, layout, groups, first, last, meta, *refs):
    refs = list(refs)
    count = len(entries)
    x_refs = take_blocks(refs, count)
    weight_refs = [refs.pop(0) for _ in range(6)]
    if not first:
        acc_in, square_in = refs.pop(0), refs.pop(0)
    if last:
        head_gains = refs.pop(0)
    fetched, arrived = refs.pop(-2), refs.pop(-1)
    span, width = fetched.shape[2:]
    half = 2 * x_refs[0][1].shape[0]
    heads = width // HD

    def fetch(index):
        rows = pl.ds(pl.multiple_of(chip_of(meta, *layout, entries[index]) * span, span), span)
        return [
            pltpu.make_async_copy(
                weight_refs[part].at[rows, :], fetched.at[index % 2, part], arrived.at[index % 2, part]
            )
            for part in range(6)
        ]

    copies = fetch(0)
    for copy in copies:
        copy.start()
    square = None if first else square_in[...]
    if last:
        acc, outs = [None] * 6, refs
    else:
        acc_out, square_out = refs
    for index in range(count):
        following = fetch(index + 1) if index + 1 < count else []
        for copy in following:
            copy.start()
        gain = x_refs[index][0][half // 2 :, :][:1]
        value = jnp.concatenate([x_refs[index][0][: half // 2, :], x_refs[index][1][...]], axis=0)
        scaled = (value * gain).astype(BF16)
        value = value.astype(F32)
        value = value * value
        for part in range(span // HD):
            piece = value[:, part * HD : (part + 1) * HD]
            square = piece if square is None else square + piece
        for part in range(6):
            copies[part].wait()
            term = mxu(scaled, fetched[index % 2, part])
            if index == 0 and not first:
                term = term + acc_in[part]
            if last:
                acc[part] = term if index == 0 else acc[part] + term
            elif index == 0:
                acc_out[part] = term
            else:
                acc_out[part] += term
        copies = following
    if not last:
        square_out[...] = square
        return
    mean = jnp.sum(square, axis=-1, keepdims=True) * (1.0 / (groups * span))
    scale = lax.rsqrt(mean + EPSILON)
    for part in range(6):
        total = acc[part] * scale
        side, kind = part // 3, part % 3
        kv_outs = outs[2 * heads * side : 2 * heads * side + heads]
        q_outs = outs[2 * heads * side + heads : 2 * heads * side + 2 * heads]
        for head in range(heads):
            raw = total[:, head * HD : (head + 1) * HD]
            if kind == 1:
                kv_outs[head][1] = raw.astype(BF16)
                continue
            raw = raw * lax.rsqrt(jnp.mean(raw * raw, axis=-1, keepdims=True) + EPSILON)
            if kind == 0:
                kv_outs[head][0] = (raw * head_gains[1:2, :]).astype(BF16)
            else:
                q_outs[head][...] = (raw * (head_gains[0:1, :] * HD ** (-0.5))).astype(BF16)


def qkv_step(meta, layout, blocks, entries, weights, state, head_gains):
    span = blocks[0][1].shape[1]
    half = 2 * blocks[0][1].shape[0]
    width = weights[0].shape[1]
    heads = width // HD
    count, first, last = len(blocks), state is None, head_gains is not None
    groups = layout[1] * layout[2]
    inputs = [p for pieces in blocks for p in pieces]
    specs = [full(p.shape) for p in inputs]
    inputs += weights
    specs += [pl.BlockSpec(memory_space=pl.ANY)] * 6
    if not first:
        inputs += list(state)
        specs += [full(s.shape) for s in state]
    if last:
        inputs.append(head_gains)
        specs.append(full(head_gains.shape))
        kv, q = jax.ShapeDtypeStruct((2, half, HD), BF16), jax.ShapeDtypeStruct((half, HD), BF16)
        outs = ([kv] * heads + [q] * heads) * 2
    else:
        outs = [
            jax.ShapeDtypeStruct((6, half, width), F32),
            jax.ShapeDtypeStruct((half, HD), F32),
        ]
    return pl.pallas_call(
        functools.partial(qkv_kernel, entries, layout, groups, first, last),
        grid_spec=pltpu.PrefetchScalarGridSpec(
            num_scalar_prefetch=1,
            grid=(1,),
            in_specs=specs,
            out_specs=[full(o.shape) for o in outs],
            scratch_shapes=[
                pltpu.VMEM((2, 6, span, width), BF16),
                pltpu.SemaphoreType.DMA((2, 6)),
            ],
        ),
        out_shape=outs,
        compiler_params=params(40),
        cost_estimate=cost(12 * count * half * span * width, (6 + 2 * count) << 20),
        name="qkv_last" if last else "qkv_step",
    )(meta, *inputs)


def attention_kernel(images, pieces, half, meta, *refs):
    ctx, core, _, _ = split_meta(meta, images)
    ctxs = pieces // 2
    bases = []
    for piece in range(pieces):
        side = jnp.bitwise_xor(core, piece % 2)
        bases.append(lax.rem(ctx + ctxs - piece // 2, ctxs) * (2 * half) + side * half)
    q_refs, kv_refs, out_refs = refs[:2], refs[2 : 2 + pieces], refs[2 + pieces :]
    rows = q_refs[0].shape[0]
    step = pl.program_id(0)
    for side in range(2):
        place = bases[side] + step * rows + lax.broadcasted_iota(jnp.int32, (rows, 1), 0)
        limit = place
        for image in range(images):
            inner = place - meta[image]
            limit = jnp.where((inner >= 0) & (inner < IMG_TOK), meta[image] + IMG_TOK - 1, limit)
        query = q_refs[side][...]
        scores = []
        top = None
        for piece in range(pieces):
            score = lax.dot_general(
                query, kv_refs[piece][0], (((1,), (1,)), ((), ())), preferred_element_type=F32
            )
            position = lax.broadcasted_iota(jnp.int32, score.shape, 1)
            score = jnp.where(position <= limit - bases[piece], score, NEGATIVE_FILL)
            scores.append(score)
            best = jnp.max(score, axis=1, keepdims=True)
            top = best if top is None else jnp.maximum(top, best)
        total = jnp.zeros((rows, 1), F32)
        product = jnp.zeros((rows, HD), F32)
        for piece in range(pieces):
            weight = jnp.exp(scores[piece] - top)
            total = total + jnp.sum(weight, axis=1, keepdims=True)
            product = product + mxu(weight.astype(BF16), kv_refs[piece][1])
        out_refs[side][...] = (product / total).astype(BF16)


def attention(meta, queries, pieces, images):
    half = queries[0].shape[0]
    block = 256
    keys = half * len(pieces)
    rows = pl.BlockSpec((block, HD), lambda i, m: (i, 0))
    return pl.pallas_call(
        functools.partial(attention_kernel, images, len(pieces), half),
        grid_spec=pltpu.PrefetchScalarGridSpec(
            num_scalar_prefetch=1,
            grid=(half // block,),
            in_specs=[rows, rows] + [full(p.shape) for p in pieces],
            out_specs=[rows, rows],
        ),
        out_shape=[jax.ShapeDtypeStruct((half, HD), BF16)] * 2,
        compiler_params=params(24),
        cost_estimate=cost(8 * half * keys * HD, 4 * keys * HD, 2 * half * keys),
        name="attention",
    )(meta, *queries, *pieces)


def out_kernel(count, heads, first, last, meta, *refs):
    refs = list(refs)
    x_refs = take_blocks(refs, count)
    weight_refs = [[refs.pop(0), refs.pop(0)] for _ in range(count)]
    if first:
        streams = [refs.pop(0), refs.pop(0)]
        block = streams[1].shape[1]
    else:
        acc_in = refs.pop(0)
    outs = refs
    for side in range(2):
        if first:
            rows = [streams[0][side, :block, :], streams[1][side]]
            total = jnp.concatenate(rows, axis=0).astype(F32)
        else:
            total = acc_in[side]
        for index in range(count):
            weight = weight_refs[index][side]
            if heads == 2:
                for head in range(heads):
                    part = weight[0, :, head].reshape(2 * HD, weight.shape[4])
                    total = total + mxu(x_refs[index][head][...], part)
            else:
                total = total + mxu(load(x_refs[index]), weight[0, :, 0].reshape(2 * HD, weight.shape[4]))
        if last:
            outs[side][...] = total.astype(BF16)
        else:
            outs[0][side] = total


def out_step(meta, layout, blocks, entries, weights, state, last):
    width = weights[0].shape[1]
    heads = width // HD
    half = blocks[0][0].shape[0] * (1 if heads == 2 else 2)
    first = isinstance(state, list)
    count = len(blocks)
    views = [w.reshape(-1, 2, heads, HD, width) for w in weights]
    inputs = [p for pieces in blocks for p in pieces]
    specs = [full(p.shape) for p in inputs]
    for entry in entries:
        for view in views:
            inputs.append(view)
            specs.append(
                pl.BlockSpec(
                    (1, 2, heads, HD, width),
                    lambda i, m, entry=entry: (chip_of(m, *layout, entry), 0, 0, 0, 0),
                )
            )
    states = state if first else [state]
    inputs += states
    specs += [full(s.shape) for s in states]
    if last:
        outs = [jax.ShapeDtypeStruct((half, width), BF16)] * 2
    else:
        outs = [jax.ShapeDtypeStruct((2, half, width), F32)]
    result = pl.pallas_call(
        functools.partial(out_kernel, count, heads, first, last),
        grid_spec=pltpu.PrefetchScalarGridSpec(
            num_scalar_prefetch=1,
            grid=(1,),
            in_specs=specs,
            out_specs=[full(o.shape) for o in outs],
        ),
        out_shape=outs,
        compiler_params=params(24),
        cost_estimate=cost(8 * count * half * heads * HD * width, (2 + count) << 20),
        name="out_last" if last else "out_step",
    )(meta, *inputs)
    return result if last else result[0]


def pick_kernel(images, ctxs, meta, own_ref, par_ref, *out_refs):
    half = own_ref.shape[0]
    ctx, core, _, _ = split_meta(meta, images)
    for target in range(2 * ctxs):
        to_core = jnp.bitwise_xor(core, target % 2)
        slot = 2 * lax.rem(ctx + target // 2, ctxs) + to_core
        start = meta[meta[2 * images + slot]]
        place = start + lax.broadcasted_iota(jnp.int32, (IMG_TOK, half), 0)
        column = ctx * (2 * half) + lax.broadcasted_iota(jnp.int32, (IMG_TOK, half), 1)
        own = jnp.where(place == column + core * half, 1.0, 0.0).astype(BF16)
        par = jnp.where(place == column + (1 - core) * half, 1.0, 0.0).astype(BF16)
        out_refs[target][...] = (mxu(own, own_ref[...]) + mxu(par, par_ref[...])).astype(BF16)


def pick_rows(meta, own, par, images, ctxs):
    half, width = own.shape
    targets = 2 * ctxs
    return pl.pallas_call(
        functools.partial(pick_kernel, images, ctxs),
        grid_spec=pltpu.PrefetchScalarGridSpec(
            num_scalar_prefetch=1,
            grid=(1,),
            in_specs=[full(own.shape), full(par.shape)],
            out_specs=[full((IMG_TOK, width))] * targets,
        ),
        out_shape=[jax.ShapeDtypeStruct((IMG_TOK, width), BF16)] * targets,
        compiler_params=params(16),
        cost_estimate=cost(targets * 4 * IMG_TOK * half * width, 1 << 20),
        name="pick_rows",
    )(meta, own, par)


def merge_kernel(*refs):
    out_refs = refs[-2:]
    refs = refs[:-2]
    sides = refs[: len(refs) // 2], refs[len(refs) // 2 :]
    width = sides[0][0].shape[1]
    block = IMG_TOK // 2
    for side in range(2):
        total = sides[side][0][...].astype(F32)
        for part in sides[side][1:]:
            total = total + part[...].astype(F32)
        total = total.astype(BF16)
        for index in range(2):
            out_refs[index][:, side * width : (side + 1) * width] = total[index * block : (index + 1) * block]


def merge_picks(own_parts, par_parts):
    width = own_parts[0].shape[1]
    return pl.pallas_call(
        merge_kernel,
        out_shape=[jax.ShapeDtypeStruct((IMG_TOK // 2, 2 * width), BF16)] * 2,
        compiler_params=pltpu.CompilerParams(vmem_limit_bytes=8 << 20),
        cost_estimate=cost(1 << 20, 1 << 20),
        name="merge_picks",
    )(*own_parts, *par_parts)


def finish_kernel(core_ref, own_a, own_b, par_a, par_b, out_ref, sums, lines):
    core = core_ref[0]
    for side, (left, right) in enumerate(((own_a, own_b), (par_a, par_b))):
        sums[side] = left[...] + right[...]
    rows = sums.shape[1] // SIDE
    lanes = PATCH * CIN
    per = HD // lanes
    for side in range(2):
        for part in range(SIDE // per):
            cols = [sums[side, pl.ds(part * per + k, rows, stride=SIDE), :] for k in range(per)]
            for row in range(PATCH):
                pieces = [col[:, row * lanes : (row + 1) * lanes] for col in cols]
                lines[part, pl.ds(row, rows, stride=PATCH), :] = jnp.concatenate(pieces, axis=1)
        slot = jnp.bitwise_xor(core, side)
        for part in range(SIDE // per):
            out_ref[slot, :, part * HD : (part + 1) * HD] = lines[part]


def finish(core, own_a, own_b, par_a, par_b):
    count = own_a.shape[0]
    return pl.pallas_call(
        finish_kernel,
        grid_spec=pltpu.PrefetchScalarGridSpec(
            num_scalar_prefetch=1,
            grid=(1,),
            in_specs=[full(own_a.shape)] * 4,
            out_specs=full((2, count // PATCH, WL * CIN)),
            scratch_shapes=[
                pltpu.VMEM((2, count, PIX * CIN), F32),
                pltpu.VMEM((WL * CIN // HD, count // PATCH, HD), F32),
            ],
        ),
        out_shape=jax.ShapeDtypeStruct((2, count // PATCH, WL * CIN), F32),
        compiler_params=params(8),
        cost_estimate=cost(1 << 16, 1 << 18),
        name="finish",
    )(core, own_a, own_b, par_a, par_b)


def spread(active, spread_ref):
    row = lax.broadcasted_iota(jnp.int32, (IMG_TOK, PIX * CIN), 0)
    patch_row, patch_col = row >> 4, row & (SIDE - 1)
    total = None
    for index in range(9):
        down, right = index // 3 - 1, index % 3 - 1
        part = mxu(active, spread_ref[:, index * PIX * CIN : (index + 1) * PIX * CIN])
        offset = down * SIDE + right
        if offset:
            part = pltpu.roll(part, offset % IMG_TOK, 0)
        source_row, source_col = patch_row - down, patch_col - right
        inside = (source_row >= 0) & (source_row < SIDE) & (source_col >= 0) & (source_col < SIDE)
        part = jnp.where(inside, part, 0.0)
        total = part if total is None else total + part
    return total


def up_kernel(count, halves, first, last, *refs):
    refs = list(refs)
    x_refs = take_blocks(refs, count)
    weight_refs = [[[refs.pop(0) for _ in range(2)] for _ in range(halves)] for _ in range(count)]
    acc_in = None if first else refs.pop(0)
    spread_ref = refs.pop(0) if last else None
    out_ref = refs[0]
    width = x_refs[0][0].shape[1] // 2
    values = [load(pieces) for pieces in x_refs]
    totals = []
    for part in range(halves):
        total = None if first else acc_in[part]
        for block in range(count):
            for side in range(2):
                term = mxu(
                    values[block][:, side * width : (side + 1) * width],
                    weight_refs[block][part][side][0],
                )
                total = term if total is None else total + term
        totals.append(total)
        if not last:
            out_ref[part] = total
    if last:
        active = [silu(total).astype(BF16) for total in totals]
        active = jnp.concatenate(active, axis=1) if halves > 1 else active[0]
        out_ref[...] = spread(active, spread_ref)


def up_step(blocks, entries, tiles, first_weights, second_weights, state, spread_weight):
    span = blocks[0][0].shape[1]
    halves, count = len(first_weights), len(blocks)
    first, last = state is None, spread_weight is not None
    whole = lambda shape: pl.BlockSpec(shape, lambda i: (0,) * len(shape))
    inputs = [p for pieces in blocks for p in pieces]
    specs = [whole(p.shape) for p in inputs]
    for entry in entries:
        apart = entry // 2 == tiles // 2
        offset = entry % 2 if apart else entry - 2 * (entry // 2 > tiles // 2)
        for sides in second_weights if apart else first_weights:
            for weight in sides:
                inputs.append(weight)
                specs.append(pl.BlockSpec((1, span // 2, CH), lambda i, offset=offset: (offset, 0, 0)))
    if not first:
        inputs.append(state)
        specs.append(whole(state.shape))
    if last:
        inputs.append(spread_weight)
        specs.append(whole(spread_weight.shape))
        out = jax.ShapeDtypeStruct((IMG_TOK, PIX * CIN), F32)
    else:
        out = jax.ShapeDtypeStruct((halves, IMG_TOK, CH), F32)
    return pl.pallas_call(
        functools.partial(up_kernel, count, halves, first, last),
        grid=(1,),
        in_specs=specs,
        out_specs=whole(out.shape),
        out_shape=out,
        compiler_params=params(16),
        cost_estimate=cost(2 * count * IMG_TOK * span * CH * halves, (1 + count) << 20),
        name="up_last" if last else "up_step",
    )(*inputs)


def spread_weights(up_conv, pixels):
    taps = up_conv.reshape(9, CH, CIN).transpose(1, 0, 2).reshape(CH, 9 * CIN)
    shape = (pixels.shape[0], 9 * CIN, 9 * PIX * CIN)
    row = lax.broadcasted_iota(jnp.int32, shape, 1)
    col = lax.broadcasted_iota(jnp.int32, shape, 2)
    pixel = pixels[:, None, None]
    tap, channel = row >> 3, row & 7
    patch, target, out_channel = col >> 7, (col >> 3) & 15, col & 7
    tap_row, tap_col = tap // 3, tap % 3
    down, right = patch // 3 - 1, patch % 3 - 1
    hit = (
        (channel == out_channel)
        & ((pixel >> 2) + 1 - tap_row == (target >> 2) + PATCH * down)
        & ((pixel & 3) + 1 - tap_col == (target & 3) + PATCH * right)
    )
    placed = jnp.where(hit, 1.0, 0.0).astype(BF16)
    spread = jnp.einsum("ct,ptn->pcn", taps, placed, preferred_element_type=F32)
    return spread.astype(BF16).reshape(pixels.shape[0] * CH, 9 * PIX * CIN)


def by_core(core, own, other, axis):
    return jnp.where(
        core == 0, jnp.concatenate([own, other], axis), jnp.concatenate([other, own], axis)
    )


def shift(values, axis, step):
    count = lax.axis_size(axis)
    return lax.ppermute(values, axis, [(i, (i + step) % count) for i in range(count)])


def gather_small(latents, down_conv, *others):
    ctxs, tiles = lax.axis_size("ctx"), lax.axis_size("tile")
    every = jnp.concatenate([latents] + [shift(latents, "ctx", s) for s in range(1, ctxs)])
    conv = by_core(lax.axis_index("core"), down_conv, swap(down_conv), 1)
    conv = by_core(lax.axis_index("mpo"), conv, shift(conv, "mpo", 1), 1)
    every, conv, others = lax.optimization_barrier((every, conv, others))
    return [every] + [shift(every, "tile", s) for s in range(1, tiles)], conv, *others


def columns_kernel(meta, kept_in, sent_in, kept_out, sent_out):
    kept_out[0] = kept_in[...]
    sent_out[0] = sent_in[...]


def transpose_first(meta, patch_out, layout, ctxs):
    images, tiles, outer = layout
    width, features = patch_out.shape
    deep = features // (tiles * outer)
    halves = 2 if ctxs == 2 and deep == 2 * CH else 1
    size = deep // halves

    def place(other):
        def index(i, m):
            ctx, _, _, mpo = split_meta(m, images)
            chip = i * outer + lax.rem(mpo + other, outer)
            return 0, chip * halves + (ctx if halves == 2 else 0)

        return pl.BlockSpec((width, size), index)

    out = pl.BlockSpec((1, width, size), lambda i, m: (i, 0, 0))
    kept, sent = pl.pallas_call(
        columns_kernel,
        grid_spec=pltpu.PrefetchScalarGridSpec(
            num_scalar_prefetch=1, grid=(tiles,), in_specs=[place(0), place(1)], out_specs=[out, out]
        ),
        out_shape=[jax.ShapeDtypeStruct((tiles, width, size), BF16)] * 2,
        compiler_params=params(8),
        cost_estimate=cost(1 << 16, 2 << 20),
        name="columns",
    )(meta, patch_out, patch_out)
    return kept, sent, halves


def transpose_second(kept, received, step):
    tiles = lax.axis_size("tile")
    place = lax.rem(lax.axis_index("tile") + step, tiles)
    block = [lax.dynamic_index_in_dim(x, place, 0, keepdims=False) for x in (kept, received)]
    block = jnp.stack(block)
    return shift(block, "tile", step) if step else block


def transposed(blocks, halves):
    own = jnp.concatenate(blocks)
    weights = [own] if halves == 1 else [own, shift(own, "ctx", 1)]
    return [[weight, swap(weight)] for weight in weights]


def gather_pair(first, second, state, step, extras=None):
    tiles = lax.axis_size("tile")
    found, moving = [{0: first}, {}], [None, None]

    def launch(which, index):
        ring = found[which][2 * index]
        if index < tiles - 1:
            moving[which] = (shift(ring, "tile", 1), shift(ring, "mpo", 1))
        elif which:
            moving[which] = shift(found[which][2 * index - 1], "tile", 1)
        else:
            moving[which] = shift(ring, "mpo", 1)

    def work(entries, state):
        return step([[found[0][e], found[1][e]] for e in entries], entries, state, False)

    launch(0, 0)
    late = callable(second)
    if late:
        events = [(0, 1), (0, 2)]
        for index in range(1, tiles - 2):
            events += [(1, index), (0, index + 2)]
        events += [(1, tiles - 2), (1, tiles - 1)]
    else:
        found[1][0] = second
        launch(1, 0)
        events = [(which, index) for index in range(1, tiles) for which in range(2)]
    seen = first
    for which, index in events:
        ring, cross = moving[which]
        if (which, index) == (int(late), tiles - 1):
            ring, cross, seen, state = lax.optimization_barrier((ring, cross, seen, state))
        else:
            ring, cross, seen = lax.optimization_barrier((ring, cross, seen))
        found[which][2 * index], found[which][2 * index - 1] = ring, cross
        seen = ring
        launch(which, index)
        if late and (which, index) == (0, 1):
            found[1][0], extras = second(cross)
            launch(1, 0)
        if (which, index) == (1, tiles - 2):
            state = work(list(range(2 * tiles - 3)), state)
    state = work([2 * tiles - 2, 2 * tiles - 3], state)
    last = lax.optimization_barrier((moving[0], moving[1], state, extras))
    return step([[last[0], last[1]]], [2 * tiles - 1], last[2], True), last[3]


def shards(
    text_embed,
    latents,
    down_conv,
    patch_in,
    norm_gain,
    query_weight,
    key_weight,
    value_weight,
    query_gain,
    key_gain,
    out_weight,
    patch_out,
    up_conv,
    span_start,
    image_of_slot,
):
    ctxs, tiles, outer = (lax.axis_size(name) for name in ("ctx", "tile", "mpo"))
    ctx, tile, mpo, core = (lax.axis_index(name) for name in ("ctx", "tile", "mpo", "core"))
    seq_rows, width = text_embed.shape
    half = seq_rows // 2
    heads = width // HD
    images = span_start.shape[0]
    local = latents.shape[0]

    numbers = jnp.arange(images, dtype=jnp.int32)
    matches = image_of_slot[None, :] == numbers[:, None]
    slot_of_image = jnp.sum(jnp.where(matches, numbers[None, :], 0), axis=1)
    slot_place = lax.rem(ctx + ctxs - slot_of_image // local, ctxs) * local + slot_of_image % local
    meta = jnp.concatenate(
        [span_start, slot_place, image_of_slot, jnp.stack([ctx, core, tile, mpo])]
    ).astype(jnp.int32)
    layout = (images, tiles, outer)

    weights = [swap(w) for w in (key_weight, value_weight, query_weight)]
    pieces, conv, meta, weights[0], weights[1] = gather_small(latents, down_conv, meta, *weights[:2])
    kept, sent, halves = transpose_first(meta, patch_out, layout, ctxs)
    pieces, received = lax.optimization_barrier((pieces, shift(sent, "mpo", 1)))
    up_blocks = [transpose_second(kept, received, step) for step in range(tiles) if 2 * step != tiles]

    streams = down_stream(meta, pieces, conv, patch_in, text_embed, norm_gain, images)
    streams, weights[2], out_par, up_blocks = lax.optimization_barrier(
        (streams, weights[2], swap(out_weight), up_blocks)
    )
    others = [swap(s[1]) for s in streams]
    weights += [key_weight, value_weight, query_weight]

    head_gains = jnp.stack([query_gain, key_gain])

    def project(blocks, entries, state, last):
        return qkv_step(meta, layout, blocks, entries, weights, state, head_gains if last else None)

    state, up_first = gather_pair(
        *[by_core(core, s[0], o, 1) for s, o in zip(streams, others)], None, project, transposed(up_blocks, halves)
    )
    state, kept, received = lax.optimization_barrier((state, kept, received))
    up_block = transpose_second(kept, received, tiles // 2)
    kv_send, q_send = state[:heads], state[heads : 2 * heads]
    kv_own, q_own = state[2 * heads : 3 * heads], state[3 * heads :]

    def shifted(values, step, cross):
        pairs = [
            (2 * c + k, 2 * ((c + step) % ctxs) + (1 - k if cross else k))
            for c in range(ctxs)
            for k in range(2)
        ]
        return lax.ppermute(values, ("ctx", "core"), pairs)

    def pieces_of(head):
        pieces = [swap(q_send[head]), kv_own[head], swap(kv_send[head])]
        for step in range(1, ctxs):
            pieces += [shifted(kv_own[head], step, False), shifted(kv_send[head], step, True)]
        return pieces

    def attend(head, pieces, ahead):
        result = attention(meta, [q_own[head], pieces[0]], pieces[1:], images)
        (att_own, att_send), ahead = lax.optimization_barrier((result, ahead))
        return by_core(core, att_own, swap(att_send), 1), ahead

    pieces, up_block = lax.optimization_barrier((pieces_of(0), up_block))
    attended, pieces = attend(0, pieces, pieces_of(1) if heads > 1 else None)
    if heads == 1:
        attended, second = attended[: half // 2], attended[half // 2 :]
        extras = transposed([up_block], halves)
    else:
        extras = None

        def second(token):
            result, (block, _) = attend(1, pieces, (up_block, token))
            return result, transposed([block], halves)

    def project_out(blocks, entries, state, last):
        return out_step(meta, layout, blocks, entries, (out_weight, out_par), state, last)

    state = [jnp.stack([s[0], o]) for s, o in zip(streams, others)]
    state, up_second = gather_pair(attended, second, state, project_out, extras)
    out_own, out_send = state
    out_other = swap(out_send)
    layer_out = by_core(core, out_own, out_other, 0)

    picks = pick_rows(meta, out_own, out_other, images, ctxs)
    own_parts, par_parts = [picks[0]], [swap(picks[1])]
    for step in range(1, ctxs):
        own_parts.append(shifted(picks[2 * step], step, False))
        par_parts.append(shifted(picks[2 * step + 1], step, True))

    pixel = tile * outer + mpo
    pixels = jnp.stack([pixel * halves + lax.rem(ctx + h, halves) for h in range(halves)])
    spread_weight = spread_weights(up_conv, pixels)

    def project_up(blocks, entries, state, last):
        return up_step(blocks, entries, tiles, up_first, up_second, state, spread_weight if last else None)

    state, _ = gather_pair(*merge_picks(own_parts, par_parts), None, project_up)

    bands = state.reshape(tiles, IMG_TOK // tiles, PIX * CIN)
    band = lax.dynamic_index_in_dim(bands, tile, 0, keepdims=False)
    for step in range(1, tiles):
        piece = lax.dynamic_index_in_dim(bands, lax.rem(tile + step, tiles), 0, keepdims=False)
        band = band + shift(piece, "tile", step)
    quad = {}
    for name, pairs in (
        ("mpo", [(0, 2), (1, 3), (2, 0), (3, 1)]),
        ("core", [(0, 1), (1, 0), (2, 3), (3, 2)]),
        ("both", [(0, 3), (1, 2), (2, 1), (3, 0)]),
    ):
        quad[name] = lax.ppermute(band, ("mpo", "core"), pairs)
    return layer_out, finish(meta[3 * images + 1 :], band, quad["mpo"], quad["core"], quad["both"])


def solution(mesh):
    ctxs, tiles, parts = mesh.devices.shape
    fine = Mesh(
        mesh.devices.reshape(ctxs, tiles, parts // 2, 2), ("ctx", "tile", "mpo", "core")
    )
    features = ("tile", "mpo", "core")
    return jax.shard_map(
        shards,
        mesh=fine,
        in_specs=(
            P("ctx", features),
            P("ctx", "tile", None),
            P(None, ("mpo", "core")),
            P(None, features),
            P(features),
            P(None, features),
            P(None, features),
            P(None, features),
            P(),
            P(),
            P(None, features),
            P(features, None),
            P(),
            P(),
            P(),
        ),
        out_specs=(P("ctx", features), P("ctx", "tile", None)),
        check_vma=False,
    )
```

```python
import functools

import jax
import jax.numpy as jnp
from jax import lax
from jax.experimental import pallas as pl
from jax.experimental.pallas import tpu as pltpu
from jax.sharding import Mesh
from jax.sharding import PartitionSpec as P

HD = 128
CH = 256
CIN = 8
WL = 64
HL = 64
PATCH = 4
PIX = PATCH * PATCH
SIDE = WL // PATCH
IMG_TOK = 256
EPSILON = 1e-05
NEGATIVE_FILL = -1e30
WINDOW = (PATCH + 2) * CIN
TAPS = 3 * WINDOW
BF16 = jnp.bfloat16
F32 = jnp.float32


def split_meta(meta, images):
    return meta[3 * images], meta[3 * images + 1], meta[3 * images + 2], meta[3 * images + 3]


def params(mebibytes):
    return pltpu.CompilerParams(
        dimension_semantics=("arbitrary",), vmem_limit_bytes=mebibytes * 1024 * 1024
    )


def cost(flops, nbytes, transcendentals=0):
    return pl.CostEstimate(
        flops=int(flops), bytes_accessed=int(nbytes), transcendentals=int(transcendentals)
    )


def silu(values):
    half = values * 0.5
    return half + half * jnp.tanh(half)


def mxu(left, right):
    return jnp.dot(left, right, preferred_element_type=F32)


def swap(values):
    return lax.ppermute(values, "core", [(0, 1), (1, 0)])


HELD = pl.BlockSpec(memory_space=pltpu.VMEM)


GAIN_ROWS = 16
TOP = 16


def down_kernel(images, tiles, half, meta, *refs):
    lat_refs, refs = refs[:tiles], refs[tiles:]
    conv_ref, patch_ref, own_text, par_text, gain_ref = refs[:5]
    weight_refs, (first_ref, second_ref), held_refs = refs[5:11], refs[11:13], refs[13:19]
    grid_rows, conv_wide, conv_bf16, windows, total, arrived = refs[19:]
    step = pl.program_id(0)
    copies = [
        pltpu.make_async_copy(weight, held, arrived.at[index])
        for index, (weight, held) in enumerate(zip(weight_refs, held_refs))
    ]

    @pl.when(step == 0)
    def _():
        for copy in copies:
            copy.start()

    group = images * SIDE
    ctx, core, tile, _ = split_meta(meta, images)

    @pl.when(step == 0)
    def _():
        grid_rows[...] = jnp.zeros_like(grid_rows)
        blocks = grid_rows.shape[1]
        for index in range(tiles):
            band = lat_refs[index].shape[1]
            at = TOP + lax.rem(tile + tiles - index, tiles) * band
            rows = pl.ds(pl.multiple_of(at, 8), band)
            latent = lat_refs[index][...].astype(F32)
            edges = [jnp.zeros((images, band, size), F32) for size in (CIN, HD - CIN)]
            wide = jnp.concatenate([edges[0], latent, edges[1]], axis=2)
            for part in range(blocks):
                grid_rows[:, part, rows, :] = wide[:, :, part * HD : (part + 1) * HD]
        conv_wide[...] = jnp.zeros_like(conv_wide)
        conv = conv_ref[...].astype(F32)
        for col in range(PATCH):
            for tap in range(3):
                at = WINDOW * tap + CIN * col
                conv_wide[at : at + 3 * CIN, CH * col : CH * (col + 1)] = conv[
                    3 * CIN * tap : 3 * CIN * (tap + 1), :
                ]
        conv_bf16[...] = conv_wide[...].astype(BF16)

        def build(image, carry):
            for row in range(PATCH + 2):
                take = pl.ds(TOP - 1 + row, SIDE, stride=PATCH)
                line = [grid_rows[image, part, take, :] for part in range(blocks)]
                line = jnp.concatenate(line, axis=1).astype(BF16)
                for col in range(SIDE):
                    piece = line[:, PATCH * CIN * col : PATCH * CIN * col + WINDOW]
                    at = pl.ds(pl.multiple_of(group * col + image * SIDE, SIDE), SIDE)
                    for shift in range(3):
                        if 0 <= row - shift < PATCH:
                            windows[row - shift, at, WINDOW * shift : WINDOW * (shift + 1)] = piece
            return carry

        lax.fori_loop(0, images, build, 0)
        total[...] = jnp.zeros_like(total)

    chunk = 256
    for part in range(images * IMG_TOK // chunk):
        rows = slice(part * chunk, (part + 1) * chunk)
        hidden = silu(mxu(windows[step, rows, :], conv_bf16[...])).astype(BF16)
        total[rows, :] += mxu(hidden, patch_ref[...])

    @pl.when(step == PATCH - 1)
    def _():
        tokens = total[...].astype(BF16)
        block = half // 2
        for side, text_ref in enumerate((own_text, par_text)):
            base = ctx * (2 * half) + jnp.bitwise_xor(core, side) * half
            for part, out_ref in enumerate((first_ref, second_ref)):
                place = base + part * block + lax.broadcasted_iota(jnp.int32, (block, 1), 0)
                source = jnp.full((block, 1), -1, jnp.int32)
                for image in range(images):
                    inner = place - meta[image]
                    inside = (inner >= 0) & (inner < IMG_TOK)
                    index = (inner & (SIDE - 1)) * group + meta[images + image] * SIDE + (inner >> 4)
                    source = jnp.where(inside, index, source)
                choice = source == lax.broadcasted_iota(jnp.int32, (block, images * IMG_TOK), 1)
                picked = mxu(jnp.where(choice, 1.0, 0.0).astype(BF16), tokens)
                text = text_ref[0, part * block : (part + 1) * block, :].astype(F32)
                out_ref[side, :block, :] = jnp.where(source >= 0, picked, text).astype(BF16)
            gain = gain_ref[...].astype(F32)
            first_ref[side, block:, :] = jnp.broadcast_to(gain, (GAIN_ROWS, gain.shape[1])).astype(BF16)
        for copy in copies:
            copy.wait()


def down_stream(meta, pieces, conv, patch_in, text, gain, weights, images):
    seq_rows, width = text.shape
    half = seq_rows // 2
    tiles = len(pieces)
    count = images * IMG_TOK
    halves = text.reshape(2, half, width)
    core_at = 3 * images + 1
    first, second = (2, half // 2 + GAIN_ROWS, width), (2, half // 2, width)
    return pl.pallas_call(
        functools.partial(down_kernel, images, tiles, half),
        grid_spec=pltpu.PrefetchScalarGridSpec(
            num_scalar_prefetch=1,
            grid=(PATCH,),
            in_specs=[full(p.shape) for p in pieces]
            + [
                full(conv.shape),
                pl.BlockSpec((PATCH * CH, width), lambda i, m: (i, 0)),
                pl.BlockSpec((1, half, width), lambda i, m: (m[core_at], 0, 0)),
                pl.BlockSpec((1, half, width), lambda i, m: (1 - m[core_at], 0, 0)),
                full((1, width)),
            ]
            + [pl.BlockSpec(memory_space=pl.ANY)] * 6,
            out_specs=[full(first), full(second)] + [HELD] * 6,
            scratch_shapes=[
                pltpu.VMEM((images, WL * CIN // HD + 1, TOP + HL + 16, HD), F32),
                pltpu.VMEM((TAPS, PATCH * CH), F32),
                pltpu.VMEM((TAPS, PATCH * CH), BF16),
                pltpu.VMEM((PATCH, count, TAPS), BF16),
                pltpu.VMEM((count, width), F32),
                pltpu.SemaphoreType.DMA((6,)),
            ],
        ),
        out_shape=[jax.ShapeDtypeStruct(first, BF16), jax.ShapeDtypeStruct(second, BF16)]
        + [pltpu.VMEM(w.shape, w.dtype) for w in weights],
        compiler_params=params(32),
        cost_estimate=cost(2 * count * PIX * CH * (256 + width), 4 << 20, count * PIX * CH),
        name="down_stream",
    )(meta, *pieces, conv, patch_in, halves, halves, gain.reshape(1, width), *weights)


def full(shape):
    return pl.BlockSpec(shape, lambda i, m: (0,) * len(shape))


def load(pieces):
    return jnp.concatenate([piece[...] for piece in pieces], axis=0)


def take_blocks(refs, count):
    return [[refs.pop(0), refs.pop(0)] for _ in range(count)]


def chip_of(meta, images, tiles, outer, entry):
    _, _, tile, mpo = split_meta(meta, images)
    return lax.rem(tile + tiles - entry // 2, tiles) * outer + lax.rem(mpo + entry % 2, outer)


def qkv_kernel(entries, layout, groups, first, last, meta, *refs):
    refs = list(refs)
    count = len(entries)
    x_refs = take_blocks(refs, count)
    weight_refs = [refs.pop(0) for _ in range(6)]
    if not first:
        acc_in, square_in = refs.pop(0), refs.pop(0)
    if last:
        head_gains = refs.pop(0)
    scaled_ref = refs.pop(-1)
    half, span = scaled_ref.shape
    width = weight_refs[0].shape[1]
    heads = width // HD
    square = None if first else square_in[...]
    if last:
        acc, outs = [None] * 6, refs
    else:
        acc_out, square_out = refs
    for index in range(count):
        rows = pl.ds(pl.multiple_of(chip_of(meta, *layout, entries[index]) * span, span), span)
        gain = x_refs[index][0][half // 2 :, :][:1]
        for part in range(2):
            at = slice(part * half // 2, (part + 1) * half // 2)
            scaled_ref[at, :] = (x_refs[index][part][: half // 2, :] * gain).astype(BF16)
        value = jnp.concatenate([x_refs[index][0][: half // 2, :], x_refs[index][1][...]], axis=0)
        value = value.astype(F32)
        value = value * value
        for part in range(span // HD):
            piece = value[:, part * HD : (part + 1) * HD]
            square = piece if square is None else square + piece
        for part in range(6):
            term = mxu(scaled_ref[...], weight_refs[part][rows, :])
            if index == 0 and not first:
                term = term + acc_in[part]
            if last:
                acc[part] = term if index == 0 else acc[part] + term
            elif index == 0:
                acc_out[part] = term
            else:
                acc_out[part] += term
    if not last:
        square_out[...] = square
        return
    mean = jnp.sum(square, axis=-1, keepdims=True) * (1.0 / (groups * span))
    scale = lax.rsqrt(mean + EPSILON)
    for part in range(6):
        total = acc[part] * scale
        side, kind = part // 3, part % 3
        kv_outs = outs[2 * heads * side : 2 * heads * side + heads]
        q_outs = outs[2 * heads * side + heads : 2 * heads * side + 2 * heads]
        for head in range(heads):
            raw = total[:, head * HD : (head + 1) * HD]
            if kind == 1:
                kv_outs[head][1] = raw.astype(BF16)
                continue
            raw = raw * lax.rsqrt(jnp.mean(raw * raw, axis=-1, keepdims=True) + EPSILON)
            if kind == 0:
                kv_outs[head][0] = (raw * head_gains[1:2, :]).astype(BF16)
            else:
                q_outs[head][...] = (raw * (head_gains[0:1, :] * HD ** (-0.5))).astype(BF16)


def qkv_step(meta, layout, blocks, entries, weights, state, head_gains):
    span = blocks[0][1].shape[1]
    half = 2 * blocks[0][1].shape[0]
    width = weights[0].shape[1]
    heads = width // HD
    count, first, last = len(blocks), state is None, head_gains is not None
    groups = layout[1] * layout[2]
    inputs = [p for pieces in blocks for p in pieces]
    specs = [full(p.shape) for p in inputs]
    inputs += weights
    specs += [HELD] * 6
    if not first:
        inputs += list(state)
        specs += [HELD] * 2
    if last:
        inputs.append(head_gains)
        specs.append(full(head_gains.shape))
        kv, q = jax.ShapeDtypeStruct((2, half, HD), BF16), jax.ShapeDtypeStruct((half, HD), BF16)
        outs = ([kv] * heads + [q] * heads) * 2
    else:
        outs = [pltpu.VMEM((6, half, width), F32), pltpu.VMEM((half, HD), F32)]
    return pl.pallas_call(
        functools.partial(qkv_kernel, entries, layout, groups, first, last),
        grid_spec=pltpu.PrefetchScalarGridSpec(
            num_scalar_prefetch=1,
            grid=(1,),
            in_specs=specs,
            out_specs=[full(o.shape) if last else HELD for o in outs],
            scratch_shapes=[pltpu.VMEM((half, span), BF16)],
        ),
        out_shape=outs,
        compiler_params=params(20),
        cost_estimate=cost(12 * count * half * span * width, (6 + 2 * count) << 20),
        name="qkv_last" if last else "qkv_step",
    )(meta, *inputs)


def attention_kernel(images, pieces, half, meta, *refs):
    ctx, core, _, _ = split_meta(meta, images)
    ctxs = pieces // 2
    bases = []
    for piece in range(pieces):
        side = jnp.bitwise_xor(core, piece % 2)
        bases.append(lax.rem(ctx + ctxs - piece // 2, ctxs) * (2 * half) + side * half)
    q_refs, kv_refs, out_refs = refs[:2], refs[2 : 2 + pieces], refs[2 + pieces :]
    rows = q_refs[0].shape[0]
    step = pl.program_id(0)
    for side in range(2):
        place = bases[side] + step * rows + lax.broadcasted_iota(jnp.int32, (rows, 1), 0)
        limit = place
        for image in range(images):
            inner = place - meta[image]
            limit = jnp.where((inner >= 0) & (inner < IMG_TOK), meta[image] + IMG_TOK - 1, limit)
        query = q_refs[side][...]
        scores = []
        top = None
        for piece in range(pieces):
            score = lax.dot_general(
                query, kv_refs[piece][0], (((1,), (1,)), ((), ())), preferred_element_type=F32
            )
            position = lax.broadcasted_iota(jnp.int32, score.shape, 1)
            score = jnp.where(position <= limit - bases[piece], score, NEGATIVE_FILL)
            scores.append(score)
            best = jnp.max(score, axis=1, keepdims=True)
            top = best if top is None else jnp.maximum(top, best)
        total = jnp.zeros((rows, 1), F32)
        product = jnp.zeros((rows, HD), F32)
        for piece in range(pieces):
            weight = jnp.exp(scores[piece] - top)
            total = total + jnp.sum(weight, axis=1, keepdims=True)
            product = product + mxu(weight.astype(BF16), kv_refs[piece][1])
        out_refs[side][...] = (product / total).astype(BF16)


def attention(meta, queries, pieces, images):
    half = queries[0].shape[0]
    block = 256
    keys = half * len(pieces)
    rows = pl.BlockSpec((block, HD), lambda i, m: (i, 0))
    return pl.pallas_call(
        functools.partial(attention_kernel, images, len(pieces), half),
        grid_spec=pltpu.PrefetchScalarGridSpec(
            num_scalar_prefetch=1,
            grid=(half // block,),
            in_specs=[rows, rows] + [full(p.shape) for p in pieces],
            out_specs=[rows, rows],
        ),
        out_shape=[jax.ShapeDtypeStruct((half, HD), BF16)] * 2,
        compiler_params=params(24),
        cost_estimate=cost(8 * half * keys * HD, 4 * keys * HD, 2 * half * keys),
        name="attention",
    )(meta, *queries, *pieces)


def out_kernel(count, heads, first, last, meta, *refs):
    refs = list(refs)
    x_refs = take_blocks(refs, count)
    weight_refs = [[refs.pop(0), refs.pop(0)] for _ in range(count)]
    if first:
        streams = [refs.pop(0), refs.pop(0)]
        block = streams[1].shape[1]
    else:
        acc_in = refs.pop(0)
    outs = refs
    for side in range(2):
        if first:
            rows = [streams[0][side, :block, :], streams[1][side]]
            total = jnp.concatenate(rows, axis=0).astype(F32)
        else:
            total = acc_in[side]
        for index in range(count):
            weight = weight_refs[index][side]
            if heads == 2:
                for head in range(heads):
                    part = weight[0, :, head].reshape(2 * HD, weight.shape[4])
                    total = total + mxu(x_refs[index][head][...], part)
            else:
                total = total + mxu(load(x_refs[index]), weight[0, :, 0].reshape(2 * HD, weight.shape[4]))
        if last:
            outs[side][...] = total.astype(BF16)
        else:
            outs[0][side] = total


def out_step(meta, layout, blocks, entries, weights, state, last):
    width = weights[0].shape[1]
    heads = width // HD
    half = blocks[0][0].shape[0] * (1 if heads == 2 else 2)
    first = isinstance(state, list)
    count = len(blocks)
    views = [w.reshape(-1, 2, heads, HD, width) for w in weights]
    inputs = [p for pieces in blocks for p in pieces]
    specs = [full(p.shape) for p in inputs]
    for entry in entries:
        for view in views:
            inputs.append(view)
            specs.append(
                pl.BlockSpec(
                    (1, 2, heads, HD, width),
                    lambda i, m, entry=entry: (chip_of(m, *layout, entry), 0, 0, 0, 0),
                )
            )
    states = state if first else [state]
    inputs += states
    specs += [full(s.shape) for s in states]
    if last:
        outs = [jax.ShapeDtypeStruct((half, width), BF16)] * 2
    else:
        outs = [jax.ShapeDtypeStruct((2, half, width), F32)]
    result = pl.pallas_call(
        functools.partial(out_kernel, count, heads, first, last),
        grid_spec=pltpu.PrefetchScalarGridSpec(
            num_scalar_prefetch=1,
            grid=(1,),
            in_specs=specs,
            out_specs=[full(o.shape) for o in outs],
        ),
        out_shape=outs,
        compiler_params=params(24),
        cost_estimate=cost(8 * count * half * heads * HD * width, (2 + count) << 20),
        name="out_last" if last else "out_step",
    )(meta, *inputs)
    return result if last else result[0]


def pick_kernel(images, ctxs, meta, own_ref, par_ref, *out_refs):
    half = own_ref.shape[0]
    ctx, core, _, _ = split_meta(meta, images)
    for target in range(2 * ctxs):
        to_core = jnp.bitwise_xor(core, target % 2)
        slot = 2 * lax.rem(ctx + target // 2, ctxs) + to_core
        start = meta[meta[2 * images + slot]]
        place = start + lax.broadcasted_iota(jnp.int32, (IMG_TOK, half), 0)
        column = ctx * (2 * half) + lax.broadcasted_iota(jnp.int32, (IMG_TOK, half), 1)
        own = jnp.where(place == column + core * half, 1.0, 0.0).astype(BF16)
        par = jnp.where(place == column + (1 - core) * half, 1.0, 0.0).astype(BF16)
        out_refs[target][...] = (mxu(own, own_ref[...]) + mxu(par, par_ref[...])).astype(BF16)


def pick_rows(meta, own, par, images, ctxs):
    half, width = own.shape
    targets = 2 * ctxs
    return pl.pallas_call(
        functools.partial(pick_kernel, images, ctxs),
        grid_spec=pltpu.PrefetchScalarGridSpec(
            num_scalar_prefetch=1,
            grid=(1,),
            in_specs=[full(own.shape), full(par.shape)],
            out_specs=[full((IMG_TOK, width))] * targets,
        ),
        out_shape=[jax.ShapeDtypeStruct((IMG_TOK, width), BF16)] * targets,
        compiler_params=params(16),
        cost_estimate=cost(targets * 4 * IMG_TOK * half * width, 1 << 20),
        name="pick_rows",
    )(meta, own, par)


def merge_kernel(*refs):
    out_refs = refs[-2:]
    refs = refs[:-2]
    sides = refs[: len(refs) // 2], refs[len(refs) // 2 :]
    width = sides[0][0].shape[1]
    block = IMG_TOK // 2
    for side in range(2):
        total = sides[side][0][...].astype(F32)
        for part in sides[side][1:]:
            total = total + part[...].astype(F32)
        total = total.astype(BF16)
        for index in range(2):
            out_refs[index][:, side * width : (side + 1) * width] = total[index * block : (index + 1) * block]


def merge_picks(own_parts, par_parts):
    width = own_parts[0].shape[1]
    return pl.pallas_call(
        merge_kernel,
        out_shape=[jax.ShapeDtypeStruct((IMG_TOK // 2, 2 * width), BF16)] * 2,
        compiler_params=pltpu.CompilerParams(vmem_limit_bytes=8 << 20),
        cost_estimate=cost(1 << 20, 1 << 20),
        name="merge_picks",
    )(*own_parts, *par_parts)


def finish_kernel(core_ref, own_a, own_b, par_a, par_b, out_ref, sums, lines):
    core = core_ref[0]
    for side, (left, right) in enumerate(((own_a, own_b), (par_a, par_b))):
        sums[side] = left[...] + right[...]
    rows = sums.shape[1] // SIDE
    lanes = PATCH * CIN
    per = HD // lanes
    for side in range(2):
        for part in range(SIDE // per):
            cols = [sums[side, pl.ds(part * per + k, rows, stride=SIDE), :] for k in range(per)]
            for row in range(PATCH):
                pieces = [col[:, row * lanes : (row + 1) * lanes] for col in cols]
                lines[part, pl.ds(row, rows, stride=PATCH), :] = jnp.concatenate(pieces, axis=1)
        slot = jnp.bitwise_xor(core, side)
        for part in range(SIDE // per):
            out_ref[slot, :, part * HD : (part + 1) * HD] = lines[part]


def finish(core, own_a, own_b, par_a, par_b):
    count = own_a.shape[0]
    return pl.pallas_call(
        finish_kernel,
        grid_spec=pltpu.PrefetchScalarGridSpec(
            num_scalar_prefetch=1,
            grid=(1,),
            in_specs=[full(own_a.shape)] * 4,
            out_specs=full((2, count // PATCH, WL * CIN)),
            scratch_shapes=[
                pltpu.VMEM((2, count, PIX * CIN), F32),
                pltpu.VMEM((WL * CIN // HD, count // PATCH, HD), F32),
            ],
        ),
        out_shape=jax.ShapeDtypeStruct((2, count // PATCH, WL * CIN), F32),
        compiler_params=params(8),
        cost_estimate=cost(1 << 16, 1 << 18),
        name="finish",
    )(core, own_a, own_b, par_a, par_b)


def spread(active, spread_ref):
    row = lax.broadcasted_iota(jnp.int32, (IMG_TOK, PIX * CIN), 0)
    patch_row, patch_col = row >> 4, row & (SIDE - 1)
    total = None
    for index in range(9):
        down, right = index // 3 - 1, index % 3 - 1
        part = mxu(active, spread_ref[:, index * PIX * CIN : (index + 1) * PIX * CIN])
        offset = down * SIDE + right
        if offset:
            part = pltpu.roll(part, offset % IMG_TOK, 0)
        source_row, source_col = patch_row - down, patch_col - right
        inside = (source_row >= 0) & (source_row < SIDE) & (source_col >= 0) & (source_col < SIDE)
        part = jnp.where(inside, part, 0.0)
        total = part if total is None else total + part
    return total


def up_kernel(count, halves, first, last, *refs):
    refs = list(refs)
    x_refs = take_blocks(refs, count)
    weight_refs = [[[refs.pop(0) for _ in range(2)] for _ in range(halves)] for _ in range(count)]
    acc_in = None if first else refs.pop(0)
    spread_ref = refs.pop(0) if last else None
    out_ref = refs[0]
    width = x_refs[0][0].shape[1] // 2
    values = [load(pieces) for pieces in x_refs]
    totals = []
    for part in range(halves):
        total = None if first else acc_in[part]
        for block in range(count):
            for side in range(2):
                term = mxu(
                    values[block][:, side * width : (side + 1) * width],
                    weight_refs[block][part][side][0],
                )
                total = term if total is None else total + term
        totals.append(total)
        if not last:
            out_ref[part] = total
    if last:
        active = [silu(total).astype(BF16) for total in totals]
        active = jnp.concatenate(active, axis=1) if halves > 1 else active[0]
        out_ref[...] = spread(active, spread_ref)


def up_step(blocks, entries, tiles, weights, state, spread_weight):
    span = blocks[0][0].shape[1]
    halves, count = len(weights), len(blocks)
    first, last = state is None, spread_weight is not None
    whole = lambda shape: pl.BlockSpec(shape, lambda i: (0,) * len(shape))
    inputs = [p for pieces in blocks for p in pieces]
    specs = [whole(p.shape) for p in inputs]
    for entry in entries:
        offset = entry - 2 * (entry // 2 > tiles // 2)
        if entry // 2 == tiles // 2:
            offset = 2 * tiles - 2 + entry % 2
        for sides in weights:
            for weight in sides:
                inputs.append(weight)
                specs.append(pl.BlockSpec((1, span // 2, CH), lambda i, offset=offset: (offset, 0, 0)))
    if not first:
        inputs.append(state)
        specs.append(whole(state.shape))
    if last:
        inputs.append(spread_weight)
        specs.append(whole(spread_weight.shape))
        out = jax.ShapeDtypeStruct((IMG_TOK, PIX * CIN), F32)
    else:
        out = jax.ShapeDtypeStruct((halves, IMG_TOK, CH), F32)
    return pl.pallas_call(
        functools.partial(up_kernel, count, halves, first, last),
        grid=(1,),
        in_specs=specs,
        out_specs=whole(out.shape),
        out_shape=out,
        compiler_params=params(16),
        cost_estimate=cost(2 * count * IMG_TOK * span * CH * halves, (1 + count) << 20),
        name="up_last" if last else "up_step",
    )(*inputs)


def spread_weights(up_conv, pixels):
    taps = up_conv.reshape(9, CH, CIN).transpose(1, 0, 2).reshape(CH, 9 * CIN)
    shape = (pixels.shape[0], 9 * CIN, 9 * PIX * CIN)
    row = lax.broadcasted_iota(jnp.int32, shape, 1)
    col = lax.broadcasted_iota(jnp.int32, shape, 2)
    pixel = pixels[:, None, None]
    tap, channel = row >> 3, row & 7
    patch, target, out_channel = col >> 7, (col >> 3) & 15, col & 7
    tap_row, tap_col = tap // 3, tap % 3
    down, right = patch // 3 - 1, patch % 3 - 1
    hit = (
        (channel == out_channel)
        & ((pixel >> 2) + 1 - tap_row == (target >> 2) + PATCH * down)
        & ((pixel & 3) + 1 - tap_col == (target & 3) + PATCH * right)
    )
    placed = jnp.where(hit, 1.0, 0.0).astype(BF16)
    spread = jnp.einsum("ct,ptn->pcn", taps, placed, preferred_element_type=F32)
    return spread.astype(BF16).reshape(pixels.shape[0] * CH, 9 * PIX * CIN)


def by_core(core, own, other, axis):
    return jnp.where(
        core == 0, jnp.concatenate([own, other], axis), jnp.concatenate([other, own], axis)
    )


def shift(values, axis, step):
    count = lax.axis_size(axis)
    return lax.ppermute(values, axis, [(i, (i + step) % count) for i in range(count)])


def gather_small(latents, down_conv, *others):
    ctxs, tiles = lax.axis_size("ctx"), lax.axis_size("tile")
    every = jnp.concatenate([latents] + [shift(latents, "ctx", s) for s in range(1, ctxs)])
    conv = by_core(lax.axis_index("core"), down_conv, swap(down_conv), 1)
    conv = by_core(lax.axis_index("mpo"), conv, shift(conv, "mpo", 1), 1)
    every, conv, others = lax.optimization_barrier((every, conv, others))
    return [every] + [shift(every, "tile", s) for s in range(1, tiles)], conv, *others


def columns_kernel(meta, kept_in, sent_in, kept_out, sent_out):
    kept_out[0] = kept_in[...]
    sent_out[0] = sent_in[...]


def transpose_first(meta, patch_out, layout, ctxs):
    images, tiles, outer = layout
    width, features = patch_out.shape
    deep = features // (tiles * outer)
    halves = 2 if ctxs == 2 and deep == 2 * CH else 1
    size = deep // halves

    def place(other):
        def index(i, m):
            ctx, _, _, mpo = split_meta(m, images)
            chip = i * outer + lax.rem(mpo + other, outer)
            return 0, chip * halves + (ctx if halves == 2 else 0)

        return pl.BlockSpec((width, size), index)

    out = pl.BlockSpec((1, width, size), lambda i, m: (i, 0, 0))
    kept, sent = pl.pallas_call(
        columns_kernel,
        grid_spec=pltpu.PrefetchScalarGridSpec(
            num_scalar_prefetch=1, grid=(tiles,), in_specs=[place(0), place(1)], out_specs=[out, out]
        ),
        out_shape=[jax.ShapeDtypeStruct((tiles, width, size), BF16)] * 2,
        compiler_params=params(8),
        cost_estimate=cost(1 << 16, 2 << 20),
        name="columns",
    )(meta, patch_out, patch_out)
    return kept, sent, halves


def transpose_second(kept, received, step):
    tiles = lax.axis_size("tile")
    place = lax.rem(lax.axis_index("tile") + step, tiles)
    block = [lax.dynamic_index_in_dim(x, place, 0, keepdims=False) for x in (kept, received)]
    block = jnp.stack(block)
    return shift(block, "tile", step) if step else block


def transposed(blocks, halves):
    own = jnp.concatenate(blocks)
    weights = [own] if halves == 1 else [own, shift(own, "ctx", 1)]
    return [[weight, swap(weight)] for weight in weights]


def gather_pair(first, second, state, step, extras=None):
    tiles = lax.axis_size("tile")
    found, moving = [{0: first}, {}], [None, None]

    def launch(which, index):
        ring = found[which][2 * index]
        if index < tiles - 1:
            moving[which] = (shift(ring, "tile", 1), shift(ring, "mpo", 1))
        elif which:
            moving[which] = shift(found[which][2 * index - 1], "tile", 1)
        else:
            moving[which] = shift(ring, "mpo", 1)

    def work(entries, state):
        return step([[found[0][e], found[1][e]] for e in entries], entries, state, False)

    launch(0, 0)
    late = callable(second)
    if late:
        events = [(0, 1), (0, 2)]
        for index in range(1, tiles - 2):
            events += [(1, index), (0, index + 2)]
        events += [(1, tiles - 2), (1, tiles - 1)]
    else:
        found[1][0] = second
        launch(1, 0)
        events = [(which, index) for index in range(1, tiles) for which in range(2)]
    seen = first
    for which, index in events:
        ring, cross = moving[which]
        if (which, index) == (int(late), tiles - 1):
            ring, cross, seen, state = lax.optimization_barrier((ring, cross, seen, state))
        else:
            ring, cross, seen = lax.optimization_barrier((ring, cross, seen))
        found[which][2 * index], found[which][2 * index - 1] = ring, cross
        seen = ring
        launch(which, index)
        if late and (which, index) == (0, 1):
            found[1][0], extras = second(cross)
            launch(1, 0)
        if (which, index) == (1, tiles - 2):
            state = work(list(range(2 * tiles - 3)), state)
    state = work([2 * tiles - 2, 2 * tiles - 3], state)
    last = lax.optimization_barrier((moving[0], moving[1], state, extras))
    return step([[last[0], last[1]]], [2 * tiles - 1], last[2], True), last[3]


def shards(
    text_embed,
    latents,
    down_conv,
    patch_in,
    norm_gain,
    query_weight,
    key_weight,
    value_weight,
    query_gain,
    key_gain,
    out_weight,
    patch_out,
    up_conv,
    span_start,
    image_of_slot,
):
    ctxs, tiles, outer = (lax.axis_size(name) for name in ("ctx", "tile", "mpo"))
    ctx, tile, mpo, core = (lax.axis_index(name) for name in ("ctx", "tile", "mpo", "core"))
    seq_rows, width = text_embed.shape
    half = seq_rows // 2
    heads = width // HD
    images = span_start.shape[0]
    local = latents.shape[0]

    numbers = jnp.arange(images, dtype=jnp.int32)
    matches = image_of_slot[None, :] == numbers[:, None]
    slot_of_image = jnp.sum(jnp.where(matches, numbers[None, :], 0), axis=1)
    slot_place = lax.rem(ctx + ctxs - slot_of_image // local, ctxs) * local + slot_of_image % local
    meta = jnp.concatenate(
        [span_start, slot_place, image_of_slot, jnp.stack([ctx, core, tile, mpo])]
    ).astype(jnp.int32)
    layout = (images, tiles, outer)

    weights = [swap(w) for w in (key_weight, value_weight, query_weight)]
    pieces, conv, meta, weights[0], weights[1] = gather_small(latents, down_conv, meta, *weights[:2])
    kept, sent, halves = transpose_first(meta, patch_out, layout, ctxs)
    pieces, received = lax.optimization_barrier((pieces, shift(sent, "mpo", 1)))
    up_blocks = [transpose_second(kept, received, step) for step in range(tiles) if 2 * step != tiles]

    weights += [key_weight, value_weight, query_weight]
    streams = down_stream(meta, pieces, conv, patch_in, text_embed, norm_gain, weights, images)
    streams, weights = streams[:2], streams[2:]
    streams, up_blocks = lax.optimization_barrier((streams, up_blocks))
    others = [swap(s[1]) for s in streams]
    others = lax.optimization_barrier(others)

    head_gains = jnp.stack([query_gain, key_gain])

    def project(blocks, entries, state, last):
        return qkv_step(meta, layout, blocks, entries, weights, state, head_gains if last else None)

    state, out_par = gather_pair(
        *[by_core(core, s[0], o, 1) for s, o in zip(streams, others)], None, project, swap(out_weight)
    )
    state, kept, received = lax.optimization_barrier((state, kept, received))
    up_block = transpose_second(kept, received, tiles // 2)
    kv_send, q_send = state[:heads], state[heads : 2 * heads]
    kv_own, q_own = state[2 * heads : 3 * heads], state[3 * heads :]

    def shifted(values, step, cross):
        pairs = [
            (2 * c + k, 2 * ((c + step) % ctxs) + (1 - k if cross else k))
            for c in range(ctxs)
            for k in range(2)
        ]
        return lax.ppermute(values, ("ctx", "core"), pairs)

    def pieces_of(head):
        pieces = [swap(q_send[head]), kv_own[head], swap(kv_send[head])]
        for step in range(1, ctxs):
            pieces += [shifted(kv_own[head], step, False), shifted(kv_send[head], step, True)]
        return pieces

    def attend(head, pieces, ahead):
        result = attention(meta, [q_own[head], pieces[0]], pieces[1:], images)
        (att_own, att_send), ahead = lax.optimization_barrier((result, ahead))
        return by_core(core, att_own, swap(att_send), 1), ahead

    pieces, up_block = lax.optimization_barrier((pieces_of(0), up_block))
    attended, pieces = attend(0, pieces, pieces_of(1) if heads > 1 else None)
    if heads == 1:
        attended, second = attended[: half // 2], attended[half // 2 :]
        extras = transposed(up_blocks + [up_block], halves)
    else:
        extras = None

        def second(token):
            result, (up, _) = attend(1, pieces, (up_blocks + [up_block], token))
            return result, transposed(up, halves)

    def project_out(blocks, entries, state, last):
        return out_step(meta, layout, blocks, entries, (out_weight, out_par), state, last)

    state = [jnp.stack([s[0], o]) for s, o in zip(streams, others)]
    state, up_weights = gather_pair(attended, second, state, project_out, extras)
    out_own, out_send = state
    out_other = swap(out_send)
    layer_out = by_core(core, out_own, out_other, 0)

    picks = pick_rows(meta, out_own, out_other, images, ctxs)
    own_parts, par_parts = [picks[0]], [swap(picks[1])]
    for step in range(1, ctxs):
        own_parts.append(shifted(picks[2 * step], step, False))
        par_parts.append(shifted(picks[2 * step + 1], step, True))

    pixel = tile * outer + mpo
    pixels = jnp.stack([pixel * halves + lax.rem(ctx + h, halves) for h in range(halves)])
    spread_weight = spread_weights(up_conv, pixels)

    def project_up(blocks, entries, state, last):
        return up_step(blocks, entries, tiles, up_weights, state, spread_weight if last else None)

    state, _ = gather_pair(*merge_picks(own_parts, par_parts), None, project_up)

    bands = state.reshape(tiles, IMG_TOK // tiles, PIX * CIN)
    band = lax.dynamic_index_in_dim(bands, tile, 0, keepdims=False)
    for step in range(1, tiles):
        piece = lax.dynamic_index_in_dim(bands, lax.rem(tile + step, tiles), 0, keepdims=False)
        band = band + shift(piece, "tile", step)
    quad = {}
    for name, pairs in (
        ("mpo", [(0, 2), (1, 3), (2, 0), (3, 1)]),
        ("core", [(0, 1), (1, 0), (2, 3), (3, 2)]),
        ("both", [(0, 3), (1, 2), (2, 1), (3, 0)]),
    ):
        quad[name] = lax.ppermute(band, ("mpo", "core"), pairs)
    return layer_out, finish(meta[3 * images + 1 :], band, quad["mpo"], quad["core"], quad["both"])


def solution(mesh):
    ctxs, tiles, parts = mesh.devices.shape
    fine = Mesh(
        mesh.devices.reshape(ctxs, tiles, parts // 2, 2), ("ctx", "tile", "mpo", "core")
    )
    features = ("tile", "mpo", "core")
    return jax.shard_map(
        shards,
        mesh=fine,
        in_specs=(
            P("ctx", features),
            P("ctx", "tile", None),
            P(None, ("mpo", "core")),
            P(None, features),
            P(features),
            P(None, features),
            P(None, features),
            P(None, features),
            P(),
            P(),
            P(None, features),
            P(features, None),
            P(),
            P(),
            P(),
        ),
        out_specs=(P("ctx", features), P("ctx", "tile", None)),
        check_vma=False,
    )
```

```python
import functools

import jax
import jax.numpy as jnp
from jax import lax
from jax.experimental import pallas as pl
from jax.experimental.pallas import tpu as pltpu
from jax.sharding import Mesh
from jax.sharding import PartitionSpec as P

HD = 128
CH = 256
CIN = 8
WL = 64
HL = 64
PATCH = 4
PIX = PATCH * PATCH
SIDE = WL // PATCH
IMG_TOK = 256
EPSILON = 1e-05
NEGATIVE_FILL = -1e30
WINDOW = (PATCH + 2) * CIN
TAPS = 3 * WINDOW
BF16 = jnp.bfloat16
F32 = jnp.float32


def split_meta(meta, images):
    return meta[3 * images], meta[3 * images + 1], meta[3 * images + 2], meta[3 * images + 3]


def params(mebibytes):
    return pltpu.CompilerParams(
        dimension_semantics=("arbitrary",), vmem_limit_bytes=mebibytes * 1024 * 1024
    )


def cost(flops, nbytes, transcendentals=0):
    return pl.CostEstimate(
        flops=int(flops), bytes_accessed=int(nbytes), transcendentals=int(transcendentals)
    )


def silu(values):
    half = values * 0.5
    return half + half * jnp.tanh(half)


def mxu(left, right):
    return jnp.dot(left, right, preferred_element_type=F32)


def swap(values):
    return lax.ppermute(values, "core", [(0, 1), (1, 0)])


HELD = pl.BlockSpec(memory_space=pltpu.VMEM)


GAIN_ROWS = 16
TOP = 16


def down_kernel(images, tiles, half, meta, *refs):
    lat_refs, refs = refs[:tiles], refs[tiles:]
    conv_ref, patch_ref, own_text, par_text, gain_ref = refs[:5]
    weight_refs, (first_ref, second_ref), held_refs = refs[5:11], refs[11:13], refs[13:19]
    grid_rows, conv_wide, conv_bf16, windows, total, arrived = refs[19:]
    step = pl.program_id(0)
    copies = [
        pltpu.make_async_copy(weight, held, arrived.at[index])
        for index, (weight, held) in enumerate(zip(weight_refs, held_refs))
    ]

    @pl.when(step == 0)
    def _():
        for copy in copies:
            copy.start()

    group = images * SIDE
    ctx, core, tile, _ = split_meta(meta, images)

    @pl.when(step == 0)
    def _():
        grid_rows[...] = jnp.zeros_like(grid_rows)
        blocks = grid_rows.shape[1]
        for index in range(tiles):
            band = lat_refs[index].shape[1]
            at = TOP + lax.rem(tile + tiles - index, tiles) * band
            rows = pl.ds(pl.multiple_of(at, 8), band)
            latent = lat_refs[index][...].astype(F32)
            edges = [jnp.zeros((images, band, size), F32) for size in (CIN, HD - CIN)]
            wide = jnp.concatenate([edges[0], latent, edges[1]], axis=2)
            for part in range(blocks):
                grid_rows[:, part, rows, :] = wide[:, :, part * HD : (part + 1) * HD]
        conv_wide[...] = jnp.zeros_like(conv_wide)
        conv = conv_ref[...].astype(F32)
        for col in range(PATCH):
            for tap in range(3):
                at = WINDOW * tap + CIN * col
                conv_wide[at : at + 3 * CIN, CH * col : CH * (col + 1)] = conv[
                    3 * CIN * tap : 3 * CIN * (tap + 1), :
                ]
        conv_bf16[...] = conv_wide[...].astype(BF16)

        def build(image, carry):
            for row in range(PATCH + 2):
                take = pl.ds(TOP - 1 + row, SIDE, stride=PATCH)
                line = [grid_rows[image, part, take, :] for part in range(blocks)]
                line = jnp.concatenate(line, axis=1).astype(BF16)
                for col in range(SIDE):
                    piece = line[:, PATCH * CIN * col : PATCH * CIN * col + WINDOW]
                    at = pl.ds(pl.multiple_of(group * col + image * SIDE, SIDE), SIDE)
                    for shift in range(3):
                        if 0 <= row - shift < PATCH:
                            windows[row - shift, at, WINDOW * shift : WINDOW * (shift + 1)] = piece
            return carry

        lax.fori_loop(0, images, build, 0)
        total[...] = jnp.zeros_like(total)

    chunk = 256
    for part in range(images * IMG_TOK // chunk):
        rows = slice(part * chunk, (part + 1) * chunk)
        hidden = silu(mxu(windows[step, rows, :], conv_bf16[...])).astype(BF16)
        total[rows, :] += mxu(hidden, patch_ref[...])

    @pl.when(step == PATCH - 1)
    def _():
        tokens = total[...].astype(BF16)
        block = half // 2
        for side, text_ref in enumerate((own_text, par_text)):
            base = ctx * (2 * half) + jnp.bitwise_xor(core, side) * half
            for part, out_ref in enumerate((first_ref, second_ref)):
                place = base + part * block + lax.broadcasted_iota(jnp.int32, (block, 1), 0)
                source = jnp.full((block, 1), -1, jnp.int32)
                for image in range(images):
                    inner = place - meta[image]
                    inside = (inner >= 0) & (inner < IMG_TOK)
                    index = (inner & (SIDE - 1)) * group + meta[images + image] * SIDE + (inner >> 4)
                    source = jnp.where(inside, index, source)
                choice = source == lax.broadcasted_iota(jnp.int32, (block, images * IMG_TOK), 1)
                picked = mxu(jnp.where(choice, 1.0, 0.0).astype(BF16), tokens)
                text = text_ref[0, part * block : (part + 1) * block, :].astype(F32)
                out_ref[side, :block, :] = jnp.where(source >= 0, picked, text).astype(BF16)
            gain = gain_ref[...].astype(F32)
            first_ref[side, block:, :] = jnp.broadcast_to(gain, (GAIN_ROWS, gain.shape[1])).astype(BF16)
        for copy in copies:
            copy.wait()


def down_stream(meta, pieces, conv, patch_in, text, gain, weights, images):
    seq_rows, width = text.shape
    half = seq_rows // 2
    tiles = len(pieces)
    count = images * IMG_TOK
    halves = text.reshape(2, half, width)
    core_at = 3 * images + 1
    first, second = (2, half // 2 + GAIN_ROWS, width), (2, half // 2, width)
    return pl.pallas_call(
        functools.partial(down_kernel, images, tiles, half),
        grid_spec=pltpu.PrefetchScalarGridSpec(
            num_scalar_prefetch=1,
            grid=(PATCH,),
            in_specs=[full(p.shape) for p in pieces]
            + [
                full(conv.shape),
                pl.BlockSpec((PATCH * CH, width), lambda i, m: (i, 0)),
                pl.BlockSpec((1, half, width), lambda i, m: (m[core_at], 0, 0)),
                pl.BlockSpec((1, half, width), lambda i, m: (1 - m[core_at], 0, 0)),
                full((1, width)),
            ]
            + [pl.BlockSpec(memory_space=pl.ANY)] * 6,
            out_specs=[full(first), full(second)] + [HELD] * 6,
            scratch_shapes=[
                pltpu.VMEM((images, WL * CIN // HD + 1, TOP + HL + 16, HD), F32),
                pltpu.VMEM((TAPS, PATCH * CH), F32),
                pltpu.VMEM((TAPS, PATCH * CH), BF16),
                pltpu.VMEM((PATCH, count, TAPS), BF16),
                pltpu.VMEM((count, width), F32),
                pltpu.SemaphoreType.DMA((6,)),
            ],
        ),
        out_shape=[jax.ShapeDtypeStruct(first, BF16), jax.ShapeDtypeStruct(second, BF16)]
        + [pltpu.VMEM(w.shape, w.dtype) for w in weights],
        compiler_params=params(32),
        cost_estimate=cost(2 * count * PIX * CH * (256 + width), 4 << 20, count * PIX * CH),
        name="down_stream",
    )(meta, *pieces, conv, patch_in, halves, halves, gain.reshape(1, width), *weights)


def full(shape):
    return pl.BlockSpec(shape, lambda i, m: (0,) * len(shape))


def load(pieces):
    return jnp.concatenate([piece[...] for piece in pieces], axis=0)


def take_blocks(refs, count):
    return [[refs.pop(0), refs.pop(0)] for _ in range(count)]


def chip_of(meta, images, tiles, outer, entry):
    _, _, tile, mpo = split_meta(meta, images)
    return lax.rem(tile + tiles - entry // 2, tiles) * outer + lax.rem(mpo + entry % 2, outer)


def qkv_kernel(entries, layout, groups, held, first, last, meta, *refs):
    refs = list(refs)
    count = len(entries)
    x_refs = take_blocks(refs, count)
    weight_refs = [refs.pop(0) for _ in range(6 if held else 6 * count)]
    if not first:
        acc_in, square_in = refs.pop(0), refs.pop(0)
    if last:
        head_gains = refs.pop(0)
    scaled_ref = refs.pop(-1)
    half, span = scaled_ref.shape
    width = weight_refs[0].shape[1]
    heads = width // HD
    square = None if first else square_in[...]
    if last:
        acc, outs = [None] * 6, refs
    else:
        acc_out, square_out = refs
    for index in range(count):
        rows = pl.ds(pl.multiple_of(chip_of(meta, *layout, entries[index]) * span, span), span)
        gain = x_refs[index][0][half // 2 :, :][:1]
        for part in range(2):
            at = slice(part * half // 2, (part + 1) * half // 2)
            scaled_ref[at, :] = (x_refs[index][part][: half // 2, :] * gain).astype(BF16)
        value = jnp.concatenate([x_refs[index][0][: half // 2, :], x_refs[index][1][...]], axis=0)
        value = value.astype(F32)
        value = value * value
        for part in range(span // HD):
            piece = value[:, part * HD : (part + 1) * HD]
            square = piece if square is None else square + piece
        for part in range(6):
            if held:
                weight = weight_refs[part][rows, :]
            else:
                weight = weight_refs[6 * index + part][...]
            term = mxu(scaled_ref[...], weight)
            if index == 0 and not first:
                term = term + acc_in[part]
            if last:
                acc[part] = term if index == 0 else acc[part] + term
            elif index == 0:
                acc_out[part] = term
            else:
                acc_out[part] += term
    if not last:
        square_out[...] = square
        return
    mean = jnp.sum(square, axis=-1, keepdims=True) * (1.0 / (groups * span))
    scale = lax.rsqrt(mean + EPSILON)
    for part in range(6):
        total = acc[part] * scale
        side, kind = part // 3, part % 3
        kv_outs = outs[2 * heads * side : 2 * heads * side + heads]
        q_outs = outs[2 * heads * side + heads : 2 * heads * side + 2 * heads]
        for head in range(heads):
            raw = total[:, head * HD : (head + 1) * HD]
            if kind == 1:
                kv_outs[head][1] = raw.astype(BF16)
                continue
            raw = raw * lax.rsqrt(jnp.mean(raw * raw, axis=-1, keepdims=True) + EPSILON)
            if kind == 0:
                kv_outs[head][0] = (raw * head_gains[1:2, :]).astype(BF16)
            else:
                q_outs[head][...] = (raw * (head_gains[0:1, :] * HD ** (-0.5))).astype(BF16)


def qkv_step(meta, layout, blocks, entries, weights, held, state, head_gains):
    span = blocks[0][1].shape[1]
    half = 2 * blocks[0][1].shape[0]
    width = weights[0].shape[1]
    heads = width // HD
    count, first, last = len(blocks), state is None, head_gains is not None
    groups = layout[1] * layout[2]
    inputs = [p for pieces in blocks for p in pieces]
    specs = [full(p.shape) for p in inputs]
    if held:
        inputs += weights
        specs += [HELD] * 6
    else:
        for entry in entries:
            inputs += weights
            index = lambda i, m, entry=entry: (chip_of(m, *layout, entry), 0)
            specs += [pl.BlockSpec((span, width), index)] * 6
    if not first:
        inputs += list(state)
        specs += [HELD] * 2
    if last:
        inputs.append(head_gains)
        specs.append(full(head_gains.shape))
        kv, q = jax.ShapeDtypeStruct((2, half, HD), BF16), jax.ShapeDtypeStruct((half, HD), BF16)
        outs = ([kv] * heads + [q] * heads) * 2
    else:
        outs = [pltpu.VMEM((6, half, width), F32), pltpu.VMEM((half, HD), F32)]
    return pl.pallas_call(
        functools.partial(qkv_kernel, entries, layout, groups, held, first, last),
        grid_spec=pltpu.PrefetchScalarGridSpec(
            num_scalar_prefetch=1,
            grid=(1,),
            in_specs=specs,
            out_specs=[full(o.shape) if last else HELD for o in outs],
            scratch_shapes=[pltpu.VMEM((half, span), BF16)],
        ),
        out_shape=outs,
        compiler_params=params(20),
        cost_estimate=cost(12 * count * half * span * width, (6 + 2 * count) << 20),
        name="qkv_last" if last else "qkv_step",
    )(meta, *inputs)


def attention_kernel(images, pieces, half, meta, *refs):
    ctx, core, _, _ = split_meta(meta, images)
    ctxs = pieces // 2
    bases = []
    for piece in range(pieces):
        side = jnp.bitwise_xor(core, piece % 2)
        bases.append(lax.rem(ctx + ctxs - piece // 2, ctxs) * (2 * half) + side * half)
    q_refs, kv_refs, out_refs = refs[:2], refs[2 : 2 + pieces], refs[2 + pieces :]
    rows = q_refs[0].shape[0]
    step = pl.program_id(0)
    for side in range(2):
        place = bases[side] + step * rows + lax.broadcasted_iota(jnp.int32, (rows, 1), 0)
        limit = place
        for image in range(images):
            inner = place - meta[image]
            limit = jnp.where((inner >= 0) & (inner < IMG_TOK), meta[image] + IMG_TOK - 1, limit)
        query = q_refs[side][...]
        scores = []
        top = None
        for piece in range(pieces):
            score = lax.dot_general(
                query, kv_refs[piece][0], (((1,), (1,)), ((), ())), preferred_element_type=F32
            )
            position = lax.broadcasted_iota(jnp.int32, score.shape, 1)
            score = jnp.where(position <= limit - bases[piece], score, NEGATIVE_FILL)
            scores.append(score)
            best = jnp.max(score, axis=1, keepdims=True)
            top = best if top is None else jnp.maximum(top, best)
        total = jnp.zeros((rows, 1), F32)
        product = jnp.zeros((rows, HD), F32)
        for piece in range(pieces):
            weight = jnp.exp(scores[piece] - top)
            total = total + jnp.sum(weight, axis=1, keepdims=True)
            product = product + mxu(weight.astype(BF16), kv_refs[piece][1])
        out_refs[side][...] = (product / total).astype(BF16)


def attention(meta, queries, pieces, images):
    half = queries[0].shape[0]
    block = 256
    keys = half * len(pieces)
    rows = pl.BlockSpec((block, HD), lambda i, m: (i, 0))
    return pl.pallas_call(
        functools.partial(attention_kernel, images, len(pieces), half),
        grid_spec=pltpu.PrefetchScalarGridSpec(
            num_scalar_prefetch=1,
            grid=(half // block,),
            in_specs=[rows, rows] + [full(p.shape) for p in pieces],
            out_specs=[rows, rows],
        ),
        out_shape=[jax.ShapeDtypeStruct((half, HD), BF16)] * 2,
        compiler_params=params(24),
        cost_estimate=cost(8 * half * keys * HD, 4 * keys * HD, 2 * half * keys),
        name="attention",
    )(meta, *queries, *pieces)


def out_kernel(count, heads, first, last, meta, *refs):
    refs = list(refs)
    x_refs = take_blocks(refs, count)
    weight_refs = [[refs.pop(0), refs.pop(0)] for _ in range(count)]
    if first:
        streams = [refs.pop(0), refs.pop(0)]
        block = streams[1].shape[1]
    else:
        acc_in = refs.pop(0)
    outs = refs
    for side in range(2):
        if first:
            rows = [streams[0][side, :block, :], streams[1][side]]
            total = jnp.concatenate(rows, axis=0).astype(F32)
        else:
            total = acc_in[side]
        for index in range(count):
            weight = weight_refs[index][side]
            if heads == 2:
                for head in range(heads):
                    part = weight[0, :, head].reshape(2 * HD, weight.shape[4])
                    total = total + mxu(x_refs[index][head][...], part)
            else:
                total = total + mxu(load(x_refs[index]), weight[0, :, 0].reshape(2 * HD, weight.shape[4]))
        if last:
            outs[side][...] = total.astype(BF16)
        else:
            outs[0][side] = total


def out_step(meta, layout, blocks, entries, weights, state, last):
    width = weights[0].shape[1]
    heads = width // HD
    half = blocks[0][0].shape[0] * (1 if heads == 2 else 2)
    first = isinstance(state, list)
    count = len(blocks)
    views = [w.reshape(-1, 2, heads, HD, width) for w in weights]
    inputs = [p for pieces in blocks for p in pieces]
    specs = [full(p.shape) for p in inputs]
    for entry in entries:
        for view in views:
            inputs.append(view)
            specs.append(
                pl.BlockSpec(
                    (1, 2, heads, HD, width),
                    lambda i, m, entry=entry: (chip_of(m, *layout, entry), 0, 0, 0, 0),
                )
            )
    states = state if first else [state]
    inputs += states
    specs += [full(s.shape) for s in states]
    if last:
        outs = [jax.ShapeDtypeStruct((half, width), BF16)] * 2
    else:
        outs = [jax.ShapeDtypeStruct((2, half, width), F32)]
    result = pl.pallas_call(
        functools.partial(out_kernel, count, heads, first, last),
        grid_spec=pltpu.PrefetchScalarGridSpec(
            num_scalar_prefetch=1,
            grid=(1,),
            in_specs=specs,
            out_specs=[full(o.shape) for o in outs],
        ),
        out_shape=outs,
        compiler_params=params(24),
        cost_estimate=cost(8 * count * half * heads * HD * width, (2 + count) << 20),
        name="out_last" if last else "out_step",
    )(meta, *inputs)
    return result if last else result[0]


def pick_kernel(images, ctxs, meta, own_ref, par_ref, *out_refs):
    half = own_ref.shape[0]
    ctx, core, _, _ = split_meta(meta, images)
    for target in range(2 * ctxs):
        to_core = jnp.bitwise_xor(core, target % 2)
        slot = 2 * lax.rem(ctx + target // 2, ctxs) + to_core
        start = meta[meta[2 * images + slot]]
        place = start + lax.broadcasted_iota(jnp.int32, (IMG_TOK, half), 0)
        column = ctx * (2 * half) + lax.broadcasted_iota(jnp.int32, (IMG_TOK, half), 1)
        own = jnp.where(place == column + core * half, 1.0, 0.0).astype(BF16)
        par = jnp.where(place == column + (1 - core) * half, 1.0, 0.0).astype(BF16)
        out_refs[target][...] = (mxu(own, own_ref[...]) + mxu(par, par_ref[...])).astype(BF16)


def pick_rows(meta, own, par, images, ctxs):
    half, width = own.shape
    targets = 2 * ctxs
    return pl.pallas_call(
        functools.partial(pick_kernel, images, ctxs),
        grid_spec=pltpu.PrefetchScalarGridSpec(
            num_scalar_prefetch=1,
            grid=(1,),
            in_specs=[full(own.shape), full(par.shape)],
            out_specs=[full((IMG_TOK, width))] * targets,
        ),
        out_shape=[jax.ShapeDtypeStruct((IMG_TOK, width), BF16)] * targets,
        compiler_params=params(16),
        cost_estimate=cost(targets * 4 * IMG_TOK * half * width, 1 << 20),
        name="pick_rows",
    )(meta, own, par)


def merge_kernel(*refs):
    out_refs = refs[-2:]
    refs = refs[:-2]
    sides = refs[: len(refs) // 2], refs[len(refs) // 2 :]
    width = sides[0][0].shape[1]
    block = IMG_TOK // 2
    for side in range(2):
        total = sides[side][0][...].astype(F32)
        for part in sides[side][1:]:
            total = total + part[...].astype(F32)
        total = total.astype(BF16)
        for index in range(2):
            out_refs[index][:, side * width : (side + 1) * width] = total[index * block : (index + 1) * block]


def merge_picks(own_parts, par_parts):
    width = own_parts[0].shape[1]
    return pl.pallas_call(
        merge_kernel,
        out_shape=[jax.ShapeDtypeStruct((IMG_TOK // 2, 2 * width), BF16)] * 2,
        compiler_params=pltpu.CompilerParams(vmem_limit_bytes=8 << 20),
        cost_estimate=cost(1 << 20, 1 << 20),
        name="merge_picks",
    )(*own_parts, *par_parts)


def finish_kernel(core_ref, own_a, own_b, par_a, par_b, out_ref, sums, lines):
    core = core_ref[0]
    for side, (left, right) in enumerate(((own_a, own_b), (par_a, par_b))):
        sums[side] = left[...] + right[...]
    rows = sums.shape[1] // SIDE
    lanes = PATCH * CIN
    per = HD // lanes
    for side in range(2):
        for part in range(SIDE // per):
            cols = [sums[side, pl.ds(part * per + k, rows, stride=SIDE), :] for k in range(per)]
            for row in range(PATCH):
                pieces = [col[:, row * lanes : (row + 1) * lanes] for col in cols]
                lines[part, pl.ds(row, rows, stride=PATCH), :] = jnp.concatenate(pieces, axis=1)
        slot = jnp.bitwise_xor(core, side)
        for part in range(SIDE // per):
            out_ref[slot, :, part * HD : (part + 1) * HD] = lines[part]


def finish(core, own_a, own_b, par_a, par_b):
    count = own_a.shape[0]
    return pl.pallas_call(
        finish_kernel,
        grid_spec=pltpu.PrefetchScalarGridSpec(
            num_scalar_prefetch=1,
            grid=(1,),
            in_specs=[full(own_a.shape)] * 4,
            out_specs=full((2, count // PATCH, WL * CIN)),
            scratch_shapes=[
                pltpu.VMEM((2, count, PIX * CIN), F32),
                pltpu.VMEM((WL * CIN // HD, count // PATCH, HD), F32),
            ],
        ),
        out_shape=jax.ShapeDtypeStruct((2, count // PATCH, WL * CIN), F32),
        compiler_params=params(8),
        cost_estimate=cost(1 << 16, 1 << 18),
        name="finish",
    )(core, own_a, own_b, par_a, par_b)


def spread(active, spread_ref):
    row = lax.broadcasted_iota(jnp.int32, (IMG_TOK, PIX * CIN), 0)
    patch_row, patch_col = row >> 4, row & (SIDE - 1)
    total = None
    for index in range(9):
        down, right = index // 3 - 1, index % 3 - 1
        part = mxu(active, spread_ref[:, index * PIX * CIN : (index + 1) * PIX * CIN])
        offset = down * SIDE + right
        if offset:
            part = pltpu.roll(part, offset % IMG_TOK, 0)
        source_row, source_col = patch_row - down, patch_col - right
        inside = (source_row >= 0) & (source_row < SIDE) & (source_col >= 0) & (source_col < SIDE)
        part = jnp.where(inside, part, 0.0)
        total = part if total is None else total + part
    return total


def up_kernel(count, halves, first, last, *refs):
    refs = list(refs)
    x_refs = take_blocks(refs, count)
    weight_refs = [[[refs.pop(0) for _ in range(2)] for _ in range(halves)] for _ in range(count)]
    acc_in = None if first else refs.pop(0)
    spread_ref = refs.pop(0) if last else None
    out_ref = refs[0]
    width = x_refs[0][0].shape[1] // 2
    values = [load(pieces) for pieces in x_refs]
    totals = []
    for part in range(halves):
        total = None if first else acc_in[part]
        for block in range(count):
            for side in range(2):
                term = mxu(
                    values[block][:, side * width : (side + 1) * width],
                    weight_refs[block][part][side][0],
                )
                total = term if total is None else total + term
        totals.append(total)
        if not last:
            out_ref[part] = total
    if last:
        active = [silu(total).astype(BF16) for total in totals]
        active = jnp.concatenate(active, axis=1) if halves > 1 else active[0]
        out_ref[...] = spread(active, spread_ref)


def up_step(blocks, entries, weights, state, spread_weight):
    span = blocks[0][0].shape[1]
    halves, count = len(weights), len(blocks)
    first, last = state is None, spread_weight is not None
    whole = lambda shape: pl.BlockSpec(shape, lambda i: (0,) * len(shape))
    inputs = [p for pieces in blocks for p in pieces]
    specs = [whole(p.shape) for p in inputs]
    for entry in entries:
        for sides in weights:
            for weight in sides:
                inputs.append(weight)
                specs.append(pl.BlockSpec((1, span // 2, CH), lambda i, entry=entry: (entry, 0, 0)))
    if not first:
        inputs.append(state)
        specs.append(whole(state.shape))
    if last:
        inputs.append(spread_weight)
        specs.append(whole(spread_weight.shape))
        out = jax.ShapeDtypeStruct((IMG_TOK, PIX * CIN), F32)
    else:
        out = jax.ShapeDtypeStruct((halves, IMG_TOK, CH), F32)
    return pl.pallas_call(
        functools.partial(up_kernel, count, halves, first, last),
        grid=(1,),
        in_specs=specs,
        out_specs=whole(out.shape),
        out_shape=out,
        compiler_params=params(16),
        cost_estimate=cost(2 * count * IMG_TOK * span * CH * halves, (1 + count) << 20),
        name="up_last" if last else "up_step",
    )(*inputs)


def spread_weights(up_conv, pixels):
    taps = up_conv.reshape(9, CH, CIN).transpose(1, 0, 2).reshape(CH, 9 * CIN)
    shape = (pixels.shape[0], 9 * CIN, 9 * PIX * CIN)
    row = lax.broadcasted_iota(jnp.int32, shape, 1)
    col = lax.broadcasted_iota(jnp.int32, shape, 2)
    pixel = pixels[:, None, None]
    tap, channel = row >> 3, row & 7
    patch, target, out_channel = col >> 7, (col >> 3) & 15, col & 7
    tap_row, tap_col = tap // 3, tap % 3
    down, right = patch // 3 - 1, patch % 3 - 1
    hit = (
        (channel == out_channel)
        & ((pixel >> 2) + 1 - tap_row == (target >> 2) + PATCH * down)
        & ((pixel & 3) + 1 - tap_col == (target & 3) + PATCH * right)
    )
    placed = jnp.where(hit, 1.0, 0.0).astype(BF16)
    spread = jnp.einsum("ct,ptn->pcn", taps, placed, preferred_element_type=F32)
    return spread.astype(BF16).reshape(pixels.shape[0] * CH, 9 * PIX * CIN)


def by_core(core, own, other, axis):
    return jnp.where(
        core == 0, jnp.concatenate([own, other], axis), jnp.concatenate([other, own], axis)
    )


def shift(values, axis, step):
    count = lax.axis_size(axis)
    return lax.ppermute(values, axis, [(i, (i + step) % count) for i in range(count)])


def gather_small(latents, down_conv, *others):
    ctxs, tiles = lax.axis_size("ctx"), lax.axis_size("tile")
    every = jnp.concatenate([latents] + [shift(latents, "ctx", s) for s in range(1, ctxs)])
    conv = by_core(lax.axis_index("core"), down_conv, swap(down_conv), 1)
    conv = by_core(lax.axis_index("mpo"), conv, shift(conv, "mpo", 1), 1)
    every, conv, others = lax.optimization_barrier((every, conv, others))
    return [every] + [shift(every, "tile", s) for s in range(1, tiles)], conv, *others


def columns_kernel(meta, kept_in, sent_in, kept_out, sent_out):
    kept_out[0] = kept_in[...]
    sent_out[0] = sent_in[...]


def transpose_first(meta, patch_out, layout, ctxs):
    images, tiles, outer = layout
    width, features = patch_out.shape
    deep = features // (tiles * outer)
    halves = 2 if ctxs == 2 and deep == 2 * CH else 1
    size = deep // halves

    def place(other):
        def index(i, m):
            ctx, _, _, mpo = split_meta(m, images)
            chip = i * outer + lax.rem(mpo + other, outer)
            return 0, chip * halves + (ctx if halves == 2 else 0)

        return pl.BlockSpec((width, size), index)

    out = pl.BlockSpec((1, width, size), lambda i, m: (i, 0, 0))
    kept, sent = pl.pallas_call(
        columns_kernel,
        grid_spec=pltpu.PrefetchScalarGridSpec(
            num_scalar_prefetch=1, grid=(tiles,), in_specs=[place(0), place(1)], out_specs=[out, out]
        ),
        out_shape=[jax.ShapeDtypeStruct((tiles, width, size), BF16)] * 2,
        compiler_params=params(8),
        cost_estimate=cost(1 << 16, 2 << 20),
        name="columns",
    )(meta, patch_out, patch_out)
    return kept, sent, halves


def transpose_second(kept, received, step):
    tiles = lax.axis_size("tile")
    place = lax.rem(lax.axis_index("tile") + step, tiles)
    block = [lax.dynamic_index_in_dim(x, place, 0, keepdims=False) for x in (kept, received)]
    block = jnp.stack(block)
    return shift(block, "tile", step) if step else block


def gather_pair(first, second, state, step, extras=None):
    tiles = lax.axis_size("tile")
    found, moving = [{0: first}, {}], [None, None]

    def launch(which, index):
        ring = found[which][2 * index]
        if index < tiles - 1:
            moving[which] = (shift(ring, "tile", 1), shift(ring, "mpo", 1))
        elif which:
            moving[which] = shift(found[which][2 * index - 1], "tile", 1)
        else:
            moving[which] = shift(ring, "mpo", 1)

    def work(entries, state):
        return step([[found[0][e], found[1][e]] for e in entries], entries, state, False)

    launch(0, 0)
    late = callable(second)
    if late:
        events = [(0, 1), (0, 2)]
        for index in range(1, tiles - 2):
            events += [(1, index), (0, index + 2)]
        events += [(1, tiles - 2), (1, tiles - 1)]
    else:
        found[1][0] = second
        launch(1, 0)
        events = [(which, index) for index in range(1, tiles) for which in range(2)]
    seen = first
    for which, index in events:
        ring, cross = moving[which]
        if (which, index) == (int(late), tiles - 1):
            ring, cross, seen, state = lax.optimization_barrier((ring, cross, seen, state))
        elif late and (which, index) == (1, tiles - 2):
            ring, cross, seen, extras = lax.optimization_barrier((ring, cross, seen, extras))
        else:
            ring, cross, seen = lax.optimization_barrier((ring, cross, seen))
        found[which][2 * index], found[which][2 * index - 1] = ring, cross
        seen = ring
        launch(which, index)
        if late and (which, index) == (0, 1):
            found[1][0], extras = second(cross)
            launch(1, 0)
        if (which, index) == (1, tiles - 2):
            state = work(list(range(2 * tiles - 3)), state)
    state = work([2 * tiles - 2, 2 * tiles - 3], state)
    last = lax.optimization_barrier((moving[0], moving[1], state, extras))
    return step([[last[0], last[1]]], [2 * tiles - 1], last[2], True), last[3]


def shards(
    text_embed,
    latents,
    down_conv,
    patch_in,
    norm_gain,
    query_weight,
    key_weight,
    value_weight,
    query_gain,
    key_gain,
    out_weight,
    patch_out,
    up_conv,
    span_start,
    image_of_slot,
):
    ctxs, tiles, outer = (lax.axis_size(name) for name in ("ctx", "tile", "mpo"))
    ctx, tile, mpo, core = (lax.axis_index(name) for name in ("ctx", "tile", "mpo", "core"))
    seq_rows, width = text_embed.shape
    half = seq_rows // 2
    heads = width // HD
    images = span_start.shape[0]
    local = latents.shape[0]

    numbers = jnp.arange(images, dtype=jnp.int32)
    matches = image_of_slot[None, :] == numbers[:, None]
    slot_of_image = jnp.sum(jnp.where(matches, numbers[None, :], 0), axis=1)
    slot_place = lax.rem(ctx + ctxs - slot_of_image // local, ctxs) * local + slot_of_image % local
    meta = jnp.concatenate(
        [span_start, slot_place, image_of_slot, jnp.stack([ctx, core, tile, mpo])]
    ).astype(jnp.int32)
    layout = (images, tiles, outer)

    weights = [swap(w) for w in (key_weight, value_weight, query_weight)]
    pieces, conv, meta, weights[0], weights[1] = gather_small(latents, down_conv, meta, *weights[:2])
    later, pieces[1] = lax.optimization_barrier((meta, pieces[1]))
    kept, sent, halves = transpose_first(later, patch_out, layout, ctxs)
    pieces, sent = lax.optimization_barrier((pieces, sent))
    received = shift(sent, "mpo", 1)
    weights += [key_weight, value_weight, query_weight]
    streams = down_stream(meta, pieces, conv, patch_in, text_embed, norm_gain, weights, images)
    streams, held_weights = streams[:2], streams[2:]
    streams, received = lax.optimization_barrier((streams, received))
    others = [swap(s[1]) for s in streams]
    others = lax.optimization_barrier(others)

    head_gains = jnp.stack([query_gain, key_gain])

    def project(blocks, entries, state, last):
        held = state is None
        return qkv_step(
            meta, layout, blocks, entries, held_weights if held else weights, held, state, head_gains if last else None
        )

    state, out_par = gather_pair(
        *[by_core(core, s[0], o, 1) for s, o in zip(streams, others)], None, project, swap(out_weight)
    )
    state, kept, received = lax.optimization_barrier((state, kept, received))
    up_blocks = [transpose_second(kept, received, step) for step in range(tiles)]
    kv_send, q_send = state[:heads], state[heads : 2 * heads]
    kv_own, q_own = state[2 * heads : 3 * heads], state[3 * heads :]

    def shifted(values, step, cross):
        pairs = [
            (2 * c + k, 2 * ((c + step) % ctxs) + (1 - k if cross else k))
            for c in range(ctxs)
            for k in range(2)
        ]
        return lax.ppermute(values, ("ctx", "core"), pairs)

    def pieces_of(head):
        pieces = [swap(q_send[head]), kv_own[head], swap(kv_send[head])]
        for step in range(1, ctxs):
            pieces += [shifted(kv_own[head], step, False), shifted(kv_send[head], step, True)]
        return pieces

    def attend(head, pieces, ahead):
        result = attention(meta, [q_own[head], pieces[0]], pieces[1:], images)
        (att_own, att_send), ahead = lax.optimization_barrier((result, ahead))
        return by_core(core, att_own, swap(att_send), 1), ahead

    attended, (pieces, up_blocks) = attend(
        0, pieces_of(0), (pieces_of(1) if heads > 1 else None, up_blocks)
    )
    if heads == 1:
        attended, second = attended[: half // 2], attended[half // 2 :]
        own = jnp.concatenate(up_blocks)
        extras = [own, swap(own)] + ([shift(own, "ctx", 1)] if halves == 2 else [])
    else:
        extras = None

        def second(token):
            result, (up, _) = attend(1, pieces, (up_blocks, token))
            own = jnp.concatenate(up)
            result, own, par = lax.optimization_barrier((result, own, swap(own)))
            return result, [own, par] + ([shift(own, "ctx", 1)] if halves == 2 else [])

    def project_out(blocks, entries, state, last):
        return out_step(meta, layout, blocks, entries, (out_weight, out_par), state, last)

    state = [jnp.stack([s[0], o]) for s, o in zip(streams, others)]
    state, up_weights = gather_pair(attended, second, state, project_out, extras)
    out_own, out_send = state
    out_other = swap(out_send)
    layer_out = by_core(core, out_own, out_other, 0)

    picks, swapped = lax.optimization_barrier(
        (pick_rows(meta, out_own, out_other, images, ctxs), [swap(other) for other in up_weights[2:]])
    )
    up_weights = [up_weights[:2]] + [[up_weights[2], other] for other in swapped]
    own_parts, par_parts = [picks[0]], [swap(picks[1])]
    for step in range(1, ctxs):
        own_parts.append(shifted(picks[2 * step], step, False))
        par_parts.append(shifted(picks[2 * step + 1], step, True))

    pixel = tile * outer + mpo
    pixels = jnp.stack([pixel * halves + lax.rem(ctx + h, halves) for h in range(halves)])
    spread_weight = spread_weights(up_conv, pixels)

    def project_up(blocks, entries, state, last):
        return up_step(blocks, entries, up_weights, state, spread_weight if last else None)

    state, _ = gather_pair(*merge_picks(own_parts, par_parts), None, project_up)

    bands = state.reshape(tiles, IMG_TOK // tiles, PIX * CIN)
    band = lax.dynamic_index_in_dim(bands, tile, 0, keepdims=False)
    for step in range(1, tiles):
        piece = lax.dynamic_index_in_dim(bands, lax.rem(tile + step, tiles), 0, keepdims=False)
        band = band + shift(piece, "tile", step)
    quad = {}
    for name, pairs in (
        ("mpo", [(0, 2), (1, 3), (2, 0), (3, 1)]),
        ("core", [(0, 1), (1, 0), (2, 3), (3, 2)]),
        ("both", [(0, 3), (1, 2), (2, 1), (3, 0)]),
    ):
        quad[name] = lax.ppermute(band, ("mpo", "core"), pairs)
    return layer_out, finish(meta[3 * images + 1 :], band, quad["mpo"], quad["core"], quad["both"])


def solution(mesh):
    ctxs, tiles, parts = mesh.devices.shape
    fine = Mesh(
        mesh.devices.reshape(ctxs, tiles, parts // 2, 2), ("ctx", "tile", "mpo", "core")
    )
    features = ("tile", "mpo", "core")
    return jax.shard_map(
        shards,
        mesh=fine,
        in_specs=(
            P("ctx", features),
            P("ctx", "tile", None),
            P(None, ("mpo", "core")),
            P(None, features),
            P(features),
            P(None, features),
            P(None, features),
            P(None, features),
            P(),
            P(),
            P(None, features),
            P(features, None),
            P(),
            P(),
            P(),
        ),
        out_specs=(P("ctx", features), P("ctx", "tile", None)),
        check_vma=False,
    )
```

```python
import functools

import jax
import jax.numpy as jnp
from jax import lax
from jax.experimental import pallas as pl
from jax.experimental.pallas import tpu as pltpu
from jax.sharding import Mesh
from jax.sharding import PartitionSpec as P

HD = 128
CH = 256
CIN = 8
WL = 64
HL = 64
PATCH = 4
PIX = PATCH * PATCH
SIDE = WL // PATCH
IMG_TOK = 256
EPSILON = 1e-05
NEGATIVE_FILL = -1e30
WINDOW = (PATCH + 2) * CIN
TAPS = 3 * WINDOW
BF16 = jnp.bfloat16
F32 = jnp.float32


def split_meta(meta, images):
    return meta[3 * images], meta[3 * images + 1], meta[3 * images + 2], meta[3 * images + 3]


def params(mebibytes):
    return pltpu.CompilerParams(
        dimension_semantics=("arbitrary",), vmem_limit_bytes=mebibytes * 1024 * 1024
    )


def cost(flops, nbytes, transcendentals=0):
    return pl.CostEstimate(
        flops=int(flops), bytes_accessed=int(nbytes), transcendentals=int(transcendentals)
    )


def silu(values):
    half = values * 0.5
    return half + half * jnp.tanh(half)


def mxu(left, right):
    return jnp.dot(left, right, preferred_element_type=F32)


def swap(values):
    return lax.ppermute(values, "core", [(0, 1), (1, 0)])


HELD = pl.BlockSpec(memory_space=pltpu.VMEM)


GAIN_ROWS = 16
TOP = 16


def down_kernel(images, tiles, half, meta, *refs):
    lat_refs, refs = refs[:tiles], refs[tiles:]
    conv_ref, patch_ref, own_text, par_text, gain_ref = refs[:5]
    weight_refs, (first_ref, second_ref), held_refs = refs[5:11], refs[11:13], refs[13:19]
    grid_rows, conv_wide, conv_bf16, windows, total, arrived = refs[19:]
    step = pl.program_id(0)
    copies = [
        pltpu.make_async_copy(weight, held, arrived.at[index])
        for index, (weight, held) in enumerate(zip(weight_refs, held_refs))
    ]

    @pl.when(step == 0)
    def _():
        for copy in copies:
            copy.start()

    group = images * SIDE
    ctx, core, tile, _ = split_meta(meta, images)

    @pl.when(step == 0)
    def _():
        grid_rows[...] = jnp.zeros_like(grid_rows)
        blocks = grid_rows.shape[1]
        for index in range(tiles):
            band = lat_refs[index].shape[1]
            at = TOP + lax.rem(tile + tiles - index, tiles) * band
            rows = pl.ds(pl.multiple_of(at, 8), band)
            latent = lat_refs[index][...].astype(F32)
            edges = [jnp.zeros((images, band, size), F32) for size in (CIN, HD - CIN)]
            wide = jnp.concatenate([edges[0], latent, edges[1]], axis=2)
            for part in range(blocks):
                grid_rows[:, part, rows, :] = wide[:, :, part * HD : (part + 1) * HD]
        conv_wide[...] = jnp.zeros_like(conv_wide)
        conv = conv_ref[...].astype(F32)
        for col in range(PATCH):
            for tap in range(3):
                at = WINDOW * tap + CIN * col
                conv_wide[at : at + 3 * CIN, CH * col : CH * (col + 1)] = conv[
                    3 * CIN * tap : 3 * CIN * (tap + 1), :
                ]
        conv_bf16[...] = conv_wide[...].astype(BF16)

        def build(image, carry):
            for row in range(PATCH + 2):
                take = pl.ds(TOP - 1 + row, SIDE, stride=PATCH)
                line = [grid_rows[image, part, take, :] for part in range(blocks)]
                line = jnp.concatenate(line, axis=1).astype(BF16)
                for col in range(SIDE):
                    piece = line[:, PATCH * CIN * col : PATCH * CIN * col + WINDOW]
                    at = pl.ds(pl.multiple_of(group * col + image * SIDE, SIDE), SIDE)
                    for shift in range(3):
                        if 0 <= row - shift < PATCH:
                            windows[row - shift, at, WINDOW * shift : WINDOW * (shift + 1)] = piece
            return carry

        lax.fori_loop(0, images, build, 0)
        total[...] = jnp.zeros_like(total)

    chunk = 256
    for part in range(images * IMG_TOK // chunk):
        rows = slice(part * chunk, (part + 1) * chunk)
        hidden = silu(mxu(windows[step, rows, :], conv_bf16[...])).astype(BF16)
        total[rows, :] += mxu(hidden, patch_ref[...])

    @pl.when(step == PATCH - 1)
    def _():
        tokens = total[...].astype(BF16)
        block = half // 2
        for side, text_ref in enumerate((own_text, par_text)):
            base = ctx * (2 * half) + jnp.bitwise_xor(core, side) * half
            for part, out_ref in enumerate((first_ref, second_ref)):
                place = base + part * block + lax.broadcasted_iota(jnp.int32, (block, 1), 0)
                source = jnp.full((block, 1), -1, jnp.int32)
                for image in range(images):
                    inner = place - meta[image]
                    inside = (inner >= 0) & (inner < IMG_TOK)
                    index = (inner & (SIDE - 1)) * group + meta[images + image] * SIDE + (inner >> 4)
                    source = jnp.where(inside, index, source)
                choice = source == lax.broadcasted_iota(jnp.int32, (block, images * IMG_TOK), 1)
                picked = mxu(jnp.where(choice, 1.0, 0.0).astype(BF16), tokens)
                text = text_ref[0, part * block : (part + 1) * block, :].astype(F32)
                out_ref[side, :block, :] = jnp.where(source >= 0, picked, text).astype(BF16)
            gain = gain_ref[...].astype(F32)
            first_ref[side, block:, :] = jnp.broadcast_to(gain, (GAIN_ROWS, gain.shape[1])).astype(BF16)
        for copy in copies:
            copy.wait()


def down_stream(meta, pieces, conv, patch_in, text, gain, weights, images):
    seq_rows, width = text.shape
    half = seq_rows // 2
    tiles = len(pieces)
    count = images * IMG_TOK
    halves = text.reshape(2, half, width)
    core_at = 3 * images + 1
    first, second = (2, half // 2 + GAIN_ROWS, width), (2, half // 2, width)
    return pl.pallas_call(
        functools.partial(down_kernel, images, tiles, half),
        grid_spec=pltpu.PrefetchScalarGridSpec(
            num_scalar_prefetch=1,
            grid=(PATCH,),
            in_specs=[full(p.shape) for p in pieces]
            + [
                full(conv.shape),
                pl.BlockSpec((PATCH * CH, width), lambda i, m: (i, 0)),
                pl.BlockSpec((1, half, width), lambda i, m: (m[core_at], 0, 0)),
                pl.BlockSpec((1, half, width), lambda i, m: (1 - m[core_at], 0, 0)),
                full((1, width)),
            ]
            + [pl.BlockSpec(memory_space=pl.ANY)] * 6,
            out_specs=[full(first), full(second)] + [HELD] * 6,
            scratch_shapes=[
                pltpu.VMEM((images, WL * CIN // HD + 1, TOP + HL + 16, HD), F32),
                pltpu.VMEM((TAPS, PATCH * CH), F32),
                pltpu.VMEM((TAPS, PATCH * CH), BF16),
                pltpu.VMEM((PATCH, count, TAPS), BF16),
                pltpu.VMEM((count, width), F32),
                pltpu.SemaphoreType.DMA((6,)),
            ],
        ),
        out_shape=[jax.ShapeDtypeStruct(first, BF16), jax.ShapeDtypeStruct(second, BF16)]
        + [pltpu.VMEM(w.shape, w.dtype) for w in weights],
        compiler_params=params(32),
        cost_estimate=cost(2 * count * PIX * CH * (256 + width), 4 << 20, count * PIX * CH),
        name="down_stream",
    )(meta, *pieces, conv, patch_in, halves, halves, gain.reshape(1, width), *weights)


def full(shape):
    return pl.BlockSpec(shape, lambda i, m: (0,) * len(shape))


def load(pieces):
    return jnp.concatenate([piece[...] for piece in pieces], axis=0)


def take_blocks(refs, count):
    return [[refs.pop(0), refs.pop(0)] for _ in range(count)]


def chip_of(meta, images, tiles, outer, entry):
    _, _, tile, mpo = split_meta(meta, images)
    return lax.rem(tile + tiles - entry // 2, tiles) * outer + lax.rem(mpo + entry % 2, outer)


def qkv_kernel(entries, layout, groups, last, meta, *refs):
    refs = list(refs)
    count = len(entries)
    x_refs = take_blocks(refs, count)
    weight_refs = [refs.pop(0) for _ in range(6)]
    if last:
        acc_in, square_in, head_gains = refs.pop(0), refs.pop(0), refs.pop(0)
        fetched, arrived = refs.pop(-3), refs.pop(-2)
        span = fetched.shape[1]
        rows = pl.ds(pl.multiple_of(chip_of(meta, *layout, entries[0]) * span, span), span)
        copies = [
            pltpu.make_async_copy(weight.at[rows, :], fetched.at[part], arrived.at[part])
            for part, weight in enumerate(weight_refs)
        ]
        for copy in copies:
            copy.start()
    scaled_ref = refs.pop(-1)
    half, span = scaled_ref.shape
    width = weight_refs[0].shape[1]
    heads = width // HD
    square = square_in[...] if last else None
    if last:
        acc, outs = [None] * 6, refs
    else:
        acc_out, square_out = refs
    for index in range(count):
        rows = pl.ds(pl.multiple_of(chip_of(meta, *layout, entries[index]) * span, span), span)
        gain = x_refs[index][0][half // 2 :, :][:1]
        for part in range(2):
            at = slice(part * half // 2, (part + 1) * half // 2)
            scaled_ref[at, :] = (x_refs[index][part][: half // 2, :] * gain).astype(BF16)
        value = jnp.concatenate([x_refs[index][0][: half // 2, :], x_refs[index][1][...]], axis=0)
        value = value.astype(F32)
        value = value * value
        for part in range(span // HD):
            piece = value[:, part * HD : (part + 1) * HD]
            square = piece if square is None else square + piece
        for part in range(6):
            if last:
                copies[part].wait()
                acc[part] = acc_in[part] + mxu(scaled_ref[...], fetched[part])
                continue
            term = mxu(scaled_ref[...], weight_refs[part][rows, :])
            if index == 0:
                acc_out[part] = term
            else:
                acc_out[part] += term
    if not last:
        square_out[...] = square
        return
    mean = jnp.sum(square, axis=-1, keepdims=True) * (1.0 / (groups * span))
    scale = lax.rsqrt(mean + EPSILON)
    for part in range(6):
        total = acc[part] * scale
        side, kind = part // 3, part % 3
        kv_outs = outs[2 * heads * side : 2 * heads * side + heads]
        q_outs = outs[2 * heads * side + heads : 2 * heads * side + 2 * heads]
        for head in range(heads):
            raw = total[:, head * HD : (head + 1) * HD]
            if kind == 1:
                kv_outs[head][1] = raw.astype(BF16)
                continue
            raw = raw * lax.rsqrt(jnp.mean(raw * raw, axis=-1, keepdims=True) + EPSILON)
            if kind == 0:
                kv_outs[head][0] = (raw * head_gains[1:2, :]).astype(BF16)
            else:
                q_outs[head][...] = (raw * (head_gains[0:1, :] * HD ** (-0.5))).astype(BF16)


def qkv_step(meta, layout, blocks, entries, weights, state, head_gains):
    span = blocks[0][1].shape[1]
    half = 2 * blocks[0][1].shape[0]
    width = weights[0].shape[1]
    heads = width // HD
    count, last = len(blocks), state is not None
    groups = layout[1] * layout[2]
    inputs = [p for pieces in blocks for p in pieces] + list(weights)
    specs = [full(p.shape) for pieces in blocks for p in pieces]
    scratch = [pltpu.VMEM((half, span), BF16)]
    if last:
        specs += [pl.BlockSpec(memory_space=pltpu.HBM)] * 6 + [HELD] * 2 + [full(head_gains.shape)]
        inputs += list(state) + [head_gains]
        kv, q = jax.ShapeDtypeStruct((2, half, HD), BF16), jax.ShapeDtypeStruct((half, HD), BF16)
        outs = ([kv] * heads + [q] * heads) * 2
        scratch = [pltpu.VMEM((6, span, width), BF16), pltpu.SemaphoreType.DMA((6,))] + scratch
    else:
        specs += [HELD] * 6
        outs = [pltpu.VMEM((6, half, width), F32), pltpu.VMEM((half, HD), F32)]
    return pl.pallas_call(
        functools.partial(qkv_kernel, entries, layout, groups, last),
        grid_spec=pltpu.PrefetchScalarGridSpec(
            num_scalar_prefetch=1,
            grid=(1,),
            in_specs=specs,
            out_specs=[full(o.shape) if last else HELD for o in outs],
            scratch_shapes=scratch,
        ),
        out_shape=outs,
        compiler_params=params(20),
        cost_estimate=cost(12 * count * half * span * width, (6 + 2 * count) << 20),
        name="qkv_last" if last else "qkv_step",
    )(meta, *inputs)


def attention_kernel(images, pieces, half, meta, *refs):
    ctx, core, _, _ = split_meta(meta, images)
    ctxs = pieces // 2
    bases = []
    for piece in range(pieces):
        side = jnp.bitwise_xor(core, piece % 2)
        bases.append(lax.rem(ctx + ctxs - piece // 2, ctxs) * (2 * half) + side * half)
    q_refs, kv_refs, out_refs = refs[:2], refs[2 : 2 + pieces], refs[2 + pieces :]
    rows = q_refs[0].shape[0]
    step = pl.program_id(0)
    for side in range(2):
        place = bases[side] + step * rows + lax.broadcasted_iota(jnp.int32, (rows, 1), 0)
        limit = place
        for image in range(images):
            inner = place - meta[image]
            limit = jnp.where((inner >= 0) & (inner < IMG_TOK), meta[image] + IMG_TOK - 1, limit)
        query = q_refs[side][...]
        scores = []
        top = None
        for piece in range(pieces):
            score = lax.dot_general(
                query, kv_refs[piece][0], (((1,), (1,)), ((), ())), preferred_element_type=F32
            )
            position = lax.broadcasted_iota(jnp.int32, score.shape, 1)
            score = jnp.where(position <= limit - bases[piece], score, NEGATIVE_FILL)
            scores.append(score)
            best = jnp.max(score, axis=1, keepdims=True)
            top = best if top is None else jnp.maximum(top, best)
        total = jnp.zeros((rows, 1), F32)
        product = jnp.zeros((rows, HD), F32)
        for piece in range(pieces):
            weight = jnp.exp(scores[piece] - top)
            total = total + jnp.sum(weight, axis=1, keepdims=True)
            product = product + mxu(weight.astype(BF16), kv_refs[piece][1])
        out_refs[side][...] = (product / total).astype(BF16)


def attention(meta, queries, pieces, images):
    half = queries[0].shape[0]
    block = 256
    keys = half * len(pieces)
    rows = pl.BlockSpec((block, HD), lambda i, m: (i, 0))
    return pl.pallas_call(
        functools.partial(attention_kernel, images, len(pieces), half),
        grid_spec=pltpu.PrefetchScalarGridSpec(
            num_scalar_prefetch=1,
            grid=(half // block,),
            in_specs=[rows, rows] + [full(p.shape) for p in pieces],
            out_specs=[rows, rows],
        ),
        out_shape=[jax.ShapeDtypeStruct((half, HD), BF16)] * 2,
        compiler_params=params(24),
        cost_estimate=cost(8 * half * keys * HD, 4 * keys * HD, 2 * half * keys),
        name="attention",
    )(meta, *queries, *pieces)


def out_kernel(count, heads, first, last, meta, *refs):
    refs = list(refs)
    x_refs = take_blocks(refs, count)
    weight_refs = [[refs.pop(0), refs.pop(0)] for _ in range(count)]
    if first:
        streams = [refs.pop(0), refs.pop(0)]
        block = streams[1].shape[1]
    else:
        acc_in = refs.pop(0)
    outs = refs
    for side in range(2):
        if first:
            rows = [streams[0][side, :block, :], streams[1][side]]
            total = jnp.concatenate(rows, axis=0).astype(F32)
        else:
            total = acc_in[side]
        for index in range(count):
            weight = weight_refs[index][side]
            if heads == 2:
                for head in range(heads):
                    part = weight[0, :, head].reshape(2 * HD, weight.shape[4])
                    total = total + mxu(x_refs[index][head][...], part)
            else:
                total = total + mxu(load(x_refs[index]), weight[0, :, 0].reshape(2 * HD, weight.shape[4]))
        if last:
            outs[side][...] = total.astype(BF16)
        else:
            outs[0][side] = total


def out_step(meta, layout, blocks, entries, weights, state, last):
    width = weights[0].shape[1]
    heads = width // HD
    half = blocks[0][0].shape[0] * (1 if heads == 2 else 2)
    first = isinstance(state, list)
    count = len(blocks)
    views = [w.reshape(-1, 2, heads, HD, width) for w in weights]
    inputs = [p for pieces in blocks for p in pieces]
    specs = [full(p.shape) for p in inputs]
    for entry in entries:
        for view in views:
            inputs.append(view)
            specs.append(
                pl.BlockSpec(
                    (1, 2, heads, HD, width),
                    lambda i, m, entry=entry: (chip_of(m, *layout, entry), 0, 0, 0, 0),
                )
            )
    states = state if first else [state]
    inputs += states
    specs += [full(s.shape) for s in states]
    if last:
        outs = [jax.ShapeDtypeStruct((half, width), BF16)] * 2
    else:
        outs = [jax.ShapeDtypeStruct((2, half, width), F32)]
    result = pl.pallas_call(
        functools.partial(out_kernel, count, heads, first, last),
        grid_spec=pltpu.PrefetchScalarGridSpec(
            num_scalar_prefetch=1,
            grid=(1,),
            in_specs=specs,
            out_specs=[full(o.shape) for o in outs],
        ),
        out_shape=outs,
        compiler_params=params(24),
        cost_estimate=cost(8 * count * half * heads * HD * width, (2 + count) << 20),
        name="out_last" if last else "out_step",
    )(meta, *inputs)
    return result if last else result[0]


def pick_kernel(images, ctxs, meta, own_ref, par_ref, *out_refs):
    half = own_ref.shape[0]
    ctx, core, _, _ = split_meta(meta, images)
    for target in range(2 * ctxs):
        to_core = jnp.bitwise_xor(core, target % 2)
        slot = 2 * lax.rem(ctx + target // 2, ctxs) + to_core
        start = meta[meta[2 * images + slot]]
        place = start + lax.broadcasted_iota(jnp.int32, (IMG_TOK, half), 0)
        column = ctx * (2 * half) + lax.broadcasted_iota(jnp.int32, (IMG_TOK, half), 1)
        own = jnp.where(place == column + core * half, 1.0, 0.0).astype(BF16)
        par = jnp.where(place == column + (1 - core) * half, 1.0, 0.0).astype(BF16)
        out_refs[target][...] = (mxu(own, own_ref[...]) + mxu(par, par_ref[...])).astype(BF16)


def pick_rows(meta, own, par, images, ctxs):
    half, width = own.shape
    targets = 2 * ctxs
    return pl.pallas_call(
        functools.partial(pick_kernel, images, ctxs),
        grid_spec=pltpu.PrefetchScalarGridSpec(
            num_scalar_prefetch=1,
            grid=(1,),
            in_specs=[full(own.shape), full(par.shape)],
            out_specs=[full((IMG_TOK, width))] * targets,
        ),
        out_shape=[jax.ShapeDtypeStruct((IMG_TOK, width), BF16)] * targets,
        compiler_params=params(16),
        cost_estimate=cost(targets * 4 * IMG_TOK * half * width, 1 << 20),
        name="pick_rows",
    )(meta, own, par)


def merge_kernel(*refs):
    out_refs = refs[-2:]
    refs = refs[:-2]
    sides = refs[: len(refs) // 2], refs[len(refs) // 2 :]
    width = sides[0][0].shape[1]
    block = IMG_TOK // 2
    for side in range(2):
        total = sides[side][0][...].astype(F32)
        for part in sides[side][1:]:
            total = total + part[...].astype(F32)
        total = total.astype(BF16)
        for index in range(2):
            out_refs[index][:, side * width : (side + 1) * width] = total[index * block : (index + 1) * block]


def merge_picks(own_parts, par_parts):
    width = own_parts[0].shape[1]
    return pl.pallas_call(
        merge_kernel,
        out_shape=[jax.ShapeDtypeStruct((IMG_TOK // 2, 2 * width), BF16)] * 2,
        compiler_params=pltpu.CompilerParams(vmem_limit_bytes=8 << 20),
        cost_estimate=cost(1 << 20, 1 << 20),
        name="merge_picks",
    )(*own_parts, *par_parts)


def finish_kernel(core_ref, own_a, own_b, par_a, par_b, out_ref, sums, lines):
    core = core_ref[0]
    for side, (left, right) in enumerate(((own_a, own_b), (par_a, par_b))):
        sums[side] = left[...] + right[...]
    rows = sums.shape[1] // SIDE
    lanes = PATCH * CIN
    per = HD // lanes
    for side in range(2):
        for part in range(SIDE // per):
            cols = [sums[side, pl.ds(part * per + k, rows, stride=SIDE), :] for k in range(per)]
            for row in range(PATCH):
                pieces = [col[:, row * lanes : (row + 1) * lanes] for col in cols]
                lines[part, pl.ds(row, rows, stride=PATCH), :] = jnp.concatenate(pieces, axis=1)
        slot = jnp.bitwise_xor(core, side)
        for part in range(SIDE // per):
            out_ref[slot, :, part * HD : (part + 1) * HD] = lines[part]


def finish(core, own_a, own_b, par_a, par_b):
    count = own_a.shape[0]
    return pl.pallas_call(
        finish_kernel,
        grid_spec=pltpu.PrefetchScalarGridSpec(
            num_scalar_prefetch=1,
            grid=(1,),
            in_specs=[full(own_a.shape)] * 4,
            out_specs=full((2, count // PATCH, WL * CIN)),
            scratch_shapes=[
                pltpu.VMEM((2, count, PIX * CIN), F32),
                pltpu.VMEM((WL * CIN // HD, count // PATCH, HD), F32),
            ],
        ),
        out_shape=jax.ShapeDtypeStruct((2, count // PATCH, WL * CIN), F32),
        compiler_params=params(8),
        cost_estimate=cost(1 << 16, 1 << 18),
        name="finish",
    )(core, own_a, own_b, par_a, par_b)


def spread(active, spread_ref):
    row = lax.broadcasted_iota(jnp.int32, (IMG_TOK, PIX * CIN), 0)
    patch_row, patch_col = row >> 4, row & (SIDE - 1)
    total = None
    for index in range(9):
        down, right = index // 3 - 1, index % 3 - 1
        part = mxu(active, spread_ref[:, index * PIX * CIN : (index + 1) * PIX * CIN])
        offset = down * SIDE + right
        if offset:
            part = pltpu.roll(part, offset % IMG_TOK, 0)
        source_row, source_col = patch_row - down, patch_col - right
        inside = (source_row >= 0) & (source_row < SIDE) & (source_col >= 0) & (source_col < SIDE)
        part = jnp.where(inside, part, 0.0)
        total = part if total is None else total + part
    return total


def up_kernel(count, halves, first, last, *refs):
    refs = list(refs)
    x_refs = take_blocks(refs, count)
    weight_refs = [[[refs.pop(0) for _ in range(2)] for _ in range(halves)] for _ in range(count)]
    acc_in = None if first else refs.pop(0)
    spread_ref = refs.pop(0) if last else None
    out_ref = refs[0]
    width = x_refs[0][0].shape[1] // 2
    values = [load(pieces) for pieces in x_refs]
    totals = []
    for part in range(halves):
        total = None if first else acc_in[part]
        for block in range(count):
            for side in range(2):
                term = mxu(
                    values[block][:, side * width : (side + 1) * width],
                    weight_refs[block][part][side][0],
                )
                total = term if total is None else total + term
        totals.append(total)
        if not last:
            out_ref[part] = total
    if last:
        active = [silu(total).astype(BF16) for total in totals]
        active = jnp.concatenate(active, axis=1) if halves > 1 else active[0]
        out_ref[...] = spread(active, spread_ref)


def up_step(blocks, entries, weights, state, spread_weight):
    span = blocks[0][0].shape[1]
    halves, count = len(weights), len(blocks)
    first, last = state is None, spread_weight is not None
    whole = lambda shape: pl.BlockSpec(shape, lambda i: (0,) * len(shape))
    inputs = [p for pieces in blocks for p in pieces]
    specs = [whole(p.shape) for p in inputs]
    for entry in entries:
        for sides in weights:
            for weight in sides:
                inputs.append(weight)
                specs.append(pl.BlockSpec((1, span // 2, CH), lambda i, entry=entry: (entry, 0, 0)))
    if not first:
        inputs.append(state)
        specs.append(whole(state.shape))
    if last:
        inputs.append(spread_weight)
        specs.append(whole(spread_weight.shape))
        out = jax.ShapeDtypeStruct((IMG_TOK, PIX * CIN), F32)
    else:
        out = jax.ShapeDtypeStruct((halves, IMG_TOK, CH), F32)
    return pl.pallas_call(
        functools.partial(up_kernel, count, halves, first, last),
        grid=(1,),
        in_specs=specs,
        out_specs=whole(out.shape),
        out_shape=out,
        compiler_params=params(16),
        cost_estimate=cost(2 * count * IMG_TOK * span * CH * halves, (1 + count) << 20),
        name="up_last" if last else "up_step",
    )(*inputs)


def spread_weights(up_conv, pixels):
    taps = up_conv.reshape(9, CH, CIN).transpose(1, 0, 2).reshape(CH, 9 * CIN)
    shape = (pixels.shape[0], 9 * CIN, 9 * PIX * CIN)
    row = lax.broadcasted_iota(jnp.int32, shape, 1)
    col = lax.broadcasted_iota(jnp.int32, shape, 2)
    pixel = pixels[:, None, None]
    tap, channel = row >> 3, row & 7
    patch, target, out_channel = col >> 7, (col >> 3) & 15, col & 7
    tap_row, tap_col = tap // 3, tap % 3
    down, right = patch // 3 - 1, patch % 3 - 1
    hit = (
        (channel == out_channel)
        & ((pixel >> 2) + 1 - tap_row == (target >> 2) + PATCH * down)
        & ((pixel & 3) + 1 - tap_col == (target & 3) + PATCH * right)
    )
    placed = jnp.where(hit, 1.0, 0.0).astype(BF16)
    spread = jnp.einsum("ct,ptn->pcn", taps, placed, preferred_element_type=F32)
    return spread.astype(BF16).reshape(pixels.shape[0] * CH, 9 * PIX * CIN)


def by_core(core, own, other, axis):
    return jnp.where(
        core == 0, jnp.concatenate([own, other], axis), jnp.concatenate([other, own], axis)
    )


def shift(values, axis, step):
    count = lax.axis_size(axis)
    return lax.ppermute(values, axis, [(i, (i + step) % count) for i in range(count)])


def gather_small(latents, down_conv, *others):
    ctxs, tiles = lax.axis_size("ctx"), lax.axis_size("tile")
    every = jnp.concatenate([latents] + [shift(latents, "ctx", s) for s in range(1, ctxs)])
    conv = by_core(lax.axis_index("core"), down_conv, swap(down_conv), 1)
    conv = by_core(lax.axis_index("mpo"), conv, shift(conv, "mpo", 1), 1)
    every, others = lax.optimization_barrier((every, others))
    return [every] + [shift(every, "tile", s) for s in range(1, tiles)], conv, *others


def columns_kernel(meta, kept_in, sent_in, kept_out, sent_out):
    kept_out[0] = kept_in[...]
    sent_out[0] = sent_in[...]


def transpose_first(meta, patch_out, layout, ctxs):
    images, tiles, outer = layout
    width, features = patch_out.shape
    deep = features // (tiles * outer)
    halves = 2 if ctxs == 2 and deep == 2 * CH else 1
    size = deep // halves

    def place(other):
        def index(i, m):
            ctx, _, _, mpo = split_meta(m, images)
            chip = i * outer + lax.rem(mpo + other, outer)
            return 0, chip * halves + (ctx if halves == 2 else 0)

        return pl.BlockSpec((width, size), index)

    out = pl.BlockSpec((1, width, size), lambda i, m: (i, 0, 0))
    kept, sent = pl.pallas_call(
        columns_kernel,
        grid_spec=pltpu.PrefetchScalarGridSpec(
            num_scalar_prefetch=1, grid=(tiles,), in_specs=[place(0), place(1)], out_specs=[out, out]
        ),
        out_shape=[jax.ShapeDtypeStruct((tiles, width, size), BF16)] * 2,
        compiler_params=params(8),
        cost_estimate=cost(1 << 16, 2 << 20),
        name="columns",
    )(meta, patch_out, patch_out)
    return kept, sent, halves


def transpose_second(kept, received, step):
    tiles = lax.axis_size("tile")
    place = lax.rem(lax.axis_index("tile") + step, tiles)
    block = [lax.dynamic_index_in_dim(x, place, 0, keepdims=False) for x in (kept, received)]
    block = jnp.stack(block)
    return shift(block, "tile", step) if step else block


def gather_pair(first, second, state, step, extras=None):
    tiles = lax.axis_size("tile")
    found, moving = [{0: first}, {}], [None, None]

    def launch(which, index):
        ring = found[which][2 * index]
        if index < tiles - 1:
            moving[which] = (shift(ring, "tile", 1), shift(ring, "mpo", 1))
        elif which:
            moving[which] = shift(found[which][2 * index - 1], "tile", 1)
        else:
            moving[which] = shift(ring, "mpo", 1)

    launch(0, 0)
    late = callable(second)
    if late:
        second, extras = second()
        events = [(0, 1), (0, 2)]
        for index in range(1, tiles - 2):
            events += [(1, index), (0, index + 2)]
        events += [(1, tiles - 2), (1, tiles - 1)]
    else:
        events = [(which, index) for index in range(1, tiles) for which in range(2)]
    found[1][0] = second
    if not late:
        launch(1, 0)
    seen = first
    for which, index in events:
        ring, cross = moving[which]
        if late and (which, index) == (0, 1):
            ring, cross, found[1][0] = lax.optimization_barrier((ring, cross, second))
        elif late and (which, index) == (1, tiles - 2):
            ring, cross, seen, extras = lax.optimization_barrier((ring, cross, seen, extras))
        else:
            ring, cross, seen = lax.optimization_barrier((ring, cross, seen))
        found[which][2 * index], found[which][2 * index - 1] = ring, cross
        seen = ring
        launch(which, index)
        if late and (which, index) == (0, 1):
            launch(1, 0)
    entries = list(range(2 * tiles - 1))
    state = step([[found[0][e], found[1][e]] for e in entries], entries, state, False)
    last = lax.optimization_barrier((moving[0], moving[1], state, extras))
    return step([[last[0], last[1]]], [2 * tiles - 1], last[2], True), last[3]


def shards(
    text_embed,
    latents,
    down_conv,
    patch_in,
    norm_gain,
    query_weight,
    key_weight,
    value_weight,
    query_gain,
    key_gain,
    out_weight,
    patch_out,
    up_conv,
    span_start,
    image_of_slot,
):
    ctxs, tiles, outer = (lax.axis_size(name) for name in ("ctx", "tile", "mpo"))
    ctx, tile, mpo, core = (lax.axis_index(name) for name in ("ctx", "tile", "mpo", "core"))
    seq_rows, width = text_embed.shape
    half = seq_rows // 2
    heads = width // HD
    images = span_start.shape[0]
    local = latents.shape[0]

    numbers = jnp.arange(images, dtype=jnp.int32)
    matches = image_of_slot[None, :] == numbers[:, None]
    slot_of_image = jnp.sum(jnp.where(matches, numbers[None, :], 0), axis=1)
    slot_place = lax.rem(ctx + ctxs - slot_of_image // local, ctxs) * local + slot_of_image % local
    meta = jnp.concatenate(
        [span_start, slot_place, image_of_slot, jnp.stack([ctx, core, tile, mpo])]
    ).astype(jnp.int32)
    layout = (images, tiles, outer)

    weights = [swap(w) for w in (key_weight, value_weight, query_weight)]
    pieces, conv, meta, weights[0], weights[1] = gather_small(latents, down_conv, meta, *weights[:2])
    later, pieces[1] = lax.optimization_barrier((meta, pieces[1]))
    kept, sent, halves = transpose_first(later, patch_out, layout, ctxs)
    pieces, sent = lax.optimization_barrier((pieces, sent))
    received = shift(sent, "mpo", 1)
    weights += [key_weight, value_weight, query_weight]
    streams = down_stream(meta, pieces, conv, patch_in, text_embed, norm_gain, weights, images)
    streams, held_weights = streams[:2], streams[2:]
    streams, received = lax.optimization_barrier((streams, received))
    others = [swap(s[1]) for s in streams]
    others = lax.optimization_barrier(others)

    head_gains = jnp.stack([query_gain, key_gain])

    def project(blocks, entries, state, last):
        return qkv_step(
            meta, layout, blocks, entries, weights if last else held_weights, state, head_gains
        )

    state, out_par = gather_pair(
        *[by_core(core, s[0], o, 1) for s, o in zip(streams, others)], None, project, swap(out_weight)
    )
    kv_send, q_send = state[:heads], state[heads : 2 * heads]
    kv_own, q_own = state[2 * heads : 3 * heads], state[3 * heads :]

    def shifted(values, step, cross):
        pairs = [
            (2 * c + k, 2 * ((c + step) % ctxs) + (1 - k if cross else k))
            for c in range(ctxs)
            for k in range(2)
        ]
        return lax.ppermute(values, ("ctx", "core"), pairs)

    def pieces_of(head):
        pieces = [swap(q_send[head]), kv_own[head], swap(kv_send[head])]
        for step in range(1, ctxs):
            pieces += [shifted(kv_own[head], step, False), shifted(kv_send[head], step, True)]
        return pieces

    def attend(head, pieces, ahead):
        result = attention(meta, [q_own[head], pieces[0]], pieces[1:], images)
        (att_own, att_send), ahead = lax.optimization_barrier((result, ahead))
        return by_core(core, att_own, swap(att_send), 1), ahead

    pieces = pieces_of(0)
    pieces[0], q_send, kv_own, kv_send, kept, received = lax.optimization_barrier(
        (pieces[0], q_send, kv_own, kv_send, kept, received)
    )
    up_blocks = [transpose_second(kept, received, step) for step in range(tiles)]
    pieces, up_blocks[tiles // 2] = lax.optimization_barrier((pieces, up_blocks[tiles // 2]))
    attended, (other_pieces, up_blocks) = attend(
        0, pieces, (pieces_of(1) if heads > 1 else None, up_blocks)
    )
    if heads == 1:
        attended, second = attended[: half // 2], attended[half // 2 :]
        own = jnp.concatenate(up_blocks)
        extras = [own, swap(own)] + ([shift(own, "ctx", 1)] if halves == 2 else [])
    else:
        extras = None

        def second():
            pieces, _ = lax.optimization_barrier((other_pieces, attended))
            result, up = attend(1, pieces, up_blocks)
            own = jnp.concatenate(up)
            return result, [own, swap(own)] + ([shift(own, "ctx", 1)] if halves == 2 else [])

    def project_out(blocks, entries, state, last):
        return out_step(meta, layout, blocks, entries, (out_weight, out_par), state, last)

    state = [jnp.stack([s[0], o]) for s, o in zip(streams, others)]
    state, up_weights = gather_pair(attended, second, state, project_out, extras)
    out_own, out_send = state
    out_other = swap(out_send)
    layer_out = by_core(core, out_own, out_other, 0)

    picks, swapped = lax.optimization_barrier(
        (pick_rows(meta, out_own, out_other, images, ctxs), [swap(other) for other in up_weights[2:]])
    )
    up_weights = [up_weights[:2]] + [[up_weights[2], other] for other in swapped]
    own_parts, par_parts = [picks[0]], [swap(picks[1])]
    for step in range(1, ctxs):
        own_parts.append(shifted(picks[2 * step], step, False))
        par_parts.append(shifted(picks[2 * step + 1], step, True))

    pixel = tile * outer + mpo
    pixels = jnp.stack([pixel * halves + lax.rem(ctx + h, halves) for h in range(halves)])
    spread_weight = spread_weights(up_conv, pixels)

    def project_up(blocks, entries, state, last):
        return up_step(blocks, entries, up_weights, state, spread_weight if last else None)

    state, _ = gather_pair(*merge_picks(own_parts, par_parts), None, project_up)

    bands = state.reshape(tiles, IMG_TOK // tiles, PIX * CIN)
    band = lax.dynamic_index_in_dim(bands, tile, 0, keepdims=False)
    for step in range(1, tiles):
        piece = lax.dynamic_index_in_dim(bands, lax.rem(tile + step, tiles), 0, keepdims=False)
        band = band + shift(piece, "tile", step)
    quad = {}
    for name, pairs in (
        ("mpo", [(0, 2), (1, 3), (2, 0), (3, 1)]),
        ("core", [(0, 1), (1, 0), (2, 3), (3, 2)]),
        ("both", [(0, 3), (1, 2), (2, 1), (3, 0)]),
    ):
        quad[name] = lax.ppermute(band, ("mpo", "core"), pairs)
    return layer_out, finish(meta[3 * images + 1 :], band, quad["mpo"], quad["core"], quad["both"])


def solution(mesh):
    ctxs, tiles, parts = mesh.devices.shape
    fine = Mesh(
        mesh.devices.reshape(ctxs, tiles, parts // 2, 2), ("ctx", "tile", "mpo", "core")
    )
    features = ("tile", "mpo", "core")
    return jax.shard_map(
        shards,
        mesh=fine,
        in_specs=(
            P("ctx", features),
            P("ctx", "tile", None),
            P(None, ("mpo", "core")),
            P(None, features),
            P(features),
            P(None, features),
            P(None, features),
            P(None, features),
            P(),
            P(),
            P(None, features),
            P(features, None),
            P(),
            P(),
            P(),
        ),
        out_specs=(P("ctx", features), P("ctx", "tile", None)),
        check_vma=False,
    )
```

```python
import functools

import jax
import jax.numpy as jnp
from jax import lax
from jax.experimental import pallas as pl
from jax.experimental.pallas import tpu as pltpu
from jax.sharding import Mesh
from jax.sharding import PartitionSpec as P

HD = 128
CH = 256
CIN = 8
WL = 64
HL = 64
PATCH = 4
PIX = PATCH * PATCH
SIDE = WL // PATCH
IMG_TOK = 256
EPSILON = 1e-05
NEGATIVE_FILL = -1e30
WINDOW = (PATCH + 2) * CIN
TAPS = 3 * WINDOW
BF16 = jnp.bfloat16
F32 = jnp.float32


def split_meta(meta, images):
    return meta[3 * images], meta[3 * images + 1], meta[3 * images + 2], meta[3 * images + 3]


def params(mebibytes):
    return pltpu.CompilerParams(
        dimension_semantics=("arbitrary",), vmem_limit_bytes=mebibytes * 1024 * 1024
    )


def cost(flops, nbytes, transcendentals=0):
    return pl.CostEstimate(
        flops=int(flops), bytes_accessed=int(nbytes), transcendentals=int(transcendentals)
    )


def silu(values):
    half = values * 0.5
    return half + half * jnp.tanh(half)


def mxu(left, right):
    return jnp.dot(left, right, preferred_element_type=F32)


def swap(values):
    return lax.ppermute(values, "core", [(0, 1), (1, 0)])


HELD = pl.BlockSpec(memory_space=pltpu.VMEM)


GAIN_ROWS = 16
TOP = 16


def down_kernel(images, tiles, half, meta, *refs):
    lat_refs, refs = refs[:tiles], refs[tiles:]
    conv_ref, patch_ref, own_text, par_text, gain_ref = refs[:5]
    weight_refs, (first_ref, second_ref), held_refs = refs[5:11], refs[11:13], refs[13:19]
    grid_rows, conv_wide, conv_bf16, windows, total, arrived = refs[19:]
    step = pl.program_id(0)
    copies = [
        pltpu.make_async_copy(weight, held, arrived.at[index])
        for index, (weight, held) in enumerate(zip(weight_refs, held_refs))
    ]

    @pl.when(step == 0)
    def _():
        for copy in copies:
            copy.start()

    group = images * SIDE
    ctx, core, tile, _ = split_meta(meta, images)

    @pl.when(step == 0)
    def _():
        grid_rows[...] = jnp.zeros_like(grid_rows)
        blocks = grid_rows.shape[1]
        for index in range(tiles):
            band = lat_refs[index].shape[1]
            at = TOP + lax.rem(tile + tiles - index, tiles) * band
            rows = pl.ds(pl.multiple_of(at, 8), band)
            latent = lat_refs[index][...].astype(F32)
            edges = [jnp.zeros((images, band, size), F32) for size in (CIN, HD - CIN)]
            wide = jnp.concatenate([edges[0], latent, edges[1]], axis=2)
            for part in range(blocks):
                grid_rows[:, part, rows, :] = wide[:, :, part * HD : (part + 1) * HD]
        conv_wide[...] = jnp.zeros_like(conv_wide)
        conv = conv_ref[...].astype(F32)
        for col in range(PATCH):
            for tap in range(3):
                at = WINDOW * tap + CIN * col
                conv_wide[at : at + 3 * CIN, CH * col : CH * (col + 1)] = conv[
                    3 * CIN * tap : 3 * CIN * (tap + 1), :
                ]
        conv_bf16[...] = conv_wide[...].astype(BF16)

        def build(image, carry):
            for row in range(PATCH + 2):
                take = pl.ds(TOP - 1 + row, SIDE, stride=PATCH)
                line = [grid_rows[image, part, take, :] for part in range(blocks)]
                line = jnp.concatenate(line, axis=1).astype(BF16)
                for col in range(SIDE):
                    piece = line[:, PATCH * CIN * col : PATCH * CIN * col + WINDOW]
                    at = pl.ds(pl.multiple_of(group * col + image * SIDE, SIDE), SIDE)
                    for shift in range(3):
                        if 0 <= row - shift < PATCH:
                            windows[row - shift, at, WINDOW * shift : WINDOW * (shift + 1)] = piece
            return carry

        lax.fori_loop(0, images, build, 0)
        total[...] = jnp.zeros_like(total)

    chunk = 256
    for part in range(images * IMG_TOK // chunk):
        rows = slice(part * chunk, (part + 1) * chunk)
        hidden = silu(mxu(windows[step, rows, :], conv_bf16[...])).astype(BF16)
        total[rows, :] += mxu(hidden, patch_ref[...])

    @pl.when(step == PATCH - 1)
    def _():
        tokens = total[...].astype(BF16)
        block = half // 2
        for side, text_ref in enumerate((own_text, par_text)):
            base = ctx * (2 * half) + jnp.bitwise_xor(core, side) * half
            for part, out_ref in enumerate((first_ref, second_ref)):
                place = base + part * block + lax.broadcasted_iota(jnp.int32, (block, 1), 0)
                source = jnp.full((block, 1), -1, jnp.int32)
                for image in range(images):
                    inner = place - meta[image]
                    inside = (inner >= 0) & (inner < IMG_TOK)
                    index = (inner & (SIDE - 1)) * group + meta[images + image] * SIDE + (inner >> 4)
                    source = jnp.where(inside, index, source)
                choice = source == lax.broadcasted_iota(jnp.int32, (block, images * IMG_TOK), 1)
                picked = mxu(jnp.where(choice, 1.0, 0.0).astype(BF16), tokens)
                text = text_ref[0, part * block : (part + 1) * block, :].astype(F32)
                out_ref[side, :block, :] = jnp.where(source >= 0, picked, text).astype(BF16)
            gain = gain_ref[...].astype(F32)
            first_ref[side, block:, :] = jnp.broadcast_to(gain, (GAIN_ROWS, gain.shape[1])).astype(BF16)
        for copy in copies:
            copy.wait()


def down_stream(meta, pieces, conv, patch_in, text, gain, weights, images):
    seq_rows, width = text.shape
    half = seq_rows // 2
    tiles = len(pieces)
    count = images * IMG_TOK
    halves = text.reshape(2, half, width)
    core_at = 3 * images + 1
    first, second = (2, half // 2 + GAIN_ROWS, width), (2, half // 2, width)
    return pl.pallas_call(
        functools.partial(down_kernel, images, tiles, half),
        grid_spec=pltpu.PrefetchScalarGridSpec(
            num_scalar_prefetch=1,
            grid=(PATCH,),
            in_specs=[full(p.shape) for p in pieces]
            + [
                full(conv.shape),
                pl.BlockSpec((PATCH * CH, width), lambda i, m: (i, 0)),
                pl.BlockSpec((1, half, width), lambda i, m: (m[core_at], 0, 0)),
                pl.BlockSpec((1, half, width), lambda i, m: (1 - m[core_at], 0, 0)),
                full((1, width)),
            ]
            + [pl.BlockSpec(memory_space=pl.ANY)] * 6,
            out_specs=[full(first), full(second)] + [HELD] * 6,
            scratch_shapes=[
                pltpu.VMEM((images, WL * CIN // HD + 1, TOP + HL + 16, HD), F32),
                pltpu.VMEM((TAPS, PATCH * CH), F32),
                pltpu.VMEM((TAPS, PATCH * CH), BF16),
                pltpu.VMEM((PATCH, count, TAPS), BF16),
                pltpu.VMEM((count, width), F32),
                pltpu.SemaphoreType.DMA((6,)),
            ],
        ),
        out_shape=[jax.ShapeDtypeStruct(first, BF16), jax.ShapeDtypeStruct(second, BF16)]
        + [pltpu.VMEM(w.shape, w.dtype) for w in weights],
        compiler_params=params(32),
        cost_estimate=cost(2 * count * PIX * CH * (256 + width), 4 << 20, count * PIX * CH),
        name="down_stream",
    )(meta, *pieces, conv, patch_in, halves, halves, gain.reshape(1, width), *weights)


def full(shape):
    return pl.BlockSpec(shape, lambda i, m: (0,) * len(shape))


def load(pieces):
    return jnp.concatenate([piece[...] for piece in pieces], axis=0)


def take_blocks(refs, count):
    return [[refs.pop(0), refs.pop(0)] for _ in range(count)]


def chip_of(meta, images, tiles, outer, entry):
    _, _, tile, mpo = split_meta(meta, images)
    return lax.rem(tile + tiles - entry // 2, tiles) * outer + lax.rem(mpo + entry % 2, outer)


def qkv_kernel(entries, layout, groups, last, meta, *refs):
    refs = list(refs)
    count = len(entries)
    x_refs = take_blocks(refs, count)
    weight_refs = [refs.pop(0) for _ in range(6)]
    if last:
        acc_in, square_in, head_gains = refs.pop(0), refs.pop(0), refs.pop(0)
        fetched, arrived = refs.pop(-3), refs.pop(-2)
        span = fetched.shape[1]
        rows = pl.ds(pl.multiple_of(chip_of(meta, *layout, entries[0]) * span, span), span)
        copies = [
            pltpu.make_async_copy(weight.at[rows, :], fetched.at[part], arrived.at[part])
            for part, weight in enumerate(weight_refs)
        ]
        for copy in copies:
            copy.start()
    scaled_ref = refs.pop(-1)
    half, span = scaled_ref.shape
    width = weight_refs[0].shape[1]
    heads = width // HD
    square = square_in[...] if last else None
    if last:
        acc, outs = [None] * 6, refs
    else:
        acc_out, square_out = refs
    for index in range(count):
        rows = pl.ds(pl.multiple_of(chip_of(meta, *layout, entries[index]) * span, span), span)
        gain = x_refs[index][0][half // 2 :, :][:1]
        for part in range(2):
            at = slice(part * half // 2, (part + 1) * half // 2)
            scaled_ref[at, :] = (x_refs[index][part][: half // 2, :] * gain).astype(BF16)
        value = jnp.concatenate([x_refs[index][0][: half // 2, :], x_refs[index][1][...]], axis=0)
        value = value.astype(F32)
        value = value * value
        for part in range(span // HD):
            piece = value[:, part * HD : (part + 1) * HD]
            square = piece if square is None else square + piece
        for part in range(6):
            if last:
                copies[part].wait()
                acc[part] = acc_in[part] + mxu(scaled_ref[...], fetched[part])
                continue
            term = mxu(scaled_ref[...], weight_refs[part][rows, :])
            if index == 0:
                acc_out[part] = term
            else:
                acc_out[part] += term
    if not last:
        square_out[...] = square
        return
    mean = jnp.sum(square, axis=-1, keepdims=True) * (1.0 / (groups * span))
    scale = lax.rsqrt(mean + EPSILON)
    for part in range(6):
        total = acc[part] * scale
        side, kind = part // 3, part % 3
        kv_out, q_out = outs[2 * side : 2 * side + 2]
        for head in range(heads):
            lanes = slice(head * HD, (head + 1) * HD)
            raw = total[:, lanes]
            if kind == 1:
                kv_out[1, :, lanes] = raw.astype(BF16)
                continue
            raw = raw * lax.rsqrt(jnp.mean(raw * raw, axis=-1, keepdims=True) + EPSILON)
            if kind == 0:
                kv_out[0, :, lanes] = (raw * head_gains[1:2, :]).astype(BF16)
            else:
                q_out[:, lanes] = (raw * (head_gains[0:1, :] * HD ** (-0.5))).astype(BF16)


def qkv_step(meta, layout, blocks, entries, weights, state, head_gains):
    span = blocks[0][1].shape[1]
    half = 2 * blocks[0][1].shape[0]
    width = weights[0].shape[1]
    count, last = len(blocks), state is not None
    groups = layout[1] * layout[2]
    inputs = [p for pieces in blocks for p in pieces] + list(weights)
    specs = [full(p.shape) for pieces in blocks for p in pieces]
    scratch = [pltpu.VMEM((half, span), BF16)]
    if last:
        specs += [pl.BlockSpec(memory_space=pltpu.HBM)] * 6 + [HELD] * 2 + [full(head_gains.shape)]
        inputs += list(state) + [head_gains]
        outs = [pltpu.HBM((2, half, width), BF16), pltpu.HBM((half, width), BF16)] * 2
        scratch = [pltpu.VMEM((6, span, width), BF16), pltpu.SemaphoreType.DMA((6,))] + scratch
    else:
        specs += [HELD] * 6
        outs = [pltpu.VMEM((6, half, width), F32), pltpu.VMEM((half, HD), F32)]
    return pl.pallas_call(
        functools.partial(qkv_kernel, entries, layout, groups, last),
        grid_spec=pltpu.PrefetchScalarGridSpec(
            num_scalar_prefetch=1,
            grid=(1,),
            in_specs=specs,
            out_specs=[full(o.shape) if last else HELD for o in outs],
            scratch_shapes=scratch,
        ),
        out_shape=outs,
        compiler_params=params(20),
        cost_estimate=cost(12 * count * half * span * width, (6 + 2 * count) << 20),
        name="qkv_last" if last else "qkv_step",
    )(meta, *inputs)


def attention_kernel(images, pieces, half, meta, *refs):
    ctx, core, _, _ = split_meta(meta, images)
    ctxs = pieces // 2
    bases = []
    for piece in range(pieces):
        side = jnp.bitwise_xor(core, piece % 2)
        bases.append(lax.rem(ctx + ctxs - piece // 2, ctxs) * (2 * half) + side * half)
    q_refs, kv_refs, out_refs = refs[:2], refs[2 : 2 + pieces], refs[2 + pieces :]
    rows = q_refs[0].shape[0]
    step = pl.program_id(0)
    for side in range(2):
        place = bases[side] + step * rows + lax.broadcasted_iota(jnp.int32, (rows, 1), 0)
        limit = place
        for image in range(images):
            inner = place - meta[image]
            limit = jnp.where((inner >= 0) & (inner < IMG_TOK), meta[image] + IMG_TOK - 1, limit)
        for head in range(q_refs[0].shape[1] // HD):
            lanes = slice(head * HD, (head + 1) * HD)
            query = q_refs[side][:, lanes]
            scores = []
            top = None
            for piece in range(pieces):
                score = lax.dot_general(
                    query, kv_refs[piece][0, :, lanes], (((1,), (1,)), ((), ())), preferred_element_type=F32
                )
                position = lax.broadcasted_iota(jnp.int32, score.shape, 1)
                score = jnp.where(position <= limit - bases[piece], score, NEGATIVE_FILL)
                scores.append(score)
                best = jnp.max(score, axis=1, keepdims=True)
                top = best if top is None else jnp.maximum(top, best)
            total = jnp.zeros((rows, 1), F32)
            product = jnp.zeros((rows, HD), F32)
            for piece in range(pieces):
                weight = jnp.exp(scores[piece] - top)
                total = total + jnp.sum(weight, axis=1, keepdims=True)
                product = product + mxu(weight.astype(BF16), kv_refs[piece][1, :, lanes])
            out_refs[side][:, lanes] = (product / total).astype(BF16)


def attention(meta, queries, pieces, images):
    half, width = queries[0].shape
    block = 256
    keys = half * len(pieces)
    rows = pl.BlockSpec((block, width), lambda i, m: (i, 0))
    return pl.pallas_call(
        functools.partial(attention_kernel, images, len(pieces), half),
        grid_spec=pltpu.PrefetchScalarGridSpec(
            num_scalar_prefetch=1,
            grid=(half // block,),
            in_specs=[rows, rows] + [full(p.shape) for p in pieces],
            out_specs=[rows, rows],
        ),
        out_shape=[jax.ShapeDtypeStruct((half, width), BF16)] * 2,
        compiler_params=params(32),
        cost_estimate=cost(8 * half * keys * width, 4 * keys * width, 2 * half * keys * width // HD),
        name="attention",
    )(meta, *queries, *pieces)


def out_kernel(count, first, last, meta, *refs):
    refs = list(refs)
    x_refs = take_blocks(refs, count)
    weight_refs = [[refs.pop(0), refs.pop(0)] for _ in range(count)]
    if first:
        streams = [refs.pop(0), refs.pop(0)]
        block = streams[1].shape[1]
    else:
        acc_in = refs.pop(0)
    outs = refs
    for side in range(2):
        if first:
            rows = [streams[0][side, :block, :], streams[1][side]]
            total = jnp.concatenate(rows, axis=0).astype(F32)
        else:
            total = acc_in[side]
        for index in range(count):
            total = total + mxu(load(x_refs[index]), weight_refs[index][side][...])
        if last:
            outs[side][...] = total.astype(BF16)
        else:
            outs[0][side] = total


def out_step(meta, layout, blocks, entries, weights, state, last):
    span, width = blocks[0][0].shape[1], weights[0].shape[1]
    half = 2 * blocks[0][0].shape[0]
    first = isinstance(state, list)
    count = len(blocks)
    inputs = [p for pieces in blocks for p in pieces]
    specs = [full(p.shape) for p in inputs]
    for entry in entries:
        index = lambda i, m, entry=entry: (chip_of(m, *layout, entry), 0)
        inputs += weights
        specs += [pl.BlockSpec((span, width), index)] * 2
    states = state if first else [state]
    inputs += states
    specs += [full(s.shape) for s in states]
    if last:
        outs = [jax.ShapeDtypeStruct((half, width), BF16)] * 2
    else:
        outs = [jax.ShapeDtypeStruct((2, half, width), F32)]
    result = pl.pallas_call(
        functools.partial(out_kernel, count, first, last),
        grid_spec=pltpu.PrefetchScalarGridSpec(
            num_scalar_prefetch=1,
            grid=(1,),
            in_specs=specs,
            out_specs=[full(o.shape) for o in outs],
        ),
        out_shape=outs,
        compiler_params=params(24),
        cost_estimate=cost(4 * count * half * span * width, (2 + count) << 20),
        name="out_last" if last else "out_step",
    )(meta, *inputs)
    return result if last else result[0]


def pick_kernel(images, ctxs, meta, own_ref, par_ref, *out_refs):
    half = own_ref.shape[0]
    ctx, core, _, _ = split_meta(meta, images)
    for target in range(2 * ctxs):
        to_core = jnp.bitwise_xor(core, target % 2)
        slot = 2 * lax.rem(ctx + target // 2, ctxs) + to_core
        start = meta[meta[2 * images + slot]]
        place = start + lax.broadcasted_iota(jnp.int32, (IMG_TOK, half), 0)
        column = ctx * (2 * half) + lax.broadcasted_iota(jnp.int32, (IMG_TOK, half), 1)
        own = jnp.where(place == column + core * half, 1.0, 0.0).astype(BF16)
        par = jnp.where(place == column + (1 - core) * half, 1.0, 0.0).astype(BF16)
        out_refs[target][...] = (mxu(own, own_ref[...]) + mxu(par, par_ref[...])).astype(BF16)


def pick_rows(meta, own, par, images, ctxs):
    half, width = own.shape
    targets = 2 * ctxs
    return pl.pallas_call(
        functools.partial(pick_kernel, images, ctxs),
        grid_spec=pltpu.PrefetchScalarGridSpec(
            num_scalar_prefetch=1,
            grid=(1,),
            in_specs=[full(own.shape), full(par.shape)],
            out_specs=[full((IMG_TOK, width))] * targets,
        ),
        out_shape=[jax.ShapeDtypeStruct((IMG_TOK, width), BF16)] * targets,
        compiler_params=params(16),
        cost_estimate=cost(targets * 4 * IMG_TOK * half * width, 1 << 20),
        name="pick_rows",
    )(meta, own, par)


def merge_kernel(*refs):
    out_refs = refs[-2:]
    refs = refs[:-2]
    sides = refs[: len(refs) // 2], refs[len(refs) // 2 :]
    width = sides[0][0].shape[1]
    block = IMG_TOK // 2
    for side in range(2):
        total = sides[side][0][...].astype(F32)
        for part in sides[side][1:]:
            total = total + part[...].astype(F32)
        total = total.astype(BF16)
        for index in range(2):
            out_refs[index][:, side * width : (side + 1) * width] = total[index * block : (index + 1) * block]


def merge_picks(own_parts, par_parts):
    width = own_parts[0].shape[1]
    return pl.pallas_call(
        merge_kernel,
        out_shape=[jax.ShapeDtypeStruct((IMG_TOK // 2, 2 * width), BF16)] * 2,
        compiler_params=pltpu.CompilerParams(vmem_limit_bytes=8 << 20),
        cost_estimate=cost(1 << 20, 1 << 20),
        name="merge_picks",
    )(*own_parts, *par_parts)


def finish_kernel(core_ref, own_a, own_b, par_a, par_b, out_ref, sums, lines):
    core = core_ref[0]
    for side, (left, right) in enumerate(((own_a, own_b), (par_a, par_b))):
        sums[side] = left[...] + right[...]
    rows = sums.shape[1] // SIDE
    lanes = PATCH * CIN
    per = HD // lanes
    for side in range(2):
        for part in range(SIDE // per):
            cols = [sums[side, pl.ds(part * per + k, rows, stride=SIDE), :] for k in range(per)]
            for row in range(PATCH):
                pieces = [col[:, row * lanes : (row + 1) * lanes] for col in cols]
                lines[part, pl.ds(row, rows, stride=PATCH), :] = jnp.concatenate(pieces, axis=1)
        slot = jnp.bitwise_xor(core, side)
        for part in range(SIDE // per):
            out_ref[slot, :, part * HD : (part + 1) * HD] = lines[part]


def finish(core, own_a, own_b, par_a, par_b):
    count = own_a.shape[0]
    return pl.pallas_call(
        finish_kernel,
        grid_spec=pltpu.PrefetchScalarGridSpec(
            num_scalar_prefetch=1,
            grid=(1,),
            in_specs=[full(own_a.shape)] * 4,
            out_specs=full((2, count // PATCH, WL * CIN)),
            scratch_shapes=[
                pltpu.VMEM((2, count, PIX * CIN), F32),
                pltpu.VMEM((WL * CIN // HD, count // PATCH, HD), F32),
            ],
        ),
        out_shape=jax.ShapeDtypeStruct((2, count // PATCH, WL * CIN), F32),
        compiler_params=params(8),
        cost_estimate=cost(1 << 16, 1 << 18),
        name="finish",
    )(core, own_a, own_b, par_a, par_b)


def spread(active, spread_ref):
    row = lax.broadcasted_iota(jnp.int32, (IMG_TOK, PIX * CIN), 0)
    patch_row, patch_col = row >> 4, row & (SIDE - 1)
    total = None
    for index in range(9):
        down, right = index // 3 - 1, index % 3 - 1
        part = mxu(active, spread_ref[:, index * PIX * CIN : (index + 1) * PIX * CIN])
        offset = down * SIDE + right
        if offset:
            part = pltpu.roll(part, offset % IMG_TOK, 0)
        source_row, source_col = patch_row - down, patch_col - right
        inside = (source_row >= 0) & (source_row < SIDE) & (source_col >= 0) & (source_col < SIDE)
        part = jnp.where(inside, part, 0.0)
        total = part if total is None else total + part
    return total


def up_kernel(count, halves, first, last, *refs):
    refs = list(refs)
    x_refs = take_blocks(refs, count)
    weight_refs = [[[refs.pop(0) for _ in range(2)] for _ in range(halves)] for _ in range(count)]
    acc_in = None if first else refs.pop(0)
    spread_ref = refs.pop(0) if last else None
    out_ref = refs[0]
    width = x_refs[0][0].shape[1] // 2
    values = [load(pieces) for pieces in x_refs]
    totals = []
    for part in range(halves):
        total = None if first else acc_in[part]
        for block in range(count):
            for side in range(2):
                term = mxu(
                    values[block][:, side * width : (side + 1) * width],
                    weight_refs[block][part][side][0],
                )
                total = term if total is None else total + term
        totals.append(total)
        if not last:
            out_ref[part] = total
    if last:
        active = [silu(total).astype(BF16) for total in totals]
        active = jnp.concatenate(active, axis=1) if halves > 1 else active[0]
        out_ref[...] = spread(active, spread_ref)


def up_step(blocks, entries, weights, state, spread_weight):
    span = blocks[0][0].shape[1]
    halves, count = len(weights), len(blocks)
    first, last = state is None, spread_weight is not None
    whole = lambda shape: pl.BlockSpec(shape, lambda i: (0,) * len(shape))
    inputs = [p for pieces in blocks for p in pieces]
    specs = [whole(p.shape) for p in inputs]
    for entry in entries:
        for sides in weights:
            for weight in sides:
                inputs.append(weight)
                specs.append(pl.BlockSpec((1, span // 2, CH), lambda i, entry=entry: (entry, 0, 0)))
    if not first:
        inputs.append(state)
        specs.append(whole(state.shape))
    if last:
        inputs.append(spread_weight)
        specs.append(whole(spread_weight.shape))
        out = jax.ShapeDtypeStruct((IMG_TOK, PIX * CIN), F32)
    else:
        out = jax.ShapeDtypeStruct((halves, IMG_TOK, CH), F32)
    return pl.pallas_call(
        functools.partial(up_kernel, count, halves, first, last),
        grid=(1,),
        in_specs=specs,
        out_specs=whole(out.shape),
        out_shape=out,
        compiler_params=params(16),
        cost_estimate=cost(2 * count * IMG_TOK * span * CH * halves, (1 + count) << 20),
        name="up_last" if last else "up_step",
    )(*inputs)


def spread_weights(up_conv, pixels):
    taps = up_conv.reshape(9, CH, CIN).transpose(1, 0, 2).reshape(CH, 9 * CIN)
    shape = (pixels.shape[0], 9 * CIN, 9 * PIX * CIN)
    row = lax.broadcasted_iota(jnp.int32, shape, 1)
    col = lax.broadcasted_iota(jnp.int32, shape, 2)
    pixel = pixels[:, None, None]
    tap, channel = row >> 3, row & 7
    patch, target, out_channel = col >> 7, (col >> 3) & 15, col & 7
    tap_row, tap_col = tap // 3, tap % 3
    down, right = patch // 3 - 1, patch % 3 - 1
    hit = (
        (channel == out_channel)
        & ((pixel >> 2) + 1 - tap_row == (target >> 2) + PATCH * down)
        & ((pixel & 3) + 1 - tap_col == (target & 3) + PATCH * right)
    )
    placed = jnp.where(hit, 1.0, 0.0).astype(BF16)
    spread = jnp.einsum("ct,ptn->pcn", taps, placed, preferred_element_type=F32)
    return spread.astype(BF16).reshape(pixels.shape[0] * CH, 9 * PIX * CIN)


def by_core(core, own, other, axis):
    return jnp.where(
        core == 0, jnp.concatenate([own, other], axis), jnp.concatenate([other, own], axis)
    )


def shift(values, axis, step):
    count = lax.axis_size(axis)
    return lax.ppermute(values, axis, [(i, (i + step) % count) for i in range(count)])


def gather_small(latents, down_conv, *others):
    ctxs, tiles = lax.axis_size("ctx"), lax.axis_size("tile")
    every = jnp.concatenate([latents] + [shift(latents, "ctx", s) for s in range(1, ctxs)])
    conv = by_core(lax.axis_index("core"), down_conv, swap(down_conv), 1)
    conv = by_core(lax.axis_index("mpo"), conv, shift(conv, "mpo", 1), 1)
    every, others = lax.optimization_barrier((every, others))
    return [every] + [shift(every, "tile", s) for s in range(1, tiles)], conv, *others


def columns_kernel(layout, halves, meta, patch_ref, kept_ref, sent_ref, arrived):
    images, tiles, outer = layout
    ctx, _, _, mpo = split_meta(meta, images)
    size = kept_ref.shape[2]
    copies = []
    for other, out_ref in enumerate((kept_ref, sent_ref)):
        for tile in range(tiles):
            chip = tile * outer + lax.rem(mpo + other, outer)
            at = pl.multiple_of((chip * halves + (ctx if halves == 2 else 0)) * size, size)
            copies.append(
                pltpu.make_async_copy(
                    patch_ref.at[:, pl.ds(at, size)], out_ref.at[tile], arrived.at[other, tile]
                )
            )
    for copy in copies:
        copy.start()
    for copy in copies:
        copy.wait()


def transpose_first(meta, patch_out, layout, ctxs):
    images, tiles, outer = layout
    width, features = patch_out.shape
    deep = features // (tiles * outer)
    halves = 2 if ctxs == 2 and deep == 2 * CH else 1
    size = deep // halves

    place = pl.BlockSpec(memory_space=pltpu.HBM)
    kept, sent = pl.pallas_call(
        functools.partial(columns_kernel, layout, halves),
        grid_spec=pltpu.PrefetchScalarGridSpec(
            num_scalar_prefetch=1,
            grid=(1,),
            in_specs=[place],
            out_specs=[place, place],
            scratch_shapes=[pltpu.SemaphoreType.DMA((2, tiles))],
        ),
        out_shape=[pltpu.HBM((tiles, width, size), BF16)] * 2,
        compiler_params=params(8),
        cost_estimate=cost(1 << 16, 2 << 20),
        name="columns",
    )(meta, patch_out)
    return kept, sent, halves


def transpose_second(kept, received, step):
    tiles = lax.axis_size("tile")
    place = lax.rem(lax.axis_index("tile") + step, tiles)
    block = [lax.dynamic_index_in_dim(x, place, 0, keepdims=False) for x in (kept, received)]
    block = jnp.stack(block)
    return shift(block, "tile", step) if step else block


def gather_pair(first, second, state, step, extras=None):
    tiles = lax.axis_size("tile")
    found, moving = [{0: first}, {0: second}], [None, None]

    def launch(which, index):
        ring = found[which][2 * index]
        if index < tiles - 1:
            moving[which] = (shift(ring, "tile", 1), shift(ring, "mpo", 1))
        elif which:
            moving[which] = shift(found[which][2 * index - 1], "tile", 1)
        else:
            moving[which] = shift(ring, "mpo", 1)

    launch(0, 0)
    launch(1, 0)
    seen = first
    for index in range(1, tiles):
        for which in range(2):
            ring, cross = moving[which]
            ring, cross, seen = lax.optimization_barrier((ring, cross, seen))
            found[which][2 * index], found[which][2 * index - 1] = ring, cross
            seen = ring
            launch(which, index)
    entries = list(range(2 * tiles - 1))
    state = step([[found[0][e], found[1][e]] for e in entries], entries, state, False)
    last = lax.optimization_barrier((moving[0], moving[1], state, extras))
    return step([[last[0], last[1]]], [2 * tiles - 1], last[2], True), last[3]


def shards(
    text_embed,
    latents,
    down_conv,
    patch_in,
    norm_gain,
    query_weight,
    key_weight,
    value_weight,
    query_gain,
    key_gain,
    out_weight,
    patch_out,
    up_conv,
    span_start,
    image_of_slot,
):
    ctxs, tiles, outer = (lax.axis_size(name) for name in ("ctx", "tile", "mpo"))
    ctx, tile, mpo, core = (lax.axis_index(name) for name in ("ctx", "tile", "mpo", "core"))
    seq_rows, width = text_embed.shape
    half = seq_rows // 2
    images = span_start.shape[0]
    local = latents.shape[0]

    numbers = jnp.arange(images, dtype=jnp.int32)
    matches = image_of_slot[None, :] == numbers[:, None]
    slot_of_image = jnp.sum(jnp.where(matches, numbers[None, :], 0), axis=1)
    slot_place = lax.rem(ctx + ctxs - slot_of_image // local, ctxs) * local + slot_of_image % local
    meta = jnp.concatenate(
        [span_start, slot_place, image_of_slot, jnp.stack([ctx, core, tile, mpo])]
    ).astype(jnp.int32)
    layout = (images, tiles, outer)

    weights = [swap(w) for w in (key_weight, value_weight, query_weight)]
    pieces, conv, meta, weights[0], weights[1] = gather_small(latents, down_conv, meta, *weights[:2])
    later, pieces[1] = lax.optimization_barrier((meta, pieces[1]))
    kept, sent, halves = transpose_first(later, patch_out, layout, ctxs)
    pieces, sent = lax.optimization_barrier((pieces, sent))
    received = shift(sent, "mpo", 1)
    weights += [key_weight, value_weight, query_weight]
    streams = down_stream(meta, pieces, conv, patch_in, text_embed, norm_gain, weights, images)
    streams, held_weights = streams[:2], streams[2:]
    streams, received = lax.optimization_barrier((streams, received))
    others = [swap(s[1]) for s in streams]
    others = lax.optimization_barrier(others)

    head_gains = jnp.stack([query_gain, key_gain])

    def project(blocks, entries, state, last):
        return qkv_step(
            meta, layout, blocks, entries, weights if last else held_weights, state, head_gains
        )

    state, out_par = gather_pair(
        *[by_core(core, s[0], o, 1) for s, o in zip(streams, others)], None, project, swap(out_weight)
    )
    kv_send, q_send, kv_own, q_own = state

    def shifted(values, step, cross):
        pairs = [
            (2 * c + k, 2 * ((c + step) % ctxs) + (1 - k if cross else k))
            for c in range(ctxs)
            for k in range(2)
        ]
        return lax.ppermute(values, ("ctx", "core"), pairs)

    q_par = swap(q_send)
    q_par, kept, received = lax.optimization_barrier((q_par, kept, received))
    up_blocks = [transpose_second(kept, received, step) for step in range(tiles)]
    pieces = [kv_own, swap(kv_send)]
    for step in range(1, ctxs):
        pieces += [shifted(kv_own, step, False), shifted(kv_send, step, True)]
    pieces, up_blocks = lax.optimization_barrier((pieces, up_blocks))
    att_own, att_send = attention(meta, [q_own, q_par], pieces, images)
    att_par = swap(att_send)
    rows = half // 2
    attended = [
        by_core(core, att_own[at : at + rows], att_par[at : at + rows], 1) for at in (0, rows)
    ]
    up_own = jnp.concatenate(up_blocks)
    extras = [up_own, swap(up_own)] + ([shift(up_own, "ctx", 1)] if halves == 2 else [])

    def project_out(blocks, entries, state, last):
        return out_step(meta, layout, blocks, entries, (out_weight, out_par), state, last)

    state = [jnp.stack([s[0], o]) for s, o in zip(streams, others)]
    state, up_weights = gather_pair(*attended, state, project_out, extras)
    out_own, out_send = state
    out_other = swap(out_send)
    layer_out = by_core(core, out_own, out_other, 0)

    picks, swapped = lax.optimization_barrier(
        (pick_rows(meta, out_own, out_other, images, ctxs), [swap(other) for other in up_weights[2:]])
    )
    up_weights = [up_weights[:2]] + [[up_weights[2], other] for other in swapped]
    own_parts, par_parts = [picks[0]], [swap(picks[1])]
    for step in range(1, ctxs):
        own_parts.append(shifted(picks[2 * step], step, False))
        par_parts.append(shifted(picks[2 * step + 1], step, True))

    pixel = tile * outer + mpo
    pixels = jnp.stack([pixel * halves + lax.rem(ctx + h, halves) for h in range(halves)])
    spread_weight = spread_weights(up_conv, pixels)

    def project_up(blocks, entries, state, last):
        return up_step(blocks, entries, up_weights, state, spread_weight if last else None)

    state, _ = gather_pair(*merge_picks(own_parts, par_parts), None, project_up)

    bands = state.reshape(tiles, IMG_TOK // tiles, PIX * CIN)
    band = lax.dynamic_index_in_dim(bands, tile, 0, keepdims=False)
    for step in range(1, tiles):
        piece = lax.dynamic_index_in_dim(bands, lax.rem(tile + step, tiles), 0, keepdims=False)
        band = band + shift(piece, "tile", step)
    quad = {}
    for name, pairs in (
        ("mpo", [(0, 2), (1, 3), (2, 0), (3, 1)]),
        ("core", [(0, 1), (1, 0), (2, 3), (3, 2)]),
        ("both", [(0, 3), (1, 2), (2, 1), (3, 0)]),
    ):
        quad[name] = lax.ppermute(band, ("mpo", "core"), pairs)
    return layer_out, finish(meta[3 * images + 1 :], band, quad["mpo"], quad["core"], quad["both"])


def solution(mesh):
    ctxs, tiles, parts = mesh.devices.shape
    fine = Mesh(
        mesh.devices.reshape(ctxs, tiles, parts // 2, 2), ("ctx", "tile", "mpo", "core")
    )
    features = ("tile", "mpo", "core")
    return jax.shard_map(
        shards,
        mesh=fine,
        in_specs=(
            P("ctx", features),
            P("ctx", "tile", None),
            P(None, ("mpo", "core")),
            P(None, features),
            P(features),
            P(None, features),
            P(None, features),
            P(None, features),
            P(),
            P(),
            P(None, features),
            P(features, None),
            P(),
            P(),
            P(),
        ),
        out_specs=(P("ctx", features), P("ctx", "tile", None)),
        check_vma=False,
    )
```

```python
import functools

import jax
import jax.numpy as jnp
from jax import lax
from jax.experimental import pallas as pl
from jax.experimental.pallas import tpu as pltpu
from jax.sharding import Mesh
from jax.sharding import PartitionSpec as P

HD = 128
CH = 256
CIN = 8
WL = 64
HL = 64
PATCH = 4
PIX = PATCH * PATCH
SIDE = WL // PATCH
IMG_TOK = 256
EPSILON = 1e-05
NEGATIVE_FILL = -1e30
WINDOW = (PATCH + 2) * CIN
TAPS = 3 * WINDOW
BF16 = jnp.bfloat16
F32 = jnp.float32


def split_meta(meta, images):
    return meta[3 * images], meta[3 * images + 1], meta[3 * images + 2], meta[3 * images + 3]


def params(mebibytes):
    return pltpu.CompilerParams(
        dimension_semantics=("arbitrary",), vmem_limit_bytes=mebibytes * 1024 * 1024
    )


def cost(flops, nbytes, transcendentals=0):
    return pl.CostEstimate(
        flops=int(flops), bytes_accessed=int(nbytes), transcendentals=int(transcendentals)
    )


def silu(values):
    half = values * 0.5
    return half + half * jnp.tanh(half)


def mxu(left, right):
    return jnp.dot(left, right, preferred_element_type=F32)


def swap(values):
    return lax.ppermute(values, "core", [(0, 1), (1, 0)])


HELD = pl.BlockSpec(memory_space=pltpu.VMEM)


GAIN_ROWS = 16
TOP = 16


def down_kernel(images, tiles, half, meta, *refs):
    lat_refs, refs = refs[:tiles], refs[tiles:]
    conv_ref, gain_ref, patch_hbm, text_hbm = refs[:4]
    weight_refs, (first_ref, second_ref), held_refs = refs[4:10], refs[10:12], refs[12:18]
    grid_rows, conv_wide, conv_bf16, windows, total, patch_ref, text_ref = refs[18:25]
    arrived, patch_arrived, text_arrived = refs[25:]
    step = pl.program_id(0)
    deep = PATCH * CH
    patch_copies = [
        pltpu.make_async_copy(
            patch_hbm.at[index * deep : (index + 1) * deep, :], patch_ref.at[index], patch_arrived.at[index]
        )
        for index in range(PATCH)
    ]
    side_rows = [jnp.bitwise_xor(meta[3 * images + 1], side) * half for side in range(2)]
    text_copies = [
        pltpu.make_async_copy(
            text_hbm.at[pl.ds(pl.multiple_of(side_rows[side], half), half), :],
            text_ref.at[side],
            text_arrived.at[side],
        )
        for side in range(2)
    ]
    copies = [
        pltpu.make_async_copy(weight, held, arrived.at[index])
        for index, (weight, held) in enumerate(zip(weight_refs, held_refs))
    ]

    @pl.when(step == 0)
    def _():
        for copy in patch_copies + text_copies + copies:
            copy.start()

    group = images * SIDE
    ctx, core, tile, _ = split_meta(meta, images)

    @pl.when(step == 0)
    def _():
        grid_rows[...] = jnp.zeros_like(grid_rows)
        blocks = grid_rows.shape[1]
        for index in range(tiles):
            band = lat_refs[index].shape[1]
            at = TOP + lax.rem(tile + tiles - index, tiles) * band
            rows = pl.ds(pl.multiple_of(at, 8), band)
            latent = lat_refs[index][...].astype(F32)
            edges = [jnp.zeros((images, band, size), F32) for size in (CIN, HD - CIN)]
            wide = jnp.concatenate([edges[0], latent, edges[1]], axis=2)
            for part in range(blocks):
                grid_rows[:, part, rows, :] = wide[:, :, part * HD : (part + 1) * HD]
        conv_wide[...] = jnp.zeros_like(conv_wide)
        conv = conv_ref[...].astype(F32)
        for col in range(PATCH):
            for tap in range(3):
                at = WINDOW * tap + CIN * col
                conv_wide[at : at + 3 * CIN, CH * col : CH * (col + 1)] = conv[
                    3 * CIN * tap : 3 * CIN * (tap + 1), :
                ]
        conv_bf16[...] = conv_wide[...].astype(BF16)

        def build(image, carry):
            for row in range(PATCH + 2):
                take = pl.ds(TOP - 1 + row, SIDE, stride=PATCH)
                line = [grid_rows[image, part, take, :] for part in range(blocks)]
                line = jnp.concatenate(line, axis=1).astype(BF16)
                for col in range(SIDE):
                    piece = line[:, PATCH * CIN * col : PATCH * CIN * col + WINDOW]
                    at = pl.ds(pl.multiple_of(group * col + image * SIDE, SIDE), SIDE)
                    for shift in range(3):
                        if 0 <= row - shift < PATCH:
                            windows[row - shift, at, WINDOW * shift : WINDOW * (shift + 1)] = piece
            return carry

        lax.fori_loop(0, images, build, 0)
        total[...] = jnp.zeros_like(total)

    for index in range(PATCH):
        pl.when(step == index)(patch_copies[index].wait)

    chunk = 256
    for part in range(images * IMG_TOK // chunk):
        rows = slice(part * chunk, (part + 1) * chunk)
        hidden = silu(mxu(windows[step, rows, :], conv_bf16[...])).astype(BF16)
        total[rows, :] += mxu(hidden, patch_ref[step])

    @pl.when(step == PATCH - 1)
    def _():
        tokens = total[...].astype(BF16)
        block = half // 2
        for copy in text_copies:
            copy.wait()
        for side in range(2):
            base = ctx * (2 * half) + jnp.bitwise_xor(core, side) * half
            for part, out_ref in enumerate((first_ref, second_ref)):
                place = base + part * block + lax.broadcasted_iota(jnp.int32, (block, 1), 0)
                source = jnp.full((block, 1), -1, jnp.int32)
                for image in range(images):
                    inner = place - meta[image]
                    inside = (inner >= 0) & (inner < IMG_TOK)
                    index = (inner & (SIDE - 1)) * group + meta[images + image] * SIDE + (inner >> 4)
                    source = jnp.where(inside, index, source)
                choice = source == lax.broadcasted_iota(jnp.int32, (block, images * IMG_TOK), 1)
                picked = mxu(jnp.where(choice, 1.0, 0.0).astype(BF16), tokens)
                text = text_ref[side, part * block : (part + 1) * block, :].astype(F32)
                out_ref[side, :block, :] = jnp.where(source >= 0, picked, text).astype(BF16)
            gain = gain_ref[...].astype(F32)
            first_ref[side, block:, :] = jnp.broadcast_to(gain, (GAIN_ROWS, gain.shape[1])).astype(BF16)
        for copy in copies:
            copy.wait()


def down_stream(meta, pieces, conv, patch_in, text, gain, weights, images):
    seq_rows, width = text.shape
    half = seq_rows // 2
    tiles = len(pieces)
    count = images * IMG_TOK
    first, second = (2, half // 2 + GAIN_ROWS, width), (2, half // 2, width)
    return pl.pallas_call(
        functools.partial(down_kernel, images, tiles, half),
        grid_spec=pltpu.PrefetchScalarGridSpec(
            num_scalar_prefetch=1,
            grid=(PATCH,),
            in_specs=[full(p.shape) for p in pieces]
            + [
                full(conv.shape),
                full((1, width)),
            ]
            + [pl.BlockSpec(memory_space=pltpu.HBM)] * 8,
            out_specs=[full(first), full(second)] + [HELD] * 6,
            scratch_shapes=[
                pltpu.VMEM((images, WL * CIN // HD + 1, TOP + HL + 16, HD), F32),
                pltpu.VMEM((TAPS, PATCH * CH), F32),
                pltpu.VMEM((TAPS, PATCH * CH), BF16),
                pltpu.VMEM((PATCH, count, TAPS), BF16),
                pltpu.VMEM((count, width), F32),
                pltpu.VMEM((PATCH, PATCH * CH, width), BF16),
                pltpu.VMEM((2, half, width), BF16),
                pltpu.SemaphoreType.DMA((6,)),
                pltpu.SemaphoreType.DMA((PATCH,)),
                pltpu.SemaphoreType.DMA((2,)),
            ],
        ),
        out_shape=[jax.ShapeDtypeStruct(first, BF16), jax.ShapeDtypeStruct(second, BF16)]
        + [pltpu.VMEM(w.shape, w.dtype) for w in weights],
        compiler_params=params(32),
        cost_estimate=cost(2 * count * PIX * CH * (256 + width), 4 << 20, count * PIX * CH),
        name="down_stream",
    )(meta, *pieces, conv, gain.reshape(1, width), patch_in, text, *weights)


def full(shape):
    return pl.BlockSpec(shape, lambda i, m: (0,) * len(shape))


def load(pieces):
    return jnp.concatenate([piece[...] for piece in pieces], axis=0)


def take_blocks(refs, count):
    return [[refs.pop(0), refs.pop(0)] for _ in range(count)]


def chip_of(meta, images, tiles, outer, entry):
    _, _, tile, mpo = split_meta(meta, images)
    return lax.rem(tile + tiles - entry // 2, tiles) * outer + lax.rem(mpo + entry % 2, outer)


def qkv_kernel(entries, layout, groups, last, meta, *refs):
    refs = list(refs)
    count = len(entries)
    x_refs = take_blocks(refs, count)
    scaled_ref = refs.pop(-1)
    if last:
        weights_ref, acc_in, square_in, head_gains = [refs.pop(0) for _ in range(4)]
    else:
        weight_refs = [refs.pop(0) for _ in range(6)]
    half, span = scaled_ref.shape
    width = weights_ref.shape[2] if last else weight_refs[0].shape[1]
    heads = width // HD
    square = square_in[...] if last else None
    if last:
        acc, outs = [None] * 6, refs
    else:
        weights_out, acc_out, square_out = refs
    for index in range(count):
        rows = pl.ds(pl.multiple_of(chip_of(meta, *layout, entries[index]) * span, span), span)
        gain = x_refs[index][0][half // 2 :, :][:1]
        for part in range(2):
            at = slice(part * half // 2, (part + 1) * half // 2)
            scaled_ref[at, :] = (x_refs[index][part][: half // 2, :] * gain).astype(BF16)
        value = jnp.concatenate([x_refs[index][0][: half // 2, :], x_refs[index][1][...]], axis=0)
        value = value.astype(F32)
        value = value * value
        for part in range(span // HD):
            piece = value[:, part * HD : (part + 1) * HD]
            square = piece if square is None else square + piece
        for part in range(6):
            if last:
                acc[part] = acc_in[part] + mxu(scaled_ref[...], weights_ref[part])
                continue
            term = mxu(scaled_ref[...], weight_refs[part][rows, :])
            if index == 0:
                acc_out[part] = term
            else:
                acc_out[part] += term
    if not last:
        square_out[...] = square
        rows = pl.ds(pl.multiple_of(chip_of(meta, *layout, len(entries)) * span, span), span)
        for part in range(6):
            weights_out[part] = weight_refs[part][rows, :]
        return
    mean = jnp.sum(square, axis=-1, keepdims=True) * (1.0 / (groups * span))
    scale = lax.rsqrt(mean + EPSILON)
    for part in range(6):
        total = acc[part] * scale
        side, kind = part // 3, part % 3
        kv_outs = outs[2 * heads * side : 2 * heads * side + heads]
        q_outs = outs[2 * heads * side + heads : 2 * heads * (side + 1)]
        for head in range(heads):
            raw = total[:, head * HD : (head + 1) * HD]
            if kind == 1:
                kv_outs[head][1] = raw.astype(BF16)
                continue
            raw = raw * lax.rsqrt(jnp.mean(raw * raw, axis=-1, keepdims=True) + EPSILON)
            if kind == 0:
                kv_outs[head][0] = (raw * head_gains[1:2, :]).astype(BF16)
            else:
                q_outs[head][...] = (raw * (head_gains[0:1, :] * HD ** (-0.5))).astype(BF16)


def qkv_step(meta, layout, blocks, entries, weights, state, head_gains):
    span = blocks[0][1].shape[1]
    half = 2 * blocks[0][1].shape[0]
    count, last = len(blocks), state is not None
    width = state[0].shape[2] if last else weights[0].shape[1]
    groups = layout[1] * layout[2]
    inputs = [p for pieces in blocks for p in pieces]
    specs = [full(p.shape) for pieces in blocks for p in pieces]
    scratch = [pltpu.VMEM((half, span), BF16)]
    if last:
        specs += [HELD] * 3 + [full(head_gains.shape)]
        inputs += list(state) + [head_gains]
        heads = width // HD
        outs = [pltpu.HBM((2, half, HD), BF16)] * heads + [pltpu.HBM((half, HD), BF16)] * heads
        outs = outs * 2
    else:
        specs += [HELD] * 6
        inputs += list(weights)
        outs = [
            pltpu.VMEM((6, span, width), BF16),
            pltpu.VMEM((6, half, width), F32),
            pltpu.VMEM((half, HD), F32),
        ]
    return pl.pallas_call(
        functools.partial(qkv_kernel, entries, layout, groups, last),
        grid_spec=pltpu.PrefetchScalarGridSpec(
            num_scalar_prefetch=1,
            grid=(1,),
            in_specs=specs,
            out_specs=[full(o.shape) if last else HELD for o in outs],
            scratch_shapes=scratch,
        ),
        out_shape=outs,
        compiler_params=params(20),
        cost_estimate=cost(12 * count * half * span * width, (6 + 2 * count) << 20),
        name="qkv_last" if last else "qkv_step",
    )(meta, *inputs)


def attention_kernel(images, pieces, half, meta, *refs):
    ctx, core, _, _ = split_meta(meta, images)
    ctxs = pieces // 2
    bases = []
    for piece in range(pieces):
        side = jnp.bitwise_xor(core, piece % 2)
        bases.append(lax.rem(ctx + ctxs - piece // 2, ctxs) * (2 * half) + side * half)
    q_refs, kv_refs, out_refs = refs[:2], refs[2 : 2 + pieces], refs[2 + pieces :]
    rows = q_refs[0].shape[0]
    step = pl.program_id(0)
    for side in range(2):
        place = bases[side] + step * rows + lax.broadcasted_iota(jnp.int32, (rows, 1), 0)
        limit = place
        for image in range(images):
            inner = place - meta[image]
            limit = jnp.where((inner >= 0) & (inner < IMG_TOK), meta[image] + IMG_TOK - 1, limit)
        for head in range(q_refs[0].shape[1] // HD):
            lanes = slice(head * HD, (head + 1) * HD)
            query = q_refs[side][:, lanes]
            scores = []
            top = None
            for piece in range(pieces):
                score = lax.dot_general(
                    query, kv_refs[piece][0, :, lanes], (((1,), (1,)), ((), ())), preferred_element_type=F32
                )
                position = lax.broadcasted_iota(jnp.int32, score.shape, 1)
                score = jnp.where(position <= limit - bases[piece], score, NEGATIVE_FILL)
                scores.append(score)
                best = jnp.max(score, axis=1, keepdims=True)
                top = best if top is None else jnp.maximum(top, best)
            total = jnp.zeros((rows, 1), F32)
            product = jnp.zeros((rows, HD), F32)
            for piece in range(pieces):
                weight = jnp.exp(scores[piece] - top)
                total = total + jnp.sum(weight, axis=1, keepdims=True)
                product = product + mxu(weight.astype(BF16), kv_refs[piece][1, :, lanes])
            out_refs[side][:, lanes] = (product / total).astype(BF16)


def attention(meta, queries, pieces, images):
    half, width = queries[0].shape
    block = 256
    keys = half * len(pieces)
    rows = pl.BlockSpec((block, width), lambda i, m: (i, 0))
    return pl.pallas_call(
        functools.partial(attention_kernel, images, len(pieces), half),
        grid_spec=pltpu.PrefetchScalarGridSpec(
            num_scalar_prefetch=1,
            grid=(half // block,),
            in_specs=[rows, rows] + [full(p.shape) for p in pieces],
            out_specs=[rows, rows],
        ),
        out_shape=[jax.ShapeDtypeStruct((half, width), BF16)] * 2,
        compiler_params=params(24),
        cost_estimate=cost(8 * half * keys * width, 4 * keys * width, 2 * half * keys * width // HD),
        name="attention",
    )(meta, *queries, *pieces)


def out_kernel(count, first, last, meta, *refs):
    refs = list(refs)
    x_refs = take_blocks(refs, count)
    weight_refs = [[refs.pop(0), refs.pop(0)] for _ in range(count)]
    if first:
        streams = [refs.pop(0), refs.pop(0)]
        block = streams[1].shape[1]
    else:
        acc_in = refs.pop(0)
    outs = refs
    for side in range(2):
        if first:
            rows = [streams[0][side, :block, :], streams[1][side]]
            total = jnp.concatenate(rows, axis=0).astype(F32)
        else:
            total = acc_in[side]
        for index in range(count):
            total = total + mxu(load(x_refs[index]), weight_refs[index][side][...])
        if last:
            outs[side][...] = total.astype(BF16)
        else:
            outs[0][side] = total


def out_step(meta, layout, blocks, entries, weights, state, last):
    span, width = blocks[0][0].shape[1], weights[0].shape[1]
    half = 2 * blocks[0][0].shape[0]
    first = isinstance(state, list)
    count = len(blocks)
    inputs = [p for pieces in blocks for p in pieces]
    specs = [full(p.shape) for p in inputs]
    for entry in entries:
        index = lambda i, m, entry=entry: (chip_of(m, *layout, entry), 0)
        inputs += weights
        specs += [pl.BlockSpec((span, width), index)] * 2
    states = state if first else [state]
    inputs += states
    specs += [full(s.shape) for s in states]
    if last:
        outs = [jax.ShapeDtypeStruct((half, width), BF16)] * 2
    else:
        outs = [jax.ShapeDtypeStruct((2, half, width), F32)]
    result = pl.pallas_call(
        functools.partial(out_kernel, count, first, last),
        grid_spec=pltpu.PrefetchScalarGridSpec(
            num_scalar_prefetch=1,
            grid=(1,),
            in_specs=specs,
            out_specs=[full(o.shape) for o in outs],
        ),
        out_shape=outs,
        compiler_params=params(24),
        cost_estimate=cost(4 * count * half * span * width, (2 + count) << 20),
        name="out_last" if last else "out_step",
    )(meta, *inputs)
    return result if last else result[0]


def pick_kernel(images, ctxs, meta, own_ref, par_ref, *out_refs):
    half = own_ref.shape[0]
    ctx, core, _, _ = split_meta(meta, images)
    for target in range(2 * ctxs):
        to_core = jnp.bitwise_xor(core, target % 2)
        slot = 2 * lax.rem(ctx + target // 2, ctxs) + to_core
        start = meta[meta[2 * images + slot]]
        place = start + lax.broadcasted_iota(jnp.int32, (IMG_TOK, half), 0)
        column = ctx * (2 * half) + lax.broadcasted_iota(jnp.int32, (IMG_TOK, half), 1)
        own = jnp.where(place == column + core * half, 1.0, 0.0).astype(BF16)
        par = jnp.where(place == column + (1 - core) * half, 1.0, 0.0).astype(BF16)
        out_refs[target][...] = (mxu(own, own_ref[...]) + mxu(par, par_ref[...])).astype(BF16)


def pick_rows(meta, own, par, images, ctxs):
    half, width = own.shape
    targets = 2 * ctxs
    return pl.pallas_call(
        functools.partial(pick_kernel, images, ctxs),
        grid_spec=pltpu.PrefetchScalarGridSpec(
            num_scalar_prefetch=1,
            grid=(1,),
            in_specs=[full(own.shape), full(par.shape)],
            out_specs=[full((IMG_TOK, width))] * targets,
        ),
        out_shape=[jax.ShapeDtypeStruct((IMG_TOK, width), BF16)] * targets,
        compiler_params=params(16),
        cost_estimate=cost(targets * 4 * IMG_TOK * half * width, 1 << 20),
        name="pick_rows",
    )(meta, own, par)


def merge_kernel(*refs):
    out_refs = refs[-2:]
    refs = refs[:-2]
    sides = refs[: len(refs) // 2], refs[len(refs) // 2 :]
    width = sides[0][0].shape[1]
    block = IMG_TOK // 2
    for side in range(2):
        total = sides[side][0][...].astype(F32)
        for part in sides[side][1:]:
            total = total + part[...].astype(F32)
        total = total.astype(BF16)
        for index in range(2):
            out_refs[index][:, side * width : (side + 1) * width] = total[index * block : (index + 1) * block]


def merge_picks(own_parts, par_parts):
    width = own_parts[0].shape[1]
    return pl.pallas_call(
        merge_kernel,
        out_shape=[jax.ShapeDtypeStruct((IMG_TOK // 2, 2 * width), BF16)] * 2,
        compiler_params=pltpu.CompilerParams(vmem_limit_bytes=8 << 20),
        cost_estimate=cost(1 << 20, 1 << 20),
        name="merge_picks",
    )(*own_parts, *par_parts)


def finish_kernel(core_ref, own_a, own_b, par_a, par_b, out_ref, sums, lines):
    core = core_ref[0]
    for side, (left, right) in enumerate(((own_a, own_b), (par_a, par_b))):
        sums[side] = left[...] + right[...]
    rows = sums.shape[1] // SIDE
    lanes = PATCH * CIN
    per = HD // lanes
    for side in range(2):
        for part in range(SIDE // per):
            cols = [sums[side, pl.ds(part * per + k, rows, stride=SIDE), :] for k in range(per)]
            for row in range(PATCH):
                pieces = [col[:, row * lanes : (row + 1) * lanes] for col in cols]
                lines[part, pl.ds(row, rows, stride=PATCH), :] = jnp.concatenate(pieces, axis=1)
        slot = jnp.bitwise_xor(core, side)
        for part in range(SIDE // per):
            out_ref[slot, :, part * HD : (part + 1) * HD] = lines[part]


def finish(core, own_a, own_b, par_a, par_b):
    count = own_a.shape[0]
    return pl.pallas_call(
        finish_kernel,
        grid_spec=pltpu.PrefetchScalarGridSpec(
            num_scalar_prefetch=1,
            grid=(1,),
            in_specs=[full(own_a.shape)] * 4,
            out_specs=full((2, count // PATCH, WL * CIN)),
            scratch_shapes=[
                pltpu.VMEM((2, count, PIX * CIN), F32),
                pltpu.VMEM((WL * CIN // HD, count // PATCH, HD), F32),
            ],
        ),
        out_shape=jax.ShapeDtypeStruct((2, count // PATCH, WL * CIN), F32),
        compiler_params=params(8),
        cost_estimate=cost(1 << 16, 1 << 18),
        name="finish",
    )(core, own_a, own_b, par_a, par_b)


def spread(active, spread_ref):
    row = lax.broadcasted_iota(jnp.int32, (IMG_TOK, PIX * CIN), 0)
    patch_row, patch_col = row >> 4, row & (SIDE - 1)
    total = None
    for index in range(9):
        down, right = index // 3 - 1, index % 3 - 1
        part = mxu(active, spread_ref[:, index * PIX * CIN : (index + 1) * PIX * CIN])
        offset = down * SIDE + right
        if offset:
            part = pltpu.roll(part, offset % IMG_TOK, 0)
        source_row, source_col = patch_row - down, patch_col - right
        inside = (source_row >= 0) & (source_row < SIDE) & (source_col >= 0) & (source_col < SIDE)
        part = jnp.where(inside, part, 0.0)
        total = part if total is None else total + part
    return total


def up_kernel(count, halves, first, last, *refs):
    refs = list(refs)
    x_refs = take_blocks(refs, count)
    weight_refs = [[[refs.pop(0) for _ in range(2)] for _ in range(halves)] for _ in range(count)]
    acc_in = None if first else refs.pop(0)
    spread_ref = refs.pop(0) if last else None
    out_ref = refs[0]
    width = x_refs[0][0].shape[1] // 2
    values = [load(pieces) for pieces in x_refs]
    totals = []
    for part in range(halves):
        total = None if first else acc_in[part]
        for block in range(count):
            for side in range(2):
                term = mxu(
                    values[block][:, side * width : (side + 1) * width],
                    weight_refs[block][part][side][0],
                )
                total = term if total is None else total + term
        totals.append(total)
        if not last:
            out_ref[part] = total
    if last:
        active = [silu(total).astype(BF16) for total in totals]
        active = jnp.concatenate(active, axis=1) if halves > 1 else active[0]
        out_ref[...] = spread(active, spread_ref)


def up_step(blocks, entries, weights, state, spread_weight):
    span = blocks[0][0].shape[1]
    halves, count = len(weights), len(blocks)
    first, last = state is None, spread_weight is not None
    whole = lambda shape: pl.BlockSpec(shape, lambda i: (0,) * len(shape))
    inputs = [p for pieces in blocks for p in pieces]
    specs = [whole(p.shape) for p in inputs]
    for entry in entries:
        for sides in weights:
            for weight in sides:
                inputs.append(weight)
                specs.append(pl.BlockSpec((1, span // 2, CH), lambda i, entry=entry: (entry, 0, 0)))
    if not first:
        inputs.append(state)
        specs.append(whole(state.shape))
    if last:
        inputs.append(spread_weight)
        specs.append(whole(spread_weight.shape))
        out = jax.ShapeDtypeStruct((IMG_TOK, PIX * CIN), F32)
    else:
        out = jax.ShapeDtypeStruct((halves, IMG_TOK, CH), F32)
    return pl.pallas_call(
        functools.partial(up_kernel, count, halves, first, last),
        grid=(1,),
        in_specs=specs,
        out_specs=whole(out.shape),
        out_shape=out,
        compiler_params=params(16),
        cost_estimate=cost(2 * count * IMG_TOK * span * CH * halves, (1 + count) << 20),
        name="up_last" if last else "up_step",
    )(*inputs)


def spread_weights(up_conv, pixels):
    taps = up_conv.reshape(9, CH, CIN).transpose(1, 0, 2).reshape(CH, 9 * CIN)
    shape = (pixels.shape[0], 9 * CIN, 9 * PIX * CIN)
    row = lax.broadcasted_iota(jnp.int32, shape, 1)
    col = lax.broadcasted_iota(jnp.int32, shape, 2)
    pixel = pixels[:, None, None]
    tap, channel = row >> 3, row & 7
    patch, target, out_channel = col >> 7, (col >> 3) & 15, col & 7
    tap_row, tap_col = tap // 3, tap % 3
    down, right = patch // 3 - 1, patch % 3 - 1
    hit = (
        (channel == out_channel)
        & ((pixel >> 2) + 1 - tap_row == (target >> 2) + PATCH * down)
        & ((pixel & 3) + 1 - tap_col == (target & 3) + PATCH * right)
    )
    placed = jnp.where(hit, 1.0, 0.0).astype(BF16)
    spread = jnp.einsum("ct,ptn->pcn", taps, placed, preferred_element_type=F32)
    return spread.astype(BF16).reshape(pixels.shape[0] * CH, 9 * PIX * CIN)


def by_core(core, own, other, axis):
    return jnp.where(
        core == 0, jnp.concatenate([own, other], axis), jnp.concatenate([other, own], axis)
    )


def shift(values, axis, step):
    count = lax.axis_size(axis)
    return lax.ppermute(values, axis, [(i, (i + step) % count) for i in range(count)])


def gather_small(latents, down_conv, *others):
    ctxs, tiles = lax.axis_size("ctx"), lax.axis_size("tile")
    every = jnp.concatenate([latents] + [shift(latents, "ctx", s) for s in range(1, ctxs)])
    conv = by_core(lax.axis_index("core"), down_conv, swap(down_conv), 1)
    conv = by_core(lax.axis_index("mpo"), conv, shift(conv, "mpo", 1), 1)
    every, others = lax.optimization_barrier((every, others))
    return [every] + [shift(every, "tile", s) for s in range(1, tiles)], conv, *others


def columns_kernel(layout, halves, meta, patch_ref, kept_ref, sent_ref, arrived):
    images, tiles, outer = layout
    ctx, _, _, mpo = split_meta(meta, images)
    size = kept_ref.shape[2]
    copies = []
    for other, out_ref in enumerate((kept_ref, sent_ref)):
        for tile in range(tiles):
            chip = tile * outer + lax.rem(mpo + other, outer)
            at = pl.multiple_of((chip * halves + (ctx if halves == 2 else 0)) * size, size)
            copies.append(
                pltpu.make_async_copy(
                    patch_ref.at[:, pl.ds(at, size)], out_ref.at[tile], arrived.at[other, tile]
                )
            )
    for copy in copies:
        copy.start()
    for copy in copies:
        copy.wait()


def transpose_first(meta, patch_out, layout, ctxs):
    images, tiles, outer = layout
    width, features = patch_out.shape
    deep = features // (tiles * outer)
    halves = 2 if ctxs == 2 and deep == 2 * CH else 1
    size = deep // halves

    place = pl.BlockSpec(memory_space=pltpu.HBM)
    kept, sent = pl.pallas_call(
        functools.partial(columns_kernel, layout, halves),
        grid_spec=pltpu.PrefetchScalarGridSpec(
            num_scalar_prefetch=1,
            grid=(1,),
            in_specs=[place],
            out_specs=[place, place],
            scratch_shapes=[pltpu.SemaphoreType.DMA((2, tiles))],
        ),
        out_shape=[pltpu.HBM((tiles, width, size), BF16)] * 2,
        compiler_params=params(8),
        cost_estimate=cost(1 << 16, 2 << 20),
        name="columns",
    )(meta, patch_out)
    return kept, sent, halves


def transpose_second(kept, received, step):
    tiles = lax.axis_size("tile")
    place = lax.rem(lax.axis_index("tile") + step, tiles)
    block = [lax.dynamic_index_in_dim(x, place, 0, keepdims=False) for x in (kept, received)]
    block = jnp.stack(block)
    return shift(block, "tile", step) if step else block


def gather_pair(first, second, state, step, extras=None):
    tiles = lax.axis_size("tile")
    found, moving = [{0: first}, {0: second}], [None, None]

    def launch(which, index):
        ring = found[which][2 * index]
        if index < tiles - 1:
            moving[which] = (shift(ring, "tile", 1), shift(ring, "mpo", 1))
        elif which:
            moving[which] = shift(found[which][2 * index - 1], "tile", 1)
        else:
            moving[which] = shift(ring, "mpo", 1)

    launch(0, 0)
    launch(1, 0)
    seen = first
    for index in range(1, tiles):
        for which in range(2):
            ring, cross = moving[which]
            ring, cross, seen = lax.optimization_barrier((ring, cross, seen))
            found[which][2 * index], found[which][2 * index - 1] = ring, cross
            seen = ring
            launch(which, index)
    entries = list(range(2 * tiles - 1))
    state = step([[found[0][e], found[1][e]] for e in entries], entries, state, False)
    last = lax.optimization_barrier((moving[0], moving[1], state, extras))
    return step([[last[0], last[1]]], [2 * tiles - 1], last[2], True), last[3]


def shards(
    text_embed,
    latents,
    down_conv,
    patch_in,
    norm_gain,
    query_weight,
    key_weight,
    value_weight,
    query_gain,
    key_gain,
    out_weight,
    patch_out,
    up_conv,
    span_start,
    image_of_slot,
):
    ctxs, tiles, outer = (lax.axis_size(name) for name in ("ctx", "tile", "mpo"))
    ctx, tile, mpo, core = (lax.axis_index(name) for name in ("ctx", "tile", "mpo", "core"))
    seq_rows, width = text_embed.shape
    half = seq_rows // 2
    images = span_start.shape[0]
    local = latents.shape[0]

    numbers = jnp.arange(images, dtype=jnp.int32)
    matches = image_of_slot[None, :] == numbers[:, None]
    slot_of_image = jnp.sum(jnp.where(matches, numbers[None, :], 0), axis=1)
    slot_place = lax.rem(ctx + ctxs - slot_of_image // local, ctxs) * local + slot_of_image % local
    meta = jnp.concatenate(
        [span_start, slot_place, image_of_slot, jnp.stack([ctx, core, tile, mpo])]
    ).astype(jnp.int32)
    layout = (images, tiles, outer)

    weights = [swap(w) for w in (key_weight, value_weight, query_weight)]
    pieces, conv, meta, weights[0], weights[1] = gather_small(latents, down_conv, meta, *weights[:2])
    later, pieces[1] = lax.optimization_barrier((meta, pieces[1]))
    kept, sent, halves = transpose_first(later, patch_out, layout, ctxs)
    pieces, sent = lax.optimization_barrier((pieces, sent))
    received = shift(sent, "mpo", 1)
    weights += [key_weight, value_weight, query_weight]
    streams = down_stream(meta, pieces, conv, patch_in, text_embed, norm_gain, weights, images)
    streams, held_weights = streams[:2], streams[2:]
    streams, received = lax.optimization_barrier((streams, received))
    others = [swap(s[1]) for s in streams]
    others = lax.optimization_barrier(others)

    head_gains = jnp.stack([query_gain, key_gain])

    def project(blocks, entries, state, last):
        return qkv_step(
            meta, layout, blocks, entries, held_weights, state, head_gains
        )

    state, out_par = gather_pair(
        *[by_core(core, s[0], o, 1) for s, o in zip(streams, others)], None, project, swap(out_weight)
    )
    heads = width // HD
    kv_send, q_send = state[:heads], state[heads : 2 * heads]
    kv_own, q_own = state[2 * heads : 3 * heads], state[3 * heads :]

    def shifted(values, step, cross):
        pairs = [
            (2 * c + k, 2 * ((c + step) % ctxs) + (1 - k if cross else k))
            for c in range(ctxs)
            for k in range(2)
        ]
        return lax.ppermute(values, ("ctx", "core"), pairs)

    results = []
    for head in range(heads):
        q_par = swap(q_send[head])
        pieces = [kv_own[head], swap(kv_send[head])]
        for step in range(1, ctxs):
            pieces += [shifted(kv_own[head], step, False), shifted(kv_send[head], step, True)]
        q_par, q_send, kv_send, kv_own, kept, received = lax.optimization_barrier(
            (q_par, q_send, kv_send, kv_own, kept, received)
        )
        results.append(attention(meta, [q_own[head], q_par], pieces, images))
    up_blocks = [transpose_second(kept, received, step) for step in range(tiles)]
    att_own = [result[0] for result in results]
    att_par = [swap(result[1]) for result in results]
    rows = half // 2
    attended = []
    for at in (0, rows):
        own, par = (
            jnp.concatenate([x[at : at + rows] for x in side], axis=1) for side in (att_own, att_par)
        )
        attended.append(by_core(core, own, par, 1))
    attended, up_blocks = lax.optimization_barrier((attended, up_blocks))
    up_own = jnp.concatenate(up_blocks)
    extras = [up_own, swap(up_own)] + ([shift(up_own, "ctx", 1)] if halves == 2 else [])

    def project_out(blocks, entries, state, last):
        return out_step(meta, layout, blocks, entries, (out_weight, out_par), state, last)

    state = [jnp.stack([s[0], o]) for s, o in zip(streams, others)]
    state, up_weights = gather_pair(*attended, state, project_out, extras)
    out_own, out_send = state
    out_other = swap(out_send)
    layer_out = by_core(core, out_own, out_other, 0)

    picks, swapped = lax.optimization_barrier(
        (pick_rows(meta, out_own, out_other, images, ctxs), [swap(other) for other in up_weights[2:]])
    )
    up_weights = [up_weights[:2]] + [[up_weights[2], other] for other in swapped]
    own_parts, par_parts = [picks[0]], [swap(picks[1])]
    for step in range(1, ctxs):
        own_parts.append(shifted(picks[2 * step], step, False))
        par_parts.append(shifted(picks[2 * step + 1], step, True))

    pixel = tile * outer + mpo
    pixels = jnp.stack([pixel * halves + lax.rem(ctx + h, halves) for h in range(halves)])
    spread_weight = spread_weights(up_conv, pixels)

    def project_up(blocks, entries, state, last):
        return up_step(blocks, entries, up_weights, state, spread_weight if last else None)

    state, _ = gather_pair(*merge_picks(own_parts, par_parts), None, project_up)

    bands = state.reshape(tiles, IMG_TOK // tiles, PIX * CIN)
    band = lax.dynamic_index_in_dim(bands, tile, 0, keepdims=False)
    for step in range(1, tiles):
        piece = lax.dynamic_index_in_dim(bands, lax.rem(tile + step, tiles), 0, keepdims=False)
        band = band + shift(piece, "tile", step)
    quad = {}
    for name, pairs in (
        ("mpo", [(0, 2), (1, 3), (2, 0), (3, 1)]),
        ("core", [(0, 1), (1, 0), (2, 3), (3, 2)]),
        ("both", [(0, 3), (1, 2), (2, 1), (3, 0)]),
    ):
        quad[name] = lax.ppermute(band, ("mpo", "core"), pairs)
    return layer_out, finish(meta[3 * images + 1 :], band, quad["mpo"], quad["core"], quad["both"])


def solution(mesh):
    ctxs, tiles, parts = mesh.devices.shape
    fine = Mesh(
        mesh.devices.reshape(ctxs, tiles, parts // 2, 2), ("ctx", "tile", "mpo", "core")
    )
    features = ("tile", "mpo", "core")
    return jax.shard_map(
        shards,
        mesh=fine,
        in_specs=(
            P("ctx", features),
            P("ctx", "tile", None),
            P(None, ("mpo", "core")),
            P(None, features),
            P(features),
            P(None, features),
            P(None, features),
            P(None, features),
            P(),
            P(),
            P(None, features),
            P(features, None),
            P(),
            P(),
            P(),
        ),
        out_specs=(P("ctx", features), P("ctx", "tile", None)),
        check_vma=False,
    )
```

```python
import functools

import jax
import jax.numpy as jnp
from jax import lax
from jax.experimental import pallas as pl
from jax.experimental.pallas import tpu as pltpu
from jax.sharding import Mesh
from jax.sharding import PartitionSpec as P

HD = 128
CH = 256
CIN = 8
WL = 64
HL = 64
PATCH = 4
PIX = PATCH * PATCH
SIDE = WL // PATCH
IMG_TOK = 256
EPSILON = 1e-05
NEGATIVE_FILL = -1e30
WINDOW = (PATCH + 2) * CIN
TAPS = 3 * WINDOW
BF16 = jnp.bfloat16
F32 = jnp.float32


def split_meta(meta, images):
    return meta[3 * images], meta[3 * images + 1], meta[3 * images + 2], meta[3 * images + 3]


def params(mebibytes):
    return pltpu.CompilerParams(
        dimension_semantics=("arbitrary",), vmem_limit_bytes=mebibytes * 1024 * 1024
    )


def cost(flops, nbytes, transcendentals=0):
    return pl.CostEstimate(
        flops=int(flops), bytes_accessed=int(nbytes), transcendentals=int(transcendentals)
    )


def silu(values):
    half = values * 0.5
    return half + half * jnp.tanh(half)


def mxu(left, right):
    return jnp.dot(left, right, preferred_element_type=F32)


def swap(values):
    return lax.ppermute(values, "core", [(0, 1), (1, 0)])


HELD = pl.BlockSpec(memory_space=pltpu.VMEM)


def in_hbm(values):
    return pltpu.with_memory_space_constraint(values, pltpu.HBM)


GAIN_ROWS = 16
TOP = 16


def down_kernel(images, tiles, half, meta, *refs):
    lat_refs, refs = refs[:tiles], refs[tiles:]
    conv_ref, gain_ref, patch_hbm, text_hbm = refs[:4]
    weight_refs, first_refs, second_refs, held_refs = refs[4:10], refs[10:12], refs[12:14], refs[14:20]
    grid_rows, conv_wide, conv_bf16, windows, total, patch_ref, text_ref = refs[20:27]
    arrived, patch_arrived, text_arrived = refs[27:]
    step = pl.program_id(0)
    deep = PATCH * CH
    patch_copies = [
        pltpu.make_async_copy(
            patch_hbm.at[index * deep : (index + 1) * deep, :], patch_ref.at[index], patch_arrived.at[index]
        )
        for index in range(PATCH)
    ]
    side_rows = [jnp.bitwise_xor(meta[3 * images + 1], side) * half for side in range(2)]
    text_copies = [
        pltpu.make_async_copy(
            text_hbm.at[pl.ds(pl.multiple_of(side_rows[side], half), half), :],
            text_ref.at[side],
            text_arrived.at[side],
        )
        for side in range(2)
    ]
    copies = [
        pltpu.make_async_copy(weight, held, arrived.at[index])
        for index, (weight, held) in enumerate(zip(weight_refs, held_refs))
    ]

    @pl.when(step == 0)
    def _():
        for copy in patch_copies + text_copies + copies:
            copy.start()

    group = images * SIDE
    ctx, core, tile, _ = split_meta(meta, images)

    @pl.when(step == 0)
    def _():
        grid_rows[...] = jnp.zeros_like(grid_rows)
        blocks = grid_rows.shape[1]
        for index in range(tiles):
            band = lat_refs[index].shape[1]
            at = TOP + lax.rem(tile + tiles - index, tiles) * band
            rows = pl.ds(pl.multiple_of(at, 8), band)
            latent = lat_refs[index][...].astype(F32)
            edges = [jnp.zeros((images, band, size), F32) for size in (CIN, HD - CIN)]
            wide = jnp.concatenate([edges[0], latent, edges[1]], axis=2)
            for part in range(blocks):
                grid_rows[:, part, rows, :] = wide[:, :, part * HD : (part + 1) * HD]
        conv_wide[...] = jnp.zeros_like(conv_wide)
        conv = conv_ref[...].astype(F32)
        for col in range(PATCH):
            for tap in range(3):
                at = WINDOW * tap + CIN * col
                conv_wide[at : at + 3 * CIN, CH * col : CH * (col + 1)] = conv[
                    3 * CIN * tap : 3 * CIN * (tap + 1), :
                ]
        conv_bf16[...] = conv_wide[...].astype(BF16)

        def build(image, carry):
            for row in range(PATCH + 2):
                take = pl.ds(TOP - 1 + row, SIDE, stride=PATCH)
                line = [grid_rows[image, part, take, :] for part in range(blocks)]
                line = jnp.concatenate(line, axis=1).astype(BF16)
                for col in range(SIDE):
                    piece = line[:, PATCH * CIN * col : PATCH * CIN * col + WINDOW]
                    at = pl.ds(pl.multiple_of(group * col + image * SIDE, SIDE), SIDE)
                    for shift in range(3):
                        if 0 <= row - shift < PATCH:
                            windows[row - shift, at, WINDOW * shift : WINDOW * (shift + 1)] = piece
            return carry

        lax.fori_loop(0, images, build, 0)
        total[...] = jnp.zeros_like(total)

    for index in range(PATCH):
        pl.when(step == index)(patch_copies[index].wait)

    chunk = 256
    for part in range(images * IMG_TOK // chunk):
        rows = slice(part * chunk, (part + 1) * chunk)
        hidden = silu(mxu(windows[step, rows, :], conv_bf16[...])).astype(BF16)
        total[rows, :] += mxu(hidden, patch_ref[step])

    @pl.when(step == PATCH - 1)
    def _():
        tokens = total[...].astype(BF16)
        block = half // 2
        for copy in text_copies:
            copy.wait()
        for side in range(2):
            base = ctx * (2 * half) + jnp.bitwise_xor(core, side) * half
            for part, out_ref in enumerate((first_refs[side], second_refs[side])):
                place = base + part * block + lax.broadcasted_iota(jnp.int32, (block, 1), 0)
                source = jnp.full((block, 1), -1, jnp.int32)
                for image in range(images):
                    inner = place - meta[image]
                    inside = (inner >= 0) & (inner < IMG_TOK)
                    index = (inner & (SIDE - 1)) * group + meta[images + image] * SIDE + (inner >> 4)
                    source = jnp.where(inside, index, source)
                choice = source == lax.broadcasted_iota(jnp.int32, (block, images * IMG_TOK), 1)
                picked = mxu(jnp.where(choice, 1.0, 0.0).astype(BF16), tokens)
                text = text_ref[side, part * block : (part + 1) * block, :].astype(F32)
                out_ref[:block, :] = jnp.where(source >= 0, picked, text).astype(BF16)
            gain = gain_ref[...].astype(F32)
            first_refs[side][block:, :] = jnp.broadcast_to(gain, (GAIN_ROWS, gain.shape[1])).astype(BF16)
        for copy in copies:
            copy.wait()


def down_stream(meta, pieces, conv, patch_in, text, gain, weights, images):
    seq_rows, width = text.shape
    half = seq_rows // 2
    tiles = len(pieces)
    count = images * IMG_TOK
    first, second = (half // 2 + GAIN_ROWS, width), (half // 2, width)
    pieces_out = [first, first, second, second]
    return pl.pallas_call(
        functools.partial(down_kernel, images, tiles, half),
        grid_spec=pltpu.PrefetchScalarGridSpec(
            num_scalar_prefetch=1,
            grid=(PATCH,),
            in_specs=[full(p.shape) for p in pieces]
            + [
                full(conv.shape),
                full((1, width)),
            ]
            + [pl.BlockSpec(memory_space=pltpu.HBM)] * 8,
            out_specs=[full(shape) for shape in pieces_out] + [HELD] * 6,
            scratch_shapes=[
                pltpu.VMEM((images, WL * CIN // HD + 1, TOP + HL + 16, HD), F32),
                pltpu.VMEM((TAPS, PATCH * CH), F32),
                pltpu.VMEM((TAPS, PATCH * CH), BF16),
                pltpu.VMEM((PATCH, count, TAPS), BF16),
                pltpu.VMEM((count, width), F32),
                pltpu.VMEM((PATCH, PATCH * CH, width), BF16),
                pltpu.VMEM((2, half, width), BF16),
                pltpu.SemaphoreType.DMA((6,)),
                pltpu.SemaphoreType.DMA((PATCH,)),
                pltpu.SemaphoreType.DMA((2,)),
            ],
        ),
        out_shape=[jax.ShapeDtypeStruct(shape, BF16) for shape in pieces_out]
        + [pltpu.VMEM(w.shape, w.dtype) for w in weights],
        compiler_params=params(32),
        cost_estimate=cost(2 * count * PIX * CH * (256 + width), 4 << 20, count * PIX * CH),
        name="down_stream",
    )(meta, *pieces, conv, gain.reshape(1, width), in_hbm(patch_in), in_hbm(text), *[in_hbm(w) for w in weights])


def full(shape):
    return pl.BlockSpec(shape, lambda i, m: (0,) * len(shape))


def load(pieces):
    return jnp.concatenate([piece[...] for piece in pieces], axis=0)


def take_blocks(refs, count):
    return [[refs.pop(0), refs.pop(0)] for _ in range(count)]


def chip_of(meta, images, tiles, outer, entry):
    _, _, tile, mpo = split_meta(meta, images)
    return lax.rem(tile + tiles - entry // 2, tiles) * outer + lax.rem(mpo + entry % 2, outer)


def qkv_kernel(entries, layout, groups, last, meta, *refs):
    refs = list(refs)
    count = len(entries)
    x_refs = take_blocks(refs, count)
    scaled_ref = refs.pop(-1)
    if last:
        weights_ref, acc_in, square_in, head_gains = [refs.pop(0) for _ in range(4)]
    else:
        weight_refs = [refs.pop(0) for _ in range(6)]
    half, span = scaled_ref.shape
    width = weights_ref.shape[2] if last else weight_refs[0].shape[1]
    heads = width // HD
    square = square_in[...] if last else None
    if last:
        acc, outs = [None] * 6, refs
    else:
        weights_out, acc_out, square_out = refs
    for index in range(count):
        rows = pl.ds(pl.multiple_of(chip_of(meta, *layout, entries[index]) * span, span), span)
        gain = x_refs[index][0][half // 2 :, :][:1]
        for part in range(2):
            at = slice(part * half // 2, (part + 1) * half // 2)
            scaled_ref[at, :] = (x_refs[index][part][: half // 2, :] * gain).astype(BF16)
        value = jnp.concatenate([x_refs[index][0][: half // 2, :], x_refs[index][1][...]], axis=0)
        value = value.astype(F32)
        value = value * value
        for part in range(span // HD):
            piece = value[:, part * HD : (part + 1) * HD]
            square = piece if square is None else square + piece
        for part in range(6):
            if last:
                acc[part] = acc_in[part] + mxu(scaled_ref[...], weights_ref[part])
                continue
            term = mxu(scaled_ref[...], weight_refs[part][rows, :])
            if index == 0:
                acc_out[part] = term
            else:
                acc_out[part] += term
    if not last:
        square_out[...] = square
        rows = pl.ds(pl.multiple_of(chip_of(meta, *layout, len(entries)) * span, span), span)
        for part in range(6):
            weights_out[part] = weight_refs[part][rows, :]
        return
    mean = jnp.sum(square, axis=-1, keepdims=True) * (1.0 / (groups * span))
    scale = lax.rsqrt(mean + EPSILON)
    for part in range(6):
        total = acc[part] * scale
        side, kind = part // 3, part % 3
        kv_outs = outs[2 * heads * side : 2 * heads * side + heads]
        q_outs = outs[2 * heads * side + heads : 2 * heads * (side + 1)]
        for head in range(heads):
            raw = total[:, head * HD : (head + 1) * HD]
            if kind == 1:
                kv_outs[head][1] = raw.astype(BF16)
                continue
            raw = raw * lax.rsqrt(jnp.mean(raw * raw, axis=-1, keepdims=True) + EPSILON)
            if kind == 0:
                kv_outs[head][0] = (raw * head_gains[1:2, :]).astype(BF16)
            else:
                q_outs[head][...] = (raw * (head_gains[0:1, :] * HD ** (-0.5))).astype(BF16)


def qkv_step(meta, layout, blocks, entries, weights, state, head_gains):
    span = blocks[0][1].shape[1]
    half = 2 * blocks[0][1].shape[0]
    count, last = len(blocks), state is not None
    width = state[0].shape[2] if last else weights[0].shape[1]
    groups = layout[1] * layout[2]
    inputs = [p for pieces in blocks for p in pieces]
    specs = [full(p.shape) for pieces in blocks for p in pieces]
    scratch = [pltpu.VMEM((half, span), BF16)]
    if last:
        specs += [HELD] * 3 + [full(head_gains.shape)]
        inputs += list(state) + [head_gains]
        heads = width // HD
        outs = [pltpu.HBM((2, half, HD), BF16)] * heads + [pltpu.HBM((half, HD), BF16)] * heads
        outs = outs * 2
    else:
        specs += [HELD] * 6
        inputs += list(weights)
        outs = [
            pltpu.VMEM((6, span, width), BF16),
            pltpu.VMEM((6, half, width), F32),
            pltpu.VMEM((half, HD), F32),
        ]
    return pl.pallas_call(
        functools.partial(qkv_kernel, entries, layout, groups, last),
        grid_spec=pltpu.PrefetchScalarGridSpec(
            num_scalar_prefetch=1,
            grid=(1,),
            in_specs=specs,
            out_specs=[full(o.shape) if last else HELD for o in outs],
            scratch_shapes=scratch,
        ),
        out_shape=outs,
        compiler_params=params(20),
        cost_estimate=cost(12 * count * half * span * width, (6 + 2 * count) << 20),
        name="qkv_last" if last else "qkv_step",
    )(meta, *inputs)


def attention_kernel(images, pieces, half, meta, *refs):
    ctx, core, _, _ = split_meta(meta, images)
    ctxs = pieces // 2
    bases = []
    for piece in range(pieces):
        side = jnp.bitwise_xor(core, piece % 2)
        bases.append(lax.rem(ctx + ctxs - piece // 2, ctxs) * (2 * half) + side * half)
    q_refs, kv_refs, out_refs = refs[:2], refs[2 : 2 + pieces], refs[2 + pieces :]
    rows = q_refs[0].shape[0]
    step = pl.program_id(0)
    for side in range(2):
        place = bases[side] + step * rows + lax.broadcasted_iota(jnp.int32, (rows, 1), 0)
        limit = place
        for image in range(images):
            inner = place - meta[image]
            limit = jnp.where((inner >= 0) & (inner < IMG_TOK), meta[image] + IMG_TOK - 1, limit)
        for head in range(q_refs[0].shape[1] // HD):
            lanes = slice(head * HD, (head + 1) * HD)
            query = q_refs[side][:, lanes]
            scores = []
            top = None
            for piece in range(pieces):
                score = lax.dot_general(
                    query, kv_refs[piece][0, :, lanes], (((1,), (1,)), ((), ())), preferred_element_type=F32
                )
                position = lax.broadcasted_iota(jnp.int32, score.shape, 1)
                score = jnp.where(position <= limit - bases[piece], score, NEGATIVE_FILL)
                scores.append(score)
                best = jnp.max(score, axis=1, keepdims=True)
                top = best if top is None else jnp.maximum(top, best)
            total = jnp.zeros((rows, 1), F32)
            product = jnp.zeros((rows, HD), F32)
            for piece in range(pieces):
                weight = jnp.exp(scores[piece] - top)
                total = total + jnp.sum(weight, axis=1, keepdims=True)
                product = product + mxu(weight.astype(BF16), kv_refs[piece][1, :, lanes])
            out_refs[side][:, lanes] = (product / total).astype(BF16)


def attention(meta, queries, pieces, images):
    half, width = queries[0].shape
    block = 256
    keys = half * len(pieces)
    rows = pl.BlockSpec((block, width), lambda i, m: (i, 0))
    return pl.pallas_call(
        functools.partial(attention_kernel, images, len(pieces), half),
        grid_spec=pltpu.PrefetchScalarGridSpec(
            num_scalar_prefetch=1,
            grid=(half // block,),
            in_specs=[rows, rows] + [full(p.shape) for p in pieces],
            out_specs=[rows, rows],
        ),
        out_shape=[jax.ShapeDtypeStruct((half, width), BF16)] * 2,
        compiler_params=params(24),
        cost_estimate=cost(8 * half * keys * width, 4 * keys * width, 2 * half * keys * width // HD),
        name="attention",
    )(meta, *queries, *pieces)


def out_kernel(count, first, last, meta, *refs):
    refs = list(refs)
    x_refs = take_blocks(refs, count)
    weight_refs = [[refs.pop(0), refs.pop(0)] for _ in range(count)]
    if first:
        streams = [refs.pop(0) for _ in range(4)]
        block = streams[1].shape[0]
    else:
        acc_in = refs.pop(0)
    outs = refs
    for side in range(2):
        if first:
            rows = [streams[2 * side][:block, :], streams[2 * side + 1][...]]
            total = jnp.concatenate(rows, axis=0).astype(F32)
        else:
            total = acc_in[side]
        for index in range(count):
            total = total + mxu(load(x_refs[index]), weight_refs[index][side][...])
        if last:
            outs[side][...] = total.astype(BF16)
        else:
            outs[0][side] = total


def out_step(meta, layout, blocks, entries, weights, state, last):
    span, width = blocks[0][0].shape[1], weights[0].shape[1]
    half = 2 * blocks[0][0].shape[0]
    first = isinstance(state, list)
    count = len(blocks)
    inputs = [p for pieces in blocks for p in pieces]
    specs = [full(p.shape) for p in inputs]
    for entry in entries:
        index = lambda i, m, entry=entry: (chip_of(m, *layout, entry), 0)
        inputs += weights
        specs += [pl.BlockSpec((span, width), index)] * 2
    states = state if first else [state]
    inputs += states
    specs += [full(s.shape) for s in states]
    if last:
        outs = [jax.ShapeDtypeStruct((half, width), BF16)] * 2
    else:
        outs = [jax.ShapeDtypeStruct((2, half, width), F32)]
    result = pl.pallas_call(
        functools.partial(out_kernel, count, first, last),
        grid_spec=pltpu.PrefetchScalarGridSpec(
            num_scalar_prefetch=1,
            grid=(1,),
            in_specs=specs,
            out_specs=[full(o.shape) for o in outs],
        ),
        out_shape=outs,
        compiler_params=params(24),
        cost_estimate=cost(4 * count * half * span * width, (2 + count) << 20),
        name="out_last" if last else "out_step",
    )(meta, *inputs)
    return result if last else result[0]


def pick_kernel(images, ctxs, meta, own_ref, par_ref, *out_refs):
    half = own_ref.shape[0]
    ctx, core, _, _ = split_meta(meta, images)
    for target in range(2 * ctxs):
        to_core = jnp.bitwise_xor(core, target % 2)
        slot = 2 * lax.rem(ctx + target // 2, ctxs) + to_core
        start = meta[meta[2 * images + slot]]
        place = start + lax.broadcasted_iota(jnp.int32, (IMG_TOK, half), 0)
        column = ctx * (2 * half) + lax.broadcasted_iota(jnp.int32, (IMG_TOK, half), 1)
        own = jnp.where(place == column + core * half, 1.0, 0.0).astype(BF16)
        par = jnp.where(place == column + (1 - core) * half, 1.0, 0.0).astype(BF16)
        out_refs[target][...] = (mxu(own, own_ref[...]) + mxu(par, par_ref[...])).astype(BF16)


def pick_rows(meta, own, par, images, ctxs):
    half, width = own.shape
    targets = 2 * ctxs
    return pl.pallas_call(
        functools.partial(pick_kernel, images, ctxs),
        grid_spec=pltpu.PrefetchScalarGridSpec(
            num_scalar_prefetch=1,
            grid=(1,),
            in_specs=[full(own.shape), full(par.shape)],
            out_specs=[full((IMG_TOK, width))] * targets,
        ),
        out_shape=[jax.ShapeDtypeStruct((IMG_TOK, width), BF16)] * targets,
        compiler_params=params(16),
        cost_estimate=cost(targets * 4 * IMG_TOK * half * width, 1 << 20),
        name="pick_rows",
    )(meta, own, par)


def merge_kernel(*refs):
    out_refs = refs[-2:]
    refs = refs[:-2]
    sides = refs[: len(refs) // 2], refs[len(refs) // 2 :]
    width = sides[0][0].shape[1]
    block = IMG_TOK // 2
    for side in range(2):
        total = sides[side][0][...].astype(F32)
        for part in sides[side][1:]:
            total = total + part[...].astype(F32)
        total = total.astype(BF16)
        for index in range(2):
            out_refs[index][:, side * width : (side + 1) * width] = total[index * block : (index + 1) * block]


def merge_picks(own_parts, par_parts):
    width = own_parts[0].shape[1]
    return pl.pallas_call(
        merge_kernel,
        out_shape=[jax.ShapeDtypeStruct((IMG_TOK // 2, 2 * width), BF16)] * 2,
        compiler_params=pltpu.CompilerParams(vmem_limit_bytes=8 << 20),
        cost_estimate=cost(1 << 20, 1 << 20),
        name="merge_picks",
    )(*own_parts, *par_parts)


def finish_kernel(core_ref, own_a, own_b, par_a, par_b, out_ref, sums, lines):
    core = core_ref[0]
    for side, (left, right) in enumerate(((own_a, own_b), (par_a, par_b))):
        sums[side] = left[...] + right[...]
    rows = sums.shape[1] // SIDE
    lanes = PATCH * CIN
    per = HD // lanes
    for side in range(2):
        for part in range(SIDE // per):
            cols = [sums[side, pl.ds(part * per + k, rows, stride=SIDE), :] for k in range(per)]
            for row in range(PATCH):
                pieces = [col[:, row * lanes : (row + 1) * lanes] for col in cols]
                lines[part, pl.ds(row, rows, stride=PATCH), :] = jnp.concatenate(pieces, axis=1)
        slot = jnp.bitwise_xor(core, side)
        for part in range(SIDE // per):
            out_ref[slot, :, part * HD : (part + 1) * HD] = lines[part]


def finish(core, own_a, own_b, par_a, par_b):
    count = own_a.shape[0]
    return pl.pallas_call(
        finish_kernel,
        grid_spec=pltpu.PrefetchScalarGridSpec(
            num_scalar_prefetch=1,
            grid=(1,),
            in_specs=[full(own_a.shape)] * 4,
            out_specs=full((2, count // PATCH, WL * CIN)),
            scratch_shapes=[
                pltpu.VMEM((2, count, PIX * CIN), F32),
                pltpu.VMEM((WL * CIN // HD, count // PATCH, HD), F32),
            ],
        ),
        out_shape=jax.ShapeDtypeStruct((2, count // PATCH, WL * CIN), F32),
        compiler_params=params(8),
        cost_estimate=cost(1 << 16, 1 << 18),
        name="finish",
    )(core, own_a, own_b, par_a, par_b)


def spread(active, spread_ref):
    row = lax.broadcasted_iota(jnp.int32, (IMG_TOK, PIX * CIN), 0)
    patch_row, patch_col = row >> 4, row & (SIDE - 1)
    total = None
    for index in range(9):
        down, right = index // 3 - 1, index % 3 - 1
        part = mxu(active, spread_ref[:, index * PIX * CIN : (index + 1) * PIX * CIN])
        offset = down * SIDE + right
        if offset:
            part = pltpu.roll(part, offset % IMG_TOK, 0)
        source_row, source_col = patch_row - down, patch_col - right
        inside = (source_row >= 0) & (source_row < SIDE) & (source_col >= 0) & (source_col < SIDE)
        part = jnp.where(inside, part, 0.0)
        total = part if total is None else total + part
    return total


def up_kernel(count, halves, first, last, *refs):
    refs = list(refs)
    x_refs = take_blocks(refs, count)
    weight_refs = [[[refs.pop(0) for _ in range(2)] for _ in range(halves)] for _ in range(count)]
    acc_in = None if first else refs.pop(0)
    spread_ref = refs.pop(0) if last else None
    out_ref = refs[0]
    width = x_refs[0][0].shape[1] // 2
    values = [load(pieces) for pieces in x_refs]
    totals = []
    for part in range(halves):
        total = None if first else acc_in[part]
        for block in range(count):
            for side in range(2):
                term = mxu(
                    values[block][:, side * width : (side + 1) * width],
                    weight_refs[block][part][side][0],
                )
                total = term if total is None else total + term
        totals.append(total)
        if not last:
            out_ref[part] = total
    if last:
        active = [silu(total).astype(BF16) for total in totals]
        active = jnp.concatenate(active, axis=1) if halves > 1 else active[0]
        out_ref[...] = spread(active, spread_ref)


def up_step(blocks, entries, weights, state, spread_weight):
    span = blocks[0][0].shape[1]
    halves, count = len(weights), len(blocks)
    first, last = state is None, spread_weight is not None
    whole = lambda shape: pl.BlockSpec(shape, lambda i: (0,) * len(shape))
    inputs = [p for pieces in blocks for p in pieces]
    specs = [whole(p.shape) for p in inputs]
    for entry in entries:
        for sides in weights:
            for weight in sides:
                inputs.append(weight)
                specs.append(pl.BlockSpec((1, span // 2, CH), lambda i, entry=entry: (entry, 0, 0)))
    if not first:
        inputs.append(state)
        specs.append(whole(state.shape))
    if last:
        inputs.append(spread_weight)
        specs.append(whole(spread_weight.shape))
        out = jax.ShapeDtypeStruct((IMG_TOK, PIX * CIN), F32)
    else:
        out = jax.ShapeDtypeStruct((halves, IMG_TOK, CH), F32)
    return pl.pallas_call(
        functools.partial(up_kernel, count, halves, first, last),
        grid=(1,),
        in_specs=specs,
        out_specs=whole(out.shape),
        out_shape=out,
        compiler_params=params(16),
        cost_estimate=cost(2 * count * IMG_TOK * span * CH * halves, (1 + count) << 20),
        name="up_last" if last else "up_step",
    )(*inputs)


def spread_weights(up_conv, pixels):
    taps = up_conv.reshape(9, CH, CIN).transpose(1, 0, 2).reshape(CH, 9 * CIN)
    shape = (pixels.shape[0], 9 * CIN, 9 * PIX * CIN)
    row = lax.broadcasted_iota(jnp.int32, shape, 1)
    col = lax.broadcasted_iota(jnp.int32, shape, 2)
    pixel = pixels[:, None, None]
    tap, channel = row >> 3, row & 7
    patch, target, out_channel = col >> 7, (col >> 3) & 15, col & 7
    tap_row, tap_col = tap // 3, tap % 3
    down, right = patch // 3 - 1, patch % 3 - 1
    hit = (
        (channel == out_channel)
        & ((pixel >> 2) + 1 - tap_row == (target >> 2) + PATCH * down)
        & ((pixel & 3) + 1 - tap_col == (target & 3) + PATCH * right)
    )
    placed = jnp.where(hit, 1.0, 0.0).astype(BF16)
    spread = jnp.einsum("ct,ptn->pcn", taps, placed, preferred_element_type=F32)
    return spread.astype(BF16).reshape(pixels.shape[0] * CH, 9 * PIX * CIN)


def by_core(core, own, other, axis):
    return jnp.where(
        core == 0, jnp.concatenate([own, other], axis), jnp.concatenate([other, own], axis)
    )


def shift(values, axis, step):
    count = lax.axis_size(axis)
    return lax.ppermute(values, axis, [(i, (i + step) % count) for i in range(count)])


def gather_small(latents, down_conv, *others):
    ctxs, tiles = lax.axis_size("ctx"), lax.axis_size("tile")
    every = jnp.concatenate([latents] + [shift(latents, "ctx", s) for s in range(1, ctxs)])
    conv = by_core(lax.axis_index("core"), down_conv, swap(down_conv), 1)
    conv = by_core(lax.axis_index("mpo"), conv, shift(conv, "mpo", 1), 1)
    every, others = lax.optimization_barrier((every, others))
    return [every] + [shift(every, "tile", s) for s in range(1, tiles)], conv, *others


def columns_kernel(layout, halves, meta, patch_ref, kept_ref, sent_ref, arrived):
    images, tiles, outer = layout
    ctx, _, _, mpo = split_meta(meta, images)
    size = kept_ref.shape[2]
    copies = []
    for other, out_ref in enumerate((kept_ref, sent_ref)):
        for tile in range(tiles):
            chip = tile * outer + lax.rem(mpo + other, outer)
            at = pl.multiple_of((chip * halves + (ctx if halves == 2 else 0)) * size, size)
            copies.append(
                pltpu.make_async_copy(
                    patch_ref.at[:, pl.ds(at, size)], out_ref.at[tile], arrived.at[other, tile]
                )
            )
    for copy in copies:
        copy.start()
    for copy in copies:
        copy.wait()


def transpose_first(meta, patch_out, layout, ctxs):
    images, tiles, outer = layout
    width, features = patch_out.shape
    deep = features // (tiles * outer)
    halves = 2 if ctxs == 2 and deep == 2 * CH else 1
    size = deep // halves

    place = pl.BlockSpec(memory_space=pltpu.HBM)
    kept, sent = pl.pallas_call(
        functools.partial(columns_kernel, layout, halves),
        grid_spec=pltpu.PrefetchScalarGridSpec(
            num_scalar_prefetch=1,
            grid=(1,),
            in_specs=[place],
            out_specs=[place, place],
            scratch_shapes=[pltpu.SemaphoreType.DMA((2, tiles))],
        ),
        out_shape=[pltpu.HBM((tiles, width, size), BF16)] * 2,
        compiler_params=params(8),
        cost_estimate=cost(1 << 16, 2 << 20),
        name="columns",
    )(meta, in_hbm(patch_out))
    return kept, sent, halves


def transpose_second(kept, received, step):
    tiles = lax.axis_size("tile")
    place = lax.rem(lax.axis_index("tile") + step, tiles)
    block = [lax.dynamic_index_in_dim(x, place, 0, keepdims=False) for x in (kept, received)]
    block = jnp.stack(block)
    return shift(block, "tile", step) if step else block


def gather_pair(first, second, state, step, extras=None):
    tiles = lax.axis_size("tile")
    found, moving = [{0: first}, {0: second}], [None, None]

    def launch(which, index):
        ring = found[which][2 * index]
        if index < tiles - 1:
            moving[which] = (shift(ring, "tile", 1), shift(ring, "mpo", 1))
        elif which:
            moving[which] = shift(found[which][2 * index - 1], "tile", 1)
        else:
            moving[which] = shift(ring, "mpo", 1)

    launch(0, 0)
    launch(1, 0)
    seen = first
    for index in range(1, tiles):
        for which in range(2):
            ring, cross = moving[which]
            ring, cross, seen = lax.optimization_barrier((ring, cross, seen))
            found[which][2 * index], found[which][2 * index - 1] = ring, cross
            seen = ring
            launch(which, index)
    entries = list(range(2 * tiles - 1))
    state = step([[found[0][e], found[1][e]] for e in entries], entries, state, False)
    last = lax.optimization_barrier((moving[0], moving[1], state, extras))
    return step([[last[0], last[1]]], [2 * tiles - 1], last[2], True), last[3]


def shards(
    text_embed,
    latents,
    down_conv,
    patch_in,
    norm_gain,
    query_weight,
    key_weight,
    value_weight,
    query_gain,
    key_gain,
    out_weight,
    patch_out,
    up_conv,
    span_start,
    image_of_slot,
):
    ctxs, tiles, outer = (lax.axis_size(name) for name in ("ctx", "tile", "mpo"))
    ctx, tile, mpo, core = (lax.axis_index(name) for name in ("ctx", "tile", "mpo", "core"))
    seq_rows, width = text_embed.shape
    half = seq_rows // 2
    images = span_start.shape[0]
    local = latents.shape[0]

    numbers = jnp.arange(images, dtype=jnp.int32)
    matches = image_of_slot[None, :] == numbers[:, None]
    slot_of_image = jnp.sum(jnp.where(matches, numbers[None, :], 0), axis=1)
    slot_place = lax.rem(ctx + ctxs - slot_of_image // local, ctxs) * local + slot_of_image % local
    meta = jnp.concatenate(
        [span_start, slot_place, image_of_slot, jnp.stack([ctx, core, tile, mpo])]
    ).astype(jnp.int32)
    layout = (images, tiles, outer)

    weights = [swap(w) for w in (key_weight, value_weight, query_weight)]
    pieces, conv, meta, weights[0], weights[1] = gather_small(latents, down_conv, meta, *weights[:2])
    later, pieces[1] = lax.optimization_barrier((meta, pieces[1]))
    kept, sent, halves = transpose_first(later, patch_out, layout, ctxs)
    pieces, sent = lax.optimization_barrier((pieces, sent))
    received = shift(sent, "mpo", 1)
    weights += [key_weight, value_weight, query_weight]
    streams = down_stream(meta, pieces, conv, patch_in, text_embed, norm_gain, weights, images)
    streams, held_weights = [streams[:2], streams[2:4]], streams[4:]
    streams, received = lax.optimization_barrier((streams, received))
    others = [swap(s[1]) for s in streams]
    others = lax.optimization_barrier(others)

    head_gains = jnp.stack([query_gain, key_gain])

    def project(blocks, entries, state, last):
        return qkv_step(
            meta, layout, blocks, entries, held_weights, state, head_gains
        )

    state, out_par = gather_pair(
        *[by_core(core, s[0], o, 1) for s, o in zip(streams, others)], None, project, swap(out_weight)
    )
    heads = width // HD
    kv_send, q_send = state[:heads], state[heads : 2 * heads]
    kv_own, q_own = state[2 * heads : 3 * heads], state[3 * heads :]

    def shifted(values, step, cross):
        pairs = [
            (2 * c + k, 2 * ((c + step) % ctxs) + (1 - k if cross else k))
            for c in range(ctxs)
            for k in range(2)
        ]
        return lax.ppermute(values, ("ctx", "core"), pairs)

    results = []
    for head in range(heads):
        q_par = swap(q_send[head])
        pieces = [kv_own[head], swap(kv_send[head])]
        for step in range(1, ctxs):
            pieces += [shifted(kv_own[head], step, False), shifted(kv_send[head], step, True)]
        q_par, q_send, kv_send, kv_own, kept, received = lax.optimization_barrier(
            (q_par, q_send, kv_send, kv_own, kept, received)
        )
        results.append(attention(meta, [q_own[head], q_par], pieces, images))
    up_blocks = [transpose_second(kept, received, step) for step in range(tiles)]
    att_own = [result[0] for result in results]
    att_par = [swap(result[1]) for result in results]
    rows = half // 2
    attended = []
    for at in (0, rows):
        own, par = (
            jnp.concatenate([x[at : at + rows] for x in side], axis=1) for side in (att_own, att_par)
        )
        attended.append(by_core(core, own, par, 1))
    attended, up_blocks = lax.optimization_barrier((attended, up_blocks))
    up_own = jnp.concatenate(up_blocks)
    extras = [up_own, swap(up_own)] + ([shift(up_own, "ctx", 1)] if halves == 2 else [])

    def project_out(blocks, entries, state, last):
        return out_step(meta, layout, blocks, entries, (out_weight, out_par), state, last)

    state = [streams[0][0], streams[1][0], others[0], others[1]]
    state, up_weights = gather_pair(*attended, state, project_out, extras)
    out_own, out_send = state
    out_other = swap(out_send)
    layer_out = by_core(core, out_own, out_other, 0)

    picks, swapped = lax.optimization_barrier(
        (pick_rows(meta, out_own, out_other, images, ctxs), [swap(other) for other in up_weights[2:]])
    )
    up_weights = [up_weights[:2]] + [[up_weights[2], other] for other in swapped]
    own_parts, par_parts = [picks[0]], [swap(picks[1])]
    for step in range(1, ctxs):
        own_parts.append(shifted(picks[2 * step], step, False))
        par_parts.append(shifted(picks[2 * step + 1], step, True))

    pixel = tile * outer + mpo
    pixels = jnp.stack([pixel * halves + lax.rem(ctx + h, halves) for h in range(halves)])
    spread_weight = spread_weights(up_conv, pixels)

    def project_up(blocks, entries, state, last):
        return up_step(blocks, entries, up_weights, state, spread_weight if last else None)

    state, _ = gather_pair(*merge_picks(own_parts, par_parts), None, project_up)

    bands = state.reshape(tiles, IMG_TOK // tiles, PIX * CIN)
    band = lax.dynamic_index_in_dim(bands, tile, 0, keepdims=False)
    for step in range(1, tiles):
        piece = lax.dynamic_index_in_dim(bands, lax.rem(tile + step, tiles), 0, keepdims=False)
        band = band + shift(piece, "tile", step)
    quad = {}
    for name, pairs in (
        ("mpo", [(0, 2), (1, 3), (2, 0), (3, 1)]),
        ("core", [(0, 1), (1, 0), (2, 3), (3, 2)]),
        ("both", [(0, 3), (1, 2), (2, 1), (3, 0)]),
    ):
        quad[name] = lax.ppermute(band, ("mpo", "core"), pairs)
    return layer_out, finish(meta[3 * images + 1 :], band, quad["mpo"], quad["core"], quad["both"])


def solution(mesh):
    ctxs, tiles, parts = mesh.devices.shape
    fine = Mesh(
        mesh.devices.reshape(ctxs, tiles, parts // 2, 2), ("ctx", "tile", "mpo", "core")
    )
    features = ("tile", "mpo", "core")
    return jax.shard_map(
        shards,
        mesh=fine,
        in_specs=(
            P("ctx", features),
            P("ctx", "tile", None),
            P(None, ("mpo", "core")),
            P(None, features),
            P(features),
            P(None, features),
            P(None, features),
            P(None, features),
            P(),
            P(),
            P(None, features),
            P(features, None),
            P(),
            P(),
            P(),
        ),
        out_specs=(P("ctx", features), P("ctx", "tile", None)),
        check_vma=False,
    )
```

```python
import functools

import jax
import jax.numpy as jnp
from jax import lax
from jax.experimental import pallas as pl
from jax.experimental.pallas import tpu as pltpu
from jax.sharding import Mesh
from jax.sharding import PartitionSpec as P

HD = 128
CH = 256
CIN = 8
WL = 64
HL = 64
PATCH = 4
PIX = PATCH * PATCH
SIDE = WL // PATCH
IMG_TOK = 256
EPSILON = 1e-05
NEGATIVE_FILL = -1e30
WINDOW = (PATCH + 2) * CIN
TAPS = 3 * WINDOW
BF16 = jnp.bfloat16
F32 = jnp.float32


def split_meta(meta, images):
    return meta[3 * images], meta[3 * images + 1], meta[3 * images + 2], meta[3 * images + 3]


def params(mebibytes):
    return pltpu.CompilerParams(
        dimension_semantics=("arbitrary",), vmem_limit_bytes=mebibytes * 1024 * 1024
    )


def cost(flops, nbytes, transcendentals=0):
    return pl.CostEstimate(
        flops=int(flops), bytes_accessed=int(nbytes), transcendentals=int(transcendentals)
    )


def silu(values):
    half = values * 0.5
    return half + half * jnp.tanh(half)


def mxu(left, right):
    return jnp.dot(left, right, preferred_element_type=F32)


def swap(values):
    return lax.ppermute(values, "core", [(0, 1), (1, 0)])


HELD = pl.BlockSpec(memory_space=pltpu.VMEM)


def in_hbm(values):
    return pltpu.with_memory_space_constraint(values, pltpu.HBM)


GAIN_ROWS = 16
TOP = 16


def down_kernel(images, tiles, half, meta, *refs):
    lat_refs, refs = refs[:tiles], refs[tiles:]
    conv_ref, gain_ref, patch_hbm, text_hbm = refs[:4]
    weight_refs, first_refs, second_refs, held_refs = refs[4:10], refs[10:12], refs[12:14], refs[14:20]
    grid_rows, conv_wide, conv_bf16, windows, total, patch_ref, text_ref = refs[20:27]
    arrived, patch_arrived, text_arrived = refs[27:]
    step = pl.program_id(0)
    deep = PATCH * CH
    patch_copies = [
        pltpu.make_async_copy(
            patch_hbm.at[index * deep : (index + 1) * deep, :], patch_ref.at[index], patch_arrived.at[index]
        )
        for index in range(PATCH)
    ]
    side_rows = [jnp.bitwise_xor(meta[3 * images + 1], side) * half for side in range(2)]
    text_copies = [
        pltpu.make_async_copy(
            text_hbm.at[pl.ds(pl.multiple_of(side_rows[side], half), half), :],
            text_ref.at[side],
            text_arrived.at[side],
        )
        for side in range(2)
    ]
    copies = [
        pltpu.make_async_copy(weight, held, arrived.at[index])
        for index, (weight, held) in enumerate(zip(weight_refs, held_refs))
    ]

    @pl.when(step == 0)
    def _():
        for copy in patch_copies + text_copies + copies:
            copy.start()

    group = images * SIDE
    ctx, core, tile, _ = split_meta(meta, images)

    @pl.when(step == 0)
    def _():
        grid_rows[...] = jnp.zeros_like(grid_rows)
        blocks = grid_rows.shape[1]
        for index in range(tiles):
            band = lat_refs[index].shape[1]
            at = TOP + lax.rem(tile + tiles - index, tiles) * band
            rows = pl.ds(pl.multiple_of(at, 8), band)
            latent = lat_refs[index][...].astype(F32)
            edges = [jnp.zeros((images, band, size), F32) for size in (CIN, HD - CIN)]
            wide = jnp.concatenate([edges[0], latent, edges[1]], axis=2)
            for part in range(blocks):
                grid_rows[:, part, rows, :] = wide[:, :, part * HD : (part + 1) * HD]
        conv_wide[...] = jnp.zeros_like(conv_wide)
        conv = conv_ref[...].astype(F32)
        for col in range(PATCH):
            for tap in range(3):
                at = WINDOW * tap + CIN * col
                conv_wide[at : at + 3 * CIN, CH * col : CH * (col + 1)] = conv[
                    3 * CIN * tap : 3 * CIN * (tap + 1), :
                ]
        conv_bf16[...] = conv_wide[...].astype(BF16)

        def build(image, carry):
            for row in range(PATCH + 2):
                take = pl.ds(TOP - 1 + row, SIDE, stride=PATCH)
                line = [grid_rows[image, part, take, :] for part in range(blocks)]
                line = jnp.concatenate(line, axis=1).astype(BF16)
                for col in range(SIDE):
                    piece = line[:, PATCH * CIN * col : PATCH * CIN * col + WINDOW]
                    at = pl.ds(pl.multiple_of(group * col + image * SIDE, SIDE), SIDE)
                    for shift in range(3):
                        if 0 <= row - shift < PATCH:
                            windows[row - shift, at, WINDOW * shift : WINDOW * (shift + 1)] = piece
            return carry

        lax.fori_loop(0, images, build, 0)
        total[...] = jnp.zeros_like(total)

    for index in range(PATCH):
        pl.when(step == index)(patch_copies[index].wait)

    chunk = 256
    for part in range(images * IMG_TOK // chunk):
        rows = slice(part * chunk, (part + 1) * chunk)
        hidden = silu(mxu(windows[step, rows, :], conv_bf16[...])).astype(BF16)
        total[rows, :] += mxu(hidden, patch_ref[step])

    @pl.when(step == PATCH - 1)
    def _():
        tokens = total[...].astype(BF16)
        block = half // 2
        for copy in text_copies:
            copy.wait()
        for side in range(2):
            base = ctx * (2 * half) + jnp.bitwise_xor(core, side) * half
            for part, out_ref in enumerate((first_refs[side], second_refs[side])):
                place = base + part * block + lax.broadcasted_iota(jnp.int32, (block, 1), 0)
                source = jnp.full((block, 1), -1, jnp.int32)
                for image in range(images):
                    inner = place - meta[image]
                    inside = (inner >= 0) & (inner < IMG_TOK)
                    index = (inner & (SIDE - 1)) * group + meta[images + image] * SIDE + (inner >> 4)
                    source = jnp.where(inside, index, source)
                choice = source == lax.broadcasted_iota(jnp.int32, (block, images * IMG_TOK), 1)
                picked = mxu(jnp.where(choice, 1.0, 0.0).astype(BF16), tokens)
                text = text_ref[side, part * block : (part + 1) * block, :].astype(F32)
                out_ref[:block, :] = jnp.where(source >= 0, picked, text).astype(BF16)
            gain = gain_ref[...].astype(F32)
            first_refs[side][block:, :] = jnp.broadcast_to(gain, (GAIN_ROWS, gain.shape[1])).astype(BF16)
        for copy in copies:
            copy.wait()


def down_stream(meta, pieces, conv, patch_in, text, gain, weights, images):
    seq_rows, width = text.shape
    half = seq_rows // 2
    tiles = len(pieces)
    count = images * IMG_TOK
    first, second = (half // 2 + GAIN_ROWS, width), (half // 2, width)
    pieces_out = [first, first, second, second]
    return pl.pallas_call(
        functools.partial(down_kernel, images, tiles, half),
        grid_spec=pltpu.PrefetchScalarGridSpec(
            num_scalar_prefetch=1,
            grid=(PATCH,),
            in_specs=[full(p.shape) for p in pieces]
            + [
                full(conv.shape),
                full((1, width)),
            ]
            + [pl.BlockSpec(memory_space=pltpu.HBM)] * 8,
            out_specs=[full(shape) for shape in pieces_out] + [HELD] * 6,
            scratch_shapes=[
                pltpu.VMEM((images, WL * CIN // HD + 1, TOP + HL + 16, HD), F32),
                pltpu.VMEM((TAPS, PATCH * CH), F32),
                pltpu.VMEM((TAPS, PATCH * CH), BF16),
                pltpu.VMEM((PATCH, count, TAPS), BF16),
                pltpu.VMEM((count, width), F32),
                pltpu.VMEM((PATCH, PATCH * CH, width), BF16),
                pltpu.VMEM((2, half, width), BF16),
                pltpu.SemaphoreType.DMA((6,)),
                pltpu.SemaphoreType.DMA((PATCH,)),
                pltpu.SemaphoreType.DMA((2,)),
            ],
        ),
        out_shape=[jax.ShapeDtypeStruct(shape, BF16) for shape in pieces_out]
        + [pltpu.VMEM(w.shape, w.dtype) for w in weights],
        compiler_params=params(32),
        cost_estimate=cost(2 * count * PIX * CH * (256 + width), 4 << 20, count * PIX * CH),
        name="down_stream",
    )(meta, *pieces, conv, gain.reshape(1, width), in_hbm(patch_in), in_hbm(text), *[in_hbm(w) for w in weights])


def full(shape):
    return pl.BlockSpec(shape, lambda i, m: (0,) * len(shape))


def load(pieces):
    return jnp.concatenate([piece[...] for piece in pieces], axis=0)


def take_blocks(refs, count):
    return [[refs.pop(0), refs.pop(0)] for _ in range(count)]


def chip_of(meta, images, tiles, outer, entry):
    _, _, tile, mpo = split_meta(meta, images)
    return lax.rem(tile + tiles - entry // 2, tiles) * outer + lax.rem(mpo + entry % 2, outer)


def qkv_kernel(entries, layout, groups, last, meta, *refs):
    refs = list(refs)
    count = len(entries)
    x_refs = take_blocks(refs, count)
    scaled_ref = refs.pop(-1)
    if last:
        weights_ref, acc_in, square_in, head_gains = [refs.pop(0) for _ in range(4)]
    else:
        weight_refs = [refs.pop(0) for _ in range(6)]
    half, span = scaled_ref.shape
    width = weights_ref.shape[2] if last else weight_refs[0].shape[1]
    heads = width // HD
    square = square_in[...] if last else None
    if last:
        acc, outs = [None] * 6, refs
    else:
        weights_out, acc_out, square_out = refs
    for index in range(count):
        rows = pl.ds(pl.multiple_of(chip_of(meta, *layout, entries[index]) * span, span), span)
        gain = x_refs[index][0][half // 2 :, :][:1]
        for part in range(2):
            at = slice(part * half // 2, (part + 1) * half // 2)
            scaled_ref[at, :] = (x_refs[index][part][: half // 2, :] * gain).astype(BF16)
        value = jnp.concatenate([x_refs[index][0][: half // 2, :], x_refs[index][1][...]], axis=0)
        value = value.astype(F32)
        value = value * value
        for part in range(span // HD):
            piece = value[:, part * HD : (part + 1) * HD]
            square = piece if square is None else square + piece
        for part in range(6):
            if last:
                acc[part] = acc_in[part] + mxu(scaled_ref[...], weights_ref[part])
                continue
            term = mxu(scaled_ref[...], weight_refs[part][rows, :])
            if index == 0:
                acc_out[part] = term
            else:
                acc_out[part] += term
    if not last:
        square_out[...] = square
        rows = pl.ds(pl.multiple_of(chip_of(meta, *layout, len(entries)) * span, span), span)
        for part in range(6):
            weights_out[part] = weight_refs[part][rows, :]
        return
    mean = jnp.sum(square, axis=-1, keepdims=True) * (1.0 / (groups * span))
    scale = lax.rsqrt(mean + EPSILON)
    for part in range(6):
        total = acc[part] * scale
        side, kind = part // 3, part % 3
        kv_outs = outs[2 * heads * side : 2 * heads * side + heads]
        q_outs = outs[2 * heads * side + heads : 2 * heads * (side + 1)]
        for head in range(heads):
            raw = total[:, head * HD : (head + 1) * HD]
            if kind == 1:
                kv_outs[head][1] = raw.astype(BF16)
                continue
            raw = raw * lax.rsqrt(jnp.mean(raw * raw, axis=-1, keepdims=True) + EPSILON)
            if kind == 0:
                kv_outs[head][0] = (raw * head_gains[1:2, :]).astype(BF16)
            else:
                q_outs[head][...] = (raw * (head_gains[0:1, :] * HD ** (-0.5))).astype(BF16)


def qkv_step(meta, layout, blocks, entries, weights, state, head_gains):
    span = blocks[0][1].shape[1]
    half = 2 * blocks[0][1].shape[0]
    count, last = len(blocks), state is not None
    width = state[0].shape[2] if last else weights[0].shape[1]
    groups = layout[1] * layout[2]
    inputs = [p for pieces in blocks for p in pieces]
    specs = [full(p.shape) for pieces in blocks for p in pieces]
    scratch = [pltpu.VMEM((half, span), BF16)]
    if last:
        specs += [HELD] * 3 + [full(head_gains.shape)]
        inputs += list(state) + [head_gains]
        heads = width // HD
        outs = [pltpu.HBM((2, half, HD), BF16)] * heads + [pltpu.HBM((half, HD), BF16)] * heads
        outs = outs * 2
    else:
        specs += [HELD] * 6
        inputs += list(weights)
        outs = [
            pltpu.VMEM((6, span, width), BF16),
            pltpu.VMEM((6, half, width), F32),
            pltpu.VMEM((half, HD), F32),
        ]
    return pl.pallas_call(
        functools.partial(qkv_kernel, entries, layout, groups, last),
        grid_spec=pltpu.PrefetchScalarGridSpec(
            num_scalar_prefetch=1,
            grid=(1,),
            in_specs=specs,
            out_specs=[full(o.shape) if last else HELD for o in outs],
            scratch_shapes=scratch,
        ),
        out_shape=outs,
        compiler_params=params(20),
        cost_estimate=cost(12 * count * half * span * width, (6 + 2 * count) << 20),
        name="qkv_last" if last else "qkv_step",
    )(meta, *inputs)


def attention_kernel(images, pieces, half, meta, *refs):
    ctx, core, _, _ = split_meta(meta, images)
    ctxs = pieces // 2
    bases = []
    for piece in range(pieces):
        side = jnp.bitwise_xor(core, piece % 2)
        bases.append(lax.rem(ctx + ctxs - piece // 2, ctxs) * (2 * half) + side * half)
    q_refs, kv_refs, out_refs = refs[:2], refs[2 : 2 + pieces], refs[2 + pieces :]
    rows = q_refs[0].shape[0]
    step = pl.program_id(0)
    for side in range(2):
        place = bases[side] + step * rows + lax.broadcasted_iota(jnp.int32, (rows, 1), 0)
        limit = place
        for image in range(images):
            inner = place - meta[image]
            limit = jnp.where((inner >= 0) & (inner < IMG_TOK), meta[image] + IMG_TOK - 1, limit)
        for head in range(q_refs[0].shape[1] // HD):
            lanes = slice(head * HD, (head + 1) * HD)
            query = q_refs[side][:, lanes]
            scores = []
            top = None
            for piece in range(pieces):
                score = lax.dot_general(
                    query, kv_refs[piece][0, :, lanes], (((1,), (1,)), ((), ())), preferred_element_type=F32
                )
                position = lax.broadcasted_iota(jnp.int32, score.shape, 1)
                score = jnp.where(position <= limit - bases[piece], score, NEGATIVE_FILL)
                scores.append(score)
                best = jnp.max(score, axis=1, keepdims=True)
                top = best if top is None else jnp.maximum(top, best)
            total = jnp.zeros((rows, 1), F32)
            product = jnp.zeros((rows, HD), F32)
            for piece in range(pieces):
                weight = jnp.exp(scores[piece] - top)
                total = total + jnp.sum(weight, axis=1, keepdims=True)
                product = product + mxu(weight.astype(BF16), kv_refs[piece][1, :, lanes])
            out_refs[side][:, lanes] = (product / total).astype(BF16)


def attention(meta, queries, pieces, images):
    half, width = queries[0].shape
    block = 256
    keys = half * len(pieces)
    rows = pl.BlockSpec((block, width), lambda i, m: (i, 0))
    return pl.pallas_call(
        functools.partial(attention_kernel, images, len(pieces), half),
        grid_spec=pltpu.PrefetchScalarGridSpec(
            num_scalar_prefetch=1,
            grid=(half // block,),
            in_specs=[rows, rows] + [full(p.shape) for p in pieces],
            out_specs=[rows, rows],
        ),
        out_shape=[jax.ShapeDtypeStruct((half, width), BF16)] * 2,
        compiler_params=params(24),
        cost_estimate=cost(8 * half * keys * width, 4 * keys * width, 2 * half * keys * width // HD),
        name="attention",
    )(meta, *queries, *pieces)


def out_kernel(count, first, last, meta, *refs):
    refs = list(refs)
    x_refs = take_blocks(refs, count)
    weight_refs = [[refs.pop(0), refs.pop(0)] for _ in range(count)]
    if first:
        streams = [refs.pop(0) for _ in range(4)]
        block = streams[1].shape[0]
    else:
        acc_in = refs.pop(0)
    outs = refs
    for side in range(2):
        if first:
            rows = [streams[2 * side][:block, :], streams[2 * side + 1][...]]
            total = jnp.concatenate(rows, axis=0).astype(F32)
        else:
            total = acc_in[side]
        for index in range(count):
            total = total + mxu(load(x_refs[index]), weight_refs[index][side][...])
        if last:
            outs[side][...] = total.astype(BF16)
        else:
            outs[0][side] = total


def out_step(meta, layout, blocks, entries, weights, state, last):
    span, width = blocks[0][0].shape[1], weights[0].shape[1]
    half = 2 * blocks[0][0].shape[0]
    first = isinstance(state, list)
    count = len(blocks)
    inputs = [p for pieces in blocks for p in pieces]
    specs = [full(p.shape) for p in inputs]
    for entry in entries:
        index = lambda i, m, entry=entry: (chip_of(m, *layout, entry), 0)
        inputs += weights
        specs += [pl.BlockSpec((span, width), index)] * 2
    states = state if first else [state]
    inputs += states
    specs += [full(s.shape) for s in states]
    if last:
        outs = [jax.ShapeDtypeStruct((half, width), BF16)] * 2
    else:
        outs = [jax.ShapeDtypeStruct((2, half, width), F32)]
    result = pl.pallas_call(
        functools.partial(out_kernel, count, first, last),
        grid_spec=pltpu.PrefetchScalarGridSpec(
            num_scalar_prefetch=1,
            grid=(1,),
            in_specs=specs,
            out_specs=[full(o.shape) for o in outs],
        ),
        out_shape=outs,
        compiler_params=params(24),
        cost_estimate=cost(4 * count * half * span * width, (2 + count) << 20),
        name="out_last" if last else "out_step",
    )(meta, *inputs)
    return result if last else result[0]


def pick_kernel(images, ctxs, meta, own_ref, par_ref, *out_refs):
    half = own_ref.shape[0]
    ctx, core, _, _ = split_meta(meta, images)
    for target in range(2 * ctxs):
        to_core = jnp.bitwise_xor(core, target % 2)
        slot = 2 * lax.rem(ctx + target // 2, ctxs) + to_core
        start = meta[meta[2 * images + slot]]
        place = start + lax.broadcasted_iota(jnp.int32, (IMG_TOK, half), 0)
        column = ctx * (2 * half) + lax.broadcasted_iota(jnp.int32, (IMG_TOK, half), 1)
        own = jnp.where(place == column + core * half, 1.0, 0.0).astype(BF16)
        par = jnp.where(place == column + (1 - core) * half, 1.0, 0.0).astype(BF16)
        out_refs[target][...] = (mxu(own, own_ref[...]) + mxu(par, par_ref[...])).astype(BF16)


def pick_rows(meta, own, par, images, ctxs):
    half, width = own.shape
    targets = 2 * ctxs
    return pl.pallas_call(
        functools.partial(pick_kernel, images, ctxs),
        grid_spec=pltpu.PrefetchScalarGridSpec(
            num_scalar_prefetch=1,
            grid=(1,),
            in_specs=[full(own.shape), full(par.shape)],
            out_specs=[full((IMG_TOK, width))] * targets,
        ),
        out_shape=[jax.ShapeDtypeStruct((IMG_TOK, width), BF16)] * targets,
        compiler_params=params(16),
        cost_estimate=cost(targets * 4 * IMG_TOK * half * width, 1 << 20),
        name="pick_rows",
    )(meta, own, par)


def merge_kernel(*refs):
    out_refs = refs[-2:]
    refs = refs[:-2]
    sides = refs[: len(refs) // 2], refs[len(refs) // 2 :]
    width = sides[0][0].shape[1]
    block = IMG_TOK // 2
    for side in range(2):
        total = sides[side][0][...].astype(F32)
        for part in sides[side][1:]:
            total = total + part[...].astype(F32)
        total = total.astype(BF16)
        for index in range(2):
            out_refs[index][:, side * width : (side + 1) * width] = total[index * block : (index + 1) * block]


def merge_picks(own_parts, par_parts):
    width = own_parts[0].shape[1]
    return pl.pallas_call(
        merge_kernel,
        out_shape=[jax.ShapeDtypeStruct((IMG_TOK // 2, 2 * width), BF16)] * 2,
        compiler_params=pltpu.CompilerParams(vmem_limit_bytes=8 << 20),
        cost_estimate=cost(1 << 20, 1 << 20),
        name="merge_picks",
    )(*own_parts, *par_parts)


def finish_kernel(core_ref, own_a, own_b, par_a, par_b, out_ref, sums, lines):
    core = core_ref[0]
    for side, (left, right) in enumerate(((own_a, own_b), (par_a, par_b))):
        sums[side] = left[...] + right[...]
    rows = sums.shape[1] // SIDE
    lanes = PATCH * CIN
    per = HD // lanes
    for side in range(2):
        for part in range(SIDE // per):
            cols = [sums[side, pl.ds(part * per + k, rows, stride=SIDE), :] for k in range(per)]
            for row in range(PATCH):
                pieces = [col[:, row * lanes : (row + 1) * lanes] for col in cols]
                lines[part, pl.ds(row, rows, stride=PATCH), :] = jnp.concatenate(pieces, axis=1)
        slot = jnp.bitwise_xor(core, side)
        for part in range(SIDE // per):
            out_ref[slot, :, part * HD : (part + 1) * HD] = lines[part]


def finish(core, own_a, own_b, par_a, par_b):
    count = own_a.shape[0]
    return pl.pallas_call(
        finish_kernel,
        grid_spec=pltpu.PrefetchScalarGridSpec(
            num_scalar_prefetch=1,
            grid=(1,),
            in_specs=[full(own_a.shape)] * 4,
            out_specs=full((2, count // PATCH, WL * CIN)),
            scratch_shapes=[
                pltpu.VMEM((2, count, PIX * CIN), F32),
                pltpu.VMEM((WL * CIN // HD, count // PATCH, HD), F32),
            ],
        ),
        out_shape=jax.ShapeDtypeStruct((2, count // PATCH, WL * CIN), F32),
        compiler_params=params(8),
        cost_estimate=cost(1 << 16, 1 << 18),
        name="finish",
    )(core, own_a, own_b, par_a, par_b)


def spread(active, spread_ref):
    row = lax.broadcasted_iota(jnp.int32, (IMG_TOK, PIX * CIN), 0)
    patch_row, patch_col = row >> 4, row & (SIDE - 1)
    total = None
    for index in range(9):
        down, right = index // 3 - 1, index % 3 - 1
        part = mxu(active, spread_ref[:, index * PIX * CIN : (index + 1) * PIX * CIN])
        offset = down * SIDE + right
        if offset:
            part = pltpu.roll(part, offset % IMG_TOK, 0)
        source_row, source_col = patch_row - down, patch_col - right
        inside = (source_row >= 0) & (source_row < SIDE) & (source_col >= 0) & (source_col < SIDE)
        part = jnp.where(inside, part, 0.0)
        total = part if total is None else total + part
    return total


def up_kernel(count, halves, first, last, *refs):
    refs = list(refs)
    x_refs = take_blocks(refs, count)
    weight_refs = [[[refs.pop(0) for _ in range(2)] for _ in range(halves)] for _ in range(count)]
    acc_in = None if first else refs.pop(0)
    spread_ref = refs.pop(0) if last else None
    out_ref = refs[0]
    width = x_refs[0][0].shape[1] // 2
    values = [load(pieces) for pieces in x_refs]
    totals = []
    for part in range(halves):
        total = None if first else acc_in[part]
        for block in range(count):
            for side in range(2):
                term = mxu(
                    values[block][:, side * width : (side + 1) * width],
                    weight_refs[block][part][side][0],
                )
                total = term if total is None else total + term
        totals.append(total)
        if not last:
            out_ref[part] = total
    if last:
        active = [silu(total).astype(BF16) for total in totals]
        active = jnp.concatenate(active, axis=1) if halves > 1 else active[0]
        out_ref[...] = spread(active, spread_ref)


def up_step(blocks, entries, weights, state, spread_weight):
    span = blocks[0][0].shape[1]
    halves, count = len(weights), len(blocks)
    first, last = state is None, spread_weight is not None
    whole = lambda shape: pl.BlockSpec(shape, lambda i: (0,) * len(shape))
    inputs = [p for pieces in blocks for p in pieces]
    specs = [whole(p.shape) for p in inputs]
    for entry in entries:
        for sides in weights:
            for weight in sides:
                inputs.append(weight)
                specs.append(pl.BlockSpec((1, span // 2, CH), lambda i, entry=entry: (entry, 0, 0)))
    if not first:
        inputs.append(state)
        specs.append(whole(state.shape))
    if last:
        inputs.append(spread_weight)
        specs.append(whole(spread_weight.shape))
        out = jax.ShapeDtypeStruct((IMG_TOK, PIX * CIN), F32)
    else:
        out = jax.ShapeDtypeStruct((halves, IMG_TOK, CH), F32)
    return pl.pallas_call(
        functools.partial(up_kernel, count, halves, first, last),
        grid=(1,),
        in_specs=specs,
        out_specs=whole(out.shape),
        out_shape=out,
        compiler_params=params(16),
        cost_estimate=cost(2 * count * IMG_TOK * span * CH * halves, (1 + count) << 20),
        name="up_last" if last else "up_step",
    )(*inputs)


def spread_weights(up_conv, pixels):
    taps = up_conv.reshape(9, CH, CIN).transpose(1, 0, 2).reshape(CH, 9 * CIN)
    shape = (pixels.shape[0], 9 * CIN, 9 * PIX * CIN)
    row = lax.broadcasted_iota(jnp.int32, shape, 1)
    col = lax.broadcasted_iota(jnp.int32, shape, 2)
    pixel = pixels[:, None, None]
    tap, channel = row >> 3, row & 7
    patch, target, out_channel = col >> 7, (col >> 3) & 15, col & 7
    tap_row, tap_col = tap // 3, tap % 3
    down, right = patch // 3 - 1, patch % 3 - 1
    hit = (
        (channel == out_channel)
        & ((pixel >> 2) + 1 - tap_row == (target >> 2) + PATCH * down)
        & ((pixel & 3) + 1 - tap_col == (target & 3) + PATCH * right)
    )
    placed = jnp.where(hit, 1.0, 0.0).astype(BF16)
    spread = jnp.einsum("ct,ptn->pcn", taps, placed, preferred_element_type=F32)
    return spread.astype(BF16).reshape(pixels.shape[0] * CH, 9 * PIX * CIN)


def by_core(core, own, other, axis):
    return jnp.where(
        core == 0, jnp.concatenate([own, other], axis), jnp.concatenate([other, own], axis)
    )


def shift(values, axis, step):
    count = lax.axis_size(axis)
    return lax.ppermute(values, axis, [(i, (i + step) % count) for i in range(count)])


def gather_small(latents, down_conv, *others):
    ctxs, tiles = lax.axis_size("ctx"), lax.axis_size("tile")
    every = jnp.concatenate([latents] + [shift(latents, "ctx", s) for s in range(1, ctxs)])
    conv = by_core(lax.axis_index("core"), down_conv, swap(down_conv), 1)
    conv = by_core(lax.axis_index("mpo"), conv, shift(conv, "mpo", 1), 1)
    every, others = lax.optimization_barrier((every, others))
    return [every] + [shift(every, "tile", s) for s in range(1, tiles)], conv, *others


def columns_kernel(meta, kept_in, sent_in, kept_out, sent_out):
    kept_out[0] = kept_in[...]
    sent_out[0] = sent_in[...]


def transpose_first(meta, patch_out, layout, ctxs):
    images, tiles, outer = layout
    width, features = patch_out.shape
    deep = features // (tiles * outer)
    halves = 2 if ctxs == 2 and deep == 2 * CH else 1
    size = deep // halves

    def place(other):
        def index(i, m):
            ctx, _, _, mpo = split_meta(m, images)
            chip = i * outer + lax.rem(mpo + other, outer)
            return 0, chip * halves + (ctx if halves == 2 else 0)

        return pl.BlockSpec((width, size), index)

    out = pl.BlockSpec((1, width, size), lambda i, m: (i, 0, 0))
    patch_out = in_hbm(patch_out)
    kept, sent = pl.pallas_call(
        columns_kernel,
        grid_spec=pltpu.PrefetchScalarGridSpec(
            num_scalar_prefetch=1, grid=(tiles,), in_specs=[place(0), place(1)], out_specs=[out, out]
        ),
        out_shape=[jax.ShapeDtypeStruct((tiles, width, size), BF16)] * 2,
        compiler_params=params(8),
        cost_estimate=cost(1 << 16, 2 << 20),
        name="columns",
    )(meta, patch_out, patch_out)
    return kept, sent, halves


def transpose_second(kept, received, step):
    tiles = lax.axis_size("tile")
    place = lax.rem(lax.axis_index("tile") + step, tiles)
    block = [lax.dynamic_index_in_dim(x, place, 0, keepdims=False) for x in (kept, received)]
    block = jnp.stack(block)
    return shift(block, "tile", step) if step else block


def gather_pair(first, second, state, step, extras=None):
    tiles = lax.axis_size("tile")
    found, moving = [{0: first}, {0: second}], [None, None]

    def launch(which, index):
        ring = found[which][2 * index]
        if index < tiles - 1:
            moving[which] = (shift(ring, "tile", 1), shift(ring, "mpo", 1))
        elif which:
            moving[which] = shift(found[which][2 * index - 1], "tile", 1)
        else:
            moving[which] = shift(ring, "mpo", 1)

    launch(0, 0)
    launch(1, 0)
    seen = first
    for index in range(1, tiles):
        for which in range(2):
            ring, cross = moving[which]
            ring, cross, seen = lax.optimization_barrier((ring, cross, seen))
            found[which][2 * index], found[which][2 * index - 1] = ring, cross
            seen = ring
            launch(which, index)
    entries = list(range(2 * tiles - 1))
    state = step([[found[0][e], found[1][e]] for e in entries], entries, state, False)
    last = lax.optimization_barrier((moving[0], moving[1], state, extras))
    return step([[last[0], last[1]]], [2 * tiles - 1], last[2], True), last[3]


def shards(
    text_embed,
    latents,
    down_conv,
    patch_in,
    norm_gain,
    query_weight,
    key_weight,
    value_weight,
    query_gain,
    key_gain,
    out_weight,
    patch_out,
    up_conv,
    span_start,
    image_of_slot,
):
    ctxs, tiles, outer = (lax.axis_size(name) for name in ("ctx", "tile", "mpo"))
    ctx, tile, mpo, core = (lax.axis_index(name) for name in ("ctx", "tile", "mpo", "core"))
    seq_rows, width = text_embed.shape
    half = seq_rows // 2
    images = span_start.shape[0]
    local = latents.shape[0]

    numbers = jnp.arange(images, dtype=jnp.int32)
    matches = image_of_slot[None, :] == numbers[:, None]
    slot_of_image = jnp.sum(jnp.where(matches, numbers[None, :], 0), axis=1)
    slot_place = lax.rem(ctx + ctxs - slot_of_image // local, ctxs) * local + slot_of_image % local
    meta = jnp.concatenate(
        [span_start, slot_place, image_of_slot, jnp.stack([ctx, core, tile, mpo])]
    ).astype(jnp.int32)
    layout = (images, tiles, outer)

    weights = [swap(w) for w in (key_weight, value_weight, query_weight)]
    pieces, conv, meta, weights[0], weights[1] = gather_small(latents, down_conv, meta, *weights[:2])
    later, pieces[1] = lax.optimization_barrier((meta, pieces[1]))
    kept, sent, halves = transpose_first(later, patch_out, layout, ctxs)
    pieces, sent = lax.optimization_barrier((pieces, sent))
    received = shift(sent, "mpo", 1)
    weights += [key_weight, value_weight, query_weight]
    streams = down_stream(meta, pieces, conv, patch_in, text_embed, norm_gain, weights, images)
    streams, held_weights = [streams[:2], streams[2:4]], streams[4:]
    streams, received = lax.optimization_barrier((streams, received))
    others = [swap(s[1]) for s in streams]
    others = lax.optimization_barrier(others)

    head_gains = jnp.stack([query_gain, key_gain])

    def project(blocks, entries, state, last):
        return qkv_step(
            meta, layout, blocks, entries, held_weights, state, head_gains
        )

    state, out_par = gather_pair(
        *[by_core(core, s[0], o, 1) for s, o in zip(streams, others)], None, project, swap(out_weight)
    )
    heads = width // HD
    kv_send, q_send = state[:heads], state[heads : 2 * heads]
    kv_own, q_own = state[2 * heads : 3 * heads], state[3 * heads :]

    def shifted(values, step, cross):
        pairs = [
            (2 * c + k, 2 * ((c + step) % ctxs) + (1 - k if cross else k))
            for c in range(ctxs)
            for k in range(2)
        ]
        return lax.ppermute(values, ("ctx", "core"), pairs)

    results = []
    for head in range(heads):
        q_par = swap(q_send[head])
        pieces = [kv_own[head], swap(kv_send[head])]
        for step in range(1, ctxs):
            pieces += [shifted(kv_own[head], step, False), shifted(kv_send[head], step, True)]
        q_par, q_send, kv_send, kv_own, kept, received = lax.optimization_barrier(
            (q_par, q_send, kv_send, kv_own, kept, received)
        )
        results.append(attention(meta, [q_own[head], q_par], pieces, images))
    up_blocks = [transpose_second(kept, received, step) for step in range(tiles)]
    att_own = [result[0] for result in results]
    att_par = [swap(result[1]) for result in results]
    rows = half // 2
    attended = []
    for at in (0, rows):
        own, par = (
            jnp.concatenate([x[at : at + rows] for x in side], axis=1) for side in (att_own, att_par)
        )
        attended.append(by_core(core, own, par, 1))
    attended, up_blocks = lax.optimization_barrier((attended, up_blocks))
    up_own = jnp.concatenate(up_blocks)
    extras = [up_own, swap(up_own)] + ([shift(up_own, "ctx", 1)] if halves == 2 else [])

    def project_out(blocks, entries, state, last):
        return out_step(meta, layout, blocks, entries, (out_weight, out_par), state, last)

    state = [streams[0][0], streams[1][0], others[0], others[1]]
    state, up_weights = gather_pair(*attended, state, project_out, extras)
    out_own, out_send = state
    out_other = swap(out_send)
    layer_out = by_core(core, out_own, out_other, 0)

    picks, swapped = lax.optimization_barrier(
        (pick_rows(meta, out_own, out_other, images, ctxs), [swap(other) for other in up_weights[2:]])
    )
    up_weights = [up_weights[:2]] + [[up_weights[2], other] for other in swapped]
    own_parts, par_parts = [picks[0]], [swap(picks[1])]
    for step in range(1, ctxs):
        own_parts.append(shifted(picks[2 * step], step, False))
        par_parts.append(shifted(picks[2 * step + 1], step, True))

    pixel = tile * outer + mpo
    pixels = jnp.stack([pixel * halves + lax.rem(ctx + h, halves) for h in range(halves)])
    spread_weight = spread_weights(up_conv, pixels)

    def project_up(blocks, entries, state, last):
        return up_step(blocks, entries, up_weights, state, spread_weight if last else None)

    state, _ = gather_pair(*merge_picks(own_parts, par_parts), None, project_up)

    bands = state.reshape(tiles, IMG_TOK // tiles, PIX * CIN)
    band = lax.dynamic_index_in_dim(bands, tile, 0, keepdims=False)
    for step in range(1, tiles):
        piece = lax.dynamic_index_in_dim(bands, lax.rem(tile + step, tiles), 0, keepdims=False)
        band = band + shift(piece, "tile", step)
    quad = {}
    for name, pairs in (
        ("mpo", [(0, 2), (1, 3), (2, 0), (3, 1)]),
        ("core", [(0, 1), (1, 0), (2, 3), (3, 2)]),
        ("both", [(0, 3), (1, 2), (2, 1), (3, 0)]),
    ):
        quad[name] = lax.ppermute(band, ("mpo", "core"), pairs)
    return layer_out, finish(meta[3 * images + 1 :], band, quad["mpo"], quad["core"], quad["both"])


def solution(mesh):
    ctxs, tiles, parts = mesh.devices.shape
    fine = Mesh(
        mesh.devices.reshape(ctxs, tiles, parts // 2, 2), ("ctx", "tile", "mpo", "core")
    )
    features = ("tile", "mpo", "core")
    return jax.shard_map(
        shards,
        mesh=fine,
        in_specs=(
            P("ctx", features),
            P("ctx", "tile", None),
            P(None, ("mpo", "core")),
            P(None, features),
            P(features),
            P(None, features),
            P(None, features),
            P(None, features),
            P(),
            P(),
            P(None, features),
            P(features, None),
            P(),
            P(),
            P(),
        ),
        out_specs=(P("ctx", features), P("ctx", "tile", None)),
        check_vma=False,
    )
```

```python
import functools

import jax
import jax.numpy as jnp
from jax import lax
from jax.experimental import pallas as pl
from jax.experimental.pallas import tpu as pltpu
from jax.sharding import Mesh
from jax.sharding import PartitionSpec as P

HD = 128
CH = 256
CIN = 8
WL = 64
HL = 64
PATCH = 4
PIX = PATCH * PATCH
SIDE = WL // PATCH
IMG_TOK = 256
EPSILON = 1e-05
NEGATIVE_FILL = -1e30
WINDOW = (PATCH + 2) * CIN
TAPS = 3 * WINDOW
BF16 = jnp.bfloat16
F32 = jnp.float32


def split_meta(meta, images):
    return meta[3 * images], meta[3 * images + 1], meta[3 * images + 2], meta[3 * images + 3]


def params(mebibytes):
    return pltpu.CompilerParams(
        dimension_semantics=("arbitrary",), vmem_limit_bytes=mebibytes * 1024 * 1024
    )


def cost(flops, nbytes, transcendentals=0):
    return pl.CostEstimate(
        flops=int(flops), bytes_accessed=int(nbytes), transcendentals=int(transcendentals)
    )


def silu(values):
    half = values * 0.5
    return half + half * jnp.tanh(half)


def mxu(left, right):
    return jnp.dot(left, right, preferred_element_type=F32)


def swap(values):
    return lax.ppermute(values, "core", [(0, 1), (1, 0)])


HELD = pl.BlockSpec(memory_space=pltpu.VMEM)


def in_hbm(values):
    return pltpu.with_memory_space_constraint(values, pltpu.HBM)


GAIN_ROWS = 16
TOP = 16


def down_kernel(images, tiles, half, meta, *refs):
    lat_refs, refs = refs[:tiles], refs[tiles:]
    conv_ref, gain_ref, patch_hbm, text_hbm = refs[:4]
    weight_refs, first_refs, second_refs, held_refs = refs[4:10], refs[10:12], refs[12:14], refs[14:20]
    grid_rows, conv_wide, conv_bf16, windows, total, patch_ref, text_ref = refs[20:27]
    arrived, patch_arrived, text_arrived = refs[27:]
    step = pl.program_id(0)
    deep = PATCH * CH
    patch_copies = [
        pltpu.make_async_copy(
            patch_hbm.at[index * deep : (index + 1) * deep, :], patch_ref.at[index], patch_arrived.at[index]
        )
        for index in range(PATCH)
    ]
    side_rows = [jnp.bitwise_xor(meta[3 * images + 1], side) * half for side in range(2)]
    text_copies = [
        pltpu.make_async_copy(
            text_hbm.at[pl.ds(pl.multiple_of(side_rows[side], half), half), :],
            text_ref.at[side],
            text_arrived.at[side],
        )
        for side in range(2)
    ]
    copies = [
        pltpu.make_async_copy(weight, held, arrived.at[index])
        for index, (weight, held) in enumerate(zip(weight_refs, held_refs))
    ]

    @pl.when(step == 0)
    def _():
        for copy in patch_copies + text_copies + copies:
            copy.start()

    group = images * SIDE
    ctx, core, tile, _ = split_meta(meta, images)

    @pl.when(step == 0)
    def _():
        grid_rows[...] = jnp.zeros_like(grid_rows)
        blocks = grid_rows.shape[1]
        for index in range(tiles):
            band = lat_refs[index].shape[1]
            at = TOP + lax.rem(tile + tiles - index, tiles) * band
            rows = pl.ds(pl.multiple_of(at, 8), band)
            latent = lat_refs[index][...].astype(F32)
            edges = [jnp.zeros((images, band, size), F32) for size in (CIN, HD - CIN)]
            wide = jnp.concatenate([edges[0], latent, edges[1]], axis=2)
            for part in range(blocks):
                grid_rows[:, part, rows, :] = wide[:, :, part * HD : (part + 1) * HD]
        conv_wide[...] = jnp.zeros_like(conv_wide)
        conv = conv_ref[...].astype(F32)
        for col in range(PATCH):
            for tap in range(3):
                at = WINDOW * tap + CIN * col
                conv_wide[at : at + 3 * CIN, CH * col : CH * (col + 1)] = conv[
                    3 * CIN * tap : 3 * CIN * (tap + 1), :
                ]
        conv_bf16[...] = conv_wide[...].astype(BF16)

        def build(image, carry):
            for row in range(PATCH + 2):
                take = pl.ds(TOP - 1 + row, SIDE, stride=PATCH)
                line = [grid_rows[image, part, take, :] for part in range(blocks)]
                line = jnp.concatenate(line, axis=1).astype(BF16)
                for col in range(SIDE):
                    piece = line[:, PATCH * CIN * col : PATCH * CIN * col + WINDOW]
                    at = pl.ds(pl.multiple_of(group * col + image * SIDE, SIDE), SIDE)
                    for shift in range(3):
                        if 0 <= row - shift < PATCH:
                            windows[row - shift, at, WINDOW * shift : WINDOW * (shift + 1)] = piece
            return carry

        lax.fori_loop(0, images, build, 0)
        total[...] = jnp.zeros_like(total)

    for index in range(PATCH):
        pl.when(step == index)(patch_copies[index].wait)

    chunk = 256
    for part in range(images * IMG_TOK // chunk):
        rows = slice(part * chunk, (part + 1) * chunk)
        hidden = silu(mxu(windows[step, rows, :], conv_bf16[...])).astype(BF16)
        total[rows, :] += mxu(hidden, patch_ref[step])

    @pl.when(step == PATCH - 1)
    def _():
        tokens = total[...].astype(BF16)
        block = half // 2
        for copy in text_copies:
            copy.wait()
        for side in range(2):
            base = ctx * (2 * half) + jnp.bitwise_xor(core, side) * half
            for part, out_ref in enumerate((first_refs[side], second_refs[side])):
                place = base + part * block + lax.broadcasted_iota(jnp.int32, (block, 1), 0)
                source = jnp.full((block, 1), -1, jnp.int32)
                for image in range(images):
                    inner = place - meta[image]
                    inside = (inner >= 0) & (inner < IMG_TOK)
                    index = (inner & (SIDE - 1)) * group + meta[images + image] * SIDE + (inner >> 4)
                    source = jnp.where(inside, index, source)
                choice = source == lax.broadcasted_iota(jnp.int32, (block, images * IMG_TOK), 1)
                picked = mxu(jnp.where(choice, 1.0, 0.0).astype(BF16), tokens)
                text = text_ref[side, part * block : (part + 1) * block, :].astype(F32)
                out_ref[:block, :] = jnp.where(source >= 0, picked, text).astype(BF16)
            gain = gain_ref[...].astype(F32)
            first_refs[side][block:, :] = jnp.broadcast_to(gain, (GAIN_ROWS, gain.shape[1])).astype(BF16)
        for copy in copies:
            copy.wait()


def down_stream(meta, pieces, conv, patch_in, text, gain, weights, images):
    seq_rows, width = text.shape
    half = seq_rows // 2
    tiles = len(pieces)
    count = images * IMG_TOK
    first, second = (half // 2 + GAIN_ROWS, width), (half // 2, width)
    pieces_out = [first, first, second, second]
    return pl.pallas_call(
        functools.partial(down_kernel, images, tiles, half),
        grid_spec=pltpu.PrefetchScalarGridSpec(
            num_scalar_prefetch=1,
            grid=(PATCH,),
            in_specs=[full(p.shape) for p in pieces]
            + [
                full(conv.shape),
                full((1, width)),
            ]
            + [pl.BlockSpec(memory_space=pltpu.HBM)] * 8,
            out_specs=[full(shape) for shape in pieces_out] + [HELD] * 6,
            scratch_shapes=[
                pltpu.VMEM((images, WL * CIN // HD + 1, TOP + HL + 16, HD), F32),
                pltpu.VMEM((TAPS, PATCH * CH), F32),
                pltpu.VMEM((TAPS, PATCH * CH), BF16),
                pltpu.VMEM((PATCH, count, TAPS), BF16),
                pltpu.VMEM((count, width), F32),
                pltpu.VMEM((PATCH, PATCH * CH, width), BF16),
                pltpu.VMEM((2, half, width), BF16),
                pltpu.SemaphoreType.DMA((6,)),
                pltpu.SemaphoreType.DMA((PATCH,)),
                pltpu.SemaphoreType.DMA((2,)),
            ],
        ),
        out_shape=[jax.ShapeDtypeStruct(shape, BF16) for shape in pieces_out]
        + [pltpu.VMEM(w.shape, w.dtype) for w in weights],
        compiler_params=params(32),
        cost_estimate=cost(2 * count * PIX * CH * (256 + width), 4 << 20, count * PIX * CH),
        name="down_stream",
    )(meta, *pieces, conv, gain.reshape(1, width), in_hbm(patch_in), in_hbm(text), *[in_hbm(w) for w in weights])


def full(shape):
    return pl.BlockSpec(shape, lambda i, m: (0,) * len(shape))


def load(pieces):
    return jnp.concatenate([piece[...] for piece in pieces], axis=0)


def take_blocks(refs, count):
    return [[refs.pop(0), refs.pop(0)] for _ in range(count)]


def chip_of(meta, images, tiles, outer, entry):
    _, _, tile, mpo = split_meta(meta, images)
    return lax.rem(tile + tiles - entry // 2, tiles) * outer + lax.rem(mpo + entry % 2, outer)


def qkv_kernel(entries, layout, groups, last, meta, *refs):
    refs = list(refs)
    count = len(entries)
    x_refs = take_blocks(refs, count)
    scaled_ref = refs.pop(-1)
    if last:
        weights_ref, acc_in, square_in, head_gains = [refs.pop(0) for _ in range(4)]
    else:
        weight_refs = [refs.pop(0) for _ in range(6)]
    half, span = scaled_ref.shape
    width = weights_ref.shape[2] if last else weight_refs[0].shape[1]
    heads = width // HD
    square = square_in[...] if last else None
    if last:
        acc, outs = [None] * 6, refs
    else:
        weights_out, acc_out, square_out = refs
    for index in range(count):
        rows = pl.ds(pl.multiple_of(chip_of(meta, *layout, entries[index]) * span, span), span)
        gain = x_refs[index][0][half // 2 :, :][:1]
        for part in range(2):
            at = slice(part * half // 2, (part + 1) * half // 2)
            scaled_ref[at, :] = (x_refs[index][part][: half // 2, :] * gain).astype(BF16)
        value = jnp.concatenate([x_refs[index][0][: half // 2, :], x_refs[index][1][...]], axis=0)
        value = value.astype(F32)
        value = value * value
        for part in range(span // HD):
            piece = value[:, part * HD : (part + 1) * HD]
            square = piece if square is None else square + piece
        for part in range(6):
            if last:
                acc[part] = acc_in[part] + mxu(scaled_ref[...], weights_ref[part])
                continue
            term = mxu(scaled_ref[...], weight_refs[part][rows, :])
            if index == 0:
                acc_out[part] = term
            else:
                acc_out[part] += term
    if not last:
        square_out[...] = square
        rows = pl.ds(pl.multiple_of(chip_of(meta, *layout, len(entries)) * span, span), span)
        for part in range(6):
            weights_out[part] = weight_refs[part][rows, :]
        return
    mean = jnp.sum(square, axis=-1, keepdims=True) * (1.0 / (groups * span))
    scale = lax.rsqrt(mean + EPSILON)
    for part in range(6):
        total = acc[part] * scale
        side, kind = part // 3, part % 3
        kv_outs = outs[2 * heads * side : 2 * heads * side + heads]
        q_outs = outs[2 * heads * side + heads : 2 * heads * (side + 1)]
        for head in range(heads):
            raw = total[:, head * HD : (head + 1) * HD]
            if kind == 1:
                kv_outs[head][1] = raw.astype(BF16)
                continue
            raw = raw * lax.rsqrt(jnp.mean(raw * raw, axis=-1, keepdims=True) + EPSILON)
            if kind == 0:
                kv_outs[head][0] = (raw * head_gains[1:2, :]).astype(BF16)
            else:
                q_outs[head][...] = (raw * (head_gains[0:1, :] * HD ** (-0.5))).astype(BF16)


def qkv_step(meta, layout, blocks, entries, weights, state, head_gains):
    span = blocks[0][1].shape[1]
    half = 2 * blocks[0][1].shape[0]
    count, last = len(blocks), state is not None
    width = state[0].shape[2] if last else weights[0].shape[1]
    groups = layout[1] * layout[2]
    inputs = [p for pieces in blocks for p in pieces]
    specs = [full(p.shape) for pieces in blocks for p in pieces]
    scratch = [pltpu.VMEM((half, span), BF16)]
    if last:
        specs += [HELD] * 3 + [full(head_gains.shape)]
        inputs += list(state) + [head_gains]
        heads = width // HD
        outs = [pltpu.HBM((2, half, HD), BF16)] * heads + [pltpu.HBM((half, HD), BF16)] * heads
        outs = outs * 2
    else:
        specs += [HELD] * 6
        inputs += list(weights)
        outs = [
            pltpu.VMEM((6, span, width), BF16),
            pltpu.VMEM((6, half, width), F32),
            pltpu.VMEM((half, HD), F32),
        ]
    return pl.pallas_call(
        functools.partial(qkv_kernel, entries, layout, groups, last),
        grid_spec=pltpu.PrefetchScalarGridSpec(
            num_scalar_prefetch=1,
            grid=(1,),
            in_specs=specs,
            out_specs=[full(o.shape) if last else HELD for o in outs],
            scratch_shapes=scratch,
        ),
        out_shape=outs,
        compiler_params=params(20),
        cost_estimate=cost(12 * count * half * span * width, (6 + 2 * count) << 20),
        name="qkv_last" if last else "qkv_step",
    )(meta, *inputs)


def attention_kernel(images, pieces, half, meta, *refs):
    ctx, core, _, _ = split_meta(meta, images)
    ctxs = pieces // 2
    bases = []
    for piece in range(pieces):
        side = jnp.bitwise_xor(core, piece % 2)
        bases.append(lax.rem(ctx + ctxs - piece // 2, ctxs) * (2 * half) + side * half)
    q_refs, kv_refs, out_refs = refs[:2], refs[2 : 2 + pieces], refs[2 + pieces :]
    rows = q_refs[0].shape[0]
    step = pl.program_id(0)
    for side in range(2):
        place = bases[side] + step * rows + lax.broadcasted_iota(jnp.int32, (rows, 1), 0)
        limit = place
        for image in range(images):
            inner = place - meta[image]
            limit = jnp.where((inner >= 0) & (inner < IMG_TOK), meta[image] + IMG_TOK - 1, limit)
        for head in range(q_refs[0].shape[1] // HD):
            lanes = slice(head * HD, (head + 1) * HD)
            query = q_refs[side][:, lanes]
            scores = []
            top = None
            for piece in range(pieces):
                score = lax.dot_general(
                    query, kv_refs[piece][0, :, lanes], (((1,), (1,)), ((), ())), preferred_element_type=F32
                )
                position = lax.broadcasted_iota(jnp.int32, score.shape, 1)
                score = jnp.where(position <= limit - bases[piece], score, NEGATIVE_FILL)
                scores.append(score)
                best = jnp.max(score, axis=1, keepdims=True)
                top = best if top is None else jnp.maximum(top, best)
            total = jnp.zeros((rows, 1), F32)
            product = jnp.zeros((rows, HD), F32)
            for piece in range(pieces):
                weight = jnp.exp(scores[piece] - top)
                total = total + jnp.sum(weight, axis=1, keepdims=True)
                product = product + mxu(weight.astype(BF16), kv_refs[piece][1, :, lanes])
            out_refs[side][:, lanes] = (product / total).astype(BF16)


def attention(meta, queries, pieces, images):
    half, width = queries[0].shape
    block = 256
    keys = half * len(pieces)
    rows = pl.BlockSpec((block, width), lambda i, m: (i, 0))
    return pl.pallas_call(
        functools.partial(attention_kernel, images, len(pieces), half),
        grid_spec=pltpu.PrefetchScalarGridSpec(
            num_scalar_prefetch=1,
            grid=(half // block,),
            in_specs=[rows, rows] + [full(p.shape) for p in pieces],
            out_specs=[rows, rows],
        ),
        out_shape=[jax.ShapeDtypeStruct((half, width), BF16)] * 2,
        compiler_params=params(24),
        cost_estimate=cost(8 * half * keys * width, 4 * keys * width, 2 * half * keys * width // HD),
        name="attention",
    )(meta, *queries, *pieces)


def out_kernel(count, first, last, meta, *refs):
    refs = list(refs)
    x_refs = take_blocks(refs, count)
    weight_refs = [[refs.pop(0), refs.pop(0)] for _ in range(count)]
    if first:
        streams = [refs.pop(0) for _ in range(4)]
        block = streams[1].shape[0]
    else:
        acc_in = refs.pop(0)
    outs = refs
    for side in range(2):
        if first:
            rows = [streams[2 * side][:block, :], streams[2 * side + 1][...]]
            total = jnp.concatenate(rows, axis=0).astype(F32)
        else:
            total = acc_in[side]
        for index in range(count):
            total = total + mxu(load(x_refs[index]), weight_refs[index][side][...])
        if last:
            outs[side][...] = total.astype(BF16)
        else:
            outs[0][side] = total


def out_step(meta, layout, blocks, entries, weights, state, last):
    span, width = blocks[0][0].shape[1], weights[0].shape[1]
    half = 2 * blocks[0][0].shape[0]
    first = isinstance(state, list)
    count = len(blocks)
    inputs = [p for pieces in blocks for p in pieces]
    specs = [full(p.shape) for p in inputs]
    for entry in entries:
        index = lambda i, m, entry=entry: (chip_of(m, *layout, entry), 0)
        inputs += weights
        specs += [pl.BlockSpec((span, width), index)] * 2
    states = state if first else [state]
    inputs += states
    specs += [full(s.shape) for s in states]
    if last:
        outs = [jax.ShapeDtypeStruct((half, width), BF16)] * 2
    else:
        outs = [jax.ShapeDtypeStruct((2, half, width), F32)]
    result = pl.pallas_call(
        functools.partial(out_kernel, count, first, last),
        grid_spec=pltpu.PrefetchScalarGridSpec(
            num_scalar_prefetch=1,
            grid=(1,),
            in_specs=specs,
            out_specs=[full(o.shape) for o in outs],
        ),
        out_shape=outs,
        compiler_params=params(24),
        cost_estimate=cost(4 * count * half * span * width, (2 + count) << 20),
        name="out_last" if last else "out_step",
    )(meta, *inputs)
    return result if last else result[0]


def pick_kernel(images, ctxs, meta, own_ref, par_ref, *out_refs):
    half = own_ref.shape[0]
    ctx, core, _, _ = split_meta(meta, images)
    for target in range(2 * ctxs):
        to_core = jnp.bitwise_xor(core, target % 2)
        slot = 2 * lax.rem(ctx + target // 2, ctxs) + to_core
        start = meta[meta[2 * images + slot]]
        place = start + lax.broadcasted_iota(jnp.int32, (IMG_TOK, half), 0)
        column = ctx * (2 * half) + lax.broadcasted_iota(jnp.int32, (IMG_TOK, half), 1)
        own = jnp.where(place == column + core * half, 1.0, 0.0).astype(BF16)
        par = jnp.where(place == column + (1 - core) * half, 1.0, 0.0).astype(BF16)
        out_refs[target][...] = (mxu(own, own_ref[...]) + mxu(par, par_ref[...])).astype(BF16)


def pick_rows(meta, own, par, images, ctxs):
    half, width = own.shape
    targets = 2 * ctxs
    return pl.pallas_call(
        functools.partial(pick_kernel, images, ctxs),
        grid_spec=pltpu.PrefetchScalarGridSpec(
            num_scalar_prefetch=1,
            grid=(1,),
            in_specs=[full(own.shape), full(par.shape)],
            out_specs=[full((IMG_TOK, width))] * targets,
        ),
        out_shape=[jax.ShapeDtypeStruct((IMG_TOK, width), BF16)] * targets,
        compiler_params=params(16),
        cost_estimate=cost(targets * 4 * IMG_TOK * half * width, 1 << 20),
        name="pick_rows",
    )(meta, own, par)


def merge_kernel(*refs):
    out_refs = refs[-2:]
    refs = refs[:-2]
    sides = refs[: len(refs) // 2], refs[len(refs) // 2 :]
    width = sides[0][0].shape[1]
    block = IMG_TOK // 2
    for side in range(2):
        total = sides[side][0][...].astype(F32)
        for part in sides[side][1:]:
            total = total + part[...].astype(F32)
        total = total.astype(BF16)
        for index in range(2):
            out_refs[index][:, side * width : (side + 1) * width] = total[index * block : (index + 1) * block]


def merge_picks(own_parts, par_parts):
    width = own_parts[0].shape[1]
    return pl.pallas_call(
        merge_kernel,
        out_shape=[jax.ShapeDtypeStruct((IMG_TOK // 2, 2 * width), BF16)] * 2,
        compiler_params=pltpu.CompilerParams(vmem_limit_bytes=8 << 20),
        cost_estimate=cost(1 << 20, 1 << 20),
        name="merge_picks",
    )(*own_parts, *par_parts)


def finish_kernel(core_ref, own_a, own_b, par_a, par_b, out_ref, sums, lines):
    core = core_ref[0]
    for side, (left, right) in enumerate(((own_a, own_b), (par_a, par_b))):
        sums[side] = left[...] + right[...]
    rows = sums.shape[1] // SIDE
    lanes = PATCH * CIN
    per = HD // lanes
    for side in range(2):
        for part in range(SIDE // per):
            cols = [sums[side, pl.ds(part * per + k, rows, stride=SIDE), :] for k in range(per)]
            for row in range(PATCH):
                pieces = [col[:, row * lanes : (row + 1) * lanes] for col in cols]
                lines[part, pl.ds(row, rows, stride=PATCH), :] = jnp.concatenate(pieces, axis=1)
        slot = jnp.bitwise_xor(core, side)
        for part in range(SIDE // per):
            out_ref[slot, :, part * HD : (part + 1) * HD] = lines[part]


def finish(core, own_a, own_b, par_a, par_b):
    count = own_a.shape[0]
    return pl.pallas_call(
        finish_kernel,
        grid_spec=pltpu.PrefetchScalarGridSpec(
            num_scalar_prefetch=1,
            grid=(1,),
            in_specs=[full(own_a.shape)] * 4,
            out_specs=full((2, count // PATCH, WL * CIN)),
            scratch_shapes=[
                pltpu.VMEM((2, count, PIX * CIN), F32),
                pltpu.VMEM((WL * CIN // HD, count // PATCH, HD), F32),
            ],
        ),
        out_shape=jax.ShapeDtypeStruct((2, count // PATCH, WL * CIN), F32),
        compiler_params=params(8),
        cost_estimate=cost(1 << 16, 1 << 18),
        name="finish",
    )(core, own_a, own_b, par_a, par_b)


def spread(active, spread_ref):
    row = lax.broadcasted_iota(jnp.int32, (IMG_TOK, PIX * CIN), 0)
    patch_row, patch_col = row >> 4, row & (SIDE - 1)
    total = None
    for index in range(9):
        down, right = index // 3 - 1, index % 3 - 1
        part = mxu(active, spread_ref[:, index * PIX * CIN : (index + 1) * PIX * CIN])
        offset = down * SIDE + right
        if offset:
            part = pltpu.roll(part, offset % IMG_TOK, 0)
        source_row, source_col = patch_row - down, patch_col - right
        inside = (source_row >= 0) & (source_row < SIDE) & (source_col >= 0) & (source_col < SIDE)
        part = jnp.where(inside, part, 0.0)
        total = part if total is None else total + part
    return total


def up_kernel(count, halves, first, last, *refs):
    refs = list(refs)
    x_refs = take_blocks(refs, count)
    weight_refs = [[[refs.pop(0) for _ in range(2)] for _ in range(halves)] for _ in range(count)]
    acc_in = None if first else refs.pop(0)
    spread_ref = refs.pop(0) if last else None
    out_ref = refs[0]
    width = x_refs[0][0].shape[1] // 2
    values = [load(pieces) for pieces in x_refs]
    totals = []
    for part in range(halves):
        total = None if first else acc_in[part]
        for block in range(count):
            for side in range(2):
                term = mxu(
                    values[block][:, side * width : (side + 1) * width],
                    weight_refs[block][part][side][0],
                )
                total = term if total is None else total + term
        totals.append(total)
        if not last:
            out_ref[part] = total
    if last:
        active = [silu(total).astype(BF16) for total in totals]
        active = jnp.concatenate(active, axis=1) if halves > 1 else active[0]
        out_ref[...] = spread(active, spread_ref)


def up_step(blocks, entries, weights, state, spread_weight):
    span = blocks[0][0].shape[1]
    halves, count = len(weights), len(blocks)
    first, last = state is None, spread_weight is not None
    whole = lambda shape: pl.BlockSpec(shape, lambda i: (0,) * len(shape))
    inputs = [p for pieces in blocks for p in pieces]
    specs = [whole(p.shape) for p in inputs]
    for entry in entries:
        for sides in weights:
            for weight in sides:
                inputs.append(weight)
                specs.append(pl.BlockSpec((1, span // 2, CH), lambda i, entry=entry: (entry, 0, 0)))
    if not first:
        inputs.append(state)
        specs.append(whole(state.shape))
    if last:
        inputs.append(spread_weight)
        specs.append(whole(spread_weight.shape))
        out = jax.ShapeDtypeStruct((IMG_TOK, PIX * CIN), F32)
    else:
        out = jax.ShapeDtypeStruct((halves, IMG_TOK, CH), F32)
    return pl.pallas_call(
        functools.partial(up_kernel, count, halves, first, last),
        grid=(1,),
        in_specs=specs,
        out_specs=whole(out.shape),
        out_shape=out,
        compiler_params=params(16),
        cost_estimate=cost(2 * count * IMG_TOK * span * CH * halves, (1 + count) << 20),
        name="up_last" if last else "up_step",
    )(*inputs)


def spread_weights(up_conv, pixels):
    taps = up_conv.reshape(9, CH, CIN).transpose(1, 0, 2).reshape(CH, 9 * CIN)
    shape = (pixels.shape[0], 9 * CIN, 9 * PIX * CIN)
    row = lax.broadcasted_iota(jnp.int32, shape, 1)
    col = lax.broadcasted_iota(jnp.int32, shape, 2)
    pixel = pixels[:, None, None]
    tap, channel = row >> 3, row & 7
    patch, target, out_channel = col >> 7, (col >> 3) & 15, col & 7
    tap_row, tap_col = tap // 3, tap % 3
    down, right = patch // 3 - 1, patch % 3 - 1
    hit = (
        (channel == out_channel)
        & ((pixel >> 2) + 1 - tap_row == (target >> 2) + PATCH * down)
        & ((pixel & 3) + 1 - tap_col == (target & 3) + PATCH * right)
    )
    placed = jnp.where(hit, 1.0, 0.0).astype(BF16)
    spread = jnp.einsum("ct,ptn->pcn", taps, placed, preferred_element_type=F32)
    return spread.astype(BF16).reshape(pixels.shape[0] * CH, 9 * PIX * CIN)


def by_core(core, own, other, axis):
    return jnp.where(
        core == 0, jnp.concatenate([own, other], axis), jnp.concatenate([other, own], axis)
    )


def shift(values, axis, step):
    count = lax.axis_size(axis)
    return lax.ppermute(values, axis, [(i, (i + step) % count) for i in range(count)])


def gather_small(latents, down_conv, *others):
    ctxs, tiles = lax.axis_size("ctx"), lax.axis_size("tile")
    every = jnp.concatenate([latents] + [shift(latents, "ctx", s) for s in range(1, ctxs)])
    conv = by_core(lax.axis_index("core"), down_conv, swap(down_conv), 1)
    conv = by_core(lax.axis_index("mpo"), conv, shift(conv, "mpo", 1), 1)
    every, others = lax.optimization_barrier((every, others))
    return [every] + [shift(every, "tile", s) for s in range(1, tiles)], conv, *others


def columns_kernel(meta, kept_in, sent_in, kept_out, sent_out):
    kept_out[0] = kept_in[...]
    sent_out[0] = sent_in[...]


def transpose_first(meta, patch_out, layout, ctxs):
    images, tiles, outer = layout
    width, features = patch_out.shape
    deep = features // (tiles * outer)
    halves = 2 if ctxs == 2 and deep == 2 * CH else 1
    size = deep // halves

    def place(other):
        def index(i, m):
            ctx, _, _, mpo = split_meta(m, images)
            chip = i * outer + lax.rem(mpo + other, outer)
            return 0, chip * halves + (ctx if halves == 2 else 0)

        return pl.BlockSpec((width, size), index)

    out = pl.BlockSpec((1, width, size), lambda i, m: (i, 0, 0))
    patch_out = in_hbm(patch_out)
    kept, sent = pl.pallas_call(
        columns_kernel,
        grid_spec=pltpu.PrefetchScalarGridSpec(
            num_scalar_prefetch=1, grid=(tiles,), in_specs=[place(0), place(1)], out_specs=[out, out]
        ),
        out_shape=[jax.ShapeDtypeStruct((tiles, width, size), BF16)] * 2,
        compiler_params=params(8),
        cost_estimate=cost(1 << 16, 2 << 20),
        name="columns",
    )(meta, patch_out, patch_out)
    return kept, sent, halves


def transpose_second(kept, received, step):
    tiles = lax.axis_size("tile")
    place = lax.rem(lax.axis_index("tile") + step, tiles)
    block = [lax.dynamic_index_in_dim(x, place, 0, keepdims=False) for x in (kept, received)]
    block = jnp.stack(block)
    return shift(block, "tile", step) if step else block


def gather_pair(first, second, state, step, extras=None):
    tiles = lax.axis_size("tile")
    found, moving = [{0: first}, {0: second}], [None, None]

    def launch(which, index):
        ring = found[which][2 * index]
        if index < tiles - 1:
            moving[which] = (shift(ring, "tile", 1), shift(ring, "mpo", 1))
        elif which:
            moving[which] = shift(found[which][2 * index - 1], "tile", 1)
        else:
            moving[which] = shift(ring, "mpo", 1)

    launch(0, 0)
    launch(1, 0)
    seen = first
    for index in range(1, tiles):
        for which in range(2):
            ring, cross = moving[which]
            ring, cross, seen = lax.optimization_barrier((ring, cross, seen))
            found[which][2 * index], found[which][2 * index - 1] = ring, cross
            seen = ring
            launch(which, index)
    entries = list(range(2 * tiles - 1))
    state = step([[found[0][e], found[1][e]] for e in entries], entries, state, False)
    last = lax.optimization_barrier((moving[0], moving[1], state, extras))
    return step([[last[0], last[1]]], [2 * tiles - 1], last[2], True), last[3]


def shards(
    text_embed,
    latents,
    down_conv,
    patch_in,
    norm_gain,
    query_weight,
    key_weight,
    value_weight,
    query_gain,
    key_gain,
    out_weight,
    patch_out,
    up_conv,
    span_start,
    image_of_slot,
):
    ctxs, tiles, outer = (lax.axis_size(name) for name in ("ctx", "tile", "mpo"))
    ctx, tile, mpo, core = (lax.axis_index(name) for name in ("ctx", "tile", "mpo", "core"))
    seq_rows, width = text_embed.shape
    half = seq_rows // 2
    images = span_start.shape[0]
    local = latents.shape[0]

    numbers = jnp.arange(images, dtype=jnp.int32)
    matches = image_of_slot[None, :] == numbers[:, None]
    slot_of_image = jnp.sum(jnp.where(matches, numbers[None, :], 0), axis=1)
    slot_place = lax.rem(ctx + ctxs - slot_of_image // local, ctxs) * local + slot_of_image % local
    meta = jnp.concatenate(
        [span_start, slot_place, image_of_slot, jnp.stack([ctx, core, tile, mpo])]
    ).astype(jnp.int32)
    layout = (images, tiles, outer)

    weights = [swap(w) for w in (key_weight, value_weight, query_weight)]
    pieces, conv, meta, weights[0], weights[1] = gather_small(latents, down_conv, meta, *weights[:2])
    later, pieces[1] = lax.optimization_barrier((meta, pieces[1]))
    kept, sent, halves = transpose_first(later, patch_out, layout, ctxs)
    pieces, sent = lax.optimization_barrier((pieces, sent))
    received = shift(sent, "mpo", 1)
    weights += [key_weight, value_weight, query_weight]
    streams = down_stream(meta, pieces, conv, patch_in, text_embed, norm_gain, weights, images)
    streams, held_weights = [streams[:2], streams[2:4]], streams[4:]
    streams, received = lax.optimization_barrier((streams, received))
    others = [swap(s[1]) for s in streams]
    others = lax.optimization_barrier(others)

    head_gains = jnp.stack([query_gain, key_gain])

    def project(blocks, entries, state, last):
        return qkv_step(
            meta, layout, blocks, entries, held_weights, state, head_gains
        )

    state, out_par = gather_pair(
        *[by_core(core, s[0], o, 1) for s, o in zip(streams, others)], None, project, swap(out_weight)
    )
    heads = width // HD
    state, kept, received = lax.optimization_barrier((state, kept, received))
    kv_send, q_send = state[:heads], state[heads : 2 * heads]
    kv_own, q_own = state[2 * heads : 3 * heads], state[3 * heads :]

    def shifted(values, step, cross):
        pairs = [
            (2 * c + k, 2 * ((c + step) % ctxs) + (1 - k if cross else k))
            for c in range(ctxs)
            for k in range(2)
        ]
        return lax.ppermute(values, ("ctx", "core"), pairs)

    results = []
    for head in range(heads):
        q_par = swap(q_send[head])
        pieces = [kv_own[head], swap(kv_send[head])]
        for step in range(1, ctxs):
            pieces += [shifted(kv_own[head], step, False), shifted(kv_send[head], step, True)]
        q_par, q_send, kv_send, kv_own = lax.optimization_barrier((q_par, q_send, kv_send, kv_own))
        if head == 0:
            up_blocks = [transpose_second(kept, received, step) for step in range(tiles)]
            pieces, up_blocks[tiles // 2] = lax.optimization_barrier((pieces, up_blocks[tiles // 2]))
        results.append(attention(meta, [q_own[head], q_par], pieces, images))
    att_own = [result[0] for result in results]
    att_par = [swap(result[1]) for result in results]
    rows = half // 2
    attended = []
    for at in (0, rows):
        own, par = (
            jnp.concatenate([x[at : at + rows] for x in side], axis=1) for side in (att_own, att_par)
        )
        attended.append(by_core(core, own, par, 1))
    attended, up_blocks = lax.optimization_barrier((attended, up_blocks))
    up_own = jnp.concatenate(up_blocks)
    extras = [up_own, swap(up_own)] + ([shift(up_own, "ctx", 1)] if halves == 2 else [])

    def project_out(blocks, entries, state, last):
        return out_step(meta, layout, blocks, entries, (out_weight, out_par), state, last)

    state = [streams[0][0], streams[1][0], others[0], others[1]]
    state, up_weights = gather_pair(*attended, state, project_out, extras)
    out_own, out_send = state
    out_other = swap(out_send)
    layer_out = by_core(core, out_own, out_other, 0)

    picks, swapped = lax.optimization_barrier(
        (pick_rows(meta, out_own, out_other, images, ctxs), [swap(other) for other in up_weights[2:]])
    )
    up_weights = [up_weights[:2]] + [[up_weights[2], other] for other in swapped]
    own_parts, par_parts = [picks[0]], [swap(picks[1])]
    for step in range(1, ctxs):
        own_parts.append(shifted(picks[2 * step], step, False))
        par_parts.append(shifted(picks[2 * step + 1], step, True))

    pixel = tile * outer + mpo
    pixels = jnp.stack([pixel * halves + lax.rem(ctx + h, halves) for h in range(halves)])
    spread_weight = spread_weights(up_conv, pixels)

    def project_up(blocks, entries, state, last):
        return up_step(blocks, entries, up_weights, state, spread_weight if last else None)

    state, _ = gather_pair(*merge_picks(own_parts, par_parts), None, project_up)

    bands = state.reshape(tiles, IMG_TOK // tiles, PIX * CIN)
    band = lax.dynamic_index_in_dim(bands, tile, 0, keepdims=False)
    for step in range(1, tiles):
        piece = lax.dynamic_index_in_dim(bands, lax.rem(tile + step, tiles), 0, keepdims=False)
        band = band + shift(piece, "tile", step)
    quad = {}
    for name, pairs in (
        ("mpo", [(0, 2), (1, 3), (2, 0), (3, 1)]),
        ("core", [(0, 1), (1, 0), (2, 3), (3, 2)]),
        ("both", [(0, 3), (1, 2), (2, 1), (3, 0)]),
    ):
        quad[name] = lax.ppermute(band, ("mpo", "core"), pairs)
    return layer_out, finish(meta[3 * images + 1 :], band, quad["mpo"], quad["core"], quad["both"])


def solution(mesh):
    ctxs, tiles, parts = mesh.devices.shape
    fine = Mesh(
        mesh.devices.reshape(ctxs, tiles, parts // 2, 2), ("ctx", "tile", "mpo", "core")
    )
    features = ("tile", "mpo", "core")
    return jax.shard_map(
        shards,
        mesh=fine,
        in_specs=(
            P("ctx", features),
            P("ctx", "tile", None),
            P(None, ("mpo", "core")),
            P(None, features),
            P(features),
            P(None, features),
            P(None, features),
            P(None, features),
            P(),
            P(),
            P(None, features),
            P(features, None),
            P(),
            P(),
            P(),
        ),
        out_specs=(P("ctx", features), P("ctx", "tile", None)),
        check_vma=False,
    )
```

```python
import functools

import jax
import jax.numpy as jnp
from jax import lax
from jax.experimental import pallas as pl
from jax.experimental.pallas import tpu as pltpu
from jax.sharding import Mesh
from jax.sharding import PartitionSpec as P

HD = 128
CH = 256
CIN = 8
WL = 64
HL = 64
PATCH = 4
PIX = PATCH * PATCH
SIDE = WL // PATCH
IMG_TOK = 256
EPSILON = 1e-05
NEGATIVE_FILL = -1e30
WINDOW = (PATCH + 2) * CIN
TAPS = 3 * WINDOW
BF16 = jnp.bfloat16
F32 = jnp.float32


def split_meta(meta, images):
    return meta[3 * images], meta[3 * images + 1], meta[3 * images + 2], meta[3 * images + 3]


def params(mebibytes):
    return pltpu.CompilerParams(
        dimension_semantics=("arbitrary",), vmem_limit_bytes=mebibytes * 1024 * 1024
    )


def cost(flops, nbytes, transcendentals=0):
    return pl.CostEstimate(
        flops=int(flops), bytes_accessed=int(nbytes), transcendentals=int(transcendentals)
    )


def silu(values):
    half = values * 0.5
    return half + half * jnp.tanh(half)


def mxu(left, right):
    return jnp.dot(left, right, preferred_element_type=F32)


def swap(values):
    return lax.ppermute(values, "core", [(0, 1), (1, 0)])


HELD = pl.BlockSpec(memory_space=pltpu.VMEM)


def in_hbm(values):
    return pltpu.with_memory_space_constraint(values, pltpu.HBM)


GAIN_ROWS = 16
TOP = 16


def down_kernel(images, tiles, half, meta, *refs):
    lat_refs, refs = refs[:tiles], refs[tiles:]
    conv_ref, gain_ref, patch_hbm, text_hbm = refs[:4]
    weight_refs, first_refs, second_refs, held_refs = refs[4:10], refs[10:12], refs[12:14], refs[14:20]
    grid_rows, conv_wide, conv_bf16, windows, total, patch_ref, text_ref = refs[20:27]
    arrived, patch_arrived, text_arrived = refs[27:]
    step = pl.program_id(0)
    deep = PATCH * CH
    patch_copies = [
        pltpu.make_async_copy(
            patch_hbm.at[index * deep : (index + 1) * deep, :], patch_ref.at[index], patch_arrived.at[index]
        )
        for index in range(PATCH)
    ]
    side_rows = [jnp.bitwise_xor(meta[3 * images + 1], side) * half for side in range(2)]
    text_copies = [
        pltpu.make_async_copy(
            text_hbm.at[pl.ds(pl.multiple_of(side_rows[side], half), half), :],
            text_ref.at[side],
            text_arrived.at[side],
        )
        for side in range(2)
    ]
    copies = [
        pltpu.make_async_copy(weight, held, arrived.at[index])
        for index, (weight, held) in enumerate(zip(weight_refs, held_refs))
    ]

    @pl.when(step == 0)
    def _():
        for copy in patch_copies + text_copies + copies:
            copy.start()

    group = images * SIDE
    ctx, core, tile, _ = split_meta(meta, images)

    @pl.when(step == 0)
    def _():
        grid_rows[...] = jnp.zeros_like(grid_rows)
        blocks = grid_rows.shape[1]
        for index in range(tiles):
            band = lat_refs[index].shape[1]
            at = TOP + lax.rem(tile + tiles - index, tiles) * band
            rows = pl.ds(pl.multiple_of(at, 8), band)
            latent = lat_refs[index][...].astype(F32)
            edges = [jnp.zeros((images, band, size), F32) for size in (CIN, HD - CIN)]
            wide = jnp.concatenate([edges[0], latent, edges[1]], axis=2)
            for part in range(blocks):
                grid_rows[:, part, rows, :] = wide[:, :, part * HD : (part + 1) * HD]
        conv_wide[...] = jnp.zeros_like(conv_wide)
        conv = conv_ref[...].astype(F32)
        for col in range(PATCH):
            for tap in range(3):
                at = WINDOW * tap + CIN * col
                conv_wide[at : at + 3 * CIN, CH * col : CH * (col + 1)] = conv[
                    3 * CIN * tap : 3 * CIN * (tap + 1), :
                ]
        conv_bf16[...] = conv_wide[...].astype(BF16)

        def build(image, carry):
            for row in range(PATCH + 2):
                take = pl.ds(TOP - 1 + row, SIDE, stride=PATCH)
                line = [grid_rows[image, part, take, :] for part in range(blocks)]
                line = jnp.concatenate(line, axis=1).astype(BF16)
                for col in range(SIDE):
                    piece = line[:, PATCH * CIN * col : PATCH * CIN * col + WINDOW]
                    at = pl.ds(pl.multiple_of(group * col + image * SIDE, SIDE), SIDE)
                    for shift in range(3):
                        if 0 <= row - shift < PATCH:
                            windows[row - shift, at, WINDOW * shift : WINDOW * (shift + 1)] = piece
            return carry

        lax.fori_loop(0, images, build, 0)
        total[...] = jnp.zeros_like(total)

    for index in range(PATCH):
        pl.when(step == index)(patch_copies[index].wait)

    chunk = 256
    for part in range(images * IMG_TOK // chunk):
        rows = slice(part * chunk, (part + 1) * chunk)
        hidden = silu(mxu(windows[step, rows, :], conv_bf16[...])).astype(BF16)
        total[rows, :] += mxu(hidden, patch_ref[step])

    @pl.when(step == PATCH - 1)
    def _():
        tokens = total[...].astype(BF16)
        block = half // 2
        for copy in text_copies:
            copy.wait()
        for side in range(2):
            base = ctx * (2 * half) + jnp.bitwise_xor(core, side) * half
            for part, out_ref in enumerate((first_refs[side], second_refs[side])):
                place = base + part * block + lax.broadcasted_iota(jnp.int32, (block, 1), 0)
                source = jnp.full((block, 1), -1, jnp.int32)
                for image in range(images):
                    inner = place - meta[image]
                    inside = (inner >= 0) & (inner < IMG_TOK)
                    index = (inner & (SIDE - 1)) * group + meta[images + image] * SIDE + (inner >> 4)
                    source = jnp.where(inside, index, source)
                choice = source == lax.broadcasted_iota(jnp.int32, (block, images * IMG_TOK), 1)
                picked = mxu(jnp.where(choice, 1.0, 0.0).astype(BF16), tokens)
                text = text_ref[side, part * block : (part + 1) * block, :].astype(F32)
                out_ref[:block, :] = jnp.where(source >= 0, picked, text).astype(BF16)
            gain = gain_ref[...].astype(F32)
            first_refs[side][block:, :] = jnp.broadcast_to(gain, (GAIN_ROWS, gain.shape[1])).astype(BF16)
        for copy in copies:
            copy.wait()


def down_stream(meta, pieces, conv, patch_in, text, gain, weights, images):
    seq_rows, width = text.shape
    half = seq_rows // 2
    tiles = len(pieces)
    count = images * IMG_TOK
    first, second = (half // 2 + GAIN_ROWS, width), (half // 2, width)
    pieces_out = [first, first, second, second]
    return pl.pallas_call(
        functools.partial(down_kernel, images, tiles, half),
        grid_spec=pltpu.PrefetchScalarGridSpec(
            num_scalar_prefetch=1,
            grid=(PATCH,),
            in_specs=[full(p.shape) for p in pieces]
            + [
                full(conv.shape),
                full((1, width)),
            ]
            + [pl.BlockSpec(memory_space=pltpu.HBM)] * 8,
            out_specs=[full(shape) for shape in pieces_out] + [HELD] * 6,
            scratch_shapes=[
                pltpu.VMEM((images, WL * CIN // HD + 1, TOP + HL + 16, HD), F32),
                pltpu.VMEM((TAPS, PATCH * CH), F32),
                pltpu.VMEM((TAPS, PATCH * CH), BF16),
                pltpu.VMEM((PATCH, count, TAPS), BF16),
                pltpu.VMEM((count, width), F32),
                pltpu.VMEM((PATCH, PATCH * CH, width), BF16),
                pltpu.VMEM((2, half, width), BF16),
                pltpu.SemaphoreType.DMA((6,)),
                pltpu.SemaphoreType.DMA((PATCH,)),
                pltpu.SemaphoreType.DMA((2,)),
            ],
        ),
        out_shape=[jax.ShapeDtypeStruct(shape, BF16) for shape in pieces_out]
        + [pltpu.VMEM(w.shape, w.dtype) for w in weights],
        compiler_params=params(32),
        cost_estimate=cost(2 * count * PIX * CH * (256 + width), 4 << 20, count * PIX * CH),
        name="down_stream",
    )(meta, *pieces, conv, gain.reshape(1, width), in_hbm(patch_in), in_hbm(text), *[in_hbm(w) for w in weights])


def full(shape):
    return pl.BlockSpec(shape, lambda i, m: (0,) * len(shape))


def load(pieces):
    return jnp.concatenate([piece[...] for piece in pieces], axis=0)


def take_blocks(refs, count):
    return [[refs.pop(0), refs.pop(0)] for _ in range(count)]


def chip_of(meta, images, tiles, outer, entry):
    _, _, tile, mpo = split_meta(meta, images)
    return lax.rem(tile + tiles - entry // 2, tiles) * outer + lax.rem(mpo + entry % 2, outer)


def qkv_kernel(entries, layout, groups, last, meta, *refs):
    refs = list(refs)
    count = len(entries)
    x_refs = take_blocks(refs, count)
    scaled_ref = refs.pop(-1)
    if last:
        weights_ref, acc_in, square_in, head_gains = [refs.pop(0) for _ in range(4)]
    else:
        weight_refs = [refs.pop(0) for _ in range(6)]
    half, span = scaled_ref.shape[1:]
    width = weights_ref.shape[2] if last else weight_refs[0].shape[1]
    heads = width // HD
    square = square_in[...] if last else None
    if last:
        acc, outs = [None] * 6, refs
    else:
        weights_out, acc_out, square_out = refs
    for index in range(count):
        rows = pl.ds(pl.multiple_of(chip_of(meta, *layout, entries[index]) * span, span), span)
        gain = x_refs[index][0][half // 2 :, :][:1]
        for part in range(2):
            at = slice(part * half // 2, (part + 1) * half // 2)
            scaled_ref[index, at, :] = (x_refs[index][part][: half // 2, :] * gain).astype(BF16)
        value = jnp.concatenate([x_refs[index][0][: half // 2, :], x_refs[index][1][...]], axis=0)
        value = value.astype(F32)
        value = value * value
        for part in range(span // HD):
            piece = value[:, part * HD : (part + 1) * HD]
            square = piece if square is None else square + piece
    for part in range(6):
        if last:
            acc[part] = acc_in[part] + mxu(scaled_ref[0], weights_ref[part])
            continue
        total = None
        for index in range(count):
            rows = pl.ds(pl.multiple_of(chip_of(meta, *layout, entries[index]) * span, span), span)
            term = mxu(scaled_ref[index], weight_refs[part][rows, :])
            total = term if total is None else total + term
        acc_out[part] = total
    if not last:
        square_out[...] = square
        rows = pl.ds(pl.multiple_of(chip_of(meta, *layout, len(entries)) * span, span), span)
        for part in range(6):
            weights_out[part] = weight_refs[part][rows, :]
        return
    mean = jnp.sum(square, axis=-1, keepdims=True) * (1.0 / (groups * span))
    scale = lax.rsqrt(mean + EPSILON)
    for part in range(6):
        total = acc[part] * scale
        side, kind = part // 3, part % 3
        kv_outs = outs[2 * heads * side : 2 * heads * side + heads]
        q_outs = outs[2 * heads * side + heads : 2 * heads * (side + 1)]
        for head in range(heads):
            raw = total[:, head * HD : (head + 1) * HD]
            if kind == 1:
                kv_outs[head][1] = raw.astype(BF16)
                continue
            raw = raw * lax.rsqrt(jnp.mean(raw * raw, axis=-1, keepdims=True) + EPSILON)
            if kind == 0:
                kv_outs[head][0] = (raw * head_gains[1:2, :]).astype(BF16)
            else:
                q_outs[head][...] = (raw * (head_gains[0:1, :] * HD ** (-0.5))).astype(BF16)


def qkv_step(meta, layout, blocks, entries, weights, state, head_gains):
    span = blocks[0][1].shape[1]
    half = 2 * blocks[0][1].shape[0]
    count, last = len(blocks), state is not None
    width = state[0].shape[2] if last else weights[0].shape[1]
    groups = layout[1] * layout[2]
    inputs = [p for pieces in blocks for p in pieces]
    specs = [full(p.shape) for pieces in blocks for p in pieces]
    scratch = [pltpu.VMEM((count, half, span), BF16)]
    if last:
        specs += [HELD] * 3 + [full(head_gains.shape)]
        inputs += list(state) + [head_gains]
        heads = width // HD
        outs = [pltpu.HBM((2, half, HD), BF16)] * heads + [pltpu.HBM((half, HD), BF16)] * heads
        outs = outs * 2
    else:
        specs += [HELD] * 6
        inputs += list(weights)
        outs = [
            pltpu.VMEM((6, span, width), BF16),
            pltpu.VMEM((6, half, width), F32),
            pltpu.VMEM((half, HD), F32),
        ]
    return pl.pallas_call(
        functools.partial(qkv_kernel, entries, layout, groups, last),
        grid_spec=pltpu.PrefetchScalarGridSpec(
            num_scalar_prefetch=1,
            grid=(1,),
            in_specs=specs,
            out_specs=[full(o.shape) if last else HELD for o in outs],
            scratch_shapes=scratch,
        ),
        out_shape=outs,
        compiler_params=params(20),
        cost_estimate=cost(12 * count * half * span * width, (6 + 2 * count) << 20),
        name="qkv_last" if last else "qkv_step",
    )(meta, *inputs)


def attention_kernel(images, pieces, half, meta, *refs):
    ctx, core, _, _ = split_meta(meta, images)
    ctxs = pieces // 2
    bases = []
    for piece in range(pieces):
        side = jnp.bitwise_xor(core, piece % 2)
        bases.append(lax.rem(ctx + ctxs - piece // 2, ctxs) * (2 * half) + side * half)
    q_refs, kv_refs, out_refs = refs[:2], refs[2 : 2 + pieces], refs[2 + pieces :]
    rows = q_refs[0].shape[0]
    step = pl.program_id(0)
    for side in range(2):
        place = bases[side] + step * rows + lax.broadcasted_iota(jnp.int32, (rows, 1), 0)
        limit = place
        for image in range(images):
            inner = place - meta[image]
            limit = jnp.where((inner >= 0) & (inner < IMG_TOK), meta[image] + IMG_TOK - 1, limit)
        for head in range(q_refs[0].shape[1] // HD):
            lanes = slice(head * HD, (head + 1) * HD)
            query = q_refs[side][:, lanes]
            scores = []
            top = None
            for piece in range(pieces):
                score = lax.dot_general(
                    query, kv_refs[piece][0, :, lanes], (((1,), (1,)), ((), ())), preferred_element_type=F32
                )
                position = lax.broadcasted_iota(jnp.int32, score.shape, 1)
                score = jnp.where(position <= limit - bases[piece], score, NEGATIVE_FILL)
                scores.append(score)
                best = jnp.max(score, axis=1, keepdims=True)
                top = best if top is None else jnp.maximum(top, best)
            total = jnp.zeros((rows, 1), F32)
            product = jnp.zeros((rows, HD), F32)
            for piece in range(pieces):
                weight = jnp.exp(scores[piece] - top)
                total = total + jnp.sum(weight, axis=1, keepdims=True)
                product = product + mxu(weight.astype(BF16), kv_refs[piece][1, :, lanes])
            out_refs[side][:, lanes] = (product / total).astype(BF16)


def attention(meta, queries, pieces, images):
    half, width = queries[0].shape
    block = 256
    keys = half * len(pieces)
    rows = pl.BlockSpec((block, width), lambda i, m: (i, 0))
    return pl.pallas_call(
        functools.partial(attention_kernel, images, len(pieces), half),
        grid_spec=pltpu.PrefetchScalarGridSpec(
            num_scalar_prefetch=1,
            grid=(half // block,),
            in_specs=[rows, rows] + [full(p.shape) for p in pieces],
            out_specs=[rows, rows],
        ),
        out_shape=[jax.ShapeDtypeStruct((half, width), BF16)] * 2,
        compiler_params=params(24),
        cost_estimate=cost(8 * half * keys * width, 4 * keys * width, 2 * half * keys * width // HD),
        name="attention",
    )(meta, *queries, *pieces)


def out_kernel(count, first, last, meta, *refs):
    refs = list(refs)
    x_refs = take_blocks(refs, count)
    weight_refs = [[refs.pop(0), refs.pop(0)] for _ in range(count)]
    if first:
        streams = [refs.pop(0) for _ in range(4)]
        block = streams[1].shape[0]
    else:
        acc_in = refs.pop(0)
    outs = refs
    for side in range(2):
        if first:
            rows = [streams[2 * side][:block, :], streams[2 * side + 1][...]]
            total = jnp.concatenate(rows, axis=0).astype(F32)
        else:
            total = acc_in[side]
        for index in range(count):
            total = total + mxu(load(x_refs[index]), weight_refs[index][side][...])
        if last:
            outs[side][...] = total.astype(BF16)
        else:
            outs[0][side] = total


def out_step(meta, layout, blocks, entries, weights, state, last):
    span, width = blocks[0][0].shape[1], weights[0].shape[1]
    half = 2 * blocks[0][0].shape[0]
    first = isinstance(state, list)
    count = len(blocks)
    inputs = [p for pieces in blocks for p in pieces]
    specs = [full(p.shape) for p in inputs]
    for entry in entries:
        index = lambda i, m, entry=entry: (chip_of(m, *layout, entry), 0)
        inputs += weights
        specs += [pl.BlockSpec((span, width), index)] * 2
    states = state if first else [state]
    inputs += states
    specs += [full(s.shape) for s in states]
    if last:
        outs = [jax.ShapeDtypeStruct((half, width), BF16)] * 2
    else:
        outs = [jax.ShapeDtypeStruct((2, half, width), F32)]
    result = pl.pallas_call(
        functools.partial(out_kernel, count, first, last),
        grid_spec=pltpu.PrefetchScalarGridSpec(
            num_scalar_prefetch=1,
            grid=(1,),
            in_specs=specs,
            out_specs=[full(o.shape) for o in outs],
        ),
        out_shape=outs,
        compiler_params=params(24),
        cost_estimate=cost(4 * count * half * span * width, (2 + count) << 20),
        name="out_last" if last else "out_step",
    )(meta, *inputs)
    return result if last else result[0]


def pick_kernel(images, ctxs, meta, own_ref, par_ref, *out_refs):
    half = own_ref.shape[0]
    ctx, core, _, _ = split_meta(meta, images)
    for target in range(2 * ctxs):
        to_core = jnp.bitwise_xor(core, target % 2)
        slot = 2 * lax.rem(ctx + target // 2, ctxs) + to_core
        start = meta[meta[2 * images + slot]]
        place = start + lax.broadcasted_iota(jnp.int32, (IMG_TOK, half), 0)
        column = ctx * (2 * half) + lax.broadcasted_iota(jnp.int32, (IMG_TOK, half), 1)
        own = jnp.where(place == column + core * half, 1.0, 0.0).astype(BF16)
        par = jnp.where(place == column + (1 - core) * half, 1.0, 0.0).astype(BF16)
        out_refs[target][...] = (mxu(own, own_ref[...]) + mxu(par, par_ref[...])).astype(BF16)


def pick_rows(meta, own, par, images, ctxs):
    half, width = own.shape
    targets = 2 * ctxs
    return pl.pallas_call(
        functools.partial(pick_kernel, images, ctxs),
        grid_spec=pltpu.PrefetchScalarGridSpec(
            num_scalar_prefetch=1,
            grid=(1,),
            in_specs=[full(own.shape), full(par.shape)],
            out_specs=[full((IMG_TOK, width))] * targets,
        ),
        out_shape=[jax.ShapeDtypeStruct((IMG_TOK, width), BF16)] * targets,
        compiler_params=params(16),
        cost_estimate=cost(targets * 4 * IMG_TOK * half * width, 1 << 20),
        name="pick_rows",
    )(meta, own, par)


def merge_kernel(*refs):
    out_refs = refs[-2:]
    refs = refs[:-2]
    sides = refs[: len(refs) // 2], refs[len(refs) // 2 :]
    width = sides[0][0].shape[1]
    block = IMG_TOK // 2
    for side in range(2):
        total = sides[side][0][...].astype(F32)
        for part in sides[side][1:]:
            total = total + part[...].astype(F32)
        total = total.astype(BF16)
        for index in range(2):
            out_refs[index][:, side * width : (side + 1) * width] = total[index * block : (index + 1) * block]


def merge_picks(own_parts, par_parts):
    width = own_parts[0].shape[1]
    return pl.pallas_call(
        merge_kernel,
        out_shape=[jax.ShapeDtypeStruct((IMG_TOK // 2, 2 * width), BF16)] * 2,
        compiler_params=pltpu.CompilerParams(vmem_limit_bytes=8 << 20),
        cost_estimate=cost(1 << 20, 1 << 20),
        name="merge_picks",
    )(*own_parts, *par_parts)


def finish_kernel(core_ref, own_a, own_b, par_a, par_b, out_ref, sums, lines):
    core = core_ref[0]
    for side, (left, right) in enumerate(((own_a, own_b), (par_a, par_b))):
        sums[side] = left[...] + right[...]
    rows = sums.shape[1] // SIDE
    lanes = PATCH * CIN
    per = HD // lanes
    for side in range(2):
        for part in range(SIDE // per):
            cols = [sums[side, pl.ds(part * per + k, rows, stride=SIDE), :] for k in range(per)]
            for row in range(PATCH):
                pieces = [col[:, row * lanes : (row + 1) * lanes] for col in cols]
                lines[part, pl.ds(row, rows, stride=PATCH), :] = jnp.concatenate(pieces, axis=1)
        slot = jnp.bitwise_xor(core, side)
        for part in range(SIDE // per):
            out_ref[slot, :, part * HD : (part + 1) * HD] = lines[part]


def finish(core, own_a, own_b, par_a, par_b):
    count = own_a.shape[0]
    return pl.pallas_call(
        finish_kernel,
        grid_spec=pltpu.PrefetchScalarGridSpec(
            num_scalar_prefetch=1,
            grid=(1,),
            in_specs=[full(own_a.shape)] * 4,
            out_specs=full((2, count // PATCH, WL * CIN)),
            scratch_shapes=[
                pltpu.VMEM((2, count, PIX * CIN), F32),
                pltpu.VMEM((WL * CIN // HD, count // PATCH, HD), F32),
            ],
        ),
        out_shape=jax.ShapeDtypeStruct((2, count // PATCH, WL * CIN), F32),
        compiler_params=params(8),
        cost_estimate=cost(1 << 16, 1 << 18),
        name="finish",
    )(core, own_a, own_b, par_a, par_b)


def spread(active, spread_ref):
    row = lax.broadcasted_iota(jnp.int32, (IMG_TOK, PIX * CIN), 0)
    patch_row, patch_col = row >> 4, row & (SIDE - 1)
    total = None
    for index in range(9):
        down, right = index // 3 - 1, index % 3 - 1
        part = mxu(active, spread_ref[:, index * PIX * CIN : (index + 1) * PIX * CIN])
        offset = down * SIDE + right
        if offset:
            part = pltpu.roll(part, offset % IMG_TOK, 0)
        source_row, source_col = patch_row - down, patch_col - right
        inside = (source_row >= 0) & (source_row < SIDE) & (source_col >= 0) & (source_col < SIDE)
        part = jnp.where(inside, part, 0.0)
        total = part if total is None else total + part
    return total


def up_kernel(count, halves, first, last, *refs):
    refs = list(refs)
    x_refs = take_blocks(refs, count)
    weight_refs = [[[refs.pop(0) for _ in range(2)] for _ in range(halves)] for _ in range(count)]
    acc_in = None if first else refs.pop(0)
    spread_ref = refs.pop(0) if last else None
    out_ref = refs[0]
    width = x_refs[0][0].shape[1] // 2
    values = [load(pieces) for pieces in x_refs]
    totals = []
    for part in range(halves):
        total = None if first else acc_in[part]
        for block in range(count):
            for side in range(2):
                term = mxu(
                    values[block][:, side * width : (side + 1) * width],
                    weight_refs[block][part][side][0],
                )
                total = term if total is None else total + term
        totals.append(total)
        if not last:
            out_ref[part] = total
    if last:
        active = [silu(total).astype(BF16) for total in totals]
        active = jnp.concatenate(active, axis=1) if halves > 1 else active[0]
        out_ref[...] = spread(active, spread_ref)


def up_step(blocks, entries, weights, state, spread_weight):
    span = blocks[0][0].shape[1]
    halves, count = len(weights), len(blocks)
    first, last = state is None, spread_weight is not None
    whole = lambda shape: pl.BlockSpec(shape, lambda i: (0,) * len(shape))
    inputs = [p for pieces in blocks for p in pieces]
    specs = [whole(p.shape) for p in inputs]
    for entry in entries:
        for sides in weights:
            for weight in sides:
                inputs.append(weight)
                specs.append(pl.BlockSpec((1, span // 2, CH), lambda i, entry=entry: (entry, 0, 0)))
    if not first:
        inputs.append(state)
        specs.append(whole(state.shape))
    if last:
        inputs.append(spread_weight)
        specs.append(whole(spread_weight.shape))
        out = jax.ShapeDtypeStruct((IMG_TOK, PIX * CIN), F32)
    else:
        out = jax.ShapeDtypeStruct((halves, IMG_TOK, CH), F32)
    return pl.pallas_call(
        functools.partial(up_kernel, count, halves, first, last),
        grid=(1,),
        in_specs=specs,
        out_specs=whole(out.shape),
        out_shape=out,
        compiler_params=params(16),
        cost_estimate=cost(2 * count * IMG_TOK * span * CH * halves, (1 + count) << 20),
        name="up_last" if last else "up_step",
    )(*inputs)


def spread_weights(up_conv, pixels):
    taps = up_conv.reshape(9, CH, CIN).transpose(1, 0, 2).reshape(CH, 9 * CIN)
    shape = (pixels.shape[0], 9 * CIN, 9 * PIX * CIN)
    row = lax.broadcasted_iota(jnp.int32, shape, 1)
    col = lax.broadcasted_iota(jnp.int32, shape, 2)
    pixel = pixels[:, None, None]
    tap, channel = row >> 3, row & 7
    patch, target, out_channel = col >> 7, (col >> 3) & 15, col & 7
    tap_row, tap_col = tap // 3, tap % 3
    down, right = patch // 3 - 1, patch % 3 - 1
    hit = (
        (channel == out_channel)
        & ((pixel >> 2) + 1 - tap_row == (target >> 2) + PATCH * down)
        & ((pixel & 3) + 1 - tap_col == (target & 3) + PATCH * right)
    )
    placed = jnp.where(hit, 1.0, 0.0).astype(BF16)
    spread = jnp.einsum("ct,ptn->pcn", taps, placed, preferred_element_type=F32)
    return spread.astype(BF16).reshape(pixels.shape[0] * CH, 9 * PIX * CIN)


def by_core(core, own, other, axis):
    return jnp.where(
        core == 0, jnp.concatenate([own, other], axis), jnp.concatenate([other, own], axis)
    )


def shift(values, axis, step):
    count = lax.axis_size(axis)
    return lax.ppermute(values, axis, [(i, (i + step) % count) for i in range(count)])


def gather_small(latents, down_conv, *others):
    ctxs, tiles = lax.axis_size("ctx"), lax.axis_size("tile")
    every = jnp.concatenate([latents] + [shift(latents, "ctx", s) for s in range(1, ctxs)])
    conv = by_core(lax.axis_index("core"), down_conv, swap(down_conv), 1)
    conv = by_core(lax.axis_index("mpo"), conv, shift(conv, "mpo", 1), 1)
    every, others = lax.optimization_barrier((every, others))
    return [every] + [shift(every, "tile", s) for s in range(1, tiles)], conv, *others


def columns_kernel(meta, kept_in, sent_in, kept_out, sent_out):
    kept_out[0] = kept_in[...]
    sent_out[0] = sent_in[...]


def transpose_first(meta, patch_out, layout, ctxs):
    images, tiles, outer = layout
    width, features = patch_out.shape
    deep = features // (tiles * outer)
    halves = 2 if ctxs == 2 and deep == 2 * CH else 1
    size = deep // halves

    def place(other):
        def index(i, m):
            ctx, _, _, mpo = split_meta(m, images)
            chip = i * outer + lax.rem(mpo + other, outer)
            return 0, chip * halves + (ctx if halves == 2 else 0)

        return pl.BlockSpec((width, size), index)

    out = pl.BlockSpec((1, width, size), lambda i, m: (i, 0, 0))
    patch_out = in_hbm(patch_out)
    kept, sent = pl.pallas_call(
        columns_kernel,
        grid_spec=pltpu.PrefetchScalarGridSpec(
            num_scalar_prefetch=1, grid=(tiles,), in_specs=[place(0), place(1)], out_specs=[out, out]
        ),
        out_shape=[jax.ShapeDtypeStruct((tiles, width, size), BF16)] * 2,
        compiler_params=params(8),
        cost_estimate=cost(1 << 16, 2 << 20),
        name="columns",
    )(meta, patch_out, patch_out)
    return kept, sent, halves


def transpose_second(kept, received, step):
    tiles = lax.axis_size("tile")
    place = lax.rem(lax.axis_index("tile") + step, tiles)
    block = [lax.dynamic_index_in_dim(x, place, 0, keepdims=False) for x in (kept, received)]
    block = jnp.stack(block)
    return shift(block, "tile", step) if step else block


def gather_pair(first, second, state, step, extras=None):
    tiles = lax.axis_size("tile")
    found, moving = [{0: first}, {0: second}], [None, None]

    def launch(which, index):
        ring = found[which][2 * index]
        if index < tiles - 1:
            moving[which] = (shift(ring, "tile", 1), shift(ring, "mpo", 1))
        elif which:
            moving[which] = shift(found[which][2 * index - 1], "tile", 1)
        else:
            moving[which] = shift(ring, "mpo", 1)

    launch(0, 0)
    launch(1, 0)
    seen = first
    for index in range(1, tiles):
        for which in range(2):
            ring, cross = moving[which]
            ring, cross, seen = lax.optimization_barrier((ring, cross, seen))
            found[which][2 * index], found[which][2 * index - 1] = ring, cross
            seen = ring
            launch(which, index)
    entries = list(range(2 * tiles - 1))
    state = step([[found[0][e], found[1][e]] for e in entries], entries, state, False)
    last = lax.optimization_barrier((moving[0], moving[1], state, extras))
    return step([[last[0], last[1]]], [2 * tiles - 1], last[2], True), last[3]


def shards(
    text_embed,
    latents,
    down_conv,
    patch_in,
    norm_gain,
    query_weight,
    key_weight,
    value_weight,
    query_gain,
    key_gain,
    out_weight,
    patch_out,
    up_conv,
    span_start,
    image_of_slot,
):
    ctxs, tiles, outer = (lax.axis_size(name) for name in ("ctx", "tile", "mpo"))
    ctx, tile, mpo, core = (lax.axis_index(name) for name in ("ctx", "tile", "mpo", "core"))
    seq_rows, width = text_embed.shape
    half = seq_rows // 2
    images = span_start.shape[0]
    local = latents.shape[0]

    numbers = jnp.arange(images, dtype=jnp.int32)
    matches = image_of_slot[None, :] == numbers[:, None]
    slot_of_image = jnp.sum(jnp.where(matches, numbers[None, :], 0), axis=1)
    slot_place = lax.rem(ctx + ctxs - slot_of_image // local, ctxs) * local + slot_of_image % local
    meta = jnp.concatenate(
        [span_start, slot_place, image_of_slot, jnp.stack([ctx, core, tile, mpo])]
    ).astype(jnp.int32)
    layout = (images, tiles, outer)

    weights = [swap(w) for w in (key_weight, value_weight, query_weight)]
    pieces, conv, meta, weights[0], weights[1] = gather_small(latents, down_conv, meta, *weights[:2])
    later, pieces[1] = lax.optimization_barrier((meta, pieces[1]))
    kept, sent, halves = transpose_first(later, patch_out, layout, ctxs)
    pieces, sent = lax.optimization_barrier((pieces, sent))
    received = shift(sent, "mpo", 1)
    weights += [key_weight, value_weight, query_weight]
    streams = down_stream(meta, pieces, conv, patch_in, text_embed, norm_gain, weights, images)
    streams, held_weights = [streams[:2], streams[2:4]], streams[4:]
    streams, received = lax.optimization_barrier((streams, received))
    others = [swap(s[1]) for s in streams]
    others = lax.optimization_barrier(others)

    head_gains = jnp.stack([query_gain, key_gain])

    def project(blocks, entries, state, last):
        return qkv_step(
            meta, layout, blocks, entries, held_weights, state, head_gains
        )

    state, out_par = gather_pair(
        *[by_core(core, s[0], o, 1) for s, o in zip(streams, others)], None, project, swap(out_weight)
    )
    heads = width // HD
    kv_send, q_send = state[:heads], state[heads : 2 * heads]
    kv_own, q_own = state[2 * heads : 3 * heads], state[3 * heads :]

    def shifted(values, step, cross):
        pairs = [
            (2 * c + k, 2 * ((c + step) % ctxs) + (1 - k if cross else k))
            for c in range(ctxs)
            for k in range(2)
        ]
        return lax.ppermute(values, ("ctx", "core"), pairs)

    results = []
    for head in range(heads):
        q_par = swap(q_send[head])
        pieces = [kv_own[head], swap(kv_send[head])]
        for step in range(1, ctxs):
            pieces += [shifted(kv_own[head], step, False), shifted(kv_send[head], step, True)]
        q_par, q_send, kv_send, kv_own, kept, received = lax.optimization_barrier(
            (q_par, q_send, kv_send, kv_own, kept, received)
        )
        results.append(attention(meta, [q_own[head], q_par], pieces, images))
    up_blocks = [transpose_second(kept, received, step) for step in range(tiles)]
    att_own = [result[0] for result in results]
    att_par = [swap(result[1]) for result in results]
    rows = half // 2
    attended = []
    for at in (0, rows):
        own, par = (
            jnp.concatenate([x[at : at + rows] for x in side], axis=1) for side in (att_own, att_par)
        )
        attended.append(by_core(core, own, par, 1))
    attended, up_blocks = lax.optimization_barrier((attended, up_blocks))
    up_own = jnp.concatenate(up_blocks)
    extras = [up_own, swap(up_own)] + ([shift(up_own, "ctx", 1)] if halves == 2 else [])

    def project_out(blocks, entries, state, last):
        return out_step(meta, layout, blocks, entries, (out_weight, out_par), state, last)

    state = [streams[0][0], streams[1][0], others[0], others[1]]
    state, up_weights = gather_pair(*attended, state, project_out, extras)
    out_own, out_send = state
    out_other = swap(out_send)
    layer_out = by_core(core, out_own, out_other, 0)

    picks, swapped = lax.optimization_barrier(
        (pick_rows(meta, out_own, out_other, images, ctxs), [swap(other) for other in up_weights[2:]])
    )
    up_weights = [up_weights[:2]] + [[up_weights[2], other] for other in swapped]
    own_parts, par_parts = [picks[0]], [swap(picks[1])]
    for step in range(1, ctxs):
        own_parts.append(shifted(picks[2 * step], step, False))
        par_parts.append(shifted(picks[2 * step + 1], step, True))

    pixel = tile * outer + mpo
    pixels = jnp.stack([pixel * halves + lax.rem(ctx + h, halves) for h in range(halves)])
    spread_weight = spread_weights(up_conv, pixels)

    def project_up(blocks, entries, state, last):
        return up_step(blocks, entries, up_weights, state, spread_weight if last else None)

    state, _ = gather_pair(*merge_picks(own_parts, par_parts), None, project_up)

    bands = state.reshape(tiles, IMG_TOK // tiles, PIX * CIN)
    band = lax.dynamic_index_in_dim(bands, tile, 0, keepdims=False)
    for step in range(1, tiles):
        piece = lax.dynamic_index_in_dim(bands, lax.rem(tile + step, tiles), 0, keepdims=False)
        band = band + shift(piece, "tile", step)
    quad = {}
    for name, pairs in (
        ("mpo", [(0, 2), (1, 3), (2, 0), (3, 1)]),
        ("core", [(0, 1), (1, 0), (2, 3), (3, 2)]),
        ("both", [(0, 3), (1, 2), (2, 1), (3, 0)]),
    ):
        quad[name] = lax.ppermute(band, ("mpo", "core"), pairs)
    return layer_out, finish(meta[3 * images + 1 :], band, quad["mpo"], quad["core"], quad["both"])


def solution(mesh):
    ctxs, tiles, parts = mesh.devices.shape
    fine = Mesh(
        mesh.devices.reshape(ctxs, tiles, parts // 2, 2), ("ctx", "tile", "mpo", "core")
    )
    features = ("tile", "mpo", "core")
    return jax.shard_map(
        shards,
        mesh=fine,
        in_specs=(
            P("ctx", features),
            P("ctx", "tile", None),
            P(None, ("mpo", "core")),
            P(None, features),
            P(features),
            P(None, features),
            P(None, features),
            P(None, features),
            P(),
            P(),
            P(None, features),
            P(features, None),
            P(),
            P(),
            P(),
        ),
        out_specs=(P("ctx", features), P("ctx", "tile", None)),
        check_vma=False,
    )
```
